32 devices in a mesh: blk: 4 (over y, core), batch: 2 (over x), tensor: 4 (over z).
Axes of the slice: x: 2, y: 2, z: 4, core: 2. Of those that a mesh axis runs over, the one named last changes fastest.
Arguments:
- tokens: bfloat16 [6, 512, 768], P('batch', 'blk'), may hold values from -6 to 6
- out_grad: bfloat16 [6, 512, 768], P('batch', 'blk'), may hold values from -6 to 6
- bucket: int32 [6], P('batch'), may hold values from 0 to 1, as said below
- lengths: int32 [6, 4], P('batch'), may hold values from 1 to 512, as said below
- qkv_weight: bfloat16 [1, 3, 768, 768], P(None, None, ('blk', 'batch'), 'tensor'), may hold values from -0.21875 to 0.21875
- qv_bias: float32 [1, 2, 768], P(None, None, 'tensor'), may hold values from -3 to 3
- out_weight: bfloat16 [1, 768, 768], P(None, 'tensor', ('blk', 'batch')), may hold values from -0.625 to 0.625
- ff_in_weight: bfloat16 [1, 768, 3072], P(None, ('blk', 'batch'), 'tensor'), may hold values from -0.21875 to 0.21875
- ff_in_bias: float32 [1, 3072], P(None, 'tensor'), may hold values from -3 to 3
- ff_out_weight: bfloat16 [1, 3072, 768], P(None, 'tensor', ('blk', 'batch')), may hold values from -0.109375 to 0.109375
- branch_bias: float32 [1, 2, 768], replicated, may hold values from -3 to 3
- norm_gain: float32 [1, 2, 768], replicated, may hold values from 0.5 to 1.5
- norm_bias: float32 [1, 2, 768], replicated, may hold values from -3 to 3
Outputs:
- output: bfloat16 [6, 512, 768], P('batch', 'blk')
- tokens_grad: float32 [6, 512, 768], P('batch', 'blk')
- qkv_weight_grad: float32 [1, 3, 768, 768], P(None, None, ('blk', 'batch'), 'tensor')
- qv_bias_grad: float32 [1, 2, 768], P(None, None, 'tensor')
- out_weight_grad: float32 [1, 768, 768], P(None, 'tensor', ('blk', 'batch'))
- ff_in_weight_grad: float32 [1, 768, 3072], P(None, ('blk', 'batch'), 'tensor')
- ff_in_bias_grad: float32 [1, 3072], P(None, 'tensor')
- ff_out_weight_grad: float32 [1, 3072, 768], P(None, 'tensor', ('blk', 'batch'))
- branch_bias_grad: float32 [1, 2, 768], replicated
- norm_gain_grad: float32 [1, 2, 768], replicated
- norm_bias_grad: float32 [1, 2, 768], replicated
- stream_rms: float32 [1, 3], replicated
The draws below stay inside these ranges and needn't reach their ends.
Inputs may be any that keep to these rules, and one draw needn't show every extreme that they name: Each index of batch holds, among its 3 slots, exactly one of bucket 0, and its length is 512; all other slots are of bucket 1. `lengths`: for a slot of bucket 0 only column 0 counts; for bucket 1 column c is the valid length of the short sequence at positions c * 128 onward, at most 128.
All inputs are finite; a program needn't handle non-finite values.
Results may differ from the reference program's by a relative error of at most 0.019.
Values may be sent and summed in bfloat16 or wider, within the bound.
A program may use at most 64 MiB of HBM per device.

```python
import jax
import jax.numpy as jnp
from jax import lax

D = 768
HEADS = 12
HEAD = 64
FF = 3072
LAYERS = 1
SEQ = 512
SUB = 128
SEQ_DEV = 3
NSUB = 4
SEQS = 6
N_TENSOR = 4


def draw_plan(key):
    key_pick, key_short = jax.random.split(key, 2)
    groups = SEQS // SEQ_DEV
    chosen = jax.random.randint(key_pick, (groups,), 0, SEQ_DEV)
    forced_slot = jnp.repeat(jnp.arange(groups, dtype=jnp.int32) * SEQ_DEV + chosen, SEQ_DEV)
    is_forced = jnp.arange(SEQS, dtype=jnp.int32) == forced_slot
    bucket = jnp.where(is_forced, 0, 1)
    short_len = jax.random.randint(key_short, (SEQS, NSUB), 1, SUB + 1)
    column = jnp.arange(NSUB, dtype=jnp.int32)
    first = jnp.logical_and(is_forced[:, None], column[None, :] == 0)
    lengths = jnp.where(first, SEQ, short_len)
    return (bucket.astype(jnp.int32), lengths.astype(jnp.int32))


def draw_bucket(key, part):
    return draw_plan(key)[0]


def draw_lengths(key, part):
    return draw_plan(key)[1]


def block_scale(stream_key, extent, cuts, least, largest):
    level, own = 1.0, jax.random.fold_in(stream_key, 6)
    for position, blocks in cuts:
        draws = jnp.exp(jax.random.uniform(jax.random.fold_in(own, position), (blocks,), jnp.float32, least / len(cuts), largest / len(cuts)))
        level = level * jnp.repeat(draws, extent[position] // blocks).reshape([-1 if axis == position else 1 for axis in range(len(extent))])
    return level


def centred(own_key, dims, spread, bound, cuts=(), held_as=jnp.bfloat16):
    level = block_scale(own_key, dims, cuts, -0.22, 0.18) if cuts else 1.0
    drawn = jax.random.normal(own_key, dims, jnp.float32) * spread * level
    return jnp.minimum(jnp.maximum(drawn, -bound), bound).astype(held_as)


def setup_inputs(seed: int = 0) -> dict:
    key_list = jax.random.split(jax.random.key(seed), 14)
    return {
        "tokens": centred(key_list[0], (SEQS, SEQ, D), 1.0, 6.0, ((0, 2), (1, 4))),
        "out_grad": centred(key_list[1], (SEQS, SEQ, D), 1.0, 6.0, ((0, 2), (1, 4))),
        "bucket": draw_bucket(jax.random.fold_in(key_list[13], 71), 0),
        "lengths": draw_lengths(jax.random.fold_in(key_list[13], 71), 0),
        "qkv_weight": centred(key_list[4], (LAYERS, 3, D, D), D ** -0.5, 0.21875, ((2, 8), (3, 4))),
        "qv_bias": centred(key_list[5], (LAYERS, 2, D), 0.5, 3.0, ((2, 4),), jnp.float32),
        "out_weight": centred(key_list[6], (LAYERS, D, D), (D // 8) ** -0.5, 0.625, ((1, 4), (2, 8))),
        "ff_in_weight": centred(key_list[7], (LAYERS, D, FF), D ** -0.5, 0.21875, ((1, 8), (2, 4))),
        "ff_in_bias": centred(key_list[8], (LAYERS, FF), 0.5, 3.0, ((1, 4),), jnp.float32),
        "ff_out_weight": centred(key_list[9], (LAYERS, FF, D), FF ** -0.5, 0.109375, ((1, 4), (2, 8))),
        "branch_bias": centred(key_list[10], (LAYERS, 2, D), 0.5, 3.0, (), jnp.float32),
        "norm_gain": jnp.clip(1.0 + 0.1 * jax.random.normal(key_list[11], (LAYERS, 2, D), jnp.float32), 0.5, 1.5),
        "norm_bias": centred(key_list[12], (LAYERS, 2, D), 0.5, 3.0, (), jnp.float32),
    }


HIGH = lax.Precision.HIGHEST

@jax.custom_vjp
def low(v):
    return lax.optimization_barrier(v.astype(jnp.bfloat16)).astype(jnp.float32)

@jax.custom_vjp
def low_back(v):
    return v

def low_keep(v):
    return (low(v), None)

def low_pass(kept, grad):
    return (grad,)

def back_keep(v):
    return (v, None)

def back_low(kept, grad):
    return (low(grad),)
low.defvjp(low_keep, low_pass)
low_back.defvjp(back_keep, back_low)

def both_ways(value):
    return low(low_back(value))

def row_valid(bucket, lengths, pos):
    short = bucket[:, None] != 0
    pick = ((pos // SUB)[:, None] == jnp.arange(lengths.shape[1], dtype=jnp.int32)[None, :]).astype(jnp.int32)
    short_len = lax.optimization_barrier(jnp.sum(lengths[:, None, :] * pick[None, :, :], axis=2))
    limit = jnp.where(short, short_len, lengths[:, :1])
    place = jnp.where(short, (pos % SUB)[None, :], pos[None, :])
    return place < limit

def seq_mask(bucket, lengths, qpos, kpos):
    short = bucket[:, None, None] != 0
    same = qpos[:, None] // SUB == kpos[None, :] // SUB
    allowed = jnp.logical_or(jnp.logical_not(short), same[None, :, :])
    return jnp.logical_and(row_valid(bucket, lengths, kpos)[:, None, :], allowed)

def layer_norm(h, gain, shift):
    mean = lax.optimization_barrier(jnp.mean(h, -1, keepdims=True))
    cent = h - mean
    var = lax.optimization_barrier(jnp.mean(cent * cent, -1, keepdims=True))
    return cent * lax.rsqrt(var + 1e-12) * gain + shift

def attend(item):
    query, keys, values, bucket, lengths = item
    pos = jnp.arange(SEQ, dtype=jnp.int32)
    mask = seq_mask(bucket[None], lengths[None], pos, pos)[0]
    scores = jnp.einsum('qhe,khe->hqk', query, keys, precision=HIGH) * HEAD ** (-0.5)
    scores = low_back(jnp.where(mask[None], scores, -1e+30))
    prob = jax.nn.softmax(scores, axis=-1)
    return jnp.einsum('hqk,khe->qhe', low(prob), values, precision=HIGH)

def forward(x, params, bucket, lengths):
    qkv_w, qv_b, out_w, in_w, in_b, outf_w, br_b, gain, shift = params
    group = x.shape[0]
    pos = jnp.arange(SEQ, dtype=jnp.int32)
    valid_rows = row_valid(bucket, lengths, pos).astype(jnp.float32)[:, :, None]
    part_in = D // N_TENSOR
    part_ff = FF // N_TENSOR
    head_shape = (group, SEQ, HEADS, HEAD)
    stats = []
    for layer in range(LAYERS):
        xb = low(x)
        triple = jnp.einsum('gsd,cdk->cgsk', xb, qkv_w[layer], precision=HIGH)
        query = both_ways(triple[0] + qv_b[layer, 0])
        keys = both_ways(triple[1])
        values = both_ways(triple[2] + qv_b[layer, 1])
        att = lax.map(jax.checkpoint(attend), (query.reshape(head_shape), keys.reshape(head_shape), values.reshape(head_shape), bucket, lengths))
        att = both_ways(att.reshape(group, SEQ, N_TENSOR, part_in))
        pieces = jnp.einsum('gstk,tkd->gstd', att, out_w[layer].reshape(N_TENSOR, part_in, D), precision=HIGH)
        branch = low_back(lax.optimization_barrier(jnp.sum(low(pieces), 2)) + br_b[layer, 0])
        upper = layer_norm(x + branch, gain[layer, 0], shift[layer, 0])
        pre = low_back(jnp.einsum('gsd,df->gsf', low(upper), in_w[layer], precision=HIGH) + in_b[layer])
        act = low(jax.nn.gelu(pre, approximate=False))
        pieces = jnp.einsum('gstf,tfd->gstd', act.reshape(group, SEQ, N_TENSOR, part_ff), outf_w[layer].reshape(N_TENSOR, part_ff, D), precision=HIGH)
        feed = low_back(lax.optimization_barrier(jnp.sum(low(pieces), 2)) + br_b[layer, 1])
        stats.append(jnp.stack([jnp.sum(valid_rows * x * x), jnp.sum(valid_rows * branch * branch), jnp.sum(valid_rows * feed * feed)]))
        x = layer_norm(upper + feed, gain[layer, 1], shift[layer, 1])
    return (x, jnp.stack(stats))

def reference(tokens, out_grad, bucket, lengths, qkv_weight, qv_bias, out_weight, ff_in_weight, ff_in_bias, ff_out_weight, branch_bias, norm_gain, norm_bias):
    group = SEQS
    while group * SEQ > 4096 and group % 2 == 0:
        group = group // 2
    steps_count = SEQS // group
    params = tuple((p.astype(jnp.float32) for p in (qkv_weight, qv_bias, out_weight, ff_in_weight, ff_in_bias, ff_out_weight, branch_bias, norm_gain, norm_bias)))
    inputs = tokens.astype(jnp.float32).reshape(steps_count, group, SEQ, D)
    cotangents = out_grad.astype(jnp.float32).reshape(steps_count, group, SEQ, D)
    buckets = bucket.reshape(steps_count, group)
    lens = lengths.reshape(steps_count, group, NSUB)

    def one_group(carry, item):
        xin, cot, bk, ln = item

        def run(xx, *pp):
            return forward(xx, pp, bk, ln)
        result, back, stats = jax.vjp(run, xin, *params, has_aux=True)
        grads = back(cot)
        summed = tuple((c + g for c, g in zip(carry[0], grads[1:])))
        return ((summed, carry[1] + stats), (result.astype(jnp.bfloat16), grads[0]))
    init = (tuple((jnp.zeros_like(p) for p in params)), jnp.zeros((LAYERS, 3), jnp.float32))
    (totals, squares), (outs, dxs) = lax.scan(one_group, init, (inputs, cotangents, buckets, lens))
    count = jnp.sum(row_valid(bucket, lengths, jnp.arange(SEQ, dtype=jnp.int32)).astype(jnp.float32))
    rms = jnp.sqrt(squares / (count * D))
    return (outs.reshape(SEQS, SEQ, D), dxs.reshape(SEQS, SEQ, D), totals[0], totals[1], totals[2], totals[3], totals[4], totals[5], totals[6], totals[7], totals[8], rms)
```

```python
import functools

import jax
import jax.numpy as jnp
from jax import lax
from jax.experimental import pallas as pl
from jax.experimental.pallas import tpu as pltpu
from jax.sharding import PartitionSpec as P

HEAD = 64
SUB = 128


NEG = -1e30


def row_valid(bucket, lengths, pos):
    short = bucket[:, None] != 0
    pick = ((pos // SUB)[:, None] == jnp.arange(lengths.shape[1], dtype=jnp.int32)[None, :]).astype(
        jnp.int32
    )
    short_len = jnp.sum(lengths[:, None, :] * pick[None, :, :], axis=2)
    limit = jnp.where(short, short_len, lengths[:, :1])
    place = jnp.where(short, (pos % SUB)[None, :], pos[None, :])
    return place < limit


def seq_mask(bucket, lengths, qpos, kpos):
    short = bucket[:, None, None] != 0
    same = qpos[:, None] // SUB == kpos[None, :] // SUB
    allowed = jnp.logical_or(jnp.logical_not(short), same[None, :, :])
    return jnp.logical_and(row_valid(bucket, lengths, kpos)[:, None, :], allowed)


def layer_norm(h, gain, shift):
    mean = jnp.mean(h, -1, keepdims=True)
    cent = h - mean
    var = jnp.mean(cent * cent, -1, keepdims=True)
    return cent * lax.rsqrt(var + 1e-12) * gain + shift


def exact_gelu(value):
    return jax.nn.gelu(value, approximate=False)


def general_shards(
    tokens,
    out_grad,
    bucket,
    lengths,
    qkv_weight,
    qv_bias,
    out_weight,
    ff_in_weight,
    ff_in_bias,
    ff_out_weight,
    branch_bias,
    norm_gain,
    norm_bias,
):
    n_seq, rows_blk, width = tokens.shape
    blocks = lax.axis_size("blk")
    rank = lax.axis_index("blk")
    layers = qkv_weight.shape[0]
    local_width = qkv_weight.shape[3]
    heads_here = local_width // HEAD
    total_rows = n_seq * rows_blk
    scale = HEAD ** (-0.5)
    head_shape = (n_seq, rows_blk, heads_here, HEAD)
    qkv_full, out_full, ffin_full, ffout_full = (
        lax.all_gather(qkv_weight, ("blk", "batch"), axis=2, tiled=True),
        lax.all_gather(out_weight, ("blk", "batch"), axis=2, tiled=True),
        lax.all_gather(ff_in_weight, ("blk", "batch"), axis=1, tiled=True),
        lax.all_gather(ff_out_weight, ("blk", "batch"), axis=2, tiled=True),
    )
    local_pos = rank * rows_blk + jnp.arange(rows_blk, dtype=jnp.int32)
    row_ok = row_valid(bucket, lengths, local_pos).astype(jnp.float32).reshape(total_rows, 1)
    whole_pos = jnp.arange(blocks * rows_blk, dtype=jnp.int32)
    sub_bucket, sub_lengths = (bucket, lengths)

    def scores(query, keys, mask):
        found = (
            jnp.einsum("nqhe,nkhe->nhqk", query, keys, preferred_element_type=jnp.float32) * scale
        )
        return jnp.where(mask[:, None], found, NEG)

    x = tokens.astype(jnp.float32).reshape(total_rows, width)
    layer = 0
    xb = x.astype(jnp.bfloat16)
    triple = jnp.einsum("rd,cdk->crk", xb, qkv_full[layer], preferred_element_type=jnp.float32)
    query = (triple[0] + qv_bias[layer, 0]).astype(jnp.bfloat16).reshape(head_shape)
    keys = triple[1].astype(jnp.bfloat16).reshape(head_shape)
    values = (triple[2] + qv_bias[layer, 1]).astype(jnp.bfloat16).reshape(head_shape)
    pair = jnp.stack([keys, values])
    sub_query = query
    sub_pair = pair
    kept = lax.all_gather(sub_pair, "blk", axis=2, tiled=True)
    found = scores(sub_query, kept[0], seq_mask(sub_bucket, sub_lengths, local_pos, whole_pos))
    top = jnp.max(found, -1)
    sub_lse = top + jnp.log(jnp.sum(jnp.exp(found - top[..., None]), -1))
    weights = jnp.exp(found - sub_lse[..., None]).astype(jnp.bfloat16)
    sub_acc = jnp.einsum("nhqk,nkhe->nqhe", weights, kept[1], preferred_element_type=jnp.float32)
    lse = sub_lse
    acc = sub_acc
    att = acc.astype(jnp.bfloat16).reshape(total_rows, local_width)
    a_part = jnp.dot(att, out_full[layer], preferred_element_type=jnp.float32)
    branch = (
        lax.psum(a_part.astype(jnp.bfloat16), "tensor").astype(jnp.float32) + branch_bias[layer, 0]
    )
    upper_in = x + branch
    upper = layer_norm(upper_in, norm_gain[layer, 0], norm_bias[layer, 0])
    upper_b = upper.astype(jnp.bfloat16)
    pre = jnp.dot(upper_b, ffin_full[layer], preferred_element_type=jnp.float32) + ff_in_bias[layer]
    act = exact_gelu(pre).astype(jnp.bfloat16)
    f_part = jnp.dot(act, ffout_full[layer], preferred_element_type=jnp.float32)
    feed = (
        lax.psum(f_part.astype(jnp.bfloat16), "tensor").astype(jnp.float32) + branch_bias[layer, 1]
    )
    lower_in = upper + feed
    squares = [
        jnp.stack(
            [
                jnp.sum(row_ok * x * x),
                jnp.sum(row_ok * branch * branch),
                jnp.sum(row_ok * feed * feed),
            ]
        )
    ]
    saved = [(xb, query, pair, kept, lse, sub_lse, att, acc, upper_in, upper_b, pre, act, lower_in)]
    x = layer_norm(lower_in, norm_gain[layer, 1], norm_bias[layer, 1])
    output = x.astype(jnp.bfloat16).reshape(n_seq, rows_blk, width)
    grad = out_grad.astype(jnp.float32).reshape(total_rows, width)
    g_qkv, g_out, g_in, g_outf = ([], [], [], [])
    g_qvb, g_inb, g_branch, g_gain, g_shift = ([], [], [], [], [])
    for layer in reversed(range(layers)):
        xb, query, pair, kept, lse, sub_lse, att, acc, upper_in, upper_b, pre, act, lower_in = (
            saved[layer]
        )
        _, lower_back = jax.vjp(layer_norm, lower_in, norm_gain[layer, 1], norm_bias[layer, 1])
        d_lower, d_gain2, d_shift2 = lower_back(grad)
        d_feed = d_lower.astype(jnp.bfloat16)
        d_fbias = jnp.sum(d_feed.astype(jnp.float32), 0)
        g_outf.append(jnp.einsum("rf,rd->fd", act, d_feed, preferred_element_type=jnp.float32))
        d_act = jnp.einsum(
            "rd,fd->rf", d_feed, ffout_full[layer], preferred_element_type=jnp.float32
        )
        _, gelu_back = jax.vjp(exact_gelu, pre)
        d_pre = gelu_back(d_act)[0].astype(jnp.bfloat16)
        g_inb.append(jnp.sum(d_pre.astype(jnp.float32), 0))
        g_in.append(jnp.einsum("rd,rf->df", upper_b, d_pre, preferred_element_type=jnp.float32))
        ffn_part = jnp.einsum(
            "rf,df->rd", d_pre, ffin_full[layer], preferred_element_type=jnp.float32
        )
        d_upper = d_lower + lax.psum(ffn_part.astype(jnp.bfloat16), "tensor").astype(jnp.float32)
        _, upper_back = jax.vjp(layer_norm, upper_in, norm_gain[layer, 0], norm_bias[layer, 0])
        d_upper_in, d_gain1, d_shift1 = upper_back(d_upper)
        d_branch = d_upper_in.astype(jnp.bfloat16)
        d_abias = jnp.sum(d_branch.astype(jnp.float32), 0)
        g_out.append(jnp.einsum("rk,rd->kd", att, d_branch, preferred_element_type=jnp.float32))
        d_att = (
            jnp.einsum("rd,kd->rk", d_branch, out_full[layer], preferred_element_type=jnp.float32)
            .astype(jnp.bfloat16)
            .reshape(head_shape)
        )
        delta = jnp.einsum("nqhe,nqhe->nhq", d_att.astype(jnp.float32), acc)
        sub_query, sub_datt, sub_delta = (query, d_att, delta)
        block_keys = kept[0]
        block_found = scores(
            sub_query, block_keys, seq_mask(sub_bucket, sub_lengths, local_pos, whole_pos)
        )
        prob = jnp.exp(block_found - sub_lse[..., None])
        d_prob = jnp.einsum(
            "nqhe,nkhe->nhqk", sub_datt, kept[1], preferred_element_type=jnp.float32
        )
        d_scores = (prob * (d_prob - sub_delta[..., None])).astype(jnp.bfloat16)
        d_query = jnp.einsum(
            "nhqk,nkhe->nqhe", d_scores, block_keys, preferred_element_type=jnp.float32
        )
        d_keys = jnp.einsum(
            "nhqk,nqhe->nkhe", d_scores, sub_query, preferred_element_type=jnp.float32
        )
        d_values = jnp.einsum(
            "nhqk,nqhe->nkhe",
            prob.astype(jnp.bfloat16),
            sub_datt,
            preferred_element_type=jnp.float32,
        )
        sub_dq = d_query
        dpair_all = jnp.stack([d_keys * scale, d_values])
        sub_dpair = lax.psum_scatter(
            dpair_all.astype(jnp.bfloat16), "blk", scatter_dimension=2, tiled=True
        ).astype(jnp.float32)
        d_query, d_pair = (sub_dq, sub_dpair)
        dq_b = (d_query * scale).astype(jnp.bfloat16).reshape(total_rows, local_width)
        dk_b = d_pair[0].astype(jnp.bfloat16).reshape(total_rows, local_width)
        dv_b = d_pair[1].astype(jnp.bfloat16).reshape(total_rows, local_width)
        d_triple = jnp.stack([dq_b, dk_b, dv_b])
        g_qvb.append(
            jnp.stack([jnp.sum(dq_b.astype(jnp.float32), 0), jnp.sum(dv_b.astype(jnp.float32), 0)])
        )
        g_qkv.append(jnp.einsum("rd,crk->cdk", xb, d_triple, preferred_element_type=jnp.float32))
        attn_part = jnp.einsum(
            "crk,cdk->rd", d_triple, qkv_full[layer], preferred_element_type=jnp.float32
        )
        grad = d_upper_in + lax.psum(attn_part.astype(jnp.bfloat16), "tensor").astype(jnp.float32)
        g_branch.append(jnp.stack([d_abias, d_fbias]))
        g_gain.append(jnp.stack([d_gain1, d_gain2]))
        g_shift.append(jnp.stack([d_shift1, d_shift2]))

    def in_order(items):
        return jnp.stack(items[::-1])

    qkv_g, out_g, in_g, outf_g = (
        lax.psum_scatter(in_order(g_qkv), ("blk", "batch"), scatter_dimension=2, tiled=True),
        lax.psum_scatter(in_order(g_out), ("blk", "batch"), scatter_dimension=2, tiled=True),
        lax.psum_scatter(in_order(g_in), ("blk", "batch"), scatter_dimension=1, tiled=True),
        lax.psum_scatter(in_order(g_outf), ("blk", "batch"), scatter_dimension=2, tiled=True),
    )
    count = jnp.sum(row_ok)
    qvb_g, inb_g, branch_g, gain_g, shift_g, square_sums, count_all = lax.psum(
        (
            in_order(g_qvb),
            in_order(g_inb),
            in_order(g_branch),
            in_order(g_gain),
            in_order(g_shift),
            jnp.stack(squares),
            count,
        ),
        ("blk", "batch"),
    )
    rms = jnp.sqrt(square_sums / (count_all * width))
    tokens_grad = grad.reshape(n_seq, rows_blk, width)
    return (
        output,
        tokens_grad,
        qkv_g,
        qvb_g,
        out_g,
        in_g,
        inb_g,
        outf_g,
        branch_g,
        gain_g,
        shift_g,
        rms,
    )


MESH = pl.DeviceIdType.MESH
F32 = jnp.float32
BF16 = jnp.bfloat16
N_SEM = 160


def dot_nn(a, b):
    return lax.dot_general(a, b, (((1,), (0,)), ((), ())), preferred_element_type=F32)


def dot_nt(a, b):
    return lax.dot_general(a, b, (((1,), (1,)), ((), ())), preferred_element_type=F32)


def dot_tn(a, b):
    return lax.dot_general(a, b, (((0,), (0,)), ((), ())), preferred_element_type=F32)


def slot_order(bucket_ref):
    first = jnp.where(bucket_ref[0] == 0, 0, jnp.where(bucket_ref[1] == 0, 1, 2))
    second = jnp.where(first == 0, 1, 0)
    third = jnp.where(first == 2, 1, 2)
    return first, second, third


class Net:
    def __init__(self, send_sems, recv_sems):
        self.send_sems, self.recv_sems, self.copies = send_sems, recv_sems, []

    def send(self, src, dst, peer):
        at = len(self.copies)
        assert at < N_SEM
        copy = pltpu.make_async_remote_copy(
            src_ref=src,
            dst_ref=dst,
            send_sem=self.send_sems.at[at],
            recv_sem=self.recv_sems.at[at],
            device_id=peer,
            device_id_type=MESH,
        )
        copy.start()
        self.copies.append(copy)
        return copy

    def finish(self):
        for copy in self.copies:
            copy.wait_send()


def fused_kernel(
    bucket,
    lengths,
    tokens,
    out_grad,
    qkv_w,
    out_w,
    ffi_w,
    ffo_w,
    qv_bias,
    ffi_b,
    br_bias,
    gain,
    shift,
    out_o,
    tg_o,
    gq_o,
    go_o,
    gi_o,
    gf_o,
    vec_o,
    qvb_o,
    tok,
    cot,
    w_q,
    w_o,
    w_i,
    w_f,
    own_o,
    bias_r,
    xs,
    xs_t,
    q_r,
    k_r,
    v_r,
    kv_a,
    p_a,
    p_b,
    att,
    att_r,
    part,
    rs_s,
    rs_r,
    ab,
    xh1,
    rstd1,
    yb,
    act,
    gp,
    dh2,
    dfb,
    df_t,
    yb_t,
    dpre,
    dh1,
    da_t,
    datt,
    datt_s,
    dkv_s,
    dkv_r,
    dtri,
    dx_p,
    dx_s,
    dx_r,
    g_q,
    g_o,
    g_i,
    g_f,
    d_q,
    d_o,
    d_i,
    d_f,
    h_q,
    h_o,
    h_i,
    h_f,
    c_q,
    c_o,
    c_i,
    c_f,
    z_o,
    z_i,
    z_f,
    t_o,
    t_i,
    t_f,
    vs,
    vr,
    qs,
    qr,
    local_sems,
    send_sems,
    recv_sems,
):
    width = tok.shape[2]
    n_rows = tok.shape[1]
    blk_rows = ffi_w.shape[0]
    head_w = qkv_w.shape[2]
    heads = head_w // HEAD
    half, quart = n_rows // 2, n_rows // 4
    n_seq = tok.shape[0]
    tile = 256
    n_tile = width // tile
    scale = HEAD ** (-0.5)

    r = lax.axis_index("blk")
    t = lax.axis_index("batch")
    z = lax.axis_index("tensor")
    yy, c = r // 2, r % 2
    pz, qz = z // 2, z % 2
    r1, r2, r3 = r + 1 - 2 * c, (r + 2) % 4, 3 - r
    z1, z2, z3 = z + 1 - 2 * qz, (z + 2) % 4, 3 - z
    core, xnb, ynb, dnb = (r1, t, z), (r, 1 - t, z), (r2, t, z), (r2, 1 - t, z)
    yc = (r3, t, z)
    zn1, zn2, zn3 = (r, t, z1), (r, t, z2), (r, t, z3)
    peers = (core, xnb, ynb, dnb, yc, zn1, zn2, zn3)

    barrier = pltpu.get_barrier_semaphore()
    for peer in peers:
        pl.semaphore_signal(barrier, inc=1, device_id=peer, device_id_type=MESH)

    net = Net(send_sems, recv_sems)

    def rows_of(rr, tt):
        return pl.ds(pl.multiple_of((rr * 2 + tt) * blk_rows, 32), blk_rows)

    own = rows_of(r, t)
    blk_x, blk_y, blk_d = rows_of(r, 1 - t), rows_of(r2, t), rows_of(r2, 1 - t)
    near = (xnb, ynb, dnb)
    near_blk = (blk_x, blk_y, blk_d)

    local = [
        pltpu.make_async_copy(out_w, own_o, local_sems.at[0]),
        pltpu.make_async_copy(tokens, tok, local_sems.at[1]),
        pltpu.make_async_copy(qkv_w, w_q.at[:, own], local_sems.at[2]),
        pltpu.make_async_copy(ffi_w, w_i.at[0, own], local_sems.at[3]),
        pltpu.make_async_copy(ffo_w, w_f.at[0, own], local_sems.at[4]),
        pltpu.make_async_copy(out_grad, cot, local_sems.at[5]),
    ]
    for copy in local:
        copy.start()

    pl.semaphore_wait(barrier, len(peers))

    q_near = [net.send(qkv_w, w_q.at[:, own], peer) for peer in near]
    q_core = net.send(qkv_w, w_q.at[:, own], core)
    local[0].wait()
    w_o[0, own] = jnp.transpose(own_o[...])
    zo = net.send(w_o.at[0, own], w_o.at[1, own], zn2)
    zi = net.send(ffi_w, w_i.at[1, own], zn2)
    zf = net.send(ffo_w, w_f.at[1, own], zn2)
    zb = net.send(ffi_b, bias_r, zn2)

    def spread(buf, shard, src=None):
        at = buf.at[shard, own]
        src = at if src is None else src
        return [net.send(src, at, peer) for peer in near] + [net.send(src, at, core)]

    def pass_on(buf, shard, copies):
        later = []
        for copy, block in zip(copies, near_blk):
            copy.wait_recv()
            later.append(net.send(buf.at[shard, block], buf.at[shard, block], core))
        return later + [copies[3]]

    local[1].wait()
    order = slot_order(bucket)
    for s in range(n_seq):
        xs[s * n_rows : (s + 1) * n_rows] = tok[order[s]]
    xs_t[...] = jnp.transpose(xs[...])

    q_pass = []
    for copy, block in zip(q_near, near_blk):
        copy.wait_recv()
        q_pass.append(net.send(w_q.at[:, block], w_q.at[:, block], core))
    w_o0 = spread(w_o, 0)
    w_i0 = spread(w_i, 0, ffi_w)
    local[2].wait()
    q_core.wait_recv()
    for copy in q_pass:
        copy.wait_recv()

    k_r[...] = dot_nn(xs[...], w_q[1]).astype(BF16)
    v_r[...] = (dot_nn(xs[...], w_q[2]) + qv_bias[1:2, :]).astype(BF16)
    mine = pl.ds(pl.multiple_of(r * n_rows, n_rows), n_rows)
    kv_a[0, mine] = k_r[0:n_rows]
    kv_a[1, mine] = v_r[0:n_rows]
    kv = [net.send(kv_a.at[:, mine], kv_a.at[:, mine], peer) for peer in (core, ynb, yc)]
    q_r[...] = (dot_nn(xs[...], w_q[0]) + qv_bias[0:1, :]).astype(BF16)

    lane_head = lax.broadcasted_iota(jnp.int32, (1, head_w), 1) // HEAD

    def of_head(value, h):
        return jnp.where(lane_head == h, value, jnp.zeros_like(value))

    def limit_of(s):
        index = order[s]
        return lengths[index, r], lengths[index, 0]

    own_half = pl.ds(pl.multiple_of(pz * half, half), half)
    other_half = pl.ds(pl.multiple_of((1 - pz) * half, half), half)

    def attend(s, keys, values, probs, key_ok):
        query = q_r[s * n_rows : (s + 1) * n_rows]
        total = jnp.zeros((n_rows, head_w), F32)
        for h in range(heads):
            score = dot_nt(of_head(query, h), keys) * scale
            if key_ok is not None:
                score = jnp.where(key_ok, score, NEG)
            e = jnp.exp(score - jnp.max(score, -1, keepdims=True))
            prob = e / jnp.sum(e, -1, keepdims=True)
            probs[h] = prob
            total = total + dot_nn(prob.astype(BF16), of_head(values, h))
        att[s] = total.astype(BF16)
        return net.send(att.at[s, other_half], att_r.at[s], zn2)

    att_x = [None] * n_seq
    key_at = lax.broadcasted_iota(jnp.int32, (1, n_rows), 1)
    for s in range(1, n_seq):
        here = slice(s * n_rows, (s + 1) * n_rows)
        key_ok = key_at < limit_of(s)[0]
        att_x[s] = attend(s, k_r[here], v_r[here], p_b.at[s - 1], key_ok)

    pass_o0 = pass_on(w_o, 0, w_o0)
    zo.wait_recv()
    w_o1 = spread(w_o, 1)
    zi.wait_recv()
    w_i1 = spread(w_i, 1)
    for copy in kv:
        copy.wait_recv()
    att_x[0] = attend(0, kv_a[0], kv_a[1], p_a, None)
    w_f0 = spread(w_f, 0, ffo_w)
    zf.wait_recv()
    w_f1 = spread(w_f, 1)
    pass_o1 = pass_on(w_o, 1, w_o1)
    for copy in pass_o0 + pass_o1:
        copy.wait_recv()

    def owned(s, q):
        return pl.ds(pl.multiple_of(s * half + q * quart, quart), quart)

    def pair_send(k, s):
        rs_s[k, s] = part[owned(s, 1 - qz)].astype(BF16)
        return net.send(rs_s.at[k, s], rs_r.at[k, s], zn1)

    def pair_back(k, s, copy):
        copy.wait_recv()
        here = owned(s, qz)
        ab[k, here] = (part[here] + rs_r[k, s].astype(F32)).astype(BF16)
        return net.send(ab.at[k, here], ab.at[k, here], zn1)

    slots = (1, 2, 0)
    moved = {}
    for s in slots:
        att_x[s].wait_recv()
        part[s * half : (s + 1) * half] = dot_nt(att[s, own_half], w_o[0]) + dot_nt(
            att_r[s], w_o[1]
        )
        moved[s] = pair_send(0, s)
    back = {s: pair_back(0, s, moved[s]) for s in slots}

    pass_i = pass_on(w_i, 0, w_i0)
    ones = jnp.ones((1, width), F32)
    sums = [jnp.zeros((1, width), F32) for _ in range(4)]
    row_at = lax.broadcasted_iota(jnp.int32, (half, 1), 0)
    oks = []

    def column_sum(value):
        return jnp.sum(value, 0, keepdims=True)

    def normed(h):
        mean = jnp.mean(h, -1, keepdims=True)
        cent = h - mean
        rstd = lax.rsqrt(jnp.mean(cent * cent, -1, keepdims=True) + 1e-12)
        return cent * rstd, rstd

    for s in range(n_seq):
        short, full = limit_of(s)
        place = row_at + pz * half
        if s == 0:
            ok = (place + r * n_rows < full).astype(F32)
        else:
            ok = (place < short).astype(F32)
        oks.append(ok)
    for s in slots:
        back[s].wait_recv()
        here = slice(s * half, (s + 1) * half)
        x = xs[pl.ds(pl.multiple_of(s * n_rows + pz * half, half), half)].astype(F32)
        branch = ab[0, here].astype(F32) + br_bias[0:1, :]
        sums[0] = sums[0] + column_sum(oks[s] * (x * x))
        sums[1] = sums[1] + column_sum(oks[s] * (branch * branch))
        sums[3] = sums[3] + column_sum(oks[s] * ones)
        hat, rstd = normed(x + branch)
        xh1[here] = hat
        rstd1[here] = rstd
        yb[here] = (hat * gain[0:1, :] + shift[0:1, :]).astype(BF16)

    pass_i = pass_i + pass_on(w_i, 1, w_i1)
    zb.wait_recv()
    local[3].wait()
    for copy in pass_i:
        copy.wait_recv()
    for k in range(2):
        for n in range(n_tile):
            cols = slice(n * tile, (n + 1) * tile)
            bias = ffi_b[:, cols] if k == 0 else bias_r[:, cols]
            pre = dot_nn(yb[...], w_i[k, :, cols]) + bias
            phi = 0.5 * (1.0 + lax.erf(pre * (0.5**0.5)))
            act[k, :, cols] = (pre * phi).astype(BF16)
            gp[k, :, cols] = phi + pre * (jnp.exp(-0.5 * pre * pre) * 0.3989422804014327)

    pass_f = pass_on(w_f, 0, w_f0) + pass_on(w_f, 1, w_f1)
    local[4].wait()
    for copy in pass_f:
        copy.wait_recv()
    for n in range(n_tile):
        cols = slice(n * tile, (n + 1) * tile)
        part[:, cols] = dot_nt(act[0], w_f[0, cols]) + dot_nt(act[1], w_f[1, cols])
    moved = {s: pair_send(1, s) for s in slots}
    yb_t[...] = jnp.transpose(yb[...])
    back = {s: pair_back(1, s, moved[s]) for s in slots}
    local[5].wait()
    vec = {k: jnp.zeros((1, width), F32) for k in range(3)}
    for s in slots:
        back[s].wait_recv()
        here = slice(s * half, (s + 1) * half)
        feed = ab[1, here].astype(F32) + br_bias[1:2, :]
        sums[2] = sums[2] + column_sum(oks[s] * (feed * feed))
        hat, rstd = normed(xh1[here] * gain[0:1, :] + shift[0:1, :] + feed)
        out_o[s, own_half] = (hat * gain[1:2, :] + shift[1:2, :]).astype(BF16)
        g = cot[order[s], own_half].astype(F32)
        vec[1] = vec[1] + column_sum(g * hat)
        vec[2] = vec[2] + column_sum(g)
        g = g * gain[1:2, :]
        d = rstd * (
            g - jnp.mean(g, -1, keepdims=True) - hat * jnp.mean(g * hat, -1, keepdims=True)
        )
        dh2[here] = d
        d = d.astype(BF16)
        dfb[here] = d
        vec[0] = vec[0] + column_sum(d.astype(F32))
    out_x = net.send(out_o.at[:, own_half], out_o.at[:, own_half], zn2)
    for k in range(3):
        vs[0, k : k + 1] = vec[k]
    for k in range(4):
        vs[0, 8 + k : 9 + k] = sums[k]
    vs[0, 12:16] = jnp.zeros((4, width), F32)

    for k in range(2):
        for n in range(n_tile):
            cols = slice(n * tile, (n + 1) * tile)
            d = (dot_nn(dfb[...], w_f[k, :, cols]) * gp[k, :, cols]).astype(BF16)
            dpre[k, :, cols] = d
            vs[0, 3 + k : 4 + k, cols] = column_sum(d.astype(F32))
    for n in range(n_tile):
        cols = slice(n * tile, (n + 1) * tile)
        part[:, cols] = dot_nt(dpre[0], w_i[0, cols]) + dot_nt(dpre[1], w_i[1, cols])
    moved = {s: pair_send(2, s) for s in slots}

    def grads(lhs, rhs, out):
        value = dot_nn(lhs, rhs).astype(BF16)
        for b in range(8):
            out[b // 4, (b // 2) % 2, b % 2] = value[b * blk_rows : (b + 1) * blk_rows]

    def to_core(g, d):
        return net.send(g.at[:, 1 - c], d, core)

    def to_chip(g, d, h, got, copy):
        copy.wait_recv()
        for a in range(2):
            for b in range(2):
                h[a, b] = (g[a, c, b].astype(F32) + d[a, b].astype(F32)).astype(BF16)
        blocks = ((yy, 1 - t), (1 - yy, t), (1 - yy, 1 - t))
        return [
            net.send(h.at[a, b], got.at[k], peer) for k, ((a, b), peer) in enumerate(zip(blocks, near))
        ]

    def summed(h, got, copies):
        for copy in copies:
            copy.wait_recv()
        total = h[yy, t].astype(F32)
        for k in range(3):
            total = total + got[k].astype(F32)
        return total

    df_t[...] = jnp.transpose(dfb[...])
    for k in range(2):
        for n in range(n_tile):
            cols = slice(n * tile, (n + 1) * tile)
            grads(df_t[...], act[k, :, cols], g_f.at[k, :, :, :, :, cols])
    core_f = [to_core(g_f.at[k], d_f.at[k]) for k in range(2)]
    back = {s: pair_back(2, s, moved[s]) for s in slots}
    for k in range(2):
        for n in range(n_tile):
            cols = slice(n * tile, (n + 1) * tile)
            grads(yb_t[...], dpre[k, :, cols], g_i.at[k, :, :, :, :, cols])
    core_i = [to_core(g_i.at[k], d_i.at[k]) for k in range(2)]
    chip_f = [to_chip(g_f.at[k], d_f.at[k], h_f.at[k], c_f.at[k], core_f[k]) for k in (1, 0)][::-1]

    vec = {k: jnp.zeros((1, width), F32) for k in range(3)}
    for s in slots:
        back[s].wait_recv()
        here = slice(s * half, (s + 1) * half)
        hat = xh1[here]
        g = dh2[here] + ab[2, here].astype(F32)
        vec[1] = vec[1] + column_sum(g * hat)
        vec[2] = vec[2] + column_sum(g)
        g = g * gain[0:1, :]
        d = rstd1[here] * (
            g - jnp.mean(g, -1, keepdims=True) - hat * jnp.mean(g * hat, -1, keepdims=True)
        )
        dh1[here] = d
        d = d.astype(BF16)
        dfb[here] = d
        vec[0] = vec[0] + column_sum(d.astype(F32))
    for k in range(3):
        vs[0, 5 + k : 6 + k] = vec[k]
    d_r = dot_nn(dfb[...], w_o[1]).astype(BF16)
    for s in range(n_seq):
        datt_s[s] = d_r[s * half : (s + 1) * half]
    datt_x = net.send(datt_s, datt.at[:, own_half], zn2)
    d_l = dot_nn(dfb[...], w_o[0]).astype(BF16)
    for s in range(n_seq):
        datt[s, own_half] = d_l[s * half : (s + 1) * half]
    v_copy = net.send(vs.at[0], vr.at[0], core)

    da_t[...] = jnp.transpose(dfb[...])
    for s in range(n_seq):
        part_l = att[s, own_half] if s == 0 else jnp.concatenate([part_l, att[s, own_half]], 0)
        part_r = att_r[s] if s == 0 else jnp.concatenate([part_r, att_r[s]], 0)
    grads(da_t[...], part_l, g_o.at[0])
    grads(da_t[...], part_r, g_o.at[1])
    core_o = [to_core(g_o.at[k], d_o.at[k]) for k in range(2)]
    chip_i = [to_chip(g_i.at[k], d_i.at[k], h_i.at[k], c_i.at[k], core_i[k]) for k in (1, 0)][::-1]

    def v_step(k, copy):
        copy.wait_recv()
        vs[k + 1] = vs[k] + vr[k]

    v_step(0, v_copy)
    v_copy = net.send(vs.at[1], vr.at[1], xnb)

    def attend_back(s, keys, values, probs):
        query = q_r[s * n_rows : (s + 1) * n_rows]
        d_att = datt[s]
        dq = jnp.zeros((n_rows, head_w), F32)
        dk = jnp.zeros(keys.shape, F32)
        dv = jnp.zeros(keys.shape, F32)
        for h in range(heads):
            prob = probs[h]
            d_h = of_head(d_att, h)
            dp = dot_nt(d_h, values)
            delta = jnp.sum(prob * dp, -1, keepdims=True)
            ds = (prob * (dp - delta)).astype(BF16)
            dq = dq + dot_nn(ds, of_head(keys, h))
            dk = dk + dot_tn(ds, of_head(query, h))
            dv = dv + dot_tn(prob.astype(BF16), d_h)
        return (dq * scale).astype(BF16), (dk * scale).astype(BF16), dv.astype(BF16)

    datt_x.wait_recv()
    dq, dk, dv = attend_back(0, kv_a[0], kv_a[1], p_a)
    dtri[0, 0:n_rows] = dq
    for a in range(4):
        dkv_s[a, 0] = dk[a * n_rows : (a + 1) * n_rows]
        dkv_s[a, 1] = dv[a * n_rows : (a + 1) * n_rows]
    dkv = [
        net.send(dkv_s.at[to], dkv_r.at[k], peer)
        for k, (to, peer) in enumerate(((r1, core), (r2, ynb), (r3, yc)))
    ]
    for s in range(1, n_seq):
        here = slice(s * n_rows, (s + 1) * n_rows)
        dq, dk, dv = attend_back(s, k_r[here], v_r[here], p_b.at[s - 1])
        dtri[0, here] = dq
        dtri[1, here] = dk
        dtri[2, here] = dv

    def dx_send(s):
        here = slice(s * n_rows, (s + 1) * n_rows)
        total = dot_nt(dtri[0, here], w_q[0])
        for k in range(1, 3):
            total = total + dot_nt(dtri[k, here], w_q[k])
        dx_p[s] = total
        for a in range(4):
            dx_s[a, s] = total[a * quart : (a + 1) * quart].astype(BF16)
        return [
            net.send(dx_s.at[to, s], dx_r.at[k, s], peer)
            for k, (to, peer) in enumerate(((z1, zn1), (z2, zn2), (z3, zn3)))
        ]

    my_quart = pl.ds(pl.multiple_of(z * quart, quart), quart)

    def dx_back(s, copies):
        for copy in copies:
            copy.wait_recv()
        total = dx_p[s, my_quart] + dh1[owned(s, qz)]
        for k in range(3):
            total = total + dx_r[k, s].astype(F32)
        tg_o[s, my_quart] = total.astype(BF16)
        at = tg_o.at[s, my_quart]
        return [net.send(at, at, peer) for peer in (zn1, zn2, zn3)]

    dx_go = {s: dx_send(s) for s in (1, 2)}
    v_step(1, v_copy)
    v_copy = net.send(vs.at[2], vr.at[2], ynb)
    for copy in dkv:
        copy.wait_recv()
    for k in range(2):
        total = dkv_s[r, k].astype(F32)
        for a in range(3):
            total = total + dkv_r[a, k].astype(F32)
        dtri[1 + k, 0:n_rows] = total.astype(BF16)
    dx_go[0] = dx_send(0)
    qs[0] = jnp.zeros(qs.shape[1:], F32)
    qs[0, 0:1] = column_sum(dtri[0].astype(F32))
    qs[0, 1:2] = column_sum(dtri[2].astype(F32))
    q_copy = net.send(qs.at[0], qr.at[0], core)
    for k in range(3):
        grads(xs_t[...], dtri[k], g_q.at[:, :, :, k])
    core_q = to_core(g_q, d_q)
    chip_o = [to_chip(g_o.at[k], d_o.at[k], h_o.at[k], c_o.at[k], core_o[k]) for k in (1, 0)][::-1]
    tg_back = [dx_back(s, dx_go[s]) for s in (1, 2)]
    q_copy.wait_recv()
    qs[1] = qs[0] + qr[0]
    q_copy = net.send(qs.at[1], qr.at[1], xnb)
    chip_q = to_chip(g_q, d_q, h_q, c_q, core_q)
    tg_back.append(dx_back(0, dx_go[0]))
    v_step(2, v_copy)
    v_copy = net.send(vs.at[3], vr.at[3], zn2)
    q_copy.wait_recv()
    qs[2] = qs[1] + qr[1]
    q_copy = net.send(qs.at[2], qr.at[2], ynb)

    to_z = []
    for h, got, chips, sent, back_z in (
        (h_f, c_f, chip_f, t_f, z_f),
        (h_i, c_i, chip_i, t_i, z_i),
        (h_o, c_o, chip_o, t_o, z_o),
    ):
        sent[...] = summed(h.at[1], got.at[1], chips[1]).astype(BF16)
        to_z.append(net.send(sent, back_z, zn2))
    results = []
    for h, got, chips, out in (
        (h_f, c_f, chip_f, gf_o),
        (h_i, c_i, chip_i, gi_o),
        (h_o, c_o, chip_o, go_o),
    ):
        out[...] = summed(h.at[0], got.at[0], chips[0])
    gq_o[...] = summed(h_q, c_q, chip_q)
    v_copy.wait_recv()
    total = vs[3] + vr[3]
    vec_o[...] = total
    vec_o[3:4] = vs[3, 3:4] + vr[3, 4:5]
    vec_o[4:5] = vs[3, 4:5] + vr[3, 3:4]
    q_copy.wait_recv()
    qvb_o[...] = qs[2] + qr[2]
    for copy, out, back_z in zip(to_z, (gf_o, gi_o, go_o), (z_f, z_i, z_o)):
        copy.wait_recv()
        out[...] = out[...] + back_z[...].astype(F32)
    for copies in tg_back:
        for copy in copies:
            copy.wait_recv()
    out_x.wait_recv()
    net.finish()


def finish_kernel(
    bucket,
    out_i,
    tg_i,
    gq_i,
    go_i,
    gi_i,
    gf_i,
    vec_i,
    qvb_i,
    out_o,
    tg_o,
    gq_o,
    qvb_o,
    go_o,
    gi_o,
    inb_o,
    gf_o,
    br_o,
    gain_o,
    shift_o,
    rms_o,
):
    order = slot_order(bucket)
    for s in range(3):
        at = jnp.where(order[0] == s, 0, jnp.where(order[1] == s, 1, 2))
        out_o[s] = out_i[at]
        tg_o[s] = tg_i[at].astype(F32)
    gq_o[...] = gq_i[...]
    go_o[...] = jnp.transpose(go_i[...])
    gi_o[...] = gi_i[...]
    gf_o[...] = gf_i[...]
    qvb_o[...] = qvb_i[0:2]
    inb_o[...] = vec_i[3:4]
    br_o[0:1] = vec_i[5:6]
    br_o[1:2] = vec_i[0:1]
    gain_o[0:1] = vec_i[6:7]
    gain_o[1:2] = vec_i[1:2]
    shift_o[0:1] = vec_i[7:8]
    shift_o[1:2] = vec_i[2:3]
    width = vec_i.shape[1]
    count = vec_i[11:12, 0:1]
    square = jnp.sum(vec_i[8:11], 1, keepdims=True)
    rms = jnp.sqrt(square / (count * width))
    lane = lax.broadcasted_iota(jnp.int32, (1, 3), 1)
    out = jnp.zeros((1, 3), F32)
    for k in range(3):
        out = jnp.where(lane == k, rms[k : k + 1], out)
    rms_o[...] = out


def fused_shards(
    tokens,
    out_grad,
    bucket,
    lengths,
    qkv_weight,
    qv_bias,
    out_weight,
    ff_in_weight,
    ff_in_bias,
    ff_out_weight,
    branch_bias,
    norm_gain,
    norm_bias,
):
    n_seq, n_rows, width = tokens.shape
    blk_rows, head_w = qkv_weight.shape[2:]
    ff = ff_in_weight.shape[2]
    heads = head_w // HEAD
    rows = n_seq * n_rows
    half, quart = n_rows // 2, n_rows // 4
    few = n_seq * half
    keys = 4 * n_rows
    vmem = pl.BlockSpec(memory_space=pltpu.VMEM)
    smem = pl.BlockSpec(memory_space=pltpu.SMEM)
    hbm = pl.BlockSpec(memory_space=pl.ANY)

    def v(*shape, dtype=BF16):
        return pltpu.VMEM(shape, dtype)

    def f(*shape):
        return pltpu.VMEM(shape, F32)

    blocks = {"q": (3, blk_rows, head_w), "o": (blk_rows, head_w), "i": (blk_rows, ff), "f": (blk_rows, ff)}
    two = (2,)
    scratch = [
        v(n_seq, n_rows, width),
        v(n_seq, n_rows, width),
        v(3, width, head_w),
        v(2, width, head_w),
        v(2, width, ff),
        v(2, width, ff),
        v(head_w, blk_rows),
        f(1, ff),
        v(rows, width),
        v(width, rows),
        v(rows, head_w),
        v(rows, head_w),
        v(rows, head_w),
        v(2, keys, head_w),
        f(heads, n_rows, keys),
        f(n_seq - 1, heads, n_rows, n_rows),
        v(n_seq, n_rows, head_w),
        v(n_seq, half, head_w),
        f(few, width),
        v(3, n_seq, quart, width),
        v(3, n_seq, quart, width),
        v(3, few, width),
        f(few, width),
        f(few, 1),
        v(few, width),
        v(2, few, ff),
        f(2, few, ff),
        f(few, width),
        v(few, width),
        v(width, few),
        v(width, few),
        v(2, few, ff),
        f(few, width),
        v(width, few),
        v(n_seq, n_rows, head_w),
        v(n_seq, half, head_w),
        v(4, 2, n_rows, head_w),
        v(3, 2, n_rows, head_w),
        v(3, rows, head_w),
        f(n_seq, n_rows, width),
        v(4, n_seq, quart, width),
        v(3, n_seq, quart, width),
        v(2, 2, 2, *blocks["q"]),
        v(2, 2, 2, 2, *blocks["o"]),
        v(2, 2, 2, 2, *blocks["i"]),
        v(2, 2, 2, 2, *blocks["f"]),
        v(2, 2, *blocks["q"]),
        v(2, 2, 2, *blocks["o"]),
        v(2, 2, 2, *blocks["i"]),
        v(2, 2, 2, *blocks["f"]),
        v(2, 2, *blocks["q"]),
        v(2, 2, 2, *blocks["o"]),
        v(2, 2, 2, *blocks["i"]),
        v(2, 2, 2, *blocks["f"]),
        v(3, *blocks["q"]),
        v(2, 3, *blocks["o"]),
        v(2, 3, *blocks["i"]),
        v(2, 3, *blocks["f"]),
        v(*blocks["o"]),
        v(*blocks["i"]),
        v(*blocks["f"]),
        v(*blocks["o"]),
        v(*blocks["i"]),
        v(*blocks["f"]),
        f(4, 16, width),
        f(4, 16, width),
        f(3, 8, head_w),
        f(3, 8, head_w),
        pltpu.SemaphoreType.DMA((6,)),
        pltpu.SemaphoreType.DMA((N_SEM,)),
        pltpu.SemaphoreType.DMA((N_SEM,)),
    ]

    def shape(*dims, dtype=F32):
        return jax.ShapeDtypeStruct(dims, dtype)

    main_out = [
        shape(n_seq, n_rows, width, dtype=BF16),
        shape(n_seq, n_rows, width, dtype=BF16),
        shape(3, blk_rows, head_w),
        shape(blk_rows, head_w),
        shape(blk_rows, ff),
        shape(blk_rows, ff),
        shape(16, width),
        shape(8, head_w),
    ]
    results = pl.pallas_call(
        fused_kernel,
        out_shape=main_out,
        in_specs=[smem, smem] + [hbm] * 6 + [vmem] * 5,
        out_specs=[vmem] * 8,
        scratch_shapes=scratch,
        compiler_params=pltpu.CompilerParams(
            collective_id=0, has_side_effects=True, vmem_limit_bytes=60 * 2**20
        ),
        name="encoder_layer",
    )(
        bucket,
        lengths,
        tokens,
        out_grad,
        qkv_weight[0],
        out_weight[0],
        ff_in_weight[0],
        jnp.transpose(ff_out_weight[0]),
        qv_bias[0],
        ff_in_bias,
        branch_bias[0],
        norm_gain[0],
        norm_bias[0],
    )
    final = pl.pallas_call(
        finish_kernel,
        out_shape=[
            shape(n_seq, n_rows, width, dtype=BF16),
            shape(n_seq, n_rows, width),
            shape(3, blk_rows, head_w),
            shape(2, head_w),
            shape(head_w, blk_rows),
            shape(blk_rows, ff),
            shape(1, ff),
            shape(blk_rows, ff),
            shape(2, width),
            shape(2, width),
            shape(2, width),
            shape(1, 3),
        ],
        in_specs=[smem] + [vmem] * 8,
        out_specs=[vmem] * 12,
        compiler_params=pltpu.CompilerParams(vmem_limit_bytes=32 * 2**20),
        name="finish",
    )(bucket, *results)
    out, tg, gq, qvb, go, gi, inb, gf, br, gain, shift, rms = final
    return (
        out,
        tg,
        gq[None],
        qvb[None],
        go[None],
        gi[None],
        inb,
        jnp.transpose(gf)[None],
        br[None],
        gain[None],
        shift[None],
        rms,
    )


def solution(mesh):
    placed = (
        P("batch", "blk", None),
        P("batch", "blk", None),
        P("batch"),
        P("batch", None),
        P(None, None, ("blk", "batch"), "tensor"),
        P(None, None, "tensor"),
        P(None, "tensor", ("blk", "batch")),
        P(None, ("blk", "batch"), "tensor"),
        P(None, "tensor"),
        P(None, "tensor", ("blk", "batch")),
        P(),
        P(),
        P(),
    )
    sizes = (mesh.shape["blk"], mesh.shape["batch"], mesh.shape["tensor"])
    body = fused_shards if sizes == (4, 2, 4) else general_shards
    return jax.shard_map(
        body,
        mesh=mesh,
        in_specs=placed,
        out_specs=(
            P("batch", "blk", None),
            P("batch", "blk", None),
            P(None, None, ("blk", "batch"), "tensor"),
            P(None, None, "tensor"),
            P(None, "tensor", ("blk", "batch")),
            P(None, ("blk", "batch"), "tensor"),
            P(None, "tensor"),
            P(None, "tensor", ("blk", "batch")),
            P(),
            P(),
            P(),
            P(),
        ),
        check_vma=False,
    )
```

```python
import functools

import jax
import jax.numpy as jnp
from jax import lax
from jax.experimental import pallas as pl
from jax.experimental.pallas import tpu as pltpu
from jax.sharding import PartitionSpec as P

HEAD = 64
SUB = 128


NEG = -1e30


def row_valid(bucket, lengths, pos):
    short = bucket[:, None] != 0
    pick = ((pos // SUB)[:, None] == jnp.arange(lengths.shape[1], dtype=jnp.int32)[None, :]).astype(
        jnp.int32
    )
    short_len = jnp.sum(lengths[:, None, :] * pick[None, :, :], axis=2)
    limit = jnp.where(short, short_len, lengths[:, :1])
    place = jnp.where(short, (pos % SUB)[None, :], pos[None, :])
    return place < limit


def seq_mask(bucket, lengths, qpos, kpos):
    short = bucket[:, None, None] != 0
    same = qpos[:, None] // SUB == kpos[None, :] // SUB
    allowed = jnp.logical_or(jnp.logical_not(short), same[None, :, :])
    return jnp.logical_and(row_valid(bucket, lengths, kpos)[:, None, :], allowed)


def layer_norm(h, gain, shift):
    mean = jnp.mean(h, -1, keepdims=True)
    cent = h - mean
    var = jnp.mean(cent * cent, -1, keepdims=True)
    return cent * lax.rsqrt(var + 1e-12) * gain + shift


def exact_gelu(value):
    return jax.nn.gelu(value, approximate=False)


def general_shards(
    tokens,
    out_grad,
    bucket,
    lengths,
    qkv_weight,
    qv_bias,
    out_weight,
    ff_in_weight,
    ff_in_bias,
    ff_out_weight,
    branch_bias,
    norm_gain,
    norm_bias,
):
    n_seq, rows_blk, width = tokens.shape
    blocks = lax.axis_size("blk")
    rank = lax.axis_index("blk")
    layers = qkv_weight.shape[0]
    local_width = qkv_weight.shape[3]
    heads_here = local_width // HEAD
    total_rows = n_seq * rows_blk
    scale = HEAD ** (-0.5)
    head_shape = (n_seq, rows_blk, heads_here, HEAD)
    qkv_full, out_full, ffin_full, ffout_full = (
        lax.all_gather(qkv_weight, ("blk", "batch"), axis=2, tiled=True),
        lax.all_gather(out_weight, ("blk", "batch"), axis=2, tiled=True),
        lax.all_gather(ff_in_weight, ("blk", "batch"), axis=1, tiled=True),
        lax.all_gather(ff_out_weight, ("blk", "batch"), axis=2, tiled=True),
    )
    local_pos = rank * rows_blk + jnp.arange(rows_blk, dtype=jnp.int32)
    row_ok = row_valid(bucket, lengths, local_pos).astype(jnp.float32).reshape(total_rows, 1)
    whole_pos = jnp.arange(blocks * rows_blk, dtype=jnp.int32)
    sub_bucket, sub_lengths = (bucket, lengths)

    def scores(query, keys, mask):
        found = (
            jnp.einsum("nqhe,nkhe->nhqk", query, keys, preferred_element_type=jnp.float32) * scale
        )
        return jnp.where(mask[:, None], found, NEG)

    x = tokens.astype(jnp.float32).reshape(total_rows, width)
    layer = 0
    xb = x.astype(jnp.bfloat16)
    triple = jnp.einsum("rd,cdk->crk", xb, qkv_full[layer], preferred_element_type=jnp.float32)
    query = (triple[0] + qv_bias[layer, 0]).astype(jnp.bfloat16).reshape(head_shape)
    keys = triple[1].astype(jnp.bfloat16).reshape(head_shape)
    values = (triple[2] + qv_bias[layer, 1]).astype(jnp.bfloat16).reshape(head_shape)
    pair = jnp.stack([keys, values])
    sub_query = query
    sub_pair = pair
    kept = lax.all_gather(sub_pair, "blk", axis=2, tiled=True)
    found = scores(sub_query, kept[0], seq_mask(sub_bucket, sub_lengths, local_pos, whole_pos))
    top = jnp.max(found, -1)
    sub_lse = top + jnp.log(jnp.sum(jnp.exp(found - top[..., None]), -1))
    weights = jnp.exp(found - sub_lse[..., None]).astype(jnp.bfloat16)
    sub_acc = jnp.einsum("nhqk,nkhe->nqhe", weights, kept[1], preferred_element_type=jnp.float32)
    lse = sub_lse
    acc = sub_acc
    att = acc.astype(jnp.bfloat16).reshape(total_rows, local_width)
    a_part = jnp.dot(att, out_full[layer], preferred_element_type=jnp.float32)
    branch = (
        lax.psum(a_part.astype(jnp.bfloat16), "tensor").astype(jnp.float32) + branch_bias[layer, 0]
    )
    upper_in = x + branch
    upper = layer_norm(upper_in, norm_gain[layer, 0], norm_bias[layer, 0])
    upper_b = upper.astype(jnp.bfloat16)
    pre = jnp.dot(upper_b, ffin_full[layer], preferred_element_type=jnp.float32) + ff_in_bias[layer]
    act = exact_gelu(pre).astype(jnp.bfloat16)
    f_part = jnp.dot(act, ffout_full[layer], preferred_element_type=jnp.float32)
    feed = (
        lax.psum(f_part.astype(jnp.bfloat16), "tensor").astype(jnp.float32) + branch_bias[layer, 1]
    )
    lower_in = upper + feed
    squares = [
        jnp.stack(
            [
                jnp.sum(row_ok * x * x),
                jnp.sum(row_ok * branch * branch),
                jnp.sum(row_ok * feed * feed),
            ]
        )
    ]
    saved = [(xb, query, pair, kept, lse, sub_lse, att, acc, upper_in, upper_b, pre, act, lower_in)]
    x = layer_norm(lower_in, norm_gain[layer, 1], norm_bias[layer, 1])
    output = x.astype(jnp.bfloat16).reshape(n_seq, rows_blk, width)
    grad = out_grad.astype(jnp.float32).reshape(total_rows, width)
    g_qkv, g_out, g_in, g_outf = ([], [], [], [])
    g_qvb, g_inb, g_branch, g_gain, g_shift = ([], [], [], [], [])
    for layer in reversed(range(layers)):
        xb, query, pair, kept, lse, sub_lse, att, acc, upper_in, upper_b, pre, act, lower_in = (
            saved[layer]
        )
        _, lower_back = jax.vjp(layer_norm, lower_in, norm_gain[layer, 1], norm_bias[layer, 1])
        d_lower, d_gain2, d_shift2 = lower_back(grad)
        d_feed = d_lower.astype(jnp.bfloat16)
        d_fbias = jnp.sum(d_feed.astype(jnp.float32), 0)
        g_outf.append(jnp.einsum("rf,rd->fd", act, d_feed, preferred_element_type=jnp.float32))
        d_act = jnp.einsum(
            "rd,fd->rf", d_feed, ffout_full[layer], preferred_element_type=jnp.float32
        )
        _, gelu_back = jax.vjp(exact_gelu, pre)
        d_pre = gelu_back(d_act)[0].astype(jnp.bfloat16)
        g_inb.append(jnp.sum(d_pre.astype(jnp.float32), 0))
        g_in.append(jnp.einsum("rd,rf->df", upper_b, d_pre, preferred_element_type=jnp.float32))
        ffn_part = jnp.einsum(
            "rf,df->rd", d_pre, ffin_full[layer], preferred_element_type=jnp.float32
        )
        d_upper = d_lower + lax.psum(ffn_part.astype(jnp.bfloat16), "tensor").astype(jnp.float32)
        _, upper_back = jax.vjp(layer_norm, upper_in, norm_gain[layer, 0], norm_bias[layer, 0])
        d_upper_in, d_gain1, d_shift1 = upper_back(d_upper)
        d_branch = d_upper_in.astype(jnp.bfloat16)
        d_abias = jnp.sum(d_branch.astype(jnp.float32), 0)
        g_out.append(jnp.einsum("rk,rd->kd", att, d_branch, preferred_element_type=jnp.float32))
        d_att = (
            jnp.einsum("rd,kd->rk", d_branch, out_full[layer], preferred_element_type=jnp.float32)
            .astype(jnp.bfloat16)
            .reshape(head_shape)
        )
        delta = jnp.einsum("nqhe,nqhe->nhq", d_att.astype(jnp.float32), acc)
        sub_query, sub_datt, sub_delta = (query, d_att, delta)
        block_keys = kept[0]
        block_found = scores(
            sub_query, block_keys, seq_mask(sub_bucket, sub_lengths, local_pos, whole_pos)
        )
        prob = jnp.exp(block_found - sub_lse[..., None])
        d_prob = jnp.einsum(
            "nqhe,nkhe->nhqk", sub_datt, kept[1], preferred_element_type=jnp.float32
        )
        d_scores = (prob * (d_prob - sub_delta[..., None])).astype(jnp.bfloat16)
        d_query = jnp.einsum(
            "nhqk,nkhe->nqhe", d_scores, block_keys, preferred_element_type=jnp.float32
        )
        d_keys = jnp.einsum(
            "nhqk,nqhe->nkhe", d_scores, sub_query, preferred_element_type=jnp.float32
        )
        d_values = jnp.einsum(
            "nhqk,nqhe->nkhe",
            prob.astype(jnp.bfloat16),
            sub_datt,
            preferred_element_type=jnp.float32,
        )
        sub_dq = d_query
        dpair_all = jnp.stack([d_keys * scale, d_values])
        sub_dpair = lax.psum_scatter(
            dpair_all.astype(jnp.bfloat16), "blk", scatter_dimension=2, tiled=True
        ).astype(jnp.float32)
        d_query, d_pair = (sub_dq, sub_dpair)
        dq_b = (d_query * scale).astype(jnp.bfloat16).reshape(total_rows, local_width)
        dk_b = d_pair[0].astype(jnp.bfloat16).reshape(total_rows, local_width)
        dv_b = d_pair[1].astype(jnp.bfloat16).reshape(total_rows, local_width)
        d_triple = jnp.stack([dq_b, dk_b, dv_b])
        g_qvb.append(
            jnp.stack([jnp.sum(dq_b.astype(jnp.float32), 0), jnp.sum(dv_b.astype(jnp.float32), 0)])
        )
        g_qkv.append(jnp.einsum("rd,crk->cdk", xb, d_triple, preferred_element_type=jnp.float32))
        attn_part = jnp.einsum(
            "crk,cdk->rd", d_triple, qkv_full[layer], preferred_element_type=jnp.float32
        )
        grad = d_upper_in + lax.psum(attn_part.astype(jnp.bfloat16), "tensor").astype(jnp.float32)
        g_branch.append(jnp.stack([d_abias, d_fbias]))
        g_gain.append(jnp.stack([d_gain1, d_gain2]))
        g_shift.append(jnp.stack([d_shift1, d_shift2]))

    def in_order(items):
        return jnp.stack(items[::-1])

    qkv_g, out_g, in_g, outf_g = (
        lax.psum_scatter(in_order(g_qkv), ("blk", "batch"), scatter_dimension=2, tiled=True),
        lax.psum_scatter(in_order(g_out), ("blk", "batch"), scatter_dimension=2, tiled=True),
        lax.psum_scatter(in_order(g_in), ("blk", "batch"), scatter_dimension=1, tiled=True),
        lax.psum_scatter(in_order(g_outf), ("blk", "batch"), scatter_dimension=2, tiled=True),
    )
    count = jnp.sum(row_ok)
    qvb_g, inb_g, branch_g, gain_g, shift_g, square_sums, count_all = lax.psum(
        (
            in_order(g_qvb),
            in_order(g_inb),
            in_order(g_branch),
            in_order(g_gain),
            in_order(g_shift),
            jnp.stack(squares),
            count,
        ),
        ("blk", "batch"),
    )
    rms = jnp.sqrt(square_sums / (count_all * width))
    tokens_grad = grad.reshape(n_seq, rows_blk, width)
    return (
        output,
        tokens_grad,
        qkv_g,
        qvb_g,
        out_g,
        in_g,
        inb_g,
        outf_g,
        branch_g,
        gain_g,
        shift_g,
        rms,
    )


MESH = pl.DeviceIdType.MESH
F32 = jnp.float32
BF16 = jnp.bfloat16
N_SEND = 48
N_RECV = 128


def dot_nn(a, b):
    return lax.dot_general(a, b, (((1,), (0,)), ((), ())), preferred_element_type=F32)


def dot_nt(a, b):
    return lax.dot_general(a, b, (((1,), (1,)), ((), ())), preferred_element_type=F32)


def dot_tn(a, b):
    return lax.dot_general(a, b, (((0,), (0,)), ((), ())), preferred_element_type=F32)


def slot_order(bucket_ref):
    first = jnp.where(bucket_ref[0] == 0, 0, jnp.where(bucket_ref[1] == 0, 1, 2))
    second = jnp.where(first == 0, 1, 0)
    third = jnp.where(first == 2, 1, 2)
    return first, second, third


class Net:
    def __init__(self, send_sems, recv_sems):
        self.send_sems, self.recv_sems = send_sems, recv_sems
        self.copies, self.n_recv = [], 0

    def slot(self):
        self.n_recv += 1
        assert self.n_recv <= N_RECV
        return self.n_recv - 1

    def send(self, src, dst, peer, slot=None):
        at = len(self.copies)
        if at >= N_SEND:
            self.copies[at - N_SEND].wait_send()
        copy = pltpu.make_async_remote_copy(
            src_ref=src,
            dst_ref=dst,
            send_sem=self.send_sems.at[at % N_SEND],
            recv_sem=self.recv_sems.at[self.slot() if slot is None else slot],
            device_id=peer,
            device_id_type=MESH,
        )
        copy.start()
        self.copies.append(copy)
        return copy

    def whole(self, ref, peer, slot):
        return pltpu.make_async_remote_copy(
            src_ref=ref,
            dst_ref=ref,
            send_sem=self.send_sems.at[0],
            recv_sem=self.recv_sems.at[slot],
            device_id=peer,
            device_id_type=MESH,
        )

    def finish(self):
        for copy in self.copies[-N_SEND:]:
            copy.wait_send()


class Gather:
    def __init__(self, net, view, at, near):
        self.net, self.view, self.near = net, view, near
        self.own, self.x, self.y, self.d, self.size = at
        self.half = self.size // 2
        self.slot = net.slot()

    def part(self, start, size):
        return self.view(pl.ds(pl.multiple_of(start, 16), size))

    def to_core(self, ref):
        self.net.send(ref, ref, self.near[2], self.slot)

    def issue(self, src=None):
        xnb, ynb, core = self.near
        to = self.part(self.own, self.size)
        src = to if src is None else src
        self.from_x = self.net.send(src, to, xnb)
        self.from_y = self.net.send(src, to, ynb)
        self.net.send(src, to, core, self.slot)

    def forward(self):
        xnb, ynb, core = self.near
        self.from_x.wait_recv()
        ref = self.part(self.x, self.half)
        self.first = self.net.send(ref, ref, ynb)
        self.to_core(self.part(self.x, self.size))
        self.from_y.wait_recv()
        ref = self.part(self.y + self.half, self.half)
        self.second = self.net.send(ref, ref, xnb)
        self.to_core(self.part(self.y, self.size))

    def last(self):
        self.first.wait_recv()
        self.second.wait_recv()
        self.to_core(self.part(self.d, self.size))

    def ready(self):
        self.net.whole(self.part(0, 4 * self.size), self.near[2], self.slot).wait_recv()


class Scatter:
    def __init__(self, net, refs, spot, near):
        self.net, self.spot, self.near = net, spot, near
        self.g, self.d, self.h, self.p1, self.s, self.p2 = refs
        self.rows = self.g.shape[3]
        self.half = self.rows // 2

    def core(self):
        c = self.spot[1]
        self.c1 = self.net.send(self.g.at[:, 1 - c], self.d, self.near[2])

    def first(self):
        yy, c, t = self.spot
        xnb, ynb, _ = self.near
        lo, hi = pl.ds(0, self.half), pl.ds(self.half, self.half)
        self.c1.wait_recv()
        for a in range(2):
            for b in range(2):
                self.h[a, b] = (self.g[a, c, b].astype(F32) + self.d[a, b].astype(F32)).astype(BF16)
        self.px = self.net.send(self.h.at[:, 1 - t, lo], self.p1.at[0], xnb)
        self.py = self.net.send(self.h.at[1 - yy, :, hi], self.p1.at[1], ynb)

    def second(self):
        yy, c, t = self.spot
        xnb, ynb, _ = self.near
        lo, hi = pl.ds(0, self.half), pl.ds(self.half, self.half)
        self.px.wait_recv()
        self.s[0] = (self.h[1 - yy, t, lo].astype(F32) + self.p1[0, 1 - yy].astype(F32)).astype(BF16)
        self.qy = self.net.send(self.s.at[0], self.p2.at[0], ynb)
        self.py.wait_recv()
        self.s[1] = (self.h[yy, 1 - t, hi].astype(F32) + self.p1[1, 1 - t].astype(F32)).astype(BF16)
        self.qx = self.net.send(self.s.at[1], self.p2.at[1], xnb)

    def result(self):
        yy, c, t = self.spot
        self.qy.wait_recv()
        self.qx.wait_recv()
        lo, hi = pl.ds(0, self.half), pl.ds(self.half, self.half)
        low = self.h[yy, t, lo].astype(F32) + self.p1[0, yy].astype(F32) + self.p2[0].astype(F32)
        high = self.h[yy, t, hi].astype(F32) + self.p1[1, t].astype(F32) + self.p2[1].astype(F32)
        return low, high


def fused_kernel(*refs):
    (
        bucket, lengths, tokens, out_grad, qkv_w, out_w, ffi_w, ffo_w, qv_bias, ffi_b, br_bias, gain, shift,
        out_hbm, tg_hbm, gq_hbm, go_hbm, gi_hbm, gf_hbm, vec_hbm, qvb_hbm,
        tok, cot, w_q, w_o, w_i, w_f, own_o, bias_r, xs, xs_t, q_r, k_r, v_r, kv_a, p_a, p_b,
        att, att_r, ps, pr, xh1, rstd1, yb, act, gp, dh2, dfb, df_t, yb_t, dpre, dh1, da_t,
        datt, datt_s, dkv_s, dkv_c, dkv_t, dkv_y, dtri, dx_p, dx_s, dx_1, dx_2, dx_t, dx_a,
        sc_q, sc_o, sc_i, sc_f, z_o, z_i, z_f, t_o, t_i, t_f, vs, vr, qs, qr,
        out_v, tg_v, gq_v, go_v, gi_v, gf_v, vec_v, qvb_v,
        local_sems, send_sems, recv_sems,
    ) = refs
    n_seq, n_rows, width = tok.shape
    blk_rows = ffi_w.shape[0]
    head_w = qkv_w.shape[2]
    heads = head_w // HEAD
    half, quart = n_rows // 2, n_rows // 4
    tile = 256
    n_tile = width // tile
    scale = HEAD ** (-0.5)

    r = lax.axis_index("blk")
    t = lax.axis_index("batch")
    z = lax.axis_index("tensor")
    yy, c = r // 2, r % 2
    pz, qz = z // 2, z % 2
    r1, r2, r3 = r + 1 - 2 * c, (r + 2) % 4, 3 - r
    z1, z2, z3 = z + 1 - 2 * qz, (z + 2) % 4, 3 - z
    core, xnb, ynb = (r1, t, z), (r, 1 - t, z), (r2, t, z)
    zn1, zn2, zn3 = (r, t, z1), (r, t, z2), (r, t, z3)
    peers = (zn2, zn3, zn1, xnb, ynb, core)
    near = (xnb, ynb, core)

    barrier = pltpu.get_barrier_semaphore()
    for peer in peers:
        pl.semaphore_signal(barrier, inc=1, device_id=peer, device_id_type=MESH)

    net = Net(send_sems, recv_sems)

    def block(rr, tt):
        return (rr * 2 + tt) * blk_rows

    at = (block(r, t), block(r, 1 - t), block(r2, t), block(r2, 1 - t), blk_rows)
    own = pl.ds(pl.multiple_of(block(r, t), 32), blk_rows)

    def gather(view):
        return Gather(net, view, at, near)

    ga_q = gather(lambda rows: w_q.at[:, rows])
    ga_o = [gather(lambda rows, k=k: w_o.at[k, rows]) for k in range(2)]
    ga_i = [gather(lambda rows, k=k: w_i.at[k, rows]) for k in range(2)]
    ga_f = [gather(lambda rows, k=k: w_f.at[k, rows]) for k in range(2)]

    local = [
        pltpu.make_async_copy(src, dst, local_sems.at[k])
        for k, (src, dst) in enumerate(
            (
                (out_w, own_o),
                (tokens, tok),
                (qkv_w, w_q.at[:, own]),
                (ffi_w, w_i.at[0, own]),
                (ffo_w, w_f.at[0, own]),
                (out_grad, cot),
            )
        )
    ]
    for copy in local:
        copy.start()
    stores = []

    def store(src, dst):
        copy = pltpu.make_async_copy(src, dst, local_sems.at[len(local) + len(stores)])
        copy.start()
        stores.append(copy)

    local[0].wait()
    w_o[0, own] = jnp.transpose(own_o[...])

    pl.semaphore_wait(barrier, len(peers))

    ga_q.issue(qkv_w)
    zo = net.send(w_o.at[0, own], w_o.at[1, own], zn2)
    ga_o[0].issue()
    zi = net.send(ffi_w, w_i.at[1, own], zn2)
    zf = net.send(ffo_w, w_f.at[1, own], zn2)
    zb = net.send(ffi_b, bias_r, zn2)

    local[1].wait()
    order = slot_order(bucket)
    for s in range(n_seq):
        xs[s * n_rows : (s + 1) * n_rows] = tok[order[s]]
    xs_t[...] = jnp.transpose(xs[...])

    ga_q.forward()
    ga_i[0].issue(ffi_w)
    ga_o[0].forward()
    zo.wait_recv()
    ga_o[1].issue()
    ga_q.last()
    ga_f[0].issue(ffo_w)
    local[2].wait()
    ga_q.ready()

    k_r[...] = dot_nn(xs[...], w_q[1]).astype(BF16)
    v_r[...] = (dot_nn(xs[...], w_q[2]) + qv_bias[1:2, :]).astype(BF16)

    def keys_of(rr):
        return kv_a.at[:, pl.ds(pl.multiple_of(rr * n_rows, n_rows), n_rows)]

    mine = pl.ds(pl.multiple_of(r * n_rows, n_rows), n_rows)
    kv_a[0, mine] = k_r[0:n_rows]
    kv_a[1, mine] = v_r[0:n_rows]
    kv_y = net.send(keys_of(r), keys_of(r), ynb)
    kv_c = [net.send(keys_of(r), keys_of(r), core)]
    q_r[...] = (dot_nn(xs[...], w_q[0]) + qv_bias[0:1, :]).astype(BF16)

    lane_head = lax.broadcasted_iota(jnp.int32, (1, head_w), 1) // HEAD

    def of_head(value, h):
        return jnp.where(lane_head == h, value, jnp.zeros_like(value))

    def limit_of(s):
        index = order[s]
        return lengths[index, r], lengths[index, 0]

    own_half = pl.ds(pl.multiple_of(pz * half, half), half)
    other_half = pl.ds(pl.multiple_of((1 - pz) * half, half), half)

    def attend(s, keys, values, probs, key_ok):
        query = q_r[s * n_rows : (s + 1) * n_rows]
        total = jnp.zeros((n_rows, head_w), F32)
        for h in range(heads):
            score = dot_nt(of_head(query, h), keys) * scale
            if key_ok is not None:
                score = jnp.where(key_ok, score, NEG)
            e = jnp.exp(score - jnp.max(score, -1, keepdims=True))
            prob = e / jnp.sum(e, -1, keepdims=True)
            probs[h] = prob
            total = total + dot_nn(prob.astype(BF16), of_head(values, h))
        att[s] = total.astype(BF16)
        return net.send(att.at[s, other_half], att_r.at[s], zn2)

    att_x = [None] * n_seq
    key_at = lax.broadcasted_iota(jnp.int32, (1, n_rows), 1)
    for s in range(1, n_seq):
        here = slice(s * n_rows, (s + 1) * n_rows)
        key_ok = key_at < limit_of(s)[0]
        att_x[s] = attend(s, k_r[here], v_r[here], p_b.at[s - 1], key_ok)

    ga_i[0].forward()
    zi.wait_recv()
    ga_i[1].issue()
    ga_o[0].last()
    kv_y.wait_recv()
    kv_c.append(net.send(keys_of(r2), keys_of(r2), core))
    ga_o[1].forward()
    for copy in kv_c:
        copy.wait_recv()
    att_x[0] = attend(0, kv_a[0], kv_a[1], p_a, None)
    ga_o[1].last()
    ga_f[0].forward()
    ga_i[0].last()
    zf.wait_recv()
    ga_f[1].issue()
    for k in range(2):
        ga_o[k].ready()

    def pair_send(k, s, value):
        ps[k, s] = value.astype(BF16)
        return net.send(ps.at[k, s], pr.at[k, s], zn1)

    def pair_sum(k, s, copy):
        copy.wait_recv()
        return ps[k, s].astype(F32) + pr[k, s].astype(F32)

    moved = {}
    for s in (1, 2, 0):
        att_x[s].wait_recv()
        moved[s] = pair_send(
            0, s, dot_nt(att[s, own_half], w_o[0]) + dot_nt(att_r[s], w_o[1])
        )
    ga_i[1].forward()
    ones = jnp.ones((1, width), F32)
    sums = [jnp.zeros((1, width), F32) for _ in range(4)]
    row_at = lax.broadcasted_iota(jnp.int32, (half, 1), 0)
    oks = []

    def column_sum(value):
        return jnp.sum(value, 0, keepdims=True)

    def mean_of(value):
        return jnp.mean(value, -1, keepdims=True)

    def normed(h):
        cent = h - mean_of(h)
        rstd = lax.rsqrt(mean_of(cent * cent) + 1e-12)
        return cent * rstd, rstd

    for s in range(n_seq):
        short, full = limit_of(s)
        place = row_at + pz * half
        if s == 0:
            ok = (place + r * n_rows < full).astype(F32)
        else:
            ok = (place < short).astype(F32)
        oks.append(ok)
    for s in (1, 2, 0):
        here = slice(s * half, (s + 1) * half)
        x = xs[pl.ds(pl.multiple_of(s * n_rows + pz * half, half), half)].astype(F32)
        branch = pair_sum(0, s, moved[s]) + br_bias[0:1, :]
        sums[0] = sums[0] + column_sum(oks[s] * (x * x))
        sums[1] = sums[1] + column_sum(oks[s] * (branch * branch))
        sums[3] = sums[3] + column_sum(oks[s] * ones)
        hat, rstd = normed(x + branch)
        xh1[here] = hat
        rstd1[here] = rstd
        yb[here] = (hat * gain[0:1, :] + shift[0:1, :]).astype(BF16)
    yb_t[...] = jnp.transpose(yb[...])

    ga_f[0].last()
    ga_i[1].last()
    ga_f[1].forward()
    zb.wait_recv()
    local[3].wait()
    for k in range(2):
        ga_i[k].ready()
    for k in range(2):
        for n in range(n_tile):
            cols = slice(n * tile, (n + 1) * tile)
            bias = ffi_b[:, cols] if k == 0 else bias_r[:, cols]
            pre = dot_nn(yb[...], w_i[k, :, cols]) + bias
            phi = 0.5 * (1.0 + lax.erf(pre * (0.5**0.5)))
            act[k, :, cols] = (pre * phi).astype(BF16)
            gp[k, :, cols] = phi + pre * (jnp.exp(-0.5 * pre * pre) * 0.3989422804014327)

    ga_f[1].last()
    local[4].wait()
    for k in range(2):
        ga_f[k].ready()
    for s in range(n_seq):
        here = slice(s * half, (s + 1) * half)
        moved[s] = pair_send(1, s, dot_nt(act[0, here], w_f[0]) + dot_nt(act[1, here], w_f[1]))
    local[5].wait()
    vec = {k: jnp.zeros((1, width), F32) for k in range(8)}
    back = {}
    for s in range(n_seq):
        here = slice(s * half, (s + 1) * half)
        feed = pair_sum(1, s, moved[s]) + br_bias[1:2, :]
        sums[2] = sums[2] + column_sum(oks[s] * (feed * feed))
        hat, rstd = normed(xh1[here] * gain[0:1, :] + shift[0:1, :] + feed)
        out_v[s, own_half] = (hat * gain[1:2, :] + shift[1:2, :]).astype(BF16)
        g = cot[order[s], own_half].astype(F32)
        vec[1] = vec[1] + column_sum(g * hat)
        vec[2] = vec[2] + column_sum(g)
        g = g * gain[1:2, :]
        d = rstd * (g - mean_of(g) - hat * mean_of(g * hat))
        dh2[here] = d
        d = d.astype(BF16)
        dfb[here] = d
        vec[0] = vec[0] + column_sum(d.astype(F32))
        total = jnp.zeros((half, width), F32)
        for k in range(2):
            p = (dot_nn(d, w_f[k]) * gp[k, here]).astype(BF16)
            dpre[k, here] = p
            vec[3 + k] = vec[3 + k] + column_sum(p.astype(F32))
            total = total + dot_nt(p, w_i[k])
        back[s] = pair_send(2, s, total)

    def scatter(refs, k=None):
        views = refs if k is None else [ref.at[k] for ref in refs]
        return Scatter(net, views, (yy, c, t), near)

    rs_f = [scatter(sc_f, k) for k in range(2)]
    rs_i = [scatter(sc_i, k) for k in range(2)]
    rs_o = [scatter(sc_o, k) for k in range(2)]
    rs_q = scatter(sc_q)

    def grads(lhs, rhs, out, rows=None):
        value = dot_nn(lhs, rhs).astype(BF16)
        for b in range(8):
            piece = value[b * blk_rows : (b + 1) * blk_rows]
            if rows is None:
                out[b // 4, (b // 2) % 2, b % 2] = piece
            else:
                out[b // 4, (b // 2) % 2, b % 2, rows] = piece

    df_t[...] = jnp.transpose(dfb[...])
    for k in (1, 0):
        for n in range(n_tile):
            cols = slice(n * tile, (n + 1) * tile)
            grads(df_t[...], act[k, :, cols], rs_f[k].g.at[:, :, :, :, cols])
        rs_f[k].core()

    datt_x = [None] * n_seq

    def first_norm_back(s):
        here = slice(s * half, (s + 1) * half)
        hat = xh1[here]
        g = dh2[here] + pair_sum(2, s, back[s])
        vec[6] = vec[6] + column_sum(g * hat)
        vec[7] = vec[7] + column_sum(g)
        g = g * gain[0:1, :]
        d = rstd1[here] * (g - mean_of(g) - hat * mean_of(g * hat))
        dh1[here] = d
        d = d.astype(BF16)
        dfb[here] = d
        vec[5] = vec[5] + column_sum(d.astype(F32))
        datt_s[s] = dot_nn(d, w_o[1]).astype(BF16)
        datt_x[s] = net.send(datt_s.at[s], datt.at[s, own_half], zn2)
        datt[s, own_half] = dot_nn(d, w_o[0]).astype(BF16)

    rs_f[1].first()
    rs_f[0].first()
    for k in (1, 0):
        for n in range(n_tile):
            cols = slice(n * tile, (n + 1) * tile)
            grads(yb_t[...], dpre[k, :, cols], rs_i[k].g.at[:, :, :, :, cols])
        rs_i[k].core()
    first_norm_back(0)
    rs_i[1].first()
    rs_i[0].first()
    first_norm_back(1)
    first_norm_back(2)
    quarter = pl.ds(pl.multiple_of(z * quart, quart), quart)
    quarter_2 = pl.ds(pl.multiple_of(z2 * quart, quart), quart)
    out_2 = net.send(out_v.at[:, quarter], out_v.at[:, quarter], zn2)

    for k in range(8):
        vs[0, k : k + 1] = vec[k]
    for k in range(4):
        vs[0, 8 + k : 9 + k] = sums[k]
    vs[0, 12:16] = jnp.zeros((4, width), F32)

    def v_step(k, copy):
        copy.wait_recv()
        vs[k + 1] = vs[k] + vr[k]

    v_copy = net.send(vs.at[0], vr.at[0], core)

    def attend_back(s, keys, values, probs):
        query = q_r[s * n_rows : (s + 1) * n_rows]
        d_att = datt[s]
        dq = jnp.zeros((n_rows, head_w), F32)
        dk = jnp.zeros(keys.shape, F32)
        dv = jnp.zeros(keys.shape, F32)
        for h in range(heads):
            prob = probs[h]
            d_h = of_head(d_att, h)
            dp = dot_nt(d_h, values)
            delta = jnp.sum(prob * dp, -1, keepdims=True)
            ds = (prob * (dp - delta)).astype(BF16)
            dq = dq + dot_nn(ds, of_head(keys, h))
            dk = dk + dot_tn(ds, of_head(query, h))
            dv = dv + dot_tn(prob.astype(BF16), d_h)
        return (dq * scale).astype(BF16), (dk * scale).astype(BF16), dv.astype(BF16)

    datt_x[0].wait_recv()
    dq, dk, dv = attend_back(0, kv_a[0], kv_a[1], p_a)
    dtri[0, 0:n_rows] = dq
    for a in range(4):
        dkv_s[a // 2, a % 2, 0] = dk[a * n_rows : (a + 1) * n_rows]
        dkv_s[a // 2, a % 2, 1] = dv[a * n_rows : (a + 1) * n_rows]
    dkv_1 = net.send(dkv_s.at[:, 1 - c], dkv_c, core)

    da_t[...] = jnp.transpose(dfb[...])
    rows_l = jnp.concatenate([att[s, own_half] for s in range(n_seq)], 0)
    rows_r = jnp.concatenate([att_r[s] for s in range(n_seq)], 0)
    grads(da_t[...], rows_r, rs_o[1].g)
    grads(da_t[...], rows_l, rs_o[0].g)
    for k in (1, 0):
        rs_o[k].core()
    dkv_1.wait_recv()
    dkv_t[...] = (dkv_s[1 - yy, c].astype(F32) + dkv_c[1 - yy].astype(F32)).astype(BF16)
    dkv_2 = net.send(dkv_t, dkv_y, ynb)
    v_step(0, v_copy)
    v_copy = net.send(vs.at[1], vr.at[1], xnb)
    rs_f[1].second()
    for s in range(1, n_seq):
        datt_x[s].wait_recv()
        here = slice(s * n_rows, (s + 1) * n_rows)
        dq, dk, dv = attend_back(s, k_r[here], v_r[here], p_b.at[s - 1])
        dtri[0, here] = dq
        dtri[1, here] = dk
        dtri[2, here] = dv

    def dx_of(s):
        here = slice(s * n_rows, (s + 1) * n_rows)
        total = dot_nt(dtri[0, here], w_q[0])
        for k in range(1, 3):
            total = total + dot_nt(dtri[k, here], w_q[k])
        dx_p[s] = total
        for a in range(4):
            dx_s[a // 2, a % 2, s] = total[a * quart : (a + 1) * quart].astype(BF16)

    for s in range(1, n_seq):
        dx_of(s)
    b_1 = net.send(dx_s.at[:, 1 - qz, 1:n_seq], dx_1, zn1)
    rs_f[0].second()
    dkv_2.wait_recv()
    total = dkv_s[yy, c].astype(F32) + dkv_c[yy].astype(F32) + dkv_y[...].astype(F32)
    dtri[1, 0:n_rows] = total[0].astype(BF16)
    dtri[2, 0:n_rows] = total[1].astype(BF16)
    dx_of(0)
    a_go = [
        net.send(dx_s.at[to // 2, to % 2, 0], dx_a.at[k], peer)
        for k, (to, peer) in enumerate(((z1, zn1), (z2, zn2), (z3, zn3)))
    ]
    qs[0] = jnp.zeros(qs.shape[1:], F32)
    qs[0, 0:1] = column_sum(dtri[0].astype(F32))
    qs[0, 1:2] = column_sum(dtri[2].astype(F32))
    q_copy = net.send(qs.at[0], qr.at[0], core)
    for k in range(3):
        grads(xs_t[...], dtri[k], rs_q.g, slice(k * blk_rows, (k + 1) * blk_rows))
    rs_q.core()

    rs_o[1].first()
    rs_o[0].first()

    def rows_of(a):
        return pl.ds(pl.multiple_of(a * quart, quart), quart)

    b_1.wait_recv()
    for s in range(1, n_seq):
        dx_t[s - 1] = (dx_p[s, quarter_2] + dx_1[1 - pz, s - 1].astype(F32)).astype(BF16)
    b_2 = net.send(dx_t, dx_2, zn2)
    out_2.wait_recv()
    out_1 = net.send(out_v.at[:, quarter_2], out_v.at[:, quarter_2], zn1)
    q_copy.wait_recv()
    qs[1] = qs[0] + qr[0]
    q_copy = net.send(qs.at[1], qr.at[1], xnb)
    rs_q.first()
    v_step(1, v_copy)
    v_copy = net.send(vs.at[2], vr.at[2], ynb)
    rs_i[1].second()
    rs_i[0].second()

    def half_rows(s):
        return pl.ds(pl.multiple_of(s * half + qz * quart, quart), quart)

    def send_second(rs, buf, back_z):
        low, high = rs.result()
        n = low.shape[0]
        buf[0:n] = low.astype(BF16)
        buf[n : 2 * n] = high.astype(BF16)
        return net.send(buf, back_z, zn2)

    zg_f = send_second(rs_f[1], t_f, z_f)

    for copy in a_go:
        copy.wait_recv()
    total = dx_p[0, quarter] + dh1[half_rows(0)]
    for k in range(3):
        total = total + dx_a[k].astype(F32)
    tg_v[0, quarter] = total.astype(BF16)
    here = tg_v.at[0, quarter]
    a_back = [net.send(here, here, peer) for peer in (zn1, zn2, zn3)]
    b_2.wait_recv()
    for s in range(1, n_seq):
        total = dx_p[s, quarter] + dx_1[pz, s - 1].astype(F32) + dx_2[s - 1].astype(F32)
        tg_v[s, quarter] = (total + dh1[half_rows(s)]).astype(BF16)
    here = tg_v.at[1:n_seq, quarter]
    b_back = [net.send(here, here, zn2), net.send(here, here, zn1)]
    q_copy.wait_recv()
    qs[2] = qs[1] + qr[1]
    q_copy = net.send(qs.at[2], qr.at[2], ynb)
    rs_o[1].second()
    rs_o[0].second()
    rs_q.second()
    zg_i = send_second(rs_i[1], t_i, z_i)
    v_step(2, v_copy)
    v_copy = net.send(vs.at[3], vr.at[3], zn2)
    zg_o = send_second(rs_o[1], t_o, z_o)

    b_back[0].wait_recv()
    there = tg_v.at[1:n_seq, quarter_2]
    b_back[0] = net.send(there, there, zn1)

    def put(rs, out, copy=None, back_z=None):
        low, high = rs.result()
        n = low.shape[0]
        if copy is not None:
            copy.wait_recv()
            low = low + back_z[0:n].astype(F32)
            high = high + back_z[n : 2 * n].astype(F32)
        out[0:n] = low
        out[n : 2 * n] = high

    put(rs_f[0], gf_v, zg_f, z_f)
    store(gf_v, gf_hbm)
    put(rs_i[0], gi_v, zg_i, z_i)
    store(gi_v, gi_hbm)
    put(rs_q, gq_v)
    store(gq_v, gq_hbm)
    out_1.wait_recv()
    store(out_v, out_hbm)
    put(rs_o[0], go_v, zg_o, z_o)
    store(go_v, go_hbm)
    q_copy.wait_recv()
    qvb_v[...] = qs[2] + qr[2]
    store(qvb_v, qvb_hbm)
    v_copy.wait_recv()
    vec_v[...] = vs[3] + vr[3]
    vec_v[3:4] = vs[3, 3:4] + vr[3, 4:5]
    vec_v[4:5] = vs[3, 4:5] + vr[3, 3:4]
    store(vec_v, vec_hbm)
    for copy in a_back + b_back:
        copy.wait_recv()
    store(tg_v, tg_hbm)
    for copy in stores:
        copy.wait()
    net.finish()


def finish_kernel(
    bucket,
    out_i,
    tg_i,
    gq_i,
    go_i,
    gi_i,
    gf_i,
    vec_i,
    qvb_i,
    out_o,
    tg_o,
    gq_o,
    qvb_o,
    go_o,
    gi_o,
    inb_o,
    gf_o,
    br_o,
    gain_o,
    shift_o,
    rms_o,
):
    order = slot_order(bucket)
    for s in range(3):
        at = jnp.where(order[0] == s, 0, jnp.where(order[1] == s, 1, 2))
        out_o[s] = out_i[at]
        tg_o[s] = tg_i[at].astype(F32)
    n = gq_o.shape[1]
    for k in range(3):
        gq_o[k] = gq_i[k * n : (k + 1) * n]
    go_o[...] = jnp.transpose(go_i[...])
    gi_o[...] = gi_i[...]
    gf_o[...] = gf_i[...]
    qvb_o[...] = qvb_i[0:2]
    inb_o[...] = vec_i[3:4]
    br_o[0:1] = vec_i[5:6]
    br_o[1:2] = vec_i[0:1]
    gain_o[0:1] = vec_i[6:7]
    gain_o[1:2] = vec_i[1:2]
    shift_o[0:1] = vec_i[7:8]
    shift_o[1:2] = vec_i[2:3]
    width = vec_i.shape[1]
    count = vec_i[11:12, 0:1]
    square = jnp.sum(vec_i[8:11], 1, keepdims=True)
    rms = jnp.sqrt(square / (count * width))
    lane = lax.broadcasted_iota(jnp.int32, (1, 3), 1)
    out = jnp.zeros((1, 3), F32)
    for k in range(3):
        out = jnp.where(lane == k, rms[k : k + 1], out)
    rms_o[...] = out


def fused_shards(
    tokens,
    out_grad,
    bucket,
    lengths,
    qkv_weight,
    qv_bias,
    out_weight,
    ff_in_weight,
    ff_in_bias,
    ff_out_weight,
    branch_bias,
    norm_gain,
    norm_bias,
):
    n_seq, n_rows, width = tokens.shape
    blk_rows, head_w = qkv_weight.shape[2:]
    ff = ff_in_weight.shape[2]
    heads = head_w // HEAD
    rows = n_seq * n_rows
    half, quart = n_rows // 2, n_rows // 4
    few = n_seq * half
    keys = 4 * n_rows
    vmem = pl.BlockSpec(memory_space=pltpu.VMEM)
    smem = pl.BlockSpec(memory_space=pltpu.SMEM)
    hbm = pl.BlockSpec(memory_space=pl.ANY)

    def v(*shape, dtype=BF16):
        return pltpu.VMEM(shape, dtype)

    def f(*shape):
        return pltpu.VMEM(shape, F32)

    wide = {"q": (3 * blk_rows, head_w), "o": (blk_rows, head_w), "i": (blk_rows, ff), "f": (blk_rows, ff)}

    def scatter_bufs(kind):
        n, cols = wide[kind]
        lead = () if kind == "q" else (2,)
        dims = ((2, 2, 2, n), (2, 2, n), (2, 2, n), (2, 2, n // 2), (2, n // 2), (2, n // 2))
        return [v(*lead, *dim, cols) for dim in dims]

    scratch = [
        v(n_seq, n_rows, width),
        v(n_seq, n_rows, width),
        v(3, width, head_w),
        v(2, width, head_w),
        v(2, width, ff),
        v(2, width, ff),
        v(head_w, blk_rows),
        f(1, ff),
        v(rows, width),
        v(width, rows),
        v(rows, head_w),
        v(rows, head_w),
        v(rows, head_w),
        v(2, keys, head_w),
        f(heads, n_rows, keys),
        f(n_seq - 1, heads, n_rows, n_rows),
        v(n_seq, n_rows, head_w),
        v(n_seq, half, head_w),
        v(3, n_seq, half, width),
        v(3, n_seq, half, width),
        f(few, width),
        f(few, 1),
        v(few, width),
        v(2, few, ff),
        f(2, few, ff),
        f(few, width),
        v(few, width),
        v(width, few),
        v(width, few),
        v(2, few, ff),
        f(few, width),
        v(width, few),
        v(n_seq, n_rows, head_w),
        v(n_seq, half, head_w),
        v(2, 2, 2, n_rows, head_w),
        v(2, 2, n_rows, head_w),
        v(2, n_rows, head_w),
        v(2, n_rows, head_w),
        v(3, rows, head_w),
        f(n_seq, n_rows, width),
        v(2, 2, n_seq, quart, width),
        v(2, n_seq - 1, quart, width),
        v(n_seq - 1, quart, width),
        v(n_seq - 1, quart, width),
        v(3, quart, width),
        scatter_bufs("q"),
        scatter_bufs("o"),
        scatter_bufs("i"),
        scatter_bufs("f"),
        v(*wide["o"]),
        v(*wide["i"]),
        v(*wide["f"]),
        v(*wide["o"]),
        v(*wide["i"]),
        v(*wide["f"]),
        f(4, 16, width),
        f(4, 16, width),
        f(3, 8, head_w),
        f(3, 8, head_w),
        v(n_seq, n_rows, width),
        v(n_seq, n_rows, width),
        f(*wide["q"]),
        f(*wide["o"]),
        f(*wide["i"]),
        f(*wide["f"]),
        f(16, width),
        f(8, head_w),
        pltpu.SemaphoreType.DMA((14,)),
        pltpu.SemaphoreType.DMA((N_SEND,)),
        pltpu.SemaphoreType.DMA((N_RECV,)),
    ]

    def shape(*dims, dtype=F32):
        return jax.ShapeDtypeStruct(dims, dtype)

    main_out = [
        shape(n_seq, n_rows, width, dtype=BF16),
        shape(n_seq, n_rows, width, dtype=BF16),
        shape(*wide["q"]),
        shape(*wide["o"]),
        shape(*wide["i"]),
        shape(*wide["f"]),
        shape(16, width),
        shape(8, head_w),
    ]
    results = pl.pallas_call(
        fused_kernel,
        out_shape=main_out,
        in_specs=[smem, smem] + [hbm] * 6 + [vmem] * 5,
        out_specs=[hbm] * 8,
        scratch_shapes=scratch,
        compiler_params=pltpu.CompilerParams(
            collective_id=0, has_side_effects=True, vmem_limit_bytes=60 * 2**20
        ),
        name="encoder_layer",
    )(
        bucket,
        lengths,
        tokens,
        out_grad,
        qkv_weight[0],
        out_weight[0],
        ff_in_weight[0],
        jnp.transpose(ff_out_weight[0]),
        qv_bias[0],
        ff_in_bias,
        branch_bias[0],
        norm_gain[0],
        norm_bias[0],
    )
    final = pl.pallas_call(
        finish_kernel,
        out_shape=[
            shape(n_seq, n_rows, width, dtype=BF16),
            shape(n_seq, n_rows, width),
            shape(3, blk_rows, head_w),
            shape(2, head_w),
            shape(head_w, blk_rows),
            shape(blk_rows, ff),
            shape(1, ff),
            shape(blk_rows, ff),
            shape(2, width),
            shape(2, width),
            shape(2, width),
            shape(1, 3),
        ],
        in_specs=[smem] + [vmem] * 8,
        out_specs=[vmem] * 12,
        compiler_params=pltpu.CompilerParams(vmem_limit_bytes=60 * 2**20),
        name="finish",
    )(bucket, *results)
    out, tg, gq, qvb, go, gi, inb, gf, br, gain, shift, rms = final
    return (
        out,
        tg,
        gq[None],
        qvb[None],
        go[None],
        gi[None],
        inb,
        jnp.transpose(gf)[None],
        br[None],
        gain[None],
        shift[None],
        rms,
    )


def solution(mesh):
    placed = (
        P("batch", "blk", None),
        P("batch", "blk", None),
        P("batch"),
        P("batch", None),
        P(None, None, ("blk", "batch"), "tensor"),
        P(None, None, "tensor"),
        P(None, "tensor", ("blk", "batch")),
        P(None, ("blk", "batch"), "tensor"),
        P(None, "tensor"),
        P(None, "tensor", ("blk", "batch")),
        P(),
        P(),
        P(),
    )
    sizes = (mesh.shape["blk"], mesh.shape["batch"], mesh.shape["tensor"])
    body = fused_shards if sizes == (4, 2, 4) else general_shards
    return jax.shard_map(
        body,
        mesh=mesh,
        in_specs=placed,
        out_specs=(
            P("batch", "blk", None),
            P("batch", "blk", None),
            P(None, None, ("blk", "batch"), "tensor"),
            P(None, None, "tensor"),
            P(None, "tensor", ("blk", "batch")),
            P(None, ("blk", "batch"), "tensor"),
            P(None, "tensor"),
            P(None, "tensor", ("blk", "batch")),
            P(),
            P(),
            P(),
            P(),
        ),
        check_vma=False,
    )
```

```python
import functools

import jax
import jax.numpy as jnp
from jax import lax
from jax.experimental import pallas as pl
from jax.experimental.pallas import tpu as pltpu
from jax.sharding import PartitionSpec as P

HEAD = 64
SUB = 128


NEG = -1e30


def row_valid(bucket, lengths, pos):
    short = bucket[:, None] != 0
    pick = ((pos // SUB)[:, None] == jnp.arange(lengths.shape[1], dtype=jnp.int32)[None, :]).astype(
        jnp.int32
    )
    short_len = jnp.sum(lengths[:, None, :] * pick[None, :, :], axis=2)
    limit = jnp.where(short, short_len, lengths[:, :1])
    place = jnp.where(short, (pos % SUB)[None, :], pos[None, :])
    return place < limit


def seq_mask(bucket, lengths, qpos, kpos):
    short = bucket[:, None, None] != 0
    same = qpos[:, None] // SUB == kpos[None, :] // SUB
    allowed = jnp.logical_or(jnp.logical_not(short), same[None, :, :])
    return jnp.logical_and(row_valid(bucket, lengths, kpos)[:, None, :], allowed)


def layer_norm(h, gain, shift):
    mean = jnp.mean(h, -1, keepdims=True)
    cent = h - mean
    var = jnp.mean(cent * cent, -1, keepdims=True)
    return cent * lax.rsqrt(var + 1e-12) * gain + shift


def exact_gelu(value):
    return jax.nn.gelu(value, approximate=False)


def general_shards(
    tokens,
    out_grad,
    bucket,
    lengths,
    qkv_weight,
    qv_bias,
    out_weight,
    ff_in_weight,
    ff_in_bias,
    ff_out_weight,
    branch_bias,
    norm_gain,
    norm_bias,
):
    n_seq, rows_blk, width = tokens.shape
    blocks = lax.axis_size("blk")
    rank = lax.axis_index("blk")
    layers = qkv_weight.shape[0]
    local_width = qkv_weight.shape[3]
    heads_here = local_width // HEAD
    total_rows = n_seq * rows_blk
    scale = HEAD ** (-0.5)
    head_shape = (n_seq, rows_blk, heads_here, HEAD)
    qkv_full, out_full, ffin_full, ffout_full = (
        lax.all_gather(qkv_weight, ("blk", "batch"), axis=2, tiled=True),
        lax.all_gather(out_weight, ("blk", "batch"), axis=2, tiled=True),
        lax.all_gather(ff_in_weight, ("blk", "batch"), axis=1, tiled=True),
        lax.all_gather(ff_out_weight, ("blk", "batch"), axis=2, tiled=True),
    )
    local_pos = rank * rows_blk + jnp.arange(rows_blk, dtype=jnp.int32)
    row_ok = row_valid(bucket, lengths, local_pos).astype(jnp.float32).reshape(total_rows, 1)
    whole_pos = jnp.arange(blocks * rows_blk, dtype=jnp.int32)
    sub_bucket, sub_lengths = (bucket, lengths)

    def scores(query, keys, mask):
        found = (
            jnp.einsum("nqhe,nkhe->nhqk", query, keys, preferred_element_type=jnp.float32) * scale
        )
        return jnp.where(mask[:, None], found, NEG)

    x = tokens.astype(jnp.float32).reshape(total_rows, width)
    layer = 0
    xb = x.astype(jnp.bfloat16)
    triple = jnp.einsum("rd,cdk->crk", xb, qkv_full[layer], preferred_element_type=jnp.float32)
    query = (triple[0] + qv_bias[layer, 0]).astype(jnp.bfloat16).reshape(head_shape)
    keys = triple[1].astype(jnp.bfloat16).reshape(head_shape)
    values = (triple[2] + qv_bias[layer, 1]).astype(jnp.bfloat16).reshape(head_shape)
    pair = jnp.stack([keys, values])
    sub_query = query
    sub_pair = pair
    kept = lax.all_gather(sub_pair, "blk", axis=2, tiled=True)
    found = scores(sub_query, kept[0], seq_mask(sub_bucket, sub_lengths, local_pos, whole_pos))
    top = jnp.max(found, -1)
    sub_lse = top + jnp.log(jnp.sum(jnp.exp(found - top[..., None]), -1))
    weights = jnp.exp(found - sub_lse[..., None]).astype(jnp.bfloat16)
    sub_acc = jnp.einsum("nhqk,nkhe->nqhe", weights, kept[1], preferred_element_type=jnp.float32)
    lse = sub_lse
    acc = sub_acc
    att = acc.astype(jnp.bfloat16).reshape(total_rows, local_width)
    a_part = jnp.dot(att, out_full[layer], preferred_element_type=jnp.float32)
    branch = (
        lax.psum(a_part.astype(jnp.bfloat16), "tensor").astype(jnp.float32) + branch_bias[layer, 0]
    )
    upper_in = x + branch
    upper = layer_norm(upper_in, norm_gain[layer, 0], norm_bias[layer, 0])
    upper_b = upper.astype(jnp.bfloat16)
    pre = jnp.dot(upper_b, ffin_full[layer], preferred_element_type=jnp.float32) + ff_in_bias[layer]
    act = exact_gelu(pre).astype(jnp.bfloat16)
    f_part = jnp.dot(act, ffout_full[layer], preferred_element_type=jnp.float32)
    feed = (
        lax.psum(f_part.astype(jnp.bfloat16), "tensor").astype(jnp.float32) + branch_bias[layer, 1]
    )
    lower_in = upper + feed
    squares = [
        jnp.stack(
            [
                jnp.sum(row_ok * x * x),
                jnp.sum(row_ok * branch * branch),
                jnp.sum(row_ok * feed * feed),
            ]
        )
    ]
    saved = [(xb, query, pair, kept, lse, sub_lse, att, acc, upper_in, upper_b, pre, act, lower_in)]
    x = layer_norm(lower_in, norm_gain[layer, 1], norm_bias[layer, 1])
    output = x.astype(jnp.bfloat16).reshape(n_seq, rows_blk, width)
    grad = out_grad.astype(jnp.float32).reshape(total_rows, width)
    g_qkv, g_out, g_in, g_outf = ([], [], [], [])
    g_qvb, g_inb, g_branch, g_gain, g_shift = ([], [], [], [], [])
    for layer in reversed(range(layers)):
        xb, query, pair, kept, lse, sub_lse, att, acc, upper_in, upper_b, pre, act, lower_in = (
            saved[layer]
        )
        _, lower_back = jax.vjp(layer_norm, lower_in, norm_gain[layer, 1], norm_bias[layer, 1])
        d_lower, d_gain2, d_shift2 = lower_back(grad)
        d_feed = d_lower.astype(jnp.bfloat16)
        d_fbias = jnp.sum(d_feed.astype(jnp.float32), 0)
        g_outf.append(jnp.einsum("rf,rd->fd", act, d_feed, preferred_element_type=jnp.float32))
        d_act = jnp.einsum(
            "rd,fd->rf", d_feed, ffout_full[layer], preferred_element_type=jnp.float32
        )
        _, gelu_back = jax.vjp(exact_gelu, pre)
        d_pre = gelu_back(d_act)[0].astype(jnp.bfloat16)
        g_inb.append(jnp.sum(d_pre.astype(jnp.float32), 0))
        g_in.append(jnp.einsum("rd,rf->df", upper_b, d_pre, preferred_element_type=jnp.float32))
        ffn_part = jnp.einsum(
            "rf,df->rd", d_pre, ffin_full[layer], preferred_element_type=jnp.float32
        )
        d_upper = d_lower + lax.psum(ffn_part.astype(jnp.bfloat16), "tensor").astype(jnp.float32)
        _, upper_back = jax.vjp(layer_norm, upper_in, norm_gain[layer, 0], norm_bias[layer, 0])
        d_upper_in, d_gain1, d_shift1 = upper_back(d_upper)
        d_branch = d_upper_in.astype(jnp.bfloat16)
        d_abias = jnp.sum(d_branch.astype(jnp.float32), 0)
        g_out.append(jnp.einsum("rk,rd->kd", att, d_branch, preferred_element_type=jnp.float32))
        d_att = (
            jnp.einsum("rd,kd->rk", d_branch, out_full[layer], preferred_element_type=jnp.float32)
            .astype(jnp.bfloat16)
            .reshape(head_shape)
        )
        delta = jnp.einsum("nqhe,nqhe->nhq", d_att.astype(jnp.float32), acc)
        sub_query, sub_datt, sub_delta = (query, d_att, delta)
        block_keys = kept[0]
        block_found = scores(
            sub_query, block_keys, seq_mask(sub_bucket, sub_lengths, local_pos, whole_pos)
        )
        prob = jnp.exp(block_found - sub_lse[..., None])
        d_prob = jnp.einsum(
            "nqhe,nkhe->nhqk", sub_datt, kept[1], preferred_element_type=jnp.float32
        )
        d_scores = (prob * (d_prob - sub_delta[..., None])).astype(jnp.bfloat16)
        d_query = jnp.einsum(
            "nhqk,nkhe->nqhe", d_scores, block_keys, preferred_element_type=jnp.float32
        )
        d_keys = jnp.einsum(
            "nhqk,nqhe->nkhe", d_scores, sub_query, preferred_element_type=jnp.float32
        )
        d_values = jnp.einsum(
            "nhqk,nqhe->nkhe",
            prob.astype(jnp.bfloat16),
            sub_datt,
            preferred_element_type=jnp.float32,
        )
        sub_dq = d_query
        dpair_all = jnp.stack([d_keys * scale, d_values])
        sub_dpair = lax.psum_scatter(
            dpair_all.astype(jnp.bfloat16), "blk", scatter_dimension=2, tiled=True
        ).astype(jnp.float32)
        d_query, d_pair = (sub_dq, sub_dpair)
        dq_b = (d_query * scale).astype(jnp.bfloat16).reshape(total_rows, local_width)
        dk_b = d_pair[0].astype(jnp.bfloat16).reshape(total_rows, local_width)
        dv_b = d_pair[1].astype(jnp.bfloat16).reshape(total_rows, local_width)
        d_triple = jnp.stack([dq_b, dk_b, dv_b])
        g_qvb.append(
            jnp.stack([jnp.sum(dq_b.astype(jnp.float32), 0), jnp.sum(dv_b.astype(jnp.float32), 0)])
        )
        g_qkv.append(jnp.einsum("rd,crk->cdk", xb, d_triple, preferred_element_type=jnp.float32))
        attn_part = jnp.einsum(
            "crk,cdk->rd", d_triple, qkv_full[layer], preferred_element_type=jnp.float32
        )
        grad = d_upper_in + lax.psum(attn_part.astype(jnp.bfloat16), "tensor").astype(jnp.float32)
        g_branch.append(jnp.stack([d_abias, d_fbias]))
        g_gain.append(jnp.stack([d_gain1, d_gain2]))
        g_shift.append(jnp.stack([d_shift1, d_shift2]))

    def in_order(items):
        return jnp.stack(items[::-1])

    qkv_g, out_g, in_g, outf_g = (
        lax.psum_scatter(in_order(g_qkv), ("blk", "batch"), scatter_dimension=2, tiled=True),
        lax.psum_scatter(in_order(g_out), ("blk", "batch"), scatter_dimension=2, tiled=True),
        lax.psum_scatter(in_order(g_in), ("blk", "batch"), scatter_dimension=1, tiled=True),
        lax.psum_scatter(in_order(g_outf), ("blk", "batch"), scatter_dimension=2, tiled=True),
    )
    count = jnp.sum(row_ok)
    qvb_g, inb_g, branch_g, gain_g, shift_g, square_sums, count_all = lax.psum(
        (
            in_order(g_qvb),
            in_order(g_inb),
            in_order(g_branch),
            in_order(g_gain),
            in_order(g_shift),
            jnp.stack(squares),
            count,
        ),
        ("blk", "batch"),
    )
    rms = jnp.sqrt(square_sums / (count_all * width))
    tokens_grad = grad.reshape(n_seq, rows_blk, width)
    return (
        output,
        tokens_grad,
        qkv_g,
        qvb_g,
        out_g,
        in_g,
        inb_g,
        outf_g,
        branch_g,
        gain_g,
        shift_g,
        rms,
    )


MESH = pl.DeviceIdType.MESH
F32 = jnp.float32
BF16 = jnp.bfloat16
N_SEND = 48
N_RECV = 128
ORDER = (
    "first", "enter", "q.issue", "f0.issue", "zw", "q.fy", "q.fx", "o0.issue", "o1.issue",
    "i0.issue", "q.last", "kv", "query", "o0.fx", "f0.fx", "att2", "o1.fx", "o1.fy", "o0.fy",
    "i1.issue", "i0.fy", "o0.last", "kvpass", "att1", "f1.issue", "o1.last", "i0.fx", "att0",
    "proj2", "i1.fx", "f0.fy", "proj1", "i1.fy", "proj0", "f1.fx", "f1.fy", "ln12", "i0.last",
    "f0.last", "ln11", "i1.last", "f1.last", "ln10", "hidden", "feed0", "feed1", "turn_y",
    "feed2", "ln20", "ln21", "ln22", "gi1", "turn_x", "ln1b0", "out20", "i1.r1", "ln1b1",
    "ln1b2", "gf1", "gi0", "attb0", "out22", "out21", "i1.r2x", "i1.r2y", "attb1", "vec0",
    "attb2", "kvback", "dxb1", "f1.r1", "zi", "vec1", "i0.r1", "go", "dxa1", "bias0", "bias1",
    "vec2", "dxb2", "gq", "gf0", "q.r1", "vec3", "f1.r2x", "f1.r2y", "o1.r1", "out11", "dxa2",
    "out10", "o0.r1", "dxb3", "o0.r2x", "f0.r1", "putvec", "dxa3", "q.r2y", "out12", "o1.r2x",
    "bias2", "o1.r2y", "i0.r2x", "i0.r2y", "zf", "o0.r2y", "f0.r2x", "putout", "q.r2x",
    "f0.r2y", "dxa4", "zo", "dxb4", "putf", "puti", "putbias", "putq", "putdx", "puto",
)


def dot_nn(a, b):
    return lax.dot_general(a, b, (((1,), (0,)), ((), ())), preferred_element_type=F32)


def dot_nt(a, b):
    return lax.dot_general(a, b, (((1,), (1,)), ((), ())), preferred_element_type=F32)


def dot_tn(a, b):
    return lax.dot_general(a, b, (((0,), (0,)), ((), ())), preferred_element_type=F32)


def slot_order(bucket_ref):
    first = jnp.where(bucket_ref[0] == 0, 0, jnp.where(bucket_ref[1] == 0, 1, 2))
    second = jnp.where(first == 0, 1, 0)
    third = jnp.where(first == 2, 1, 2)
    return first, second, third


class Net:
    def __init__(self, send_sems, recv_sems):
        self.send_sems, self.recv_sems = send_sems, recv_sems
        self.copies, self.n_recv = [], 0

    def slot(self):
        self.n_recv += 1
        assert self.n_recv <= N_RECV
        return self.n_recv - 1

    def send(self, src, dst, peer, slot=None):
        at = len(self.copies)
        if at >= N_SEND:
            self.copies[at - N_SEND].wait_send()
        copy = pltpu.make_async_remote_copy(
            src_ref=src,
            dst_ref=dst,
            send_sem=self.send_sems.at[at % N_SEND],
            recv_sem=self.recv_sems.at[self.slot() if slot is None else slot],
            device_id=peer,
            device_id_type=MESH,
        )
        copy.start()
        self.copies.append(copy)
        return copy

    def whole(self, ref, peer, slot):
        return pltpu.make_async_remote_copy(
            src_ref=ref,
            dst_ref=ref,
            send_sem=self.send_sems.at[0],
            recv_sem=self.recv_sems.at[slot],
            device_id=peer,
            device_id_type=MESH,
        )

    def finish(self):
        for copy in self.copies[-N_SEND:]:
            copy.wait_send()


class Gather:
    def __init__(self, net, view, at, near):
        self.net, self.view, self.near = net, view, near
        self.own, self.x, self.y, self.d, self.size = at
        self.half = self.size // 2
        self.slot = net.slot()

    def part(self, start, size):
        return self.view(pl.ds(pl.multiple_of(start, 16), size))

    def to_core(self, ref):
        self.net.send(ref, ref, self.near[2], self.slot)

    def issue(self, src=None):
        xnb, ynb, core = self.near
        to = self.part(self.own, self.size)
        src = to if src is None else src
        self.from_x = self.net.send(src, to, xnb)
        self.from_y = self.net.send(src, to, ynb)
        self.net.send(src, to, core, self.slot)

    def forward_x(self):
        xnb, ynb, core = self.near
        self.from_x.wait_recv()
        ref = self.part(self.x, self.half)
        self.first = self.net.send(ref, ref, ynb)
        self.to_core(self.part(self.x, self.size))

    def forward_y(self):
        xnb, ynb, core = self.near
        self.from_y.wait_recv()
        ref = self.part(self.y + self.half, self.half)
        self.second = self.net.send(ref, ref, xnb)
        self.to_core(self.part(self.y, self.size))

    def last(self):
        self.first.wait_recv()
        self.second.wait_recv()
        self.to_core(self.part(self.d, self.size))

    def ready(self):
        self.net.whole(self.part(0, 4 * self.size), self.near[2], self.slot).wait_recv()


class Scatter:
    def __init__(self, net, refs, spot, near):
        self.net, self.spot, self.near = net, spot, near
        self.g, self.d, self.h, self.p1, self.s, self.p2 = refs
        self.rows = self.g.shape[3]
        self.half = self.rows // 2

    def core(self):
        c = self.spot[1]
        self.c1 = self.net.send(self.g.at[:, 1 - c], self.d, self.near[2])

    def first(self):
        yy, c, t = self.spot
        xnb, ynb, _ = self.near
        lo, hi = pl.ds(0, self.half), pl.ds(self.half, self.half)
        self.c1.wait_recv()
        for a in range(2):
            for b in range(2):
                self.h[a, b] = (self.g[a, c, b].astype(F32) + self.d[a, b].astype(F32)).astype(BF16)
        self.px = self.net.send(self.h.at[:, 1 - t, lo], self.p1.at[0], xnb)
        self.py = self.net.send(self.h.at[1 - yy, :, hi], self.p1.at[1], ynb)

    def second_x(self):
        yy, c, t = self.spot
        xnb, ynb, _ = self.near
        lo = pl.ds(0, self.half)
        self.px.wait_recv()
        self.s[0] = (self.h[1 - yy, t, lo].astype(F32) + self.p1[0, 1 - yy].astype(F32)).astype(BF16)
        self.qy = self.net.send(self.s.at[0], self.p2.at[0], ynb)

    def second_y(self):
        yy, c, t = self.spot
        xnb, ynb, _ = self.near
        hi = pl.ds(self.half, self.half)
        self.py.wait_recv()
        self.s[1] = (self.h[yy, 1 - t, hi].astype(F32) + self.p1[1, 1 - t].astype(F32)).astype(BF16)
        self.qx = self.net.send(self.s.at[1], self.p2.at[1], xnb)

    def result(self):
        yy, c, t = self.spot
        self.qy.wait_recv()
        self.qx.wait_recv()
        lo, hi = pl.ds(0, self.half), pl.ds(self.half, self.half)
        low = self.h[yy, t, lo].astype(F32) + self.p1[0, yy].astype(F32) + self.p2[0].astype(F32)
        high = self.h[yy, t, hi].astype(F32) + self.p1[1, t].astype(F32) + self.p2[1].astype(F32)
        return low, high


def fused_kernel(*refs):
    (
        bucket, lengths, tokens, out_grad, qkv_w, out_w, ffi_w, ffo_w, qv_bias, ffi_b, br_bias, gain, shift,
        out_hbm, tg_hbm, gq_hbm, go_hbm, gi_hbm, gf_hbm, vec_hbm, qvb_hbm,
        tok, cot, w_q, w_o, w_i, w_f, own_o, bias_r, xs, xs_t, q_r, k_r, v_r, kv_a, p_a, p_b,
        att, att_r, ps, pr, xh1, rstd1, yb, act, gp, dh2, dfb, dab, df_t, yb_t, dpre, dh1, da_t,
        datt, datt_s, dkv_s, dkv_c, dkv_t, dkv_y, dtri, dx_p, dx_s, dx_1, dx_2, dx_t,
        sc_q, sc_o, sc_i, sc_f, z_o, z_i, z_f, t_o, t_i, t_f, vs, vr, qs, qr,
        out_v, tg_v, gq_v, go_v, gi_v, gf_v, vec_v, qvb_v,
        local_sems, send_sems, recv_sems,
    ) = refs
    n_seq, n_rows, width = tok.shape
    blk_rows = ffi_w.shape[0]
    head_w = qkv_w.shape[2]
    heads = head_w // HEAD
    half, quart = n_rows // 2, n_rows // 4
    tile = 256
    n_tile = width // tile
    scale = HEAD ** (-0.5)

    r = lax.axis_index("blk")
    t = lax.axis_index("batch")
    z = lax.axis_index("tensor")
    yy, c = r // 2, r % 2
    pz, qz = z // 2, z % 2
    r1, r2 = r + 1 - 2 * c, (r + 2) % 4
    z1, z2 = z + 1 - 2 * qz, (z + 2) % 4
    core, xnb, ynb = (r1, t, z), (r, 1 - t, z), (r2, t, z)
    zn1, zn2 = (r, t, z1), (r, t, z2)
    peers = (zn2, zn1, xnb, ynb, core)
    near = (xnb, ynb, core)

    barrier = pltpu.get_barrier_semaphore()
    for peer in peers:
        pl.semaphore_signal(barrier, inc=1, device_id=peer, device_id_type=MESH)

    net = Net(send_sems, recv_sems)

    def block(rr, tt):
        return (rr * 2 + tt) * blk_rows

    at = (block(r, t), block(r, 1 - t), block(r2, t), block(r2, 1 - t), blk_rows)
    own = pl.ds(pl.multiple_of(block(r, t), 32), blk_rows)

    def gather(view):
        return Gather(net, view, at, near)

    ga_q = gather(lambda rows: w_q.at[:, rows])
    ga_o = [gather(lambda rows, k=k: w_o.at[k, rows]) for k in range(2)]
    ga_i = [gather(lambda rows, k=k: w_i.at[k, rows]) for k in range(2)]
    ga_f = [gather(lambda rows, k=k: w_f.at[k, rows]) for k in range(2)]

    local = [
        pltpu.make_async_copy(src, dst, local_sems.at[k])
        for k, (src, dst) in enumerate(
            (
                (out_w, own_o),
                (tokens, tok),
                (qkv_w, w_q.at[:, own]),
                (ffi_w, w_i.at[0, own]),
                (ffo_w, w_f.at[0, own]),
                (out_grad, cot),
            )
        )
    ]
    for copy in local:
        copy.start()
    stores = []

    def store(src, dst):
        copy = pltpu.make_async_copy(src, dst, local_sems.at[len(local) + len(stores)])
        copy.start()
        stores.append(copy)

    st = {}

    order = slot_order(bucket)

    def weights_first():
        local[0].wait()
        w_o[0, own] = jnp.transpose(own_o[...])
        local[1].wait()
        for s in range(n_seq):
            xs[s * n_rows : (s + 1) * n_rows] = tok[order[s]]

    def enter():
        pl.semaphore_wait(barrier, len(peers))

    def z_weights():
        st["zo"] = net.send(w_o.at[0, own], w_o.at[1, own], zn2)
        st["zi"] = net.send(ffi_w, w_i.at[1, own], zn2)
        st["zf"] = net.send(ffo_w, w_f.at[1, own], zn2)
        st["zb"] = net.send(ffi_b, bias_r, zn2)

    def issue_second(kind, gather):
        st["z" + kind].wait_recv()
        gather.issue()

    def turn_x():
        xs_t[...] = jnp.transpose(xs[...])

    def keys_of(rr):
        return kv_a.at[:, pl.ds(pl.multiple_of(rr * n_rows, n_rows), n_rows)]

    def keys_values():
        local[2].wait()
        ga_q.ready()
        k_r[...] = dot_nn(xs[...], w_q[1]).astype(BF16)
        v_r[...] = (dot_nn(xs[...], w_q[2]) + qv_bias[1:2, :]).astype(BF16)
        mine = pl.ds(pl.multiple_of(r * n_rows, n_rows), n_rows)
        kv_a[0, mine] = k_r[0:n_rows]
        kv_a[1, mine] = v_r[0:n_rows]
        st["kv_y"] = net.send(keys_of(r), keys_of(r), ynb)
        st["kv_c"] = [net.send(keys_of(r), keys_of(r), core)]

    def keys_pass():
        st["kv_y"].wait_recv()
        st["kv_c"].append(net.send(keys_of(r2), keys_of(r2), core))

    def queries():
        q_r[...] = (dot_nn(xs[...], w_q[0]) + qv_bias[0:1, :]).astype(BF16)

    lane_head = lax.broadcasted_iota(jnp.int32, (1, head_w), 1) // HEAD

    def of_head(value, h):
        return jnp.where(lane_head == h, value, jnp.zeros_like(value))

    def limit_of(s):
        index = order[s]
        return lengths[index, r], lengths[index, 0]

    own_half = pl.ds(pl.multiple_of(pz * half, half), half)
    other_half = pl.ds(pl.multiple_of((1 - pz) * half, half), half)
    key_at = lax.broadcasted_iota(jnp.int32, (1, n_rows), 1)

    def rows_at(s):
        return slice(s * n_rows, (s + 1) * n_rows)

    def few_at(s):
        return slice(s * half, (s + 1) * half)

    def attend(s):
        if s == 0:
            for copy in st["kv_c"]:
                copy.wait_recv()
            keys, values, probs, key_ok = kv_a[0], kv_a[1], p_a, None
        else:
            keys, values, probs = k_r[rows_at(s)], v_r[rows_at(s)], p_b.at[s - 1]
            key_ok = key_at < limit_of(s)[0]
        query = q_r[rows_at(s)]
        total = jnp.zeros((n_rows, head_w), F32)
        for h in range(heads):
            score = dot_nt(of_head(query, h), keys) * scale
            if key_ok is not None:
                score = jnp.where(key_ok, score, NEG)
            e = jnp.exp(score - jnp.max(score, -1, keepdims=True))
            prob = e / jnp.sum(e, -1, keepdims=True)
            probs[h] = prob
            total = total + dot_nn(prob.astype(BF16), of_head(values, h))
        att[s] = total.astype(BF16)
        st["att", s] = net.send(att.at[s, other_half], att_r.at[s], zn2)

    def pair_send(k, s, value):
        ps[k, s] = value.astype(BF16)
        st["pair", k, s] = net.send(ps.at[k, s], pr.at[k, s], zn1)

    def pair_sum(k, s):
        st["pair", k, s].wait_recv()
        return ps[k, s].astype(F32) + pr[k, s].astype(F32)

    def ready(kind, gathers):
        if ("ready", kind) not in st:
            st["ready", kind] = True
            for gather in gathers:
                gather.ready()

    def project(s):
        ready("o", ga_o)
        st["att", s].wait_recv()
        pair_send(0, s, dot_nt(att[s, own_half], w_o[0]) + dot_nt(att_r[s], w_o[1]))

    vec = {k: jnp.zeros((1, width), F32) for k in range(12)}
    row_at = lax.broadcasted_iota(jnp.int32, (half, 1), 0)

    def row_ok(s):
        short, full = limit_of(s)
        place = row_at + pz * half
        ok = place + r * n_rows < full if s == 0 else place < short
        return ok.astype(F32)

    def tally(k, value):
        vec[k] = vec[k] + jnp.sum(value, 0, keepdims=True)

    def mean_of(value):
        return jnp.mean(value, -1, keepdims=True)

    def normed(h):
        cent = h - mean_of(h)
        rstd = lax.rsqrt(mean_of(cent * cent) + 1e-12)
        return cent * rstd, rstd

    def first_norm(s):
        here = few_at(s)
        x = xs[pl.ds(pl.multiple_of(s * n_rows + pz * half, half), half)].astype(F32)
        branch = pair_sum(0, s) + br_bias[0:1, :]
        ok = row_ok(s)
        tally(8, ok * (x * x))
        tally(9, ok * (branch * branch))
        tally(11, ok * jnp.ones((1, width), F32))
        hat, rstd = normed(x + branch)
        xh1[here] = hat
        rstd1[here] = rstd
        yb[here] = (hat * gain[0:1, :] + shift[0:1, :]).astype(BF16)

    def turn_y():
        yb_t[...] = jnp.transpose(yb[...])

    def hidden():
        st["zb"].wait_recv()
        local[3].wait()
        ready("i", ga_i)
        for k in range(2):
            for n in range(n_tile):
                cols = slice(n * tile, (n + 1) * tile)
                bias = ffi_b[:, cols] if k == 0 else bias_r[:, cols]
                pre = dot_nn(yb[...], w_i[k, :, cols]) + bias
                phi = 0.5 * (1.0 + lax.erf(pre * (0.5**0.5)))
                act[k, :, cols] = (pre * phi).astype(BF16)
                gp[k, :, cols] = phi + pre * (jnp.exp(-0.5 * pre * pre) * 0.3989422804014327)

    def feed_out(s):
        if s == 0:
            local[4].wait()
            local[5].wait()
        ready("f", ga_f)
        here = few_at(s)
        pair_send(1, s, dot_nt(act[0, here], w_f[0]) + dot_nt(act[1, here], w_f[1]))

    def second_norm(s):
        here = few_at(s)
        feed = pair_sum(1, s) + br_bias[1:2, :]
        tally(10, row_ok(s) * (feed * feed))
        hat, rstd = normed(xh1[here] * gain[0:1, :] + shift[0:1, :] + feed)
        out_v[s, own_half] = (hat * gain[1:2, :] + shift[1:2, :]).astype(BF16)
        g = cot[order[s], own_half].astype(F32)
        tally(1, g * hat)
        tally(2, g)
        g = g * gain[1:2, :]
        d = rstd * (g - mean_of(g) - hat * mean_of(g * hat))
        dh2[here] = d
        d = d.astype(BF16)
        dfb[here] = d
        tally(0, d.astype(F32))
        total = jnp.zeros((half, width), F32)
        for k in range(2):
            p = (dot_nn(d, w_f[k]) * gp[k, here]).astype(BF16)
            dpre[k, here] = p
            tally(3 + k, p.astype(F32))
            total = total + dot_nt(p, w_i[k])
        pair_send(2, s, total)

    quarter = pl.ds(pl.multiple_of(z * quart, quart), quart)
    quarter_2 = pl.ds(pl.multiple_of(z2 * quart, quart), quart)

    def out_far(s):
        here = out_v.at[s, quarter]
        st["out2", s] = net.send(here, here, zn2)

    def out_near(s):
        st["out2", s].wait_recv()
        there = out_v.at[s, quarter_2]
        st["out1", s] = net.send(there, there, zn1)

    def scatter(refs, k=None):
        views = refs if k is None else [ref.at[k] for ref in refs]
        return Scatter(net, views, (yy, c, t), near)

    rs_f = [scatter(sc_f, k) for k in range(2)]
    rs_i = [scatter(sc_i, k) for k in range(2)]
    rs_o = [scatter(sc_o, k) for k in range(2)]
    rs_q = scatter(sc_q)

    def grads(lhs, rhs, out, rows=None):
        value = dot_nn(lhs, rhs).astype(BF16)
        for b in range(8):
            piece = value[b * blk_rows : (b + 1) * blk_rows]
            if rows is None:
                out[b // 4, (b // 2) % 2, b % 2] = piece
            else:
                out[b // 4, (b // 2) % 2, b % 2, rows] = piece

    def grads_wide(left, right, rs):
        for n in range(n_tile):
            cols = slice(n * tile, (n + 1) * tile)
            grads(left[...], right[:, cols], rs.g.at[:, :, :, :, cols])
        rs.core()

    def grad_f(k):
        if k == 1:
            df_t[...] = jnp.transpose(dfb[...])
        grads_wide(df_t, act.at[k], rs_f[k])

    def grad_i(k):
        grads_wide(yb_t, dpre.at[k], rs_i[k])

    def grad_o():
        da_t[...] = jnp.transpose(dab[...])
        rows_l = jnp.concatenate([att[s, own_half] for s in range(n_seq)], 0)
        rows_r = jnp.concatenate([att_r[s] for s in range(n_seq)], 0)
        grads(da_t[...], rows_r, rs_o[1].g)
        rs_o[1].core()
        grads(da_t[...], rows_l, rs_o[0].g)
        rs_o[0].core()

    def grad_q():
        for k in range(3):
            grads(xs_t[...], dtri[k], rs_q.g, slice(k * blk_rows, (k + 1) * blk_rows))
        rs_q.core()

    def first_norm_back(s):
        here = few_at(s)
        hat = xh1[here]
        g = dh2[here] + pair_sum(2, s)
        tally(6, g * hat)
        tally(7, g)
        g = g * gain[0:1, :]
        d = rstd1[here] * (g - mean_of(g) - hat * mean_of(g * hat))
        dh1[here] = d
        d = d.astype(BF16)
        dab[here] = d
        tally(5, d.astype(F32))
        datt_s[s] = dot_nn(d, w_o[1]).astype(BF16)
        st["datt", s] = net.send(datt_s.at[s], datt.at[s, own_half], zn2)
        datt[s, own_half] = dot_nn(d, w_o[0]).astype(BF16)

    def vec_step(k):
        if k == 0:
            for n in range(12):
                vs[0, n : n + 1] = vec[n]
            vs[0, 12:16] = jnp.zeros((4, width), F32)
        else:
            st["vec"].wait_recv()
            vs[k] = vs[k - 1] + vr[k - 1]
        st["vec"] = net.send(vs.at[k], vr.at[k], (core, xnb, ynb, zn2)[k])

    def attend_back(s):
        st["datt", s].wait_recv()
        if s == 0:
            keys, values, probs = kv_a[0], kv_a[1], p_a
        else:
            keys, values, probs = k_r[rows_at(s)], v_r[rows_at(s)], p_b.at[s - 1]
        query = q_r[rows_at(s)]
        d_att = datt[s]
        dq = jnp.zeros((n_rows, head_w), F32)
        dk = jnp.zeros(keys.shape, F32)
        dv = jnp.zeros(keys.shape, F32)
        for h in range(heads):
            prob = probs[h]
            d_h = of_head(d_att, h)
            dp = dot_nt(d_h, values)
            delta = jnp.sum(prob * dp, -1, keepdims=True)
            ds = (prob * (dp - delta)).astype(BF16)
            dq = dq + dot_nn(ds, of_head(keys, h))
            dk = dk + dot_tn(ds, of_head(query, h))
            dv = dv + dot_tn(prob.astype(BF16), d_h)
        dtri[0, rows_at(s)] = (dq * scale).astype(BF16)
        dk, dv = (dk * scale).astype(BF16), dv.astype(BF16)
        if s == 0:
            for a in range(4):
                dkv_s[a // 2, a % 2, 0] = dk[rows_at(a)]
                dkv_s[a // 2, a % 2, 1] = dv[rows_at(a)]
            st["dkv1"] = net.send(dkv_s.at[:, 1 - c], dkv_c, core)
        else:
            dtri[1, rows_at(s)] = dk
            dtri[2, rows_at(s)] = dv

    def keys_back():
        st["dkv1"].wait_recv()
        dkv_t[...] = (dkv_s[1 - yy, c].astype(F32) + dkv_c[1 - yy].astype(F32)).astype(BF16)
        st["dkv2"] = net.send(dkv_t, dkv_y, ynb)

    def dx_of(s):
        total = dot_nt(dtri[0, rows_at(s)], w_q[0])
        for k in range(1, 3):
            total = total + dot_nt(dtri[k, rows_at(s)], w_q[k])
        dx_p[s] = total
        for a in range(4):
            dx_s[a // 2, a % 2, s] = total[a * quart : (a + 1) * quart].astype(BF16)

    def half_rows(s):
        return pl.ds(pl.multiple_of(s * half + qz * quart, quart), quart)

    groups = {"b": (1, n_seq), "a": (0, 1)}

    def dx_first(group):
        lo, hi = groups[group]
        if group == "a":
            st["dkv2"].wait_recv()
            total = dkv_s[yy, c].astype(F32) + dkv_c[yy].astype(F32) + dkv_y[...].astype(F32)
            dtri[1, 0:n_rows] = total[0].astype(BF16)
            dtri[2, 0:n_rows] = total[1].astype(BF16)
        for s in range(lo, hi):
            dx_of(s)
        st[group, 1] = net.send(dx_s.at[:, 1 - qz, lo:hi], dx_1.at[:, lo:hi], zn1)

    def dx_second(group):
        lo, hi = groups[group]
        st[group, 1].wait_recv()
        for s in range(lo, hi):
            dx_t[s] = (dx_p[s, quarter_2] + dx_1[1 - pz, s].astype(F32)).astype(BF16)
        st[group, 2] = net.send(dx_t.at[lo:hi], dx_2.at[lo:hi], zn2)

    def dx_third(group):
        lo, hi = groups[group]
        st[group, 2].wait_recv()
        for s in range(lo, hi):
            total = dx_p[s, quarter] + dx_1[pz, s].astype(F32) + dx_2[s].astype(F32)
            tg_v[s, quarter] = (total + dh1[half_rows(s)]).astype(BF16)
        here = tg_v.at[lo:hi, quarter]
        st[group, 3], st[group, 4] = net.send(here, here, zn2), net.send(here, here, zn1)

    def dx_last(group):
        lo, hi = groups[group]
        st[group, 3].wait_recv()
        there = tg_v.at[lo:hi, quarter_2]
        st[group, 5] = net.send(there, there, zn1)

    def bias_step(k):
        if k == 0:
            qs[0] = jnp.zeros(qs.shape[1:], F32)
            for n, m in enumerate((0, 2)):
                qs[0, n : n + 1] = jnp.sum(dtri[m].astype(F32), 0, keepdims=True)
        else:
            st["bias"].wait_recv()
            qs[k] = qs[k - 1] + qr[k - 1]
        st["bias"] = net.send(qs.at[k], qr.at[k], (core, xnb, ynb)[k])

    def to_z(kind, rs, buf, got):
        low, high = rs.result()
        n = low.shape[0]
        buf[0:n] = low.astype(BF16)
        buf[n : 2 * n] = high.astype(BF16)
        st["g" + kind] = net.send(buf, got, zn2)

    def put(kind, rs, out, to, got=None):
        low, high = rs.result()
        n = low.shape[0]
        if got is not None:
            st["g" + kind].wait_recv()
            low = low + got[0:n].astype(F32)
            high = high + got[n : 2 * n].astype(F32)
        out[0:n] = low
        out[n : 2 * n] = high
        store(out, to)

    def out_store():
        for s in range(n_seq):
            st["out1", s].wait_recv()
        store(out_v, out_hbm)

    def vec_store():
        st["vec"].wait_recv()
        vec_v[...] = vs[3] + vr[3]
        vec_v[3:4] = vs[3, 3:4] + vr[3, 4:5]
        vec_v[4:5] = vs[3, 4:5] + vr[3, 3:4]
        store(vec_v, vec_hbm)

    def bias_store():
        st["bias"].wait_recv()
        qvb_v[...] = qs[2] + qr[2]
        store(qvb_v, qvb_hbm)

    def dx_store():
        for group in groups:
            for k in (4, 5):
                st[group, k].wait_recv()
        store(tg_v, tg_hbm)

    steps = {
        "first": weights_first,
        "enter": enter,
        "zw": z_weights,
        "q.issue": lambda: ga_q.issue(qkv_w),
        "o0.issue": lambda: ga_o[0].issue(),
        "i0.issue": lambda: ga_i[0].issue(ffi_w),
        "f0.issue": lambda: ga_f[0].issue(ffo_w),
        "turn_x": turn_x,
        "kv": keys_values,
        "kvpass": keys_pass,
        "query": queries,
        "turn_y": turn_y,
        "hidden": hidden,
        "go": grad_o,
        "gq": grad_q,
        "kvback": keys_back,
        "zf": lambda: to_z("f", rs_f[1], t_f, z_f),
        "zi": lambda: to_z("i", rs_i[1], t_i, z_i),
        "zo": lambda: to_z("o", rs_o[1], t_o, z_o),
        "putf": lambda: put("f", rs_f[0], gf_v, gf_hbm, z_f),
        "puti": lambda: put("i", rs_i[0], gi_v, gi_hbm, z_i),
        "puto": lambda: put("o", rs_o[0], go_v, go_hbm, z_o),
        "putq": lambda: put("q", rs_q, gq_v, gq_hbm),
        "putout": out_store,
        "putvec": vec_store,
        "putbias": bias_store,
        "putdx": dx_store,
    }
    gathers = {"q": ga_q, "o0": ga_o[0], "o1": ga_o[1], "i0": ga_i[0], "i1": ga_i[1], "f0": ga_f[0], "f1": ga_f[1]}
    for name, gather in gathers.items():
        if name[1:] == "1":
            steps[name + ".issue"] = functools.partial(issue_second, name[0], gather)
        steps[name + ".fx"] = gather.forward_x
        steps[name + ".fy"] = gather.forward_y
        steps[name + ".last"] = gather.last
    sums = {"q": rs_q, "o0": rs_o[0], "o1": rs_o[1], "i0": rs_i[0], "i1": rs_i[1], "f0": rs_f[0], "f1": rs_f[1]}
    for name, rs in sums.items():
        steps[name + ".r1"] = rs.first
        steps[name + ".r2x"] = rs.second_x
        steps[name + ".r2y"] = rs.second_y
    for s in range(n_seq):
        for name, call in (
            ("att", attend),
            ("proj", project),
            ("ln1", first_norm),
            ("feed", feed_out),
            ("ln2", second_norm),
            ("ln1b", first_norm_back),
            ("attb", attend_back),
            ("out2", out_far),
            ("out1", out_near),
        ):
            steps[name + str(s)] = functools.partial(call, s)
    for group in groups:
        for k, call in enumerate((dx_first, dx_second, dx_third, dx_last)):
            steps["dx" + group + str(k + 1)] = functools.partial(call, group)
    for k in range(2):
        steps["gf" + str(k)] = functools.partial(grad_f, k)
        steps["gi" + str(k)] = functools.partial(grad_i, k)
    for k in range(4):
        steps["vec" + str(k)] = functools.partial(vec_step, k)
    for k in range(3):
        steps["bias" + str(k)] = functools.partial(bias_step, k)

    assert set(ORDER) == set(steps) and len(ORDER) == len(steps)
    for name in ORDER:
        steps[name]()
    for copy in stores:
        copy.wait()
    net.finish()


def finish_kernel(
    bucket,
    out_i,
    tg_i,
    gq_i,
    go_i,
    gi_i,
    gf_i,
    vec_i,
    qvb_i,
    out_o,
    tg_o,
    gq_o,
    qvb_o,
    go_o,
    gi_o,
    inb_o,
    gf_o,
    br_o,
    gain_o,
    shift_o,
    rms_o,
):
    order = slot_order(bucket)
    for s in range(3):
        at = jnp.where(order[0] == s, 0, jnp.where(order[1] == s, 1, 2))
        out_o[s] = out_i[at]
        tg_o[s] = tg_i[at].astype(F32)
    n = gq_o.shape[1]
    for k in range(3):
        gq_o[k] = gq_i[k * n : (k + 1) * n]
    go_o[...] = jnp.transpose(go_i[...])
    gi_o[...] = gi_i[...]
    gf_o[...] = gf_i[...]
    qvb_o[...] = qvb_i[0:2]
    inb_o[...] = vec_i[3:4]
    br_o[0:1] = vec_i[5:6]
    br_o[1:2] = vec_i[0:1]
    gain_o[0:1] = vec_i[6:7]
    gain_o[1:2] = vec_i[1:2]
    shift_o[0:1] = vec_i[7:8]
    shift_o[1:2] = vec_i[2:3]
    width = vec_i.shape[1]
    count = vec_i[11:12, 0:1]
    square = jnp.sum(vec_i[8:11], 1, keepdims=True)
    rms = jnp.sqrt(square / (count * width))
    lane = lax.broadcasted_iota(jnp.int32, (1, 3), 1)
    out = jnp.zeros((1, 3), F32)
    for k in range(3):
        out = jnp.where(lane == k, rms[k : k + 1], out)
    rms_o[...] = out


def fused_shards(
    tokens,
    out_grad,
    bucket,
    lengths,
    qkv_weight,
    qv_bias,
    out_weight,
    ff_in_weight,
    ff_in_bias,
    ff_out_weight,
    branch_bias,
    norm_gain,
    norm_bias,
):
    n_seq, n_rows, width = tokens.shape
    blk_rows, head_w = qkv_weight.shape[2:]
    ff = ff_in_weight.shape[2]
    heads = head_w // HEAD
    rows = n_seq * n_rows
    half, quart = n_rows // 2, n_rows // 4
    few = n_seq * half
    keys = 4 * n_rows
    vmem = pl.BlockSpec(memory_space=pltpu.VMEM)
    smem = pl.BlockSpec(memory_space=pltpu.SMEM)
    hbm = pl.BlockSpec(memory_space=pl.ANY)

    def v(*shape, dtype=BF16):
        return pltpu.VMEM(shape, dtype)

    def f(*shape):
        return pltpu.VMEM(shape, F32)

    wide = {"q": (3 * blk_rows, head_w), "o": (blk_rows, head_w), "i": (blk_rows, ff), "f": (blk_rows, ff)}

    def scatter_bufs(kind):
        n, cols = wide[kind]
        lead = () if kind == "q" else (2,)
        dims = ((2, 2, 2, n), (2, 2, n), (2, 2, n), (2, 2, n // 2), (2, n // 2), (2, n // 2))
        return [v(*lead, *dim, cols) for dim in dims]

    scratch = [
        v(n_seq, n_rows, width),
        v(n_seq, n_rows, width),
        v(3, width, head_w),
        v(2, width, head_w),
        v(2, width, ff),
        v(2, width, ff),
        v(head_w, blk_rows),
        f(1, ff),
        v(rows, width),
        v(width, rows),
        v(rows, head_w),
        v(rows, head_w),
        v(rows, head_w),
        v(2, keys, head_w),
        f(heads, n_rows, keys),
        f(n_seq - 1, heads, n_rows, n_rows),
        v(n_seq, n_rows, head_w),
        v(n_seq, half, head_w),
        v(3, n_seq, half, width),
        v(3, n_seq, half, width),
        f(few, width),
        f(few, 1),
        v(few, width),
        v(2, few, ff),
        f(2, few, ff),
        f(few, width),
        v(few, width),
        v(few, width),
        v(width, few),
        v(width, few),
        v(2, few, ff),
        f(few, width),
        v(width, few),
        v(n_seq, n_rows, head_w),
        v(n_seq, half, head_w),
        v(2, 2, 2, n_rows, head_w),
        v(2, 2, n_rows, head_w),
        v(2, n_rows, head_w),
        v(2, n_rows, head_w),
        v(3, rows, head_w),
        f(n_seq, n_rows, width),
        v(2, 2, n_seq, quart, width),
        v(2, n_seq, quart, width),
        v(n_seq, quart, width),
        v(n_seq, quart, width),
        scatter_bufs("q"),
        scatter_bufs("o"),
        scatter_bufs("i"),
        scatter_bufs("f"),
        v(*wide["o"]),
        v(*wide["i"]),
        v(*wide["f"]),
        v(*wide["o"]),
        v(*wide["i"]),
        v(*wide["f"]),
        f(4, 16, width),
        f(4, 16, width),
        f(3, 8, head_w),
        f(3, 8, head_w),
        v(n_seq, n_rows, width),
        v(n_seq, n_rows, width),
        f(*wide["q"]),
        f(*wide["o"]),
        f(*wide["i"]),
        f(*wide["f"]),
        f(16, width),
        f(8, head_w),
        pltpu.SemaphoreType.DMA((14,)),
        pltpu.SemaphoreType.DMA((N_SEND,)),
        pltpu.SemaphoreType.DMA((N_RECV,)),
    ]

    def shape(*dims, dtype=F32):
        return jax.ShapeDtypeStruct(dims, dtype)

    main_out = [
        shape(n_seq, n_rows, width, dtype=BF16),
        shape(n_seq, n_rows, width, dtype=BF16),
        shape(*wide["q"]),
        shape(*wide["o"]),
        shape(*wide["i"]),
        shape(*wide["f"]),
        shape(16, width),
        shape(8, head_w),
    ]
    results = pl.pallas_call(
        fused_kernel,
        out_shape=main_out,
        in_specs=[smem, smem] + [hbm] * 6 + [vmem] * 5,
        out_specs=[hbm] * 8,
        scratch_shapes=scratch,
        compiler_params=pltpu.CompilerParams(
            collective_id=0, has_side_effects=True, vmem_limit_bytes=60 * 2**20
        ),
        name="encoder_layer",
    )(
        bucket,
        lengths,
        tokens,
        out_grad,
        qkv_weight[0],
        out_weight[0],
        ff_in_weight[0],
        jnp.transpose(ff_out_weight[0]),
        qv_bias[0],
        ff_in_bias,
        branch_bias[0],
        norm_gain[0],
        norm_bias[0],
    )
    final = pl.pallas_call(
        finish_kernel,
        out_shape=[
            shape(n_seq, n_rows, width, dtype=BF16),
            shape(n_seq, n_rows, width),
            shape(3, blk_rows, head_w),
            shape(2, head_w),
            shape(head_w, blk_rows),
            shape(blk_rows, ff),
            shape(1, ff),
            shape(blk_rows, ff),
            shape(2, width),
            shape(2, width),
            shape(2, width),
            shape(1, 3),
        ],
        in_specs=[smem] + [vmem] * 8,
        out_specs=[vmem] * 12,
        compiler_params=pltpu.CompilerParams(vmem_limit_bytes=60 * 2**20),
        name="finish",
    )(bucket, *results)
    out, tg, gq, qvb, go, gi, inb, gf, br, gain, shift, rms = final
    return (
        out,
        tg,
        gq[None],
        qvb[None],
        go[None],
        gi[None],
        inb,
        jnp.transpose(gf)[None],
        br[None],
        gain[None],
        shift[None],
        rms,
    )


def solution(mesh):
    placed = (
        P("batch", "blk", None),
        P("batch", "blk", None),
        P("batch"),
        P("batch", None),
        P(None, None, ("blk", "batch"), "tensor"),
        P(None, None, "tensor"),
        P(None, "tensor", ("blk", "batch")),
        P(None, ("blk", "batch"), "tensor"),
        P(None, "tensor"),
        P(None, "tensor", ("blk", "batch")),
        P(),
        P(),
        P(),
    )
    sizes = (mesh.shape["blk"], mesh.shape["batch"], mesh.shape["tensor"])
    body = fused_shards if sizes == (4, 2, 4) else general_shards
    return jax.shard_map(
        body,
        mesh=mesh,
        in_specs=placed,
        out_specs=(
            P("batch", "blk", None),
            P("batch", "blk", None),
            P(None, None, ("blk", "batch"), "tensor"),
            P(None, None, "tensor"),
            P(None, "tensor", ("blk", "batch")),
            P(None, ("blk", "batch"), "tensor"),
            P(None, "tensor"),
            P(None, "tensor", ("blk", "batch")),
            P(),
            P(),
            P(),
            P(),
        ),
        check_vma=False,
    )
```

```python
import functools

import jax
import jax.numpy as jnp
from jax import lax
from jax.experimental import pallas as pl
from jax.experimental.pallas import tpu as pltpu
from jax.sharding import PartitionSpec as P

HEAD = 64
SUB = 128


NEG = -1e30


def row_valid(bucket, lengths, pos):
    short = bucket[:, None] != 0
    pick = ((pos // SUB)[:, None] == jnp.arange(lengths.shape[1], dtype=jnp.int32)[None, :]).astype(
        jnp.int32
    )
    short_len = jnp.sum(lengths[:, None, :] * pick[None, :, :], axis=2)
    limit = jnp.where(short, short_len, lengths[:, :1])
    place = jnp.where(short, (pos % SUB)[None, :], pos[None, :])
    return place < limit


def seq_mask(bucket, lengths, qpos, kpos):
    short = bucket[:, None, None] != 0
    same = qpos[:, None] // SUB == kpos[None, :] // SUB
    allowed = jnp.logical_or(jnp.logical_not(short), same[None, :, :])
    return jnp.logical_and(row_valid(bucket, lengths, kpos)[:, None, :], allowed)


def layer_norm(h, gain, shift):
    mean = jnp.mean(h, -1, keepdims=True)
    cent = h - mean
    var = jnp.mean(cent * cent, -1, keepdims=True)
    return cent * lax.rsqrt(var + 1e-12) * gain + shift


def exact_gelu(value):
    return jax.nn.gelu(value, approximate=False)


def general_shards(
    tokens,
    out_grad,
    bucket,
    lengths,
    qkv_weight,
    qv_bias,
    out_weight,
    ff_in_weight,
    ff_in_bias,
    ff_out_weight,
    branch_bias,
    norm_gain,
    norm_bias,
):
    n_seq, rows_blk, width = tokens.shape
    blocks = lax.axis_size("blk")
    rank = lax.axis_index("blk")
    layers = qkv_weight.shape[0]
    local_width = qkv_weight.shape[3]
    heads_here = local_width // HEAD
    total_rows = n_seq * rows_blk
    scale = HEAD ** (-0.5)
    head_shape = (n_seq, rows_blk, heads_here, HEAD)
    qkv_full, out_full, ffin_full, ffout_full = (
        lax.all_gather(qkv_weight, ("blk", "batch"), axis=2, tiled=True),
        lax.all_gather(out_weight, ("blk", "batch"), axis=2, tiled=True),
        lax.all_gather(ff_in_weight, ("blk", "batch"), axis=1, tiled=True),
        lax.all_gather(ff_out_weight, ("blk", "batch"), axis=2, tiled=True),
    )
    local_pos = rank * rows_blk + jnp.arange(rows_blk, dtype=jnp.int32)
    row_ok = row_valid(bucket, lengths, local_pos).astype(jnp.float32).reshape(total_rows, 1)
    whole_pos = jnp.arange(blocks * rows_blk, dtype=jnp.int32)
    sub_bucket, sub_lengths = (bucket, lengths)

    def scores(query, keys, mask):
        found = (
            jnp.einsum("nqhe,nkhe->nhqk", query, keys, preferred_element_type=jnp.float32) * scale
        )
        return jnp.where(mask[:, None], found, NEG)

    x = tokens.astype(jnp.float32).reshape(total_rows, width)
    layer = 0
    xb = x.astype(jnp.bfloat16)
    triple = jnp.einsum("rd,cdk->crk", xb, qkv_full[layer], preferred_element_type=jnp.float32)
    query = (triple[0] + qv_bias[layer, 0]).astype(jnp.bfloat16).reshape(head_shape)
    keys = triple[1].astype(jnp.bfloat16).reshape(head_shape)
    values = (triple[2] + qv_bias[layer, 1]).astype(jnp.bfloat16).reshape(head_shape)
    pair = jnp.stack([keys, values])
    sub_query = query
    sub_pair = pair
    kept = lax.all_gather(sub_pair, "blk", axis=2, tiled=True)
    found = scores(sub_query, kept[0], seq_mask(sub_bucket, sub_lengths, local_pos, whole_pos))
    top = jnp.max(found, -1)
    sub_lse = top + jnp.log(jnp.sum(jnp.exp(found - top[..., None]), -1))
    weights = jnp.exp(found - sub_lse[..., None]).astype(jnp.bfloat16)
    sub_acc = jnp.einsum("nhqk,nkhe->nqhe", weights, kept[1], preferred_element_type=jnp.float32)
    lse = sub_lse
    acc = sub_acc
    att = acc.astype(jnp.bfloat16).reshape(total_rows, local_width)
    a_part = jnp.dot(att, out_full[layer], preferred_element_type=jnp.float32)
    branch = (
        lax.psum(a_part.astype(jnp.bfloat16), "tensor").astype(jnp.float32) + branch_bias[layer, 0]
    )
    upper_in = x + branch
    upper = layer_norm(upper_in, norm_gain[layer, 0], norm_bias[layer, 0])
    upper_b = upper.astype(jnp.bfloat16)
    pre = jnp.dot(upper_b, ffin_full[layer], preferred_element_type=jnp.float32) + ff_in_bias[layer]
    act = exact_gelu(pre).astype(jnp.bfloat16)
    f_part = jnp.dot(act, ffout_full[layer], preferred_element_type=jnp.float32)
    feed = (
        lax.psum(f_part.astype(jnp.bfloat16), "tensor").astype(jnp.float32) + branch_bias[layer, 1]
    )
    lower_in = upper + feed
    squares = [
        jnp.stack(
            [
                jnp.sum(row_ok * x * x),
                jnp.sum(row_ok * branch * branch),
                jnp.sum(row_ok * feed * feed),
            ]
        )
    ]
    saved = [(xb, query, pair, kept, lse, sub_lse, att, acc, upper_in, upper_b, pre, act, lower_in)]
    x = layer_norm(lower_in, norm_gain[layer, 1], norm_bias[layer, 1])
    output = x.astype(jnp.bfloat16).reshape(n_seq, rows_blk, width)
    grad = out_grad.astype(jnp.float32).reshape(total_rows, width)
    g_qkv, g_out, g_in, g_outf = ([], [], [], [])
    g_qvb, g_inb, g_branch, g_gain, g_shift = ([], [], [], [], [])
    for layer in reversed(range(layers)):
        xb, query, pair, kept, lse, sub_lse, att, acc, upper_in, upper_b, pre, act, lower_in = (
            saved[layer]
        )
        _, lower_back = jax.vjp(layer_norm, lower_in, norm_gain[layer, 1], norm_bias[layer, 1])
        d_lower, d_gain2, d_shift2 = lower_back(grad)
        d_feed = d_lower.astype(jnp.bfloat16)
        d_fbias = jnp.sum(d_feed.astype(jnp.float32), 0)
        g_outf.append(jnp.einsum("rf,rd->fd", act, d_feed, preferred_element_type=jnp.float32))
        d_act = jnp.einsum(
            "rd,fd->rf", d_feed, ffout_full[layer], preferred_element_type=jnp.float32
        )
        _, gelu_back = jax.vjp(exact_gelu, pre)
        d_pre = gelu_back(d_act)[0].astype(jnp.bfloat16)
        g_inb.append(jnp.sum(d_pre.astype(jnp.float32), 0))
        g_in.append(jnp.einsum("rd,rf->df", upper_b, d_pre, preferred_element_type=jnp.float32))
        ffn_part = jnp.einsum(
            "rf,df->rd", d_pre, ffin_full[layer], preferred_element_type=jnp.float32
        )
        d_upper = d_lower + lax.psum(ffn_part.astype(jnp.bfloat16), "tensor").astype(jnp.float32)
        _, upper_back = jax.vjp(layer_norm, upper_in, norm_gain[layer, 0], norm_bias[layer, 0])
        d_upper_in, d_gain1, d_shift1 = upper_back(d_upper)
        d_branch = d_upper_in.astype(jnp.bfloat16)
        d_abias = jnp.sum(d_branch.astype(jnp.float32), 0)
        g_out.append(jnp.einsum("rk,rd->kd", att, d_branch, preferred_element_type=jnp.float32))
        d_att = (
            jnp.einsum("rd,kd->rk", d_branch, out_full[layer], preferred_element_type=jnp.float32)
            .astype(jnp.bfloat16)
            .reshape(head_shape)
        )
        delta = jnp.einsum("nqhe,nqhe->nhq", d_att.astype(jnp.float32), acc)
        sub_query, sub_datt, sub_delta = (query, d_att, delta)
        block_keys = kept[0]
        block_found = scores(
            sub_query, block_keys, seq_mask(sub_bucket, sub_lengths, local_pos, whole_pos)
        )
        prob = jnp.exp(block_found - sub_lse[..., None])
        d_prob = jnp.einsum(
            "nqhe,nkhe->nhqk", sub_datt, kept[1], preferred_element_type=jnp.float32
        )
        d_scores = (prob * (d_prob - sub_delta[..., None])).astype(jnp.bfloat16)
        d_query = jnp.einsum(
            "nhqk,nkhe->nqhe", d_scores, block_keys, preferred_element_type=jnp.float32
        )
        d_keys = jnp.einsum(
            "nhqk,nqhe->nkhe", d_scores, sub_query, preferred_element_type=jnp.float32
        )
        d_values = jnp.einsum(
            "nhqk,nqhe->nkhe",
            prob.astype(jnp.bfloat16),
            sub_datt,
            preferred_element_type=jnp.float32,
        )
        sub_dq = d_query
        dpair_all = jnp.stack([d_keys * scale, d_values])
        sub_dpair = lax.psum_scatter(
            dpair_all.astype(jnp.bfloat16), "blk", scatter_dimension=2, tiled=True
        ).astype(jnp.float32)
        d_query, d_pair = (sub_dq, sub_dpair)
        dq_b = (d_query * scale).astype(jnp.bfloat16).reshape(total_rows, local_width)
        dk_b = d_pair[0].astype(jnp.bfloat16).reshape(total_rows, local_width)
        dv_b = d_pair[1].astype(jnp.bfloat16).reshape(total_rows, local_width)
        d_triple = jnp.stack([dq_b, dk_b, dv_b])
        g_qvb.append(
            jnp.stack([jnp.sum(dq_b.astype(jnp.float32), 0), jnp.sum(dv_b.astype(jnp.float32), 0)])
        )
        g_qkv.append(jnp.einsum("rd,crk->cdk", xb, d_triple, preferred_element_type=jnp.float32))
        attn_part = jnp.einsum(
            "crk,cdk->rd", d_triple, qkv_full[layer], preferred_element_type=jnp.float32
        )
        grad = d_upper_in + lax.psum(attn_part.astype(jnp.bfloat16), "tensor").astype(jnp.float32)
        g_branch.append(jnp.stack([d_abias, d_fbias]))
        g_gain.append(jnp.stack([d_gain1, d_gain2]))
        g_shift.append(jnp.stack([d_shift1, d_shift2]))

    def in_order(items):
        return jnp.stack(items[::-1])

    qkv_g, out_g, in_g, outf_g = (
        lax.psum_scatter(in_order(g_qkv), ("blk", "batch"), scatter_dimension=2, tiled=True),
        lax.psum_scatter(in_order(g_out), ("blk", "batch"), scatter_dimension=2, tiled=True),
        lax.psum_scatter(in_order(g_in), ("blk", "batch"), scatter_dimension=1, tiled=True),
        lax.psum_scatter(in_order(g_outf), ("blk", "batch"), scatter_dimension=2, tiled=True),
    )
    count = jnp.sum(row_ok)
    qvb_g, inb_g, branch_g, gain_g, shift_g, square_sums, count_all = lax.psum(
        (
            in_order(g_qvb),
            in_order(g_inb),
            in_order(g_branch),
            in_order(g_gain),
            in_order(g_shift),
            jnp.stack(squares),
            count,
        ),
        ("blk", "batch"),
    )
    rms = jnp.sqrt(square_sums / (count_all * width))
    tokens_grad = grad.reshape(n_seq, rows_blk, width)
    return (
        output,
        tokens_grad,
        qkv_g,
        qvb_g,
        out_g,
        in_g,
        inb_g,
        outf_g,
        branch_g,
        gain_g,
        shift_g,
        rms,
    )


MESH = pl.DeviceIdType.MESH
F32 = jnp.float32
BF16 = jnp.bfloat16
N_SEND = 48
N_RECV = 128
ORDER = (
    "first", "enter", "q.issue", "zwo", "o0.issue", "zwi", "i0.issue", "q.fy", "q.fx",
    "f0.issue", "o1.issue", "zwf", "o0.fy", "q.last", "kv", "i0.fy", "o1.fx", "o1.fy", "query",
    "att2", "o0.fx", "i1.issue", "f0.fy", "att1", "kvpass", "o0.last", "att0", "i0.fx",
    "f1.issue", "o1.last", "proj2", "i1.fy", "i1.fx", "proj1", "turn_x", "i0.last", "proj0",
    "f0.fx", "f1.fy", "f1.fx", "ln12", "i1.last", "hid2", "ln10", "fe2", "ln11", "f0.last",
    "hid1", "f1.last", "fe1", "fl2", "hid0", "fl1", "fe0", "fl0", "ln22", "out22", "turn_y",
    "ln21", "ln20", "gf1", "f1.r1", "gi0", "ln1b2", "ln1b1", "gf0", "ln1b0", "out12", "out21",
    "f1.r2y", "out20", "attb2", "f1.r2x", "attb1", "dxb1", "f0.r1", "attb0", "zf", "go",
    "kvback", "vec0", "vec1", "o1.r1", "gi1", "dxa1", "dxb2", "o1.r2x", "vec2", "o1.r2y",
    "i1.r1", "o0.r1", "gq", "out11", "bias0", "bias1", "i0.r1", "vec3", "dxa2", "out10", "dxb3",
    "i1.r2x", "zo", "dxa3", "i1.r2y", "putvec", "q.r1", "i0.r2x", "f0.r2x", "dxb4", "o0.r2x",
    "o0.r2y", "putout", "zi", "q.r2x", "f0.r2y", "bias2", "i0.r2y", "puto", "dxa4", "q.r2y",
    "putbias", "putdx", "putq", "putf", "puti",
)


def dot_nn(a, b):
    return lax.dot_general(a, b, (((1,), (0,)), ((), ())), preferred_element_type=F32)


def dot_nt(a, b):
    return lax.dot_general(a, b, (((1,), (1,)), ((), ())), preferred_element_type=F32)


def dot_tn(a, b):
    return lax.dot_general(a, b, (((0,), (0,)), ((), ())), preferred_element_type=F32)


def slot_order(bucket_ref):
    first = jnp.where(bucket_ref[0] == 0, 0, jnp.where(bucket_ref[1] == 0, 1, 2))
    second = jnp.where(first == 0, 1, 0)
    third = jnp.where(first == 2, 1, 2)
    return first, second, third


class Net:
    def __init__(self, send_sems, recv_sems):
        self.send_sems, self.recv_sems = send_sems, recv_sems
        self.copies, self.n_recv = [], 0

    def slot(self):
        self.n_recv += 1
        assert self.n_recv <= N_RECV
        return self.n_recv - 1

    def send(self, src, dst, peer, slot=None):
        at = len(self.copies)
        if at >= N_SEND:
            self.copies[at - N_SEND].wait_send()
        copy = pltpu.make_async_remote_copy(
            src_ref=src,
            dst_ref=dst,
            send_sem=self.send_sems.at[at % N_SEND],
            recv_sem=self.recv_sems.at[self.slot() if slot is None else slot],
            device_id=peer,
            device_id_type=MESH,
        )
        copy.start()
        self.copies.append(copy)
        return copy

    def whole(self, ref, peer, slot):
        return pltpu.make_async_remote_copy(
            src_ref=ref,
            dst_ref=ref,
            send_sem=self.send_sems.at[0],
            recv_sem=self.recv_sems.at[slot],
            device_id=peer,
            device_id_type=MESH,
        )

    def finish(self):
        for copy in self.copies[-N_SEND:]:
            copy.wait_send()


class Gather:
    def __init__(self, net, view, at, near, split=False):
        self.net, self.view, self.near = net, view, near
        self.own, self.x, self.y, self.d, self.size = at
        self.half = self.size // 2
        self.slot = net.slot()
        self.late = net.slot() if split else self.slot

    def part(self, start, size):
        return self.view(pl.ds(pl.multiple_of(start, 16), size))

    def to_core(self, ref, late=False):
        self.net.send(ref, ref, self.near[2], self.late if late else self.slot)

    def issue(self, src=None):
        xnb, ynb, core = self.near
        to = self.part(self.own, self.size)
        src = to if src is None else src
        self.from_x = self.net.send(src, to, xnb)
        self.from_y = self.net.send(src, to, ynb)
        self.net.send(src, to, core, self.slot)

    def forward_x(self):
        xnb, ynb, core = self.near
        self.from_x.wait_recv()
        ref = self.part(self.x, self.half)
        self.first = self.net.send(ref, ref, ynb)
        self.to_core(self.part(self.x, self.size))

    def forward_y(self):
        xnb, ynb, core = self.near
        self.from_y.wait_recv()
        ref = self.part(self.y + self.half, self.half)
        self.second = self.net.send(ref, ref, xnb)
        self.to_core(self.part(self.y, self.size), True)

    def last(self):
        self.first.wait_recv()
        self.second.wait_recv()
        self.to_core(self.part(self.d, self.size), True)

    def ready(self):
        self.net.whole(self.part(0, 4 * self.size), self.near[2], self.slot).wait_recv()

    def ready_half(self, late):
        slot = self.late if late else self.slot
        self.net.whole(self.part(0, 2 * self.size), self.near[2], slot).wait_recv()


class Scatter:
    def __init__(self, net, refs, spot, near):
        self.net, self.spot, self.near = net, spot, near
        self.g, self.d, self.h, self.p1, self.s, self.p2 = refs
        self.rows = self.g.shape[3]
        self.half = self.rows // 2

    def core(self):
        c = self.spot[1]
        self.c1 = self.net.send(self.g.at[:, 1 - c], self.d, self.near[2])

    def first(self):
        yy, c, t = self.spot
        xnb, ynb, _ = self.near
        lo, hi = pl.ds(0, self.half), pl.ds(self.half, self.half)
        self.c1.wait_recv()
        for a in range(2):
            for b in range(2):
                self.h[a, b] = (self.g[a, c, b].astype(F32) + self.d[a, b].astype(F32)).astype(BF16)
        self.px = self.net.send(self.h.at[:, 1 - t, lo], self.p1.at[0], xnb)
        self.py = self.net.send(self.h.at[1 - yy, :, hi], self.p1.at[1], ynb)

    def second_x(self):
        yy, c, t = self.spot
        xnb, ynb, _ = self.near
        lo = pl.ds(0, self.half)
        self.px.wait_recv()
        self.s[0] = (self.h[1 - yy, t, lo].astype(F32) + self.p1[0, 1 - yy].astype(F32)).astype(BF16)
        self.qy = self.net.send(self.s.at[0], self.p2.at[0], ynb)

    def second_y(self):
        yy, c, t = self.spot
        xnb, ynb, _ = self.near
        hi = pl.ds(self.half, self.half)
        self.py.wait_recv()
        self.s[1] = (self.h[yy, 1 - t, hi].astype(F32) + self.p1[1, 1 - t].astype(F32)).astype(BF16)
        self.qx = self.net.send(self.s.at[1], self.p2.at[1], xnb)

    def result(self):
        yy, c, t = self.spot
        self.qy.wait_recv()
        self.qx.wait_recv()
        lo, hi = pl.ds(0, self.half), pl.ds(self.half, self.half)
        low = self.h[yy, t, lo].astype(F32) + self.p1[0, yy].astype(F32) + self.p2[0].astype(F32)
        high = self.h[yy, t, hi].astype(F32) + self.p1[1, t].astype(F32) + self.p2[1].astype(F32)
        return low, high


def fused_kernel(*refs):
    (
        bucket, lengths, tokens, out_grad, qkv_w, out_w, ffi_w, ffo_w, qv_bias, ffi_b, br_bias, gain, shift,
        out_hbm, tg_hbm, gq_hbm, go_hbm, gi_hbm, gf_hbm, vec_hbm, qvb_hbm,
        tok, cot, w_q, w_o, w_i, w_f, own_o, bias_r, own_q, xs, xs_t, q_r, kv_r, kv_a, p_a, p_b,
        att, att_r, ps, pr, xh1, rstd1, yb, act, gp, dh2, dfb, dab, df_t, yb_t, dpre, dh1, da_t,
        datt, datt_s, dkv_s, dkv_c, dkv_t, dkv_y, dtri, dx_p, dx_s, dx_1, dx_2, dx_t,
        sc_q, sc_o, sc_i, sc_f, z_o, z_i, z_f, t_o, t_i, t_f, vs, vr, vz, qs, qr,
        out_v, tg_v, gq_v, go_v, gi_v, gf_v, vec_v, qvb_v,
        local_sems, send_sems, recv_sems,
    ) = refs
    n_seq, n_rows, width = tok.shape
    blk_rows = ffi_w.shape[0]
    head_w = qkv_w.shape[2]
    pair_w = 2 * head_w
    heads = head_w // HEAD
    half, quart = n_rows // 2, n_rows // 4
    tile = 256
    n_tile = width // tile
    scale = HEAD ** (-0.5)

    r = lax.axis_index("blk")
    t = lax.axis_index("batch")
    z = lax.axis_index("tensor")
    yy, c = r // 2, r % 2
    pz, qz = z // 2, z % 2
    r1, r2 = r + 1 - 2 * c, (r + 2) % 4
    z1, z2 = z + 1 - 2 * qz, (z + 2) % 4
    core, xnb, ynb = (r1, t, z), (r, 1 - t, z), (r2, t, z)
    zn1, zn2 = (r, t, z1), (r, t, z2)
    peers = (zn2, zn1, xnb, ynb, core)
    near = (xnb, ynb, core)

    barrier = pltpu.get_barrier_semaphore()
    for peer in peers:
        pl.semaphore_signal(barrier, inc=1, device_id=peer, device_id_type=MESH)

    net = Net(send_sems, recv_sems)

    def block(rr, tt):
        return (rr * 2 + tt) * blk_rows

    at = (block(r, t), block(r, 1 - t), block(r2, t), block(r2, 1 - t), blk_rows)
    own = pl.ds(pl.multiple_of(block(r, t), 32), blk_rows)

    def gather(view, split=False):
        return Gather(net, view, at, near, split)

    ga_q = gather(lambda rows: w_q.at[rows])
    ga_o = [gather(lambda rows, k=k: w_o.at[k, rows]) for k in range(2)]
    ga_i = [gather(lambda rows, k=k: w_i.at[k, rows]) for k in range(2)]
    ga_f = [gather(lambda rows, k=k: w_f.at[k, rows], True) for k in range(2)]

    local = [
        pltpu.make_async_copy(src, dst, local_sems.at[k])
        for k, (src, dst) in enumerate(
            (
                (out_w, own_o),
                (tokens, tok),
                (qkv_w, own_q),
                (ffi_w, w_i.at[0, own]),
                (ffo_w, w_f.at[0, own]),
                (out_grad, cot),
            )
        )
    ]
    for copy in local:
        copy.start()
    stores = []

    def store(src, dst):
        copy = pltpu.make_async_copy(src, dst, local_sems.at[len(local) + len(stores)])
        copy.start()
        stores.append(copy)

    st = {}

    order = slot_order(bucket)

    def weights_first():
        local[0].wait()
        w_o[0, own] = jnp.transpose(own_o[...])
        local[2].wait()
        w_q[own] = jnp.concatenate([own_q[1], own_q[2], own_q[0]], 1)
        local[1].wait()
        for s in range(n_seq):
            xs[s * n_rows : (s + 1) * n_rows] = tok[order[s]]

    def enter():
        pl.semaphore_wait(barrier, len(peers))

    def far_weight(kind, src, buf):
        st["z" + kind] = net.send(src, buf.at[1, own], zn2)
        if kind == "i":
            st["zb"] = net.send(ffi_b, bias_r, zn2)

    def issue_second(kind, gather):
        st["z" + kind].wait_recv()
        gather.issue()

    def turn_x():
        xs_t[...] = jnp.transpose(xs[...])

    def keys_of(rr):
        return kv_a.at[pl.ds(pl.multiple_of(rr * n_rows, n_rows), n_rows)]

    def keys_values():
        ga_q.ready()
        bias = jnp.concatenate([jnp.zeros((1, head_w), F32), qv_bias[1:2, :]], 1)
        kv_r[...] = (dot_nn(xs[...], w_q[:, 0:pair_w]) + bias).astype(BF16)
        kv_a[pl.ds(pl.multiple_of(r * n_rows, n_rows), n_rows)] = kv_r[0:n_rows]
        st["kv_y"] = net.send(keys_of(r), keys_of(r), ynb)
        st["kv_c"] = [net.send(keys_of(r), keys_of(r), core)]

    def keys_pass():
        st["kv_y"].wait_recv()
        st["kv_c"].append(net.send(keys_of(r2), keys_of(r2), core))

    def queries():
        q_r[...] = (dot_nn(xs[...], w_q[:, pair_w:]) + qv_bias[0:1, :]).astype(BF16)

    lane_head = lax.broadcasted_iota(jnp.int32, (1, head_w), 1) // HEAD

    def of_head(value, h):
        return jnp.where(lane_head == h, value, jnp.zeros_like(value))

    def limit_of(s):
        index = order[s]
        return lengths[index, r], lengths[index, 0]

    own_half = pl.ds(pl.multiple_of(pz * half, half), half)
    other_half = pl.ds(pl.multiple_of((1 - pz) * half, half), half)
    key_at = lax.broadcasted_iota(jnp.int32, (1, n_rows), 1)

    def rows_at(s):
        return slice(s * n_rows, (s + 1) * n_rows)

    def few_at(s):
        return slice(s * half, (s + 1) * half)

    def attend(s):
        if s == 0:
            for copy in st["kv_c"]:
                copy.wait_recv()
            both, probs, key_ok = kv_a[...], p_a, None
        else:
            both, probs = kv_r[rows_at(s)], p_b.at[s - 1]
            key_ok = key_at < limit_of(s)[0]
        keys, values = both[:, 0:head_w], both[:, head_w:pair_w]
        query = q_r[rows_at(s)]
        total = jnp.zeros((n_rows, head_w), F32)
        for h in range(heads):
            score = dot_nt(of_head(query, h), keys) * scale
            if key_ok is not None:
                score = jnp.where(key_ok, score, NEG)
            e = jnp.exp(score - jnp.max(score, -1, keepdims=True))
            prob = e / jnp.sum(e, -1, keepdims=True)
            probs[h] = prob
            total = total + dot_nn(prob.astype(BF16), of_head(values, h))
        att[s] = total.astype(BF16)
        st["att", s] = net.send(att.at[s, other_half], att_r.at[s], zn2)

    def pair_send(k, s, value):
        ps[k, s] = value.astype(BF16)
        st["pair", k, s] = net.send(ps.at[k, s], pr.at[k, s], zn1)

    def pair_sum(k, s):
        st["pair", k, s].wait_recv()
        return ps[k, s].astype(F32) + pr[k, s].astype(F32)

    def ready(kind, gathers):
        if ("ready", kind) not in st:
            st["ready", kind] = True
            for gather in gathers:
                gather.ready()

    def project(s):
        ready("o", ga_o)
        st["att", s].wait_recv()
        pair_send(0, s, dot_nt(att[s, own_half], w_o[0]) + dot_nt(att_r[s], w_o[1]))

    vec = {k: jnp.zeros((1, width), F32) for k in range(12)}
    row_at = lax.broadcasted_iota(jnp.int32, (half, 1), 0)

    def row_ok(s):
        short, full = limit_of(s)
        place = row_at + pz * half
        ok = place + r * n_rows < full if s == 0 else place < short
        return ok.astype(F32)

    def tally(k, value):
        vec[k] = vec[k] + jnp.sum(value, 0, keepdims=True)

    def mean_of(value):
        return jnp.mean(value, -1, keepdims=True)

    def normed(h):
        cent = h - mean_of(h)
        rstd = lax.rsqrt(mean_of(cent * cent) + 1e-12)
        return cent * rstd, rstd

    def first_norm(s):
        here = few_at(s)
        x = xs[pl.ds(pl.multiple_of(s * n_rows + pz * half, half), half)].astype(F32)
        branch = pair_sum(0, s) + br_bias[0:1, :]
        ok = row_ok(s)
        tally(8, ok * (x * x))
        tally(9, ok * (branch * branch))
        tally(11, ok * jnp.ones((1, width), F32))
        hat, rstd = normed(x + branch)
        xh1[here] = hat
        rstd1[here] = rstd
        yb[here] = (hat * gain[0:1, :] + shift[0:1, :]).astype(BF16)

    def turn_y():
        yb_t[...] = jnp.transpose(yb[...])

    def hidden(s):
        if ("ready", "i") not in st:
            st["zb"].wait_recv()
            local[3].wait()
        ready("i", ga_i)
        here = few_at(s)
        for k in range(2):
            for n in range(n_tile):
                cols = slice(n * tile, (n + 1) * tile)
                bias = ffi_b[:, cols] if k == 0 else bias_r[:, cols]
                pre = dot_nn(yb[here], w_i[k, :, cols]) + bias
                phi = 0.5 * (1.0 + lax.erf(pre * (0.5**0.5)))
                act[k, here, cols] = (pre * phi).astype(BF16)
                gp[k, here, cols] = phi + pre * (jnp.exp(-0.5 * pre * pre) * 0.3989422804014327)

    def feed_out(late, s):
        if ("feed", late) not in st:
            st["feed", late] = True
            if not late:
                local[4].wait()
            for gather in ga_f:
                gather.ready_half(late)
        here = few_at(s)
        side = width // 2
        cols = pl.ds(pl.multiple_of(((1 - yy) if late else yy) * side, 128), side)
        value = dot_nt(act[0, here], w_f[0, cols]) + dot_nt(act[1, here], w_f[1, cols])
        ps[1, s, :, cols] = value.astype(BF16)
        st["feed", late, s] = net.send(ps.at[1, s, :, cols], pr.at[1, s, :, cols], zn1)

    def second_norm(s):
        here = few_at(s)
        if "cot" not in st:
            st["cot"] = True
            local[5].wait()
        for late in range(2):
            st["feed", late, s].wait_recv()
        feed = ps[1, s].astype(F32) + pr[1, s].astype(F32) + br_bias[1:2, :]
        tally(10, row_ok(s) * (feed * feed))
        hat, rstd = normed(xh1[here] * gain[0:1, :] + shift[0:1, :] + feed)
        out_v[s, own_half] = (hat * gain[1:2, :] + shift[1:2, :]).astype(BF16)
        g = cot[order[s], own_half].astype(F32)
        tally(1, g * hat)
        tally(2, g)
        g = g * gain[1:2, :]
        d = rstd * (g - mean_of(g) - hat * mean_of(g * hat))
        dh2[here] = d
        d = d.astype(BF16)
        dfb[here] = d
        tally(0, d.astype(F32))
        total = jnp.zeros((half, width), F32)
        for k in range(2):
            p = (dot_nn(d, w_f[k]) * gp[k, here]).astype(BF16)
            dpre[k, here] = p
            tally(3 + k, p.astype(F32))
            total = total + dot_nt(p, w_i[k])
        pair_send(2, s, total)

    quarter = pl.ds(pl.multiple_of(z * quart, quart), quart)
    quarter_2 = pl.ds(pl.multiple_of(z2 * quart, quart), quart)

    def out_far(s):
        here = out_v.at[s, quarter]
        st["out2", s] = net.send(here, here, zn2)

    def out_near(s):
        st["out2", s].wait_recv()
        there = out_v.at[s, quarter_2]
        st["out1", s] = net.send(there, there, zn1)

    def scatter(refs, k=None):
        views = refs if k is None else [ref.at[k] for ref in refs]
        return Scatter(net, views, (yy, c, t), near)

    rs_f = [scatter(sc_f, k) for k in range(2)]
    rs_i = [scatter(sc_i, k) for k in range(2)]
    rs_o = [scatter(sc_o, k) for k in range(2)]
    rs_q = scatter(sc_q)

    def grads(lhs, rhs, out):
        value = dot_nn(lhs, rhs).astype(BF16)
        for b in range(8):
            piece = value[b * blk_rows : (b + 1) * blk_rows]
            out[b // 4, (b // 2) % 2, b % 2] = piece

    def grads_wide(left, right, rs):
        for n in range(n_tile):
            cols = slice(n * tile, (n + 1) * tile)
            grads(left[...], right[:, cols], rs.g.at[:, :, :, :, cols])
        rs.core()

    def grad_f(k):
        if k == 1:
            df_t[...] = jnp.transpose(dfb[...])
        grads_wide(df_t, act.at[k], rs_f[k])

    def grad_i(k):
        grads_wide(yb_t, dpre.at[k], rs_i[k])

    def grad_o():
        da_t[...] = jnp.transpose(dab[...])
        rows_l = jnp.concatenate([att[s, own_half] for s in range(n_seq)], 0)
        rows_r = jnp.concatenate([att_r[s] for s in range(n_seq)], 0)
        grads(da_t[...], rows_r, rs_o[1].g)
        rs_o[1].core()
        grads(da_t[...], rows_l, rs_o[0].g)
        rs_o[0].core()

    def grad_q():
        grads(xs_t[...], dtri[...], rs_q.g)
        rs_q.core()

    def first_norm_back(s):
        here = few_at(s)
        hat = xh1[here]
        g = dh2[here] + pair_sum(2, s)
        tally(6, g * hat)
        tally(7, g)
        g = g * gain[0:1, :]
        d = rstd1[here] * (g - mean_of(g) - hat * mean_of(g * hat))
        dh1[here] = d
        d = d.astype(BF16)
        dab[here] = d
        tally(5, d.astype(F32))
        datt_s[s] = dot_nn(d, w_o[1]).astype(BF16)
        st["datt", s] = net.send(datt_s.at[s], datt.at[s, own_half], zn2)
        datt[s, own_half] = dot_nn(d, w_o[0]).astype(BF16)

    def vec_step(k):
        if k == 0:
            for n in range(12):
                vs[0, n : n + 1] = vec[n]
            vs[0, 12:16] = jnp.zeros((4, width), F32)
        else:
            st["vec"].wait_recv()
            vs[k] = vs[k - 1] + vr[k - 1]
        if k < 3:
            st["vec"] = net.send(vs.at[k], vr.at[k], (core, xnb, ynb)[k])
            return
        lane = lax.broadcasted_iota(jnp.int32, (1, width), 1)
        last = jnp.zeros((1, width), F32)
        for n in range(4):
            last = jnp.where(lane == n, jnp.sum(vs[3, 8 + n : 9 + n], 1, keepdims=True), last)
        vz[0, 0:3] = vs[3, 0:3]
        vz[0, 3:4] = vs[3, 4:5]
        vz[0, 4:7] = vs[3, 5:8]
        vz[0, 7:8] = last
        st["vec"] = net.send(vz.at[0], vz.at[1], zn2)

    def attend_back(s):
        st["datt", s].wait_recv()
        if s == 0:
            both, probs = kv_a[...], p_a
        else:
            both, probs = kv_r[rows_at(s)], p_b.at[s - 1]
        keys, values = both[:, 0:head_w], both[:, head_w:pair_w]
        query = q_r[rows_at(s)]
        d_att = datt[s]
        dq = jnp.zeros((n_rows, head_w), F32)
        dk = jnp.zeros(keys.shape, F32)
        dv = jnp.zeros(keys.shape, F32)
        for h in range(heads):
            prob = probs[h]
            d_h = of_head(d_att, h)
            dp = dot_nt(d_h, values)
            delta = jnp.sum(prob * dp, -1, keepdims=True)
            ds = (prob * (dp - delta)).astype(BF16)
            dq = dq + dot_nn(ds, of_head(keys, h))
            dk = dk + dot_tn(ds, of_head(query, h))
            dv = dv + dot_tn(prob.astype(BF16), d_h)
        dtri[rows_at(s), pair_w:] = (dq * scale).astype(BF16)
        both = jnp.concatenate([(dk * scale).astype(BF16), dv.astype(BF16)], 1)
        if s == 0:
            for a in range(4):
                dkv_s[a // 2, a % 2] = both[rows_at(a)]
            st["dkv1"] = net.send(dkv_s.at[:, 1 - c], dkv_c, core)
        else:
            dtri[rows_at(s), 0:pair_w] = both

    def keys_back():
        st["dkv1"].wait_recv()
        dkv_t[...] = (dkv_s[1 - yy, c].astype(F32) + dkv_c[1 - yy].astype(F32)).astype(BF16)
        st["dkv2"] = net.send(dkv_t, dkv_y, ynb)

    def dx_of(s):
        total = dot_nt(dtri[rows_at(s)], w_q[...])
        dx_p[s] = total
        for a in range(4):
            dx_s[a // 2, a % 2, s] = total[a * quart : (a + 1) * quart].astype(BF16)

    def half_rows(s):
        return pl.ds(pl.multiple_of(s * half + qz * quart, quart), quart)

    groups = {"b": (1, n_seq), "a": (0, 1)}

    def dx_first(group):
        lo, hi = groups[group]
        if group == "a":
            st["dkv2"].wait_recv()
            total = dkv_s[yy, c].astype(F32) + dkv_c[yy].astype(F32) + dkv_y[...].astype(F32)
            dtri[0:n_rows, 0:pair_w] = total.astype(BF16)
        for s in range(lo, hi):
            dx_of(s)
        st[group, 1] = net.send(dx_s.at[:, 1 - qz, lo:hi], dx_1.at[:, lo:hi], zn1)

    def dx_second(group):
        lo, hi = groups[group]
        st[group, 1].wait_recv()
        for s in range(lo, hi):
            dx_t[s] = (dx_p[s, quarter_2] + dx_1[1 - pz, s].astype(F32)).astype(BF16)
        st[group, 2] = net.send(dx_t.at[lo:hi], dx_2.at[lo:hi], zn2)

    def dx_third(group):
        lo, hi = groups[group]
        st[group, 2].wait_recv()
        for s in range(lo, hi):
            total = dx_p[s, quarter] + dx_1[pz, s].astype(F32) + dx_2[s].astype(F32)
            tg_v[s, quarter] = (total + dh1[half_rows(s)]).astype(BF16)
        here = tg_v.at[lo:hi, quarter]
        st[group, 3], st[group, 4] = net.send(here, here, zn2), net.send(here, here, zn1)

    def dx_last(group):
        lo, hi = groups[group]
        st[group, 3].wait_recv()
        there = tg_v.at[lo:hi, quarter_2]
        st[group, 5] = net.send(there, there, zn1)

    def bias_step(k):
        if k == 0:
            qs[0] = jnp.zeros(qs.shape[1:], F32)
            total = jnp.sum(dtri[...].astype(F32), 0, keepdims=True)
            qs[0, 0:1] = total[:, pair_w:]
            qs[0, 1:2] = total[:, head_w:pair_w]
        else:
            st["bias"].wait_recv()
            qs[k] = qs[k - 1] + qr[k - 1]
        st["bias"] = net.send(qs.at[k], qr.at[k], (core, xnb, ynb)[k])

    def to_z(kind, rs, buf, got):
        low, high = rs.result()
        n = low.shape[0]
        buf[0:n] = low.astype(BF16)
        buf[n : 2 * n] = high.astype(BF16)
        st["g" + kind] = net.send(buf, got, zn2)

    def put(kind, rs, out, to, got=None):
        low, high = rs.result()
        n = low.shape[0]
        if got is not None:
            st["g" + kind].wait_recv()
            low = low + got[0:n].astype(F32)
            high = high + got[n : 2 * n].astype(F32)
        out[0:n] = low
        out[n : 2 * n] = high
        store(out, to)

    def out_store():
        for s in range(n_seq):
            st["out1", s].wait_recv()
        store(out_v, out_hbm)

    def vec_store():
        st["vec"].wait_recv()
        vec_v[...] = vz[0] + vz[1]
        vec_v[3:4] = vs[3, 3:4] + vz[1, 3:4]
        store(vec_v, vec_hbm)

    def bias_store():
        st["bias"].wait_recv()
        qvb_v[...] = qs[2] + qr[2]
        store(qvb_v, qvb_hbm)

    def dx_store():
        for group in groups:
            for k in (4, 5):
                st[group, k].wait_recv()
        store(tg_v, tg_hbm)

    steps = {
        "first": weights_first,
        "enter": enter,
        "zwo": lambda: far_weight("o", w_o.at[0, own], w_o),
        "zwi": lambda: far_weight("i", ffi_w, w_i),
        "zwf": lambda: far_weight("f", ffo_w, w_f),
        "q.issue": lambda: ga_q.issue(),
        "o0.issue": lambda: ga_o[0].issue(),
        "i0.issue": lambda: ga_i[0].issue(ffi_w),
        "f0.issue": lambda: ga_f[0].issue(ffo_w),
        "turn_x": turn_x,
        "kv": keys_values,
        "kvpass": keys_pass,
        "query": queries,
        "turn_y": turn_y,
        "go": grad_o,
        "gq": grad_q,
        "kvback": keys_back,
        "zf": lambda: to_z("f", rs_f[1], t_f, z_f),
        "zi": lambda: to_z("i", rs_i[1], t_i, z_i),
        "zo": lambda: to_z("o", rs_o[1], t_o, z_o),
        "putf": lambda: put("f", rs_f[0], gf_v, gf_hbm, z_f),
        "puti": lambda: put("i", rs_i[0], gi_v, gi_hbm, z_i),
        "puto": lambda: put("o", rs_o[0], go_v, go_hbm, z_o),
        "putq": lambda: put("q", rs_q, gq_v, gq_hbm),
        "putout": out_store,
        "putvec": vec_store,
        "putbias": bias_store,
        "putdx": dx_store,
    }
    gathers = {"q": ga_q, "o0": ga_o[0], "o1": ga_o[1], "i0": ga_i[0], "i1": ga_i[1], "f0": ga_f[0], "f1": ga_f[1]}
    for name, gather in gathers.items():
        if name[1:] == "1":
            steps[name + ".issue"] = functools.partial(issue_second, name[0], gather)
        steps[name + ".fx"] = gather.forward_x
        steps[name + ".fy"] = gather.forward_y
        steps[name + ".last"] = gather.last
    sums = {"q": rs_q, "o0": rs_o[0], "o1": rs_o[1], "i0": rs_i[0], "i1": rs_i[1], "f0": rs_f[0], "f1": rs_f[1]}
    for name, rs in sums.items():
        steps[name + ".r1"] = rs.first
        steps[name + ".r2x"] = rs.second_x
        steps[name + ".r2y"] = rs.second_y
    for s in range(n_seq):
        for name, call in (
            ("att", attend),
            ("proj", project),
            ("ln1", first_norm),
            ("hid", hidden),
            ("fe", functools.partial(feed_out, 0)),
            ("fl", functools.partial(feed_out, 1)),
            ("ln2", second_norm),
            ("ln1b", first_norm_back),
            ("attb", attend_back),
            ("out2", out_far),
            ("out1", out_near),
        ):
            steps[name + str(s)] = functools.partial(call, s)
    for group in groups:
        for k, call in enumerate((dx_first, dx_second, dx_third, dx_last)):
            steps["dx" + group + str(k + 1)] = functools.partial(call, group)
    for k in range(2):
        steps["gf" + str(k)] = functools.partial(grad_f, k)
        steps["gi" + str(k)] = functools.partial(grad_i, k)
    for k in range(4):
        steps["vec" + str(k)] = functools.partial(vec_step, k)
    for k in range(3):
        steps["bias" + str(k)] = functools.partial(bias_step, k)

    assert set(ORDER) == set(steps) and len(ORDER) == len(steps)
    for name in ORDER:
        steps[name]()
    for copy in stores:
        copy.wait()
    net.finish()


def finish_kernel(
    bucket,
    out_i,
    tg_i,
    gq_i,
    go_i,
    gi_i,
    gf_i,
    vec_i,
    qvb_i,
    out_o,
    tg_o,
    gq_o,
    qvb_o,
    go_o,
    gi_o,
    inb_o,
    gf_o,
    br_o,
    gain_o,
    shift_o,
    rms_o,
):
    order = slot_order(bucket)
    for s in range(3):
        at = jnp.where(order[0] == s, 0, jnp.where(order[1] == s, 1, 2))
        out_o[s] = out_i[at]
        tg_o[s] = tg_i[at].astype(F32)
    n = gq_o.shape[2]
    value = gq_i[...]
    for k, part in enumerate((1, 2, 0)):
        gq_o[part] = value[:, k * n : (k + 1) * n]
    go_o[...] = jnp.transpose(go_i[...])
    gi_o[...] = gi_i[...]
    gf_o[...] = gf_i[...]
    qvb_o[...] = qvb_i[0:2]
    inb_o[...] = vec_i[3:4]
    br_o[0:1] = vec_i[4:5]
    br_o[1:2] = vec_i[0:1]
    gain_o[0:1] = vec_i[5:6]
    gain_o[1:2] = vec_i[1:2]
    shift_o[0:1] = vec_i[6:7]
    shift_o[1:2] = vec_i[2:3]
    rms_o[...] = jnp.sqrt(vec_i[7:8, 0:3] / vec_i[7:8, 3:4])


def fused_shards(
    tokens,
    out_grad,
    bucket,
    lengths,
    qkv_weight,
    qv_bias,
    out_weight,
    ff_in_weight,
    ff_in_bias,
    ff_out_weight,
    branch_bias,
    norm_gain,
    norm_bias,
):
    n_seq, n_rows, width = tokens.shape
    blk_rows, head_w = qkv_weight.shape[2:]
    ff = ff_in_weight.shape[2]
    heads = head_w // HEAD
    rows = n_seq * n_rows
    half, quart = n_rows // 2, n_rows // 4
    few = n_seq * half
    keys = 4 * n_rows
    vmem = pl.BlockSpec(memory_space=pltpu.VMEM)
    smem = pl.BlockSpec(memory_space=pltpu.SMEM)
    hbm = pl.BlockSpec(memory_space=pl.ANY)

    def v(*shape, dtype=BF16):
        return pltpu.VMEM(shape, dtype)

    def f(*shape):
        return pltpu.VMEM(shape, F32)

    wide = {"q": (blk_rows, 3 * head_w), "o": (blk_rows, head_w), "i": (blk_rows, ff), "f": (blk_rows, ff)}

    def scatter_bufs(kind):
        n, cols = wide[kind]
        lead = () if kind == "q" else (2,)
        dims = ((2, 2, 2, n), (2, 2, n), (2, 2, n), (2, 2, n // 2), (2, n // 2), (2, n // 2))
        return [v(*lead, *dim, cols) for dim in dims]

    scratch = [
        v(n_seq, n_rows, width),
        v(n_seq, n_rows, width),
        v(width, 3 * head_w),
        v(2, width, head_w),
        v(2, width, ff),
        v(2, width, ff),
        v(head_w, blk_rows),
        f(1, ff),
        v(3, blk_rows, head_w),
        v(rows, width),
        v(width, rows),
        v(rows, head_w),
        v(rows, 2 * head_w),
        v(keys, 2 * head_w),
        f(heads, n_rows, keys),
        f(n_seq - 1, heads, n_rows, n_rows),
        v(n_seq, n_rows, head_w),
        v(n_seq, half, head_w),
        v(3, n_seq, half, width),
        v(3, n_seq, half, width),
        f(few, width),
        f(few, 1),
        v(few, width),
        v(2, few, ff),
        f(2, few, ff),
        f(few, width),
        v(few, width),
        v(few, width),
        v(width, few),
        v(width, few),
        v(2, few, ff),
        f(few, width),
        v(width, few),
        v(n_seq, n_rows, head_w),
        v(n_seq, half, head_w),
        v(2, 2, n_rows, 2 * head_w),
        v(2, n_rows, 2 * head_w),
        v(n_rows, 2 * head_w),
        v(n_rows, 2 * head_w),
        v(rows, 3 * head_w),
        f(n_seq, n_rows, width),
        v(2, 2, n_seq, quart, width),
        v(2, n_seq, quart, width),
        v(n_seq, quart, width),
        v(n_seq, quart, width),
        scatter_bufs("q"),
        scatter_bufs("o"),
        scatter_bufs("i"),
        scatter_bufs("f"),
        v(*wide["o"]),
        v(*wide["i"]),
        v(*wide["f"]),
        v(*wide["o"]),
        v(*wide["i"]),
        v(*wide["f"]),
        f(4, 16, width),
        f(3, 16, width),
        f(2, 8, width),
        f(3, 8, head_w),
        f(3, 8, head_w),
        v(n_seq, n_rows, width),
        v(n_seq, n_rows, width),
        f(*wide["q"]),
        f(*wide["o"]),
        f(*wide["i"]),
        f(*wide["f"]),
        f(8, width),
        f(8, head_w),
        pltpu.SemaphoreType.DMA((14,)),
        pltpu.SemaphoreType.DMA((N_SEND,)),
        pltpu.SemaphoreType.DMA((N_RECV,)),
    ]

    def shape(*dims, dtype=F32):
        return jax.ShapeDtypeStruct(dims, dtype)

    main_out = [
        shape(n_seq, n_rows, width, dtype=BF16),
        shape(n_seq, n_rows, width, dtype=BF16),
        shape(*wide["q"]),
        shape(*wide["o"]),
        shape(*wide["i"]),
        shape(*wide["f"]),
        shape(8, width),
        shape(8, head_w),
    ]
    results = pl.pallas_call(
        fused_kernel,
        out_shape=main_out,
        in_specs=[smem, smem] + [hbm] * 6 + [vmem] * 5,
        out_specs=[hbm] * 8,
        scratch_shapes=scratch,
        compiler_params=pltpu.CompilerParams(
            collective_id=0, has_side_effects=True, vmem_limit_bytes=60 * 2**20
        ),
        name="encoder_layer",
    )(
        bucket,
        lengths,
        tokens,
        out_grad,
        qkv_weight[0],
        out_weight[0],
        ff_in_weight[0],
        jnp.transpose(ff_out_weight[0]),
        qv_bias[0],
        ff_in_bias,
        branch_bias[0],
        norm_gain[0],
        norm_bias[0],
    )
    final = pl.pallas_call(
        finish_kernel,
        out_shape=[
            shape(n_seq, n_rows, width, dtype=BF16),
            shape(n_seq, n_rows, width),
            shape(3, blk_rows, head_w),
            shape(2, head_w),
            shape(head_w, blk_rows),
            shape(blk_rows, ff),
            shape(1, ff),
            shape(blk_rows, ff),
            shape(2, width),
            shape(2, width),
            shape(2, width),
            shape(1, 3),
        ],
        in_specs=[smem] + [vmem] * 8,
        out_specs=[vmem] * 12,
        compiler_params=pltpu.CompilerParams(vmem_limit_bytes=60 * 2**20),
        name="finish",
    )(bucket, *results)
    out, tg, gq, qvb, go, gi, inb, gf, br, gain, shift, rms = final
    return (
        out,
        tg,
        gq[None],
        qvb[None],
        go[None],
        gi[None],
        inb,
        jnp.transpose(gf)[None],
        br[None],
        gain[None],
        shift[None],
        rms,
    )


def solution(mesh):
    placed = (
        P("batch", "blk", None),
        P("batch", "blk", None),
        P("batch"),
        P("batch", None),
        P(None, None, ("blk", "batch"), "tensor"),
        P(None, None, "tensor"),
        P(None, "tensor", ("blk", "batch")),
        P(None, ("blk", "batch"), "tensor"),
        P(None, "tensor"),
        P(None, "tensor", ("blk", "batch")),
        P(),
        P(),
        P(),
    )
    sizes = (mesh.shape["blk"], mesh.shape["batch"], mesh.shape["tensor"])
    body = fused_shards if sizes == (4, 2, 4) else general_shards
    return jax.shard_map(
        body,
        mesh=mesh,
        in_specs=placed,
        out_specs=(
            P("batch", "blk", None),
            P("batch", "blk", None),
            P(None, None, ("blk", "batch"), "tensor"),
            P(None, None, "tensor"),
            P(None, "tensor", ("blk", "batch")),
            P(None, ("blk", "batch"), "tensor"),
            P(None, "tensor"),
            P(None, "tensor", ("blk", "batch")),
            P(),
            P(),
            P(),
            P(),
        ),
        check_vma=False,
    )
```

```python
import jax
import jax.numpy as jnp
from jax import lax
from jax.experimental import pallas as pl
from jax.experimental.pallas import tpu as pltpu
from jax.sharding import PartitionSpec as P

HEAD = 64
SUB = 128


NEG = -1e30


def row_valid(bucket, lengths, pos):
    short = bucket[:, None] != 0
    pick = ((pos // SUB)[:, None] == jnp.arange(lengths.shape[1], dtype=jnp.int32)[None, :]).astype(
        jnp.int32
    )
    short_len = jnp.sum(lengths[:, None, :] * pick[None, :, :], axis=2)
    limit = jnp.where(short, short_len, lengths[:, :1])
    place = jnp.where(short, (pos % SUB)[None, :], pos[None, :])
    return place < limit


def seq_mask(bucket, lengths, qpos, kpos):
    short = bucket[:, None, None] != 0
    same = qpos[:, None] // SUB == kpos[None, :] // SUB
    allowed = jnp.logical_or(jnp.logical_not(short), same[None, :, :])
    return jnp.logical_and(row_valid(bucket, lengths, kpos)[:, None, :], allowed)


def layer_norm(h, gain, shift):
    mean = jnp.mean(h, -1, keepdims=True)
    cent = h - mean
    var = jnp.mean(cent * cent, -1, keepdims=True)
    return cent * lax.rsqrt(var + 1e-12) * gain + shift


def exact_gelu(value):
    return jax.nn.gelu(value, approximate=False)


def general_shards(
    tokens,
    out_grad,
    bucket,
    lengths,
    qkv_weight,
    qv_bias,
    out_weight,
    ff_in_weight,
    ff_in_bias,
    ff_out_weight,
    branch_bias,
    norm_gain,
    norm_bias,
):
    n_seq, rows_blk, width = tokens.shape
    blocks = lax.axis_size("blk")
    rank = lax.axis_index("blk")
    layers = qkv_weight.shape[0]
    local_width = qkv_weight.shape[3]
    heads_here = local_width // HEAD
    total_rows = n_seq * rows_blk
    scale = HEAD ** (-0.5)
    head_shape = (n_seq, rows_blk, heads_here, HEAD)
    qkv_full, out_full, ffin_full, ffout_full = (
        lax.all_gather(qkv_weight, ("blk", "batch"), axis=2, tiled=True),
        lax.all_gather(out_weight, ("blk", "batch"), axis=2, tiled=True),
        lax.all_gather(ff_in_weight, ("blk", "batch"), axis=1, tiled=True),
        lax.all_gather(ff_out_weight, ("blk", "batch"), axis=2, tiled=True),
    )
    local_pos = rank * rows_blk + jnp.arange(rows_blk, dtype=jnp.int32)
    row_ok = row_valid(bucket, lengths, local_pos).astype(jnp.float32).reshape(total_rows, 1)
    whole_pos = jnp.arange(blocks * rows_blk, dtype=jnp.int32)
    sub_bucket, sub_lengths = (bucket, lengths)

    def scores(query, keys, mask):
        found = (
            jnp.einsum("nqhe,nkhe->nhqk", query, keys, preferred_element_type=jnp.float32) * scale
        )
        return jnp.where(mask[:, None], found, NEG)

    x = tokens.astype(jnp.float32).reshape(total_rows, width)
    layer = 0
    xb = x.astype(jnp.bfloat16)
    triple = jnp.einsum("rd,cdk->crk", xb, qkv_full[layer], preferred_element_type=jnp.float32)
    query = (triple[0] + qv_bias[layer, 0]).astype(jnp.bfloat16).reshape(head_shape)
    keys = triple[1].astype(jnp.bfloat16).reshape(head_shape)
    values = (triple[2] + qv_bias[layer, 1]).astype(jnp.bfloat16).reshape(head_shape)
    pair = jnp.stack([keys, values])
    sub_query = query
    sub_pair = pair
    kept = lax.all_gather(sub_pair, "blk", axis=2, tiled=True)
    found = scores(sub_query, kept[0], seq_mask(sub_bucket, sub_lengths, local_pos, whole_pos))
    top = jnp.max(found, -1)
    sub_lse = top + jnp.log(jnp.sum(jnp.exp(found - top[..., None]), -1))
    weights = jnp.exp(found - sub_lse[..., None]).astype(jnp.bfloat16)
    sub_acc = jnp.einsum("nhqk,nkhe->nqhe", weights, kept[1], preferred_element_type=jnp.float32)
    lse = sub_lse
    acc = sub_acc
    att = acc.astype(jnp.bfloat16).reshape(total_rows, local_width)
    a_part = jnp.dot(att, out_full[layer], preferred_element_type=jnp.float32)
    branch = (
        lax.psum(a_part.astype(jnp.bfloat16), "tensor").astype(jnp.float32) + branch_bias[layer, 0]
    )
    upper_in = x + branch
    upper = layer_norm(upper_in, norm_gain[layer, 0], norm_bias[layer, 0])
    upper_b = upper.astype(jnp.bfloat16)
    pre = jnp.dot(upper_b, ffin_full[layer], preferred_element_type=jnp.float32) + ff_in_bias[layer]
    act = exact_gelu(pre).astype(jnp.bfloat16)
    f_part = jnp.dot(act, ffout_full[layer], preferred_element_type=jnp.float32)
    feed = (
        lax.psum(f_part.astype(jnp.bfloat16), "tensor").astype(jnp.float32) + branch_bias[layer, 1]
    )
    lower_in = upper + feed
    squares = [
        jnp.stack(
            [
                jnp.sum(row_ok * x * x),
                jnp.sum(row_ok * branch * branch),
                jnp.sum(row_ok * feed * feed),
            ]
        )
    ]
    saved = [(xb, query, pair, kept, lse, sub_lse, att, acc, upper_in, upper_b, pre, act, lower_in)]
    x = layer_norm(lower_in, norm_gain[layer, 1], norm_bias[layer, 1])
    output = x.astype(jnp.bfloat16).reshape(n_seq, rows_blk, width)
    grad = out_grad.astype(jnp.float32).reshape(total_rows, width)
    g_qkv, g_out, g_in, g_outf = ([], [], [], [])
    g_qvb, g_inb, g_branch, g_gain, g_shift = ([], [], [], [], [])
    for layer in reversed(range(layers)):
        xb, query, pair, kept, lse, sub_lse, att, acc, upper_in, upper_b, pre, act, lower_in = (
            saved[layer]
        )
        _, lower_back = jax.vjp(layer_norm, lower_in, norm_gain[layer, 1], norm_bias[layer, 1])
        d_lower, d_gain2, d_shift2 = lower_back(grad)
        d_feed = d_lower.astype(jnp.bfloat16)
        d_fbias = jnp.sum(d_feed.astype(jnp.float32), 0)
        g_outf.append(jnp.einsum("rf,rd->fd", act, d_feed, preferred_element_type=jnp.float32))
        d_act = jnp.einsum(
            "rd,fd->rf", d_feed, ffout_full[layer], preferred_element_type=jnp.float32
        )
        _, gelu_back = jax.vjp(exact_gelu, pre)
        d_pre = gelu_back(d_act)[0].astype(jnp.bfloat16)
        g_inb.append(jnp.sum(d_pre.astype(jnp.float32), 0))
        g_in.append(jnp.einsum("rd,rf->df", upper_b, d_pre, preferred_element_type=jnp.float32))
        ffn_part = jnp.einsum(
            "rf,df->rd", d_pre, ffin_full[layer], preferred_element_type=jnp.float32
        )
        d_upper = d_lower + lax.psum(ffn_part.astype(jnp.bfloat16), "tensor").astype(jnp.float32)
        _, upper_back = jax.vjp(layer_norm, upper_in, norm_gain[layer, 0], norm_bias[layer, 0])
        d_upper_in, d_gain1, d_shift1 = upper_back(d_upper)
        d_branch = d_upper_in.astype(jnp.bfloat16)
        d_abias = jnp.sum(d_branch.astype(jnp.float32), 0)
        g_out.append(jnp.einsum("rk,rd->kd", att, d_branch, preferred_element_type=jnp.float32))
        d_att = (
            jnp.einsum("rd,kd->rk", d_branch, out_full[layer], preferred_element_type=jnp.float32)
            .astype(jnp.bfloat16)
            .reshape(head_shape)
        )
        delta = jnp.einsum("nqhe,nqhe->nhq", d_att.astype(jnp.float32), acc)
        sub_query, sub_datt, sub_delta = (query, d_att, delta)
        block_keys = kept[0]
        block_found = scores(
            sub_query, block_keys, seq_mask(sub_bucket, sub_lengths, local_pos, whole_pos)
        )
        prob = jnp.exp(block_found - sub_lse[..., None])
        d_prob = jnp.einsum(
            "nqhe,nkhe->nhqk", sub_datt, kept[1], preferred_element_type=jnp.float32
        )
        d_scores = (prob * (d_prob - sub_delta[..., None])).astype(jnp.bfloat16)
        d_query = jnp.einsum(
            "nhqk,nkhe->nqhe", d_scores, block_keys, preferred_element_type=jnp.float32
        )
        d_keys = jnp.einsum(
            "nhqk,nqhe->nkhe", d_scores, sub_query, preferred_element_type=jnp.float32
        )
        d_values = jnp.einsum(
            "nhqk,nqhe->nkhe",
            prob.astype(jnp.bfloat16),
            sub_datt,
            preferred_element_type=jnp.float32,
        )
        sub_dq = d_query
        dpair_all = jnp.stack([d_keys * scale, d_values])
        sub_dpair = lax.psum_scatter(
            dpair_all.astype(jnp.bfloat16), "blk", scatter_dimension=2, tiled=True
        ).astype(jnp.float32)
        d_query, d_pair = (sub_dq, sub_dpair)
        dq_b = (d_query * scale).astype(jnp.bfloat16).reshape(total_rows, local_width)
        dk_b = d_pair[0].astype(jnp.bfloat16).reshape(total_rows, local_width)
        dv_b = d_pair[1].astype(jnp.bfloat16).reshape(total_rows, local_width)
        d_triple = jnp.stack([dq_b, dk_b, dv_b])
        g_qvb.append(
            jnp.stack([jnp.sum(dq_b.astype(jnp.float32), 0), jnp.sum(dv_b.astype(jnp.float32), 0)])
        )
        g_qkv.append(jnp.einsum("rd,crk->cdk", xb, d_triple, preferred_element_type=jnp.float32))
        attn_part = jnp.einsum(
            "crk,cdk->rd", d_triple, qkv_full[layer], preferred_element_type=jnp.float32
        )
        grad = d_upper_in + lax.psum(attn_part.astype(jnp.bfloat16), "tensor").astype(jnp.float32)
        g_branch.append(jnp.stack([d_abias, d_fbias]))
        g_gain.append(jnp.stack([d_gain1, d_gain2]))
        g_shift.append(jnp.stack([d_shift1, d_shift2]))

    def in_order(items):
        return jnp.stack(items[::-1])

    qkv_g, out_g, in_g, outf_g = (
        lax.psum_scatter(in_order(g_qkv), ("blk", "batch"), scatter_dimension=2, tiled=True),
        lax.psum_scatter(in_order(g_out), ("blk", "batch"), scatter_dimension=2, tiled=True),
        lax.psum_scatter(in_order(g_in), ("blk", "batch"), scatter_dimension=1, tiled=True),
        lax.psum_scatter(in_order(g_outf), ("blk", "batch"), scatter_dimension=2, tiled=True),
    )
    count = jnp.sum(row_ok)
    qvb_g, inb_g, branch_g, gain_g, shift_g, square_sums, count_all = lax.psum(
        (
            in_order(g_qvb),
            in_order(g_inb),
            in_order(g_branch),
            in_order(g_gain),
            in_order(g_shift),
            jnp.stack(squares),
            count,
        ),
        ("blk", "batch"),
    )
    rms = jnp.sqrt(square_sums / (count_all * width))
    tokens_grad = grad.reshape(n_seq, rows_blk, width)
    return (
        output,
        tokens_grad,
        qkv_g,
        qvb_g,
        out_g,
        in_g,
        inb_g,
        outf_g,
        branch_g,
        gain_g,
        shift_g,
        rms,
    )


MESH = pl.DeviceIdType.MESH
F32 = jnp.float32
BF16 = jnp.bfloat16
N_SEND = 48
N_RECV = 128


def dot_nn(a, b):
    return lax.dot_general(a, b, (((1,), (0,)), ((), ())), preferred_element_type=F32)


def dot_nt(a, b):
    return lax.dot_general(a, b, (((1,), (1,)), ((), ())), preferred_element_type=F32)


def dot_tn(a, b):
    return lax.dot_general(a, b, (((0,), (0,)), ((), ())), preferred_element_type=F32)


def slot_order(bucket_ref):
    first = jnp.where(bucket_ref[0] == 0, 0, jnp.where(bucket_ref[1] == 0, 1, 2))
    second = jnp.where(first == 0, 1, 0)
    third = jnp.where(first == 2, 1, 2)
    return first, second, third


class Net:
    def __init__(self, send_sems, recv_sems):
        self.send_sems, self.recv_sems = send_sems, recv_sems
        self.copies, self.n_recv = [], 0

    def slot(self):
        self.n_recv += 1
        assert self.n_recv <= N_RECV
        return self.n_recv - 1

    def send(self, src, dst, peer, slot=None):
        at = len(self.copies)
        if at >= N_SEND:
            self.copies[at - N_SEND].wait_send()
        copy = pltpu.make_async_remote_copy(
            src_ref=src,
            dst_ref=dst,
            send_sem=self.send_sems.at[at % N_SEND],
            recv_sem=self.recv_sems.at[self.slot() if slot is None else slot],
            device_id=peer,
            device_id_type=MESH,
        )
        copy.start()
        self.copies.append(copy)
        return copy

    def whole(self, ref, peer, slot):
        return pltpu.make_async_remote_copy(
            src_ref=ref,
            dst_ref=ref,
            send_sem=self.send_sems.at[0],
            recv_sem=self.recv_sems.at[slot],
            device_id=peer,
            device_id_type=MESH,
        )

    def finish(self):
        for copy in self.copies[-N_SEND:]:
            copy.wait_send()


class Gather:
    def __init__(self, net, view, at, near, split=False):
        self.net, self.view, self.near = net, view, near
        self.own, self.x, self.y, self.d, self.size = at
        self.half = self.size // 2
        self.slot = net.slot()
        self.late = net.slot() if split else self.slot

    def part(self, start, size):
        return self.view(pl.ds(pl.multiple_of(start, 16), size))

    def to_core(self, ref, late=False):
        self.net.send(ref, ref, self.near[2], self.late if late else self.slot)

    def issue(self, src=None):
        xnb, ynb, core = self.near
        to = self.part(self.own, self.size)
        src = to if src is None else src
        self.from_x = self.net.send(src, to, xnb)
        self.from_y = self.net.send(src, to, ynb)
        self.net.send(src, to, core, self.slot)

    def forward_x(self):
        xnb, ynb, core = self.near
        self.from_x.wait_recv()
        ref = self.part(self.x, self.half)
        self.first = self.net.send(ref, ref, ynb)
        self.to_core(self.part(self.x, self.size))

    def forward_y(self):
        xnb, ynb, core = self.near
        self.from_y.wait_recv()
        ref = self.part(self.y + self.half, self.half)
        self.second = self.net.send(ref, ref, xnb)
        self.to_core(self.part(self.y, self.size), True)

    def last(self):
        self.first.wait_recv()
        self.second.wait_recv()
        self.to_core(self.part(self.d, self.size), True)

    def ready(self):
        self.net.whole(self.part(0, 4 * self.size), self.near[2], self.slot).wait_recv()

    def ready_half(self, late):
        slot = self.late if late else self.slot
        self.net.whole(self.part(0, 2 * self.size), self.near[2], slot).wait_recv()


class Scatter:
    def __init__(self, net, refs, spot, near):
        self.net, self.spot, self.near = net, spot, near
        self.g, self.d, self.h, self.p1, self.s, self.p2 = refs
        self.rows = self.g.shape[3]
        self.half = self.rows // 2

    def core(self):
        c = self.spot[1]
        self.c1 = self.net.send(self.g.at[:, 1 - c], self.d, self.near[2])

    def first(self):
        yy, c, t = self.spot
        xnb, ynb, _ = self.near
        lo, hi = pl.ds(0, self.half), pl.ds(self.half, self.half)
        self.c1.wait_recv()
        for a in range(2):
            for b in range(2):
                self.h[a, b] = (self.g[a, c, b].astype(F32) + self.d[a, b].astype(F32)).astype(BF16)
        self.px = self.net.send(self.h.at[:, 1 - t, lo], self.p1.at[0], xnb)
        self.py = self.net.send(self.h.at[1 - yy, :, hi], self.p1.at[1], ynb)

    def second_x(self):
        yy, c, t = self.spot
        xnb, ynb, _ = self.near
        lo = pl.ds(0, self.half)
        self.px.wait_recv()
        self.s[0] = (self.h[1 - yy, t, lo].astype(F32) + self.p1[0, 1 - yy].astype(F32)).astype(BF16)
        self.qy = self.net.send(self.s.at[0], self.p2.at[0], ynb)

    def second_y(self):
        yy, c, t = self.spot
        xnb, ynb, _ = self.near
        hi = pl.ds(self.half, self.half)
        self.py.wait_recv()
        self.s[1] = (self.h[yy, 1 - t, hi].astype(F32) + self.p1[1, 1 - t].astype(F32)).astype(BF16)
        self.qx = self.net.send(self.s.at[1], self.p2.at[1], xnb)

    def result(self):
        yy, c, t = self.spot
        self.qy.wait_recv()
        self.qx.wait_recv()
        lo, hi = pl.ds(0, self.half), pl.ds(self.half, self.half)
        low = self.h[yy, t, lo].astype(F32) + self.p1[0, yy].astype(F32) + self.p2[0].astype(F32)
        high = self.h[yy, t, hi].astype(F32) + self.p1[1, t].astype(F32) + self.p2[1].astype(F32)
        return low, high


def fused_kernel(*refs):
    (
        bucket, lengths, tokens, out_grad, qkv_w, out_w, ffi_w, ffo_w, qv_bias, ffi_b, br_bias, gain, shift,
        out_hbm, tg_hbm, gq_hbm, go_hbm, gi_hbm, gf_hbm, vec_hbm, qvb_hbm,
        tok, cot, w_q, w_o, w_i, w_f, own_o, bias_r, own_q, xs, xs_t, q_r, kv_r, kv_a, p_a, p_b,
        att, att_r, ps, pr, xh1, rstd1, yb, act, gp, dh2, dfb, dab, df_t, yb_t, dpre, dh1, da_t,
        datt, datt_s, dkv_s, dkv_c, dkv_t, dkv_y, dtri, dx_p, dx_s, dx_1, dx_2, dx_t,
        sc_q, sc_o, sc_i, sc_f, z_o, z_i, z_f, t_o, t_i, t_f, vs, vr, vz, qs, qr,
        out_v, tg_v, gq_v, go_v, gi_v, gf_v, vec_v, qvb_v,
        local_sems, send_sems, recv_sems,
    ) = refs
    n_seq, n_rows, width = tok.shape
    blk_rows = ffi_w.shape[0]
    head_w = qkv_w.shape[2]
    pair_w = 2 * head_w
    heads = head_w // HEAD
    half, quart = n_rows // 2, n_rows // 4
    tile = 256
    n_tile = width // tile
    scale = HEAD ** (-0.5)

    r = lax.axis_index("blk")
    t = lax.axis_index("batch")
    z = lax.axis_index("tensor")
    yy, c = r // 2, r % 2
    pz, qz = z // 2, z % 2
    r1, r2 = r + 1 - 2 * c, (r + 2) % 4
    z1, z2 = z + 1 - 2 * qz, (z + 2) % 4
    core, xnb, ynb = (r1, t, z), (r, 1 - t, z), (r2, t, z)
    zn1, zn2 = (r, t, z1), (r, t, z2)
    peers = (zn2, zn1, xnb, ynb, core)
    near = (xnb, ynb, core)

    barrier = pltpu.get_barrier_semaphore()
    for peer in peers:
        pl.semaphore_signal(barrier, inc=1, device_id=peer, device_id_type=MESH)

    net = Net(send_sems, recv_sems)

    def block(rr, tt):
        return (rr * 2 + tt) * blk_rows

    at = (block(r, t), block(r, 1 - t), block(r2, t), block(r2, 1 - t), blk_rows)
    own = pl.ds(pl.multiple_of(block(r, t), 32), blk_rows)

    def gather(view, split=False):
        return Gather(net, view, at, near, split)

    ga_q = gather(lambda rows: w_q.at[rows])
    ga_o = [gather(lambda rows, k=k: w_o.at[k, rows]) for k in range(2)]
    ga_i = [gather(lambda rows, k=k: w_i.at[k, rows]) for k in range(2)]
    ga_f = [gather(lambda rows, k=k: w_f.at[k, rows], True) for k in range(2)]

    local = [
        pltpu.make_async_copy(src, dst, local_sems.at[k])
        for k, (src, dst) in enumerate(
            (
                (out_w, own_o),
                (tokens, tok),
                (qkv_w, own_q),
                (ffi_w, w_i.at[0, own]),
                (ffo_w, w_f.at[0, own]),
                (out_grad, cot),
            )
        )
    ]
    for copy in local:
        copy.start()
    stores = []

    def store(src, dst):
        copy = pltpu.make_async_copy(src, dst, local_sems.at[len(local) + len(stores)])
        copy.start()
        stores.append(copy)

    st = {}

    order = slot_order(bucket)

    def weights_first():
        local[0].wait()
        w_o[0, own] = jnp.transpose(own_o[...])
        local[2].wait()
        w_q[own] = jnp.concatenate([own_q[1], own_q[2], own_q[0]], 1)
        local[1].wait()
        for s in range(n_seq):
            xs[s * n_rows : (s + 1) * n_rows] = tok[order[s]]

    def enter():
        pl.semaphore_wait(barrier, len(peers))

    def far_weight(kind, src, buf):
        st["z" + kind] = net.send(src, buf.at[1, own], zn2)
        if kind == "i":
            st["zb"] = net.send(ffi_b, bias_r, zn2)

    def issue_second(kind, gather):
        st["z" + kind].wait_recv()
        gather.issue()

    def turn_x():
        xs_t[...] = jnp.transpose(xs[...])

    def keys_of(rr):
        return kv_a.at[pl.ds(pl.multiple_of(rr * n_rows, n_rows), n_rows)]

    def keys_values():
        ga_q.ready()
        bias = jnp.concatenate([jnp.zeros((1, head_w), F32), qv_bias[1:2, :]], 1)
        kv_r[...] = (dot_nn(xs[...], w_q[:, 0:pair_w]) + bias).astype(BF16)
        kv_a[pl.ds(pl.multiple_of(r * n_rows, n_rows), n_rows)] = kv_r[0:n_rows]
        st["kv_y"] = net.send(keys_of(r), keys_of(r), ynb)
        st["kv_c"] = [net.send(keys_of(r), keys_of(r), core)]

    def keys_pass():
        st["kv_y"].wait_recv()
        st["kv_c"].append(net.send(keys_of(r2), keys_of(r2), core))

    def queries():
        q_r[...] = (dot_nn(xs[...], w_q[:, pair_w:]) + qv_bias[0:1, :]).astype(BF16)

    lane_head = lax.broadcasted_iota(jnp.int32, (1, head_w), 1) // HEAD

    def of_head(value, h):
        return jnp.where(lane_head == h, value, jnp.zeros_like(value))

    def limit_of(s):
        index = order[s]
        return lengths[index, r], lengths[index, 0]

    own_half = pl.ds(pl.multiple_of(pz * half, half), half)
    other_half = pl.ds(pl.multiple_of((1 - pz) * half, half), half)
    key_at = lax.broadcasted_iota(jnp.int32, (1, n_rows), 1)

    def rows_at(s):
        return slice(s * n_rows, (s + 1) * n_rows)

    def few_at(s):
        return slice(s * half, (s + 1) * half)

    def attend(s):
        if s == 0:
            for copy in st["kv_c"]:
                copy.wait_recv()
            both, probs, key_ok = kv_a[...], p_a, None
        else:
            both, probs = kv_r[rows_at(s)], p_b.at[s - 1]
            key_ok = key_at < limit_of(s)[0]
        keys, values = both[:, 0:head_w], both[:, head_w:pair_w]
        query = q_r[rows_at(s)]
        total = jnp.zeros((n_rows, head_w), F32)
        for h in range(heads):
            score = dot_nt(of_head(query, h), keys) * scale
            if key_ok is not None:
                score = jnp.where(key_ok, score, NEG)
            e = jnp.exp(score - jnp.max(score, -1, keepdims=True))
            prob = e / jnp.sum(e, -1, keepdims=True)
            probs[h] = prob
            total = total + dot_nn(prob.astype(BF16), of_head(values, h))
        att[s] = total.astype(BF16)
        st["att", s] = net.send(att.at[s, other_half], att_r.at[s], zn2)

    def pair_send(k, s, value):
        ps[k, s] = value.astype(BF16)
        st["pair", k, s] = net.send(ps.at[k, s], pr.at[k, s], zn1)

    def pair_sum(k, s):
        st["pair", k, s].wait_recv()
        return ps[k, s].astype(F32) + pr[k, s].astype(F32)

    def ready(kind, gathers):
        if ("ready", kind) not in st:
            st["ready", kind] = True
            for gather in gathers:
                gather.ready()

    def project(s):
        ready("o", ga_o)
        st["att", s].wait_recv()
        pair_send(0, s, dot_nt(att[s, own_half], w_o[0]) + dot_nt(att_r[s], w_o[1]))

    vec = {k: jnp.zeros((1, width), F32) for k in range(12)}
    row_at = lax.broadcasted_iota(jnp.int32, (half, 1), 0)

    def row_ok(s):
        short, full = limit_of(s)
        place = row_at + pz * half
        ok = place + r * n_rows < full if s == 0 else place < short
        return ok.astype(F32)

    def tally(k, value):
        vec[k] = vec[k] + jnp.sum(value, 0, keepdims=True)

    def mean_of(value):
        return jnp.mean(value, -1, keepdims=True)

    def normed(h):
        cent = h - mean_of(h)
        rstd = lax.rsqrt(mean_of(cent * cent) + 1e-12)
        return cent * rstd, rstd

    def first_norm(s):
        here = few_at(s)
        x = xs[pl.ds(pl.multiple_of(s * n_rows + pz * half, half), half)].astype(F32)
        branch = pair_sum(0, s) + br_bias[0:1, :]
        ok = row_ok(s)
        tally(8, ok * (x * x))
        tally(9, ok * (branch * branch))
        tally(11, ok * jnp.ones((1, width), F32))
        hat, rstd = normed(x + branch)
        xh1[here] = hat
        rstd1[here] = rstd
        yb[here] = (hat * gain[0:1, :] + shift[0:1, :]).astype(BF16)

    def turn_y():
        yb_t[...] = jnp.transpose(yb[...])

    def hidden(s):
        if ("ready", "i") not in st:
            st["zb"].wait_recv()
            local[3].wait()
        ready("i", ga_i)
        here = few_at(s)
        for k in range(2):
            for n in range(n_tile):
                cols = slice(n * tile, (n + 1) * tile)
                bias = ffi_b[:, cols] if k == 0 else bias_r[:, cols]
                pre = dot_nn(yb[here], w_i[k, :, cols]) + bias
                phi = 0.5 * (1.0 + lax.erf(pre * (0.5**0.5)))
                act[k, here, cols] = (pre * phi).astype(BF16)
                gp[k, here, cols] = phi + pre * (jnp.exp(-0.5 * pre * pre) * 0.3989422804014327)

    def feed_out(late, s):
        if ("feed", late) not in st:
            st["feed", late] = True
            if not late:
                local[4].wait()
            for gather in ga_f:
                gather.ready_half(late)
        here = few_at(s)
        side = width // 2
        cols = pl.ds(pl.multiple_of(((1 - yy) if late else yy) * side, 128), side)
        value = dot_nt(act[0, here], w_f[0, cols]) + dot_nt(act[1, here], w_f[1, cols])
        ps[1, s, :, cols] = value.astype(BF16)
        st["feed", late, s] = net.send(ps.at[1, s, :, cols], pr.at[1, s, :, cols], zn1)

    def second_norm(s):
        here = few_at(s)
        if "cot" not in st:
            st["cot"] = True
            local[5].wait()
        for late in range(2):
            st["feed", late, s].wait_recv()
        feed = ps[1, s].astype(F32) + pr[1, s].astype(F32) + br_bias[1:2, :]
        tally(10, row_ok(s) * (feed * feed))
        hat, rstd = normed(xh1[here] * gain[0:1, :] + shift[0:1, :] + feed)
        out_v[s, own_half] = (hat * gain[1:2, :] + shift[1:2, :]).astype(BF16)
        g = cot[order[s], own_half].astype(F32)
        tally(1, g * hat)
        tally(2, g)
        g = g * gain[1:2, :]
        d = rstd * (g - mean_of(g) - hat * mean_of(g * hat))
        dh2[here] = d
        d = d.astype(BF16)
        dfb[here] = d
        tally(0, d.astype(F32))
        total = jnp.zeros((half, width), F32)
        for k in range(2):
            p = (dot_nn(d, w_f[k]) * gp[k, here]).astype(BF16)
            dpre[k, here] = p
            tally(3 + k, p.astype(F32))
            total = total + dot_nt(p, w_i[k])
        pair_send(2, s, total)

    quarter = pl.ds(pl.multiple_of(z * quart, quart), quart)
    quarter_2 = pl.ds(pl.multiple_of(z2 * quart, quart), quart)

    def out_far(s):
        here = out_v.at[s, quarter]
        st["out2", s] = net.send(here, here, zn2)

    def out_near(s):
        st["out2", s].wait_recv()
        there = out_v.at[s, quarter_2]
        st["out1", s] = net.send(there, there, zn1)

    def scatter(refs, k=None):
        views = refs if k is None else [ref.at[k] for ref in refs]
        return Scatter(net, views, (yy, c, t), near)

    rs_f = [scatter(sc_f, k) for k in range(2)]
    rs_i = [scatter(sc_i, k) for k in range(2)]
    rs_o = [scatter(sc_o, k) for k in range(2)]
    rs_q = scatter(sc_q)

    def grads(lhs, rhs, out):
        value = dot_nn(lhs, rhs).astype(BF16)
        for b in range(8):
            piece = value[b * blk_rows : (b + 1) * blk_rows]
            out[b // 4, (b // 2) % 2, b % 2] = piece

    def grads_wide(left, right, rs):
        for n in range(n_tile):
            cols = slice(n * tile, (n + 1) * tile)
            grads(left[...], right[:, cols], rs.g.at[:, :, :, :, cols])
        rs.core()

    def grad_f(k):
        if k == 1:
            df_t[...] = jnp.transpose(dfb[...])
        grads_wide(df_t, act.at[k], rs_f[k])

    def grad_i(k):
        grads_wide(yb_t, dpre.at[k], rs_i[k])

    def grad_o():
        da_t[...] = jnp.transpose(dab[...])
        rows_l = jnp.concatenate([att[s, own_half] for s in range(n_seq)], 0)
        rows_r = jnp.concatenate([att_r[s] for s in range(n_seq)], 0)
        grads(da_t[...], rows_r, rs_o[1].g)
        rs_o[1].core()
        grads(da_t[...], rows_l, rs_o[0].g)
        rs_o[0].core()

    def grad_q():
        grads(xs_t[...], dtri[...], rs_q.g)
        rs_q.core()

    def first_norm_back(s):
        here = few_at(s)
        hat = xh1[here]
        g = dh2[here] + pair_sum(2, s)
        tally(6, g * hat)
        tally(7, g)
        g = g * gain[0:1, :]
        d = rstd1[here] * (g - mean_of(g) - hat * mean_of(g * hat))
        dh1[here] = d
        d = d.astype(BF16)
        dab[here] = d
        tally(5, d.astype(F32))
        datt_s[s] = dot_nn(d, w_o[1]).astype(BF16)
        st["datt", s] = net.send(datt_s.at[s], datt.at[s, own_half], zn2)
        datt[s, own_half] = dot_nn(d, w_o[0]).astype(BF16)

    def vec_step(k):
        if k == 0:
            for n in range(12):
                vs[0, n : n + 1] = vec[n]
            vs[0, 12:16] = jnp.zeros((4, width), F32)
        else:
            st["vec"].wait_recv()
            vs[k] = vs[k - 1] + vr[k - 1]
        if k < 3:
            st["vec"] = net.send(vs.at[k], vr.at[k], (core, xnb, ynb)[k])
            return
        lane = lax.broadcasted_iota(jnp.int32, (1, width), 1)
        last = jnp.zeros((1, width), F32)
        for n in range(4):
            last = jnp.where(lane == n, jnp.sum(vs[3, 8 + n : 9 + n], 1, keepdims=True), last)
        vz[0, 0:3] = vs[3, 0:3]
        vz[0, 3:4] = vs[3, 4:5]
        vz[0, 4:7] = vs[3, 5:8]
        vz[0, 7:8] = last
        st["vec"] = net.send(vz.at[0], vz.at[1], zn2)

    def attend_back(s):
        st["datt", s].wait_recv()
        if s == 0:
            both, probs = kv_a[...], p_a
        else:
            both, probs = kv_r[rows_at(s)], p_b.at[s - 1]
        keys, values = both[:, 0:head_w], both[:, head_w:pair_w]
        query = q_r[rows_at(s)]
        d_att = datt[s]
        dq = jnp.zeros((n_rows, head_w), F32)
        dk = jnp.zeros(keys.shape, F32)
        dv = jnp.zeros(keys.shape, F32)
        for h in range(heads):
            prob = probs[h]
            d_h = of_head(d_att, h)
            dp = dot_nt(d_h, values)
            delta = jnp.sum(prob * dp, -1, keepdims=True)
            ds = (prob * (dp - delta)).astype(BF16)
            dq = dq + dot_nn(ds, of_head(keys, h))
            dk = dk + dot_tn(ds, of_head(query, h))
            dv = dv + dot_tn(prob.astype(BF16), d_h)
        dtri[rows_at(s), pair_w:] = (dq * scale).astype(BF16)
        both = jnp.concatenate([(dk * scale).astype(BF16), dv.astype(BF16)], 1)
        if s == 0:
            for a in range(4):
                dkv_s[a // 2, a % 2] = both[rows_at(a)]
            st["dkv1"] = net.send(dkv_s.at[:, 1 - c], dkv_c, core)
        else:
            dtri[rows_at(s), 0:pair_w] = both

    def keys_back():
        st["dkv1"].wait_recv()
        dkv_t[...] = (dkv_s[1 - yy, c].astype(F32) + dkv_c[1 - yy].astype(F32)).astype(BF16)
        st["dkv2"] = net.send(dkv_t, dkv_y, ynb)

    def dx_of(s):
        total = dot_nt(dtri[rows_at(s)], w_q[...])
        dx_p[s] = total
        for a in range(4):
            dx_s[a // 2, a % 2, s] = total[a * quart : (a + 1) * quart].astype(BF16)

    def half_rows(s):
        return pl.ds(pl.multiple_of(s * half + qz * quart, quart), quart)

    groups = {"b": (1, n_seq), "a": (0, 1)}

    def dx_first(group):
        lo, hi = groups[group]
        if group == "a":
            st["dkv2"].wait_recv()
            total = dkv_s[yy, c].astype(F32) + dkv_c[yy].astype(F32) + dkv_y[...].astype(F32)
            dtri[0:n_rows, 0:pair_w] = total.astype(BF16)
        for s in range(lo, hi):
            dx_of(s)
        st[group, 1] = net.send(dx_s.at[:, 1 - qz, lo:hi], dx_1.at[:, lo:hi], zn1)

    def dx_second(group):
        lo, hi = groups[group]
        st[group, 1].wait_recv()
        for s in range(lo, hi):
            dx_t[s] = (dx_p[s, quarter_2] + dx_1[1 - pz, s].astype(F32)).astype(BF16)
        st[group, 2] = net.send(dx_t.at[lo:hi], dx_2.at[lo:hi], zn2)

    def dx_third(group):
        lo, hi = groups[group]
        st[group, 2].wait_recv()
        for s in range(lo, hi):
            total = dx_p[s, quarter] + dx_1[pz, s].astype(F32) + dx_2[s].astype(F32)
            tg_v[s, quarter] = (total + dh1[half_rows(s)]).astype(BF16)
        here = tg_v.at[lo:hi, quarter]
        st[group, 3], st[group, 4] = net.send(here, here, zn2), net.send(here, here, zn1)

    def dx_last(group):
        lo, hi = groups[group]
        st[group, 3].wait_recv()
        there = tg_v.at[lo:hi, quarter_2]
        st[group, 5] = net.send(there, there, zn1)

    def bias_step(k):
        if k == 0:
            qs[0] = jnp.zeros(qs.shape[1:], F32)
            total = jnp.sum(dtri[...].astype(F32), 0, keepdims=True)
            qs[0, 0:1] = total[:, pair_w:]
            qs[0, 1:2] = total[:, head_w:pair_w]
        else:
            st["bias"].wait_recv()
            qs[k] = qs[k - 1] + qr[k - 1]
        st["bias"] = net.send(qs.at[k], qr.at[k], (core, xnb, ynb)[k])

    def to_z(kind, rs, buf, got):
        low, high = rs.result()
        n = low.shape[0]
        buf[0:n] = low.astype(BF16)
        buf[n : 2 * n] = high.astype(BF16)
        st["g" + kind] = net.send(buf, got, zn2)

    def put(kind, rs, out, to, got=None):
        low, high = rs.result()
        n = low.shape[0]
        if got is not None:
            st["g" + kind].wait_recv()
            low = low + got[0:n].astype(F32)
            high = high + got[n : 2 * n].astype(F32)
        out[0:n] = low
        out[n : 2 * n] = high
        store(out, to)

    def out_store():
        for s in range(n_seq):
            st["out1", s].wait_recv()
        store(out_v, out_hbm)

    def vec_store():
        st["vec"].wait_recv()
        vec_v[...] = vz[0] + vz[1]
        vec_v[3:4] = vs[3, 3:4] + vz[1, 3:4]
        store(vec_v, vec_hbm)

    def bias_store():
        st["bias"].wait_recv()
        qvb_v[...] = qs[2] + qr[2]
        store(qvb_v, qvb_hbm)

    def dx_store():
        for group in groups:
            for k in (4, 5):
                st[group, k].wait_recv()
        store(tg_v, tg_hbm)

    weights_first()
    enter()
    ga_q.issue()
    far_weight("o", w_o.at[0, own], w_o)
    ga_o[0].issue()
    far_weight("i", ffi_w, w_i)
    ga_i[0].issue(ffi_w)
    ga_q.forward_y()
    ga_q.forward_x()
    ga_f[0].issue(ffo_w)
    issue_second("o", ga_o[1])
    far_weight("f", ffo_w, w_f)
    ga_o[0].forward_y()
    ga_q.last()
    keys_values()
    ga_i[0].forward_y()
    ga_o[1].forward_x()
    ga_o[1].forward_y()
    queries()
    attend(2)
    ga_o[0].forward_x()
    issue_second("i", ga_i[1])
    ga_f[0].forward_y()
    attend(1)
    keys_pass()
    ga_o[0].last()
    attend(0)
    ga_i[0].forward_x()
    issue_second("f", ga_f[1])
    ga_o[1].last()
    project(2)
    ga_i[1].forward_y()
    ga_i[1].forward_x()
    project(1)
    turn_x()
    ga_i[0].last()
    project(0)
    ga_f[0].forward_x()
    ga_f[1].forward_y()
    ga_f[1].forward_x()
    first_norm(2)
    ga_i[1].last()
    hidden(2)
    first_norm(0)
    feed_out(0, 2)
    first_norm(1)
    ga_f[0].last()
    hidden(1)
    ga_f[1].last()
    feed_out(0, 1)
    feed_out(1, 2)
    hidden(0)
    feed_out(1, 1)
    feed_out(0, 0)
    feed_out(1, 0)
    second_norm(2)
    out_far(2)
    turn_y()
    second_norm(1)
    second_norm(0)
    grad_f(1)
    rs_f[1].first()
    grad_i(0)
    first_norm_back(2)
    first_norm_back(1)
    grad_f(0)
    first_norm_back(0)
    out_near(2)
    out_far(1)
    rs_f[1].second_y()
    out_far(0)
    attend_back(2)
    rs_f[1].second_x()
    attend_back(1)
    dx_first("b")
    rs_f[0].first()
    attend_back(0)
    to_z("f", rs_f[1], t_f, z_f)
    grad_o()
    keys_back()
    vec_step(0)
    vec_step(1)
    rs_o[1].first()
    grad_i(1)
    dx_first("a")
    dx_second("b")
    rs_o[1].second_x()
    vec_step(2)
    rs_o[1].second_y()
    rs_i[1].first()
    rs_o[0].first()
    grad_q()
    out_near(1)
    bias_step(0)
    bias_step(1)
    rs_i[0].first()
    vec_step(3)
    dx_second("a")
    out_near(0)
    dx_third("b")
    rs_i[1].second_x()
    to_z("o", rs_o[1], t_o, z_o)
    dx_third("a")
    rs_i[1].second_y()
    vec_store()
    rs_q.first()
    rs_i[0].second_x()
    rs_f[0].second_x()
    dx_last("b")
    rs_o[0].second_x()
    rs_o[0].second_y()
    out_store()
    to_z("i", rs_i[1], t_i, z_i)
    rs_q.second_x()
    rs_f[0].second_y()
    bias_step(2)
    rs_i[0].second_y()
    put("o", rs_o[0], go_v, go_hbm, z_o)
    dx_last("a")
    rs_q.second_y()
    bias_store()
    dx_store()
    put("q", rs_q, gq_v, gq_hbm)
    put("f", rs_f[0], gf_v, gf_hbm, z_f)
    put("i", rs_i[0], gi_v, gi_hbm, z_i)

    for copy in stores:
        copy.wait()
    net.finish()


def finish_kernel(
    bucket,
    out_i,
    tg_i,
    gq_i,
    go_i,
    gi_i,
    gf_i,
    vec_i,
    qvb_i,
    out_o,
    tg_o,
    gq_o,
    qvb_o,
    go_o,
    gi_o,
    inb_o,
    gf_o,
    br_o,
    gain_o,
    shift_o,
    rms_o,
):
    order = slot_order(bucket)
    for s in range(3):
        at = jnp.where(order[0] == s, 0, jnp.where(order[1] == s, 1, 2))
        out_o[s] = out_i[at]
        tg_o[s] = tg_i[at].astype(F32)
    n = gq_o.shape[2]
    value = gq_i[...]
    for k, part in enumerate((1, 2, 0)):
        gq_o[part] = value[:, k * n : (k + 1) * n]
    go_o[...] = jnp.transpose(go_i[...])
    gi_o[...] = gi_i[...]
    gf_o[...] = gf_i[...]
    qvb_o[...] = qvb_i[0:2]
    inb_o[...] = vec_i[3:4]
    br_o[0:1] = vec_i[4:5]
    br_o[1:2] = vec_i[0:1]
    gain_o[0:1] = vec_i[5:6]
    gain_o[1:2] = vec_i[1:2]
    shift_o[0:1] = vec_i[6:7]
    shift_o[1:2] = vec_i[2:3]
    rms_o[...] = jnp.sqrt(vec_i[7:8, 0:3] / vec_i[7:8, 3:4])


def fused_shards(
    tokens,
    out_grad,
    bucket,
    lengths,
    qkv_weight,
    qv_bias,
    out_weight,
    ff_in_weight,
    ff_in_bias,
    ff_out_weight,
    branch_bias,
    norm_gain,
    norm_bias,
):
    n_seq, n_rows, width = tokens.shape
    blk_rows, head_w = qkv_weight.shape[2:]
    ff = ff_in_weight.shape[2]
    heads = head_w // HEAD
    rows = n_seq * n_rows
    half, quart = n_rows // 2, n_rows // 4
    few = n_seq * half
    keys = 4 * n_rows
    vmem = pl.BlockSpec(memory_space=pltpu.VMEM)
    smem = pl.BlockSpec(memory_space=pltpu.SMEM)
    hbm = pl.BlockSpec(memory_space=pl.ANY)

    def v(*shape, dtype=BF16):
        return pltpu.VMEM(shape, dtype)

    def f(*shape):
        return pltpu.VMEM(shape, F32)

    wide = {"q": (blk_rows, 3 * head_w), "o": (blk_rows, head_w), "i": (blk_rows, ff), "f": (blk_rows, ff)}

    def scatter_bufs(kind):
        n, cols = wide[kind]
        lead = () if kind == "q" else (2,)
        dims = ((2, 2, 2, n), (2, 2, n), (2, 2, n), (2, 2, n // 2), (2, n // 2), (2, n // 2))
        return [v(*lead, *dim, cols) for dim in dims]

    scratch = [
        v(n_seq, n_rows, width),
        v(n_seq, n_rows, width),
        v(width, 3 * head_w),
        v(2, width, head_w),
        v(2, width, ff),
        v(2, width, ff),
        v(head_w, blk_rows),
        f(1, ff),
        v(3, blk_rows, head_w),
        v(rows, width),
        v(width, rows),
        v(rows, head_w),
        v(rows, 2 * head_w),
        v(keys, 2 * head_w),
        f(heads, n_rows, keys),
        f(n_seq - 1, heads, n_rows, n_rows),
        v(n_seq, n_rows, head_w),
        v(n_seq, half, head_w),
        v(3, n_seq, half, width),
        v(3, n_seq, half, width),
        f(few, width),
        f(few, 1),
        v(few, width),
        v(2, few, ff),
        f(2, few, ff),
        f(few, width),
        v(few, width),
        v(few, width),
        v(width, few),
        v(width, few),
        v(2, few, ff),
        f(few, width),
        v(width, few),
        v(n_seq, n_rows, head_w),
        v(n_seq, half, head_w),
        v(2, 2, n_rows, 2 * head_w),
        v(2, n_rows, 2 * head_w),
        v(n_rows, 2 * head_w),
        v(n_rows, 2 * head_w),
        v(rows, 3 * head_w),
        f(n_seq, n_rows, width),
        v(2, 2, n_seq, quart, width),
        v(2, n_seq, quart, width),
        v(n_seq, quart, width),
        v(n_seq, quart, width),
        scatter_bufs("q"),
        scatter_bufs("o"),
        scatter_bufs("i"),
        scatter_bufs("f"),
        v(*wide["o"]),
        v(*wide["i"]),
        v(*wide["f"]),
        v(*wide["o"]),
        v(*wide["i"]),
        v(*wide["f"]),
        f(4, 16, width),
        f(3, 16, width),
        f(2, 8, width),
        f(3, 8, head_w),
        f(3, 8, head_w),
        v(n_seq, n_rows, width),
        v(n_seq, n_rows, width),
        f(*wide["q"]),
        f(*wide["o"]),
        f(*wide["i"]),
        f(*wide["f"]),
        f(8, width),
        f(8, head_w),
        pltpu.SemaphoreType.DMA((14,)),
        pltpu.SemaphoreType.DMA((N_SEND,)),
        pltpu.SemaphoreType.DMA((N_RECV,)),
    ]

    def shape(*dims, dtype=F32):
        return jax.ShapeDtypeStruct(dims, dtype)

    main_out = [
        shape(n_seq, n_rows, width, dtype=BF16),
        shape(n_seq, n_rows, width, dtype=BF16),
        shape(*wide["q"]),
        shape(*wide["o"]),
        shape(*wide["i"]),
        shape(*wide["f"]),
        shape(8, width),
        shape(8, head_w),
    ]
    results = pl.pallas_call(
        fused_kernel,
        out_shape=main_out,
        in_specs=[smem, smem] + [hbm] * 6 + [vmem] * 5,
        out_specs=[hbm] * 8,
        scratch_shapes=scratch,
        compiler_params=pltpu.CompilerParams(
            collective_id=0, has_side_effects=True, vmem_limit_bytes=60 * 2**20
        ),
        name="encoder_layer",
    )(
        bucket,
        lengths,
        tokens,
        out_grad,
        qkv_weight[0],
        out_weight[0],
        ff_in_weight[0],
        jnp.transpose(ff_out_weight[0]),
        qv_bias[0],
        ff_in_bias,
        branch_bias[0],
        norm_gain[0],
        norm_bias[0],
    )
    final = pl.pallas_call(
        finish_kernel,
        out_shape=[
            shape(n_seq, n_rows, width, dtype=BF16),
            shape(n_seq, n_rows, width),
            shape(3, blk_rows, head_w),
            shape(2, head_w),
            shape(head_w, blk_rows),
            shape(blk_rows, ff),
            shape(1, ff),
            shape(blk_rows, ff),
            shape(2, width),
            shape(2, width),
            shape(2, width),
            shape(1, 3),
        ],
        in_specs=[smem] + [vmem] * 8,
        out_specs=[vmem] * 12,
        compiler_params=pltpu.CompilerParams(vmem_limit_bytes=60 * 2**20),
        name="finish",
    )(bucket, *results)
    out, tg, gq, qvb, go, gi, inb, gf, br, gain, shift, rms = final
    return (
        out,
        tg,
        gq[None],
        qvb[None],
        go[None],
        gi[None],
        inb,
        jnp.transpose(gf)[None],
        br[None],
        gain[None],
        shift[None],
        rms,
    )


def solution(mesh):
    placed = (
        P("batch", "blk", None),
        P("batch", "blk", None),
        P("batch"),
        P("batch", None),
        P(None, None, ("blk", "batch"), "tensor"),
        P(None, None, "tensor"),
        P(None, "tensor", ("blk", "batch")),
        P(None, ("blk", "batch"), "tensor"),
        P(None, "tensor"),
        P(None, "tensor", ("blk", "batch")),
        P(),
        P(),
        P(),
    )
    sizes = (mesh.shape["blk"], mesh.shape["batch"], mesh.shape["tensor"])
    body = fused_shards if sizes == (4, 2, 4) else general_shards
    return jax.shard_map(
        body,
        mesh=mesh,
        in_specs=placed,
        out_specs=(
            P("batch", "blk", None),
            P("batch", "blk", None),
            P(None, None, ("blk", "batch"), "tensor"),
            P(None, None, "tensor"),
            P(None, "tensor", ("blk", "batch")),
            P(None, ("blk", "batch"), "tensor"),
            P(None, "tensor"),
            P(None, "tensor", ("blk", "batch")),
            P(),
            P(),
            P(),
            P(),
        ),
        check_vma=False,
    )
```

```python
import jax
import jax.numpy as jnp
from jax import lax
from jax.experimental import pallas as pl
from jax.experimental.pallas import tpu as pltpu
from jax.sharding import PartitionSpec as P

HEAD = 64
SUB = 128


NEG = -1e30


def row_valid(bucket, lengths, pos):
    short = bucket[:, None] != 0
    pick = ((pos // SUB)[:, None] == jnp.arange(lengths.shape[1], dtype=jnp.int32)[None, :]).astype(
        jnp.int32
    )
    short_len = jnp.sum(lengths[:, None, :] * pick[None, :, :], axis=2)
    limit = jnp.where(short, short_len, lengths[:, :1])
    place = jnp.where(short, (pos % SUB)[None, :], pos[None, :])
    return place < limit


def seq_mask(bucket, lengths, qpos, kpos):
    short = bucket[:, None, None] != 0
    same = qpos[:, None] // SUB == kpos[None, :] // SUB
    allowed = jnp.logical_or(jnp.logical_not(short), same[None, :, :])
    return jnp.logical_and(row_valid(bucket, lengths, kpos)[:, None, :], allowed)


def layer_norm(h, gain, shift):
    mean = jnp.mean(h, -1, keepdims=True)
    cent = h - mean
    var = jnp.mean(cent * cent, -1, keepdims=True)
    return cent * lax.rsqrt(var + 1e-12) * gain + shift


def exact_gelu(value):
    return jax.nn.gelu(value, approximate=False)


def general_shards(
    tokens,
    out_grad,
    bucket,
    lengths,
    qkv_weight,
    qv_bias,
    out_weight,
    ff_in_weight,
    ff_in_bias,
    ff_out_weight,
    branch_bias,
    norm_gain,
    norm_bias,
):
    n_seq, rows_blk, width = tokens.shape
    blocks = lax.axis_size("blk")
    rank = lax.axis_index("blk")
    layers = qkv_weight.shape[0]
    local_width = qkv_weight.shape[3]
    heads_here = local_width // HEAD
    total_rows = n_seq * rows_blk
    scale = HEAD ** (-0.5)
    head_shape = (n_seq, rows_blk, heads_here, HEAD)
    qkv_full, out_full, ffin_full, ffout_full = (
        lax.all_gather(qkv_weight, ("blk", "batch"), axis=2, tiled=True),
        lax.all_gather(out_weight, ("blk", "batch"), axis=2, tiled=True),
        lax.all_gather(ff_in_weight, ("blk", "batch"), axis=1, tiled=True),
        lax.all_gather(ff_out_weight, ("blk", "batch"), axis=2, tiled=True),
    )
    local_pos = rank * rows_blk + jnp.arange(rows_blk, dtype=jnp.int32)
    row_ok = row_valid(bucket, lengths, local_pos).astype(jnp.float32).reshape(total_rows, 1)
    whole_pos = jnp.arange(blocks * rows_blk, dtype=jnp.int32)
    sub_bucket, sub_lengths = (bucket, lengths)

    def scores(query, keys, mask):
        found = (
            jnp.einsum("nqhe,nkhe->nhqk", query, keys, preferred_element_type=jnp.float32) * scale
        )
        return jnp.where(mask[:, None], found, NEG)

    x = tokens.astype(jnp.float32).reshape(total_rows, width)
    layer = 0
    xb = x.astype(jnp.bfloat16)
    triple = jnp.einsum("rd,cdk->crk", xb, qkv_full[layer], preferred_element_type=jnp.float32)
    query = (triple[0] + qv_bias[layer, 0]).astype(jnp.bfloat16).reshape(head_shape)
    keys = triple[1].astype(jnp.bfloat16).reshape(head_shape)
    values = (triple[2] + qv_bias[layer, 1]).astype(jnp.bfloat16).reshape(head_shape)
    pair = jnp.stack([keys, values])
    sub_query = query
    sub_pair = pair
    kept = lax.all_gather(sub_pair, "blk", axis=2, tiled=True)
    found = scores(sub_query, kept[0], seq_mask(sub_bucket, sub_lengths, local_pos, whole_pos))
    top = jnp.max(found, -1)
    sub_lse = top + jnp.log(jnp.sum(jnp.exp(found - top[..., None]), -1))
    weights = jnp.exp(found - sub_lse[..., None]).astype(jnp.bfloat16)
    sub_acc = jnp.einsum("nhqk,nkhe->nqhe", weights, kept[1], preferred_element_type=jnp.float32)
    lse = sub_lse
    acc = sub_acc
    att = acc.astype(jnp.bfloat16).reshape(total_rows, local_width)
    a_part = jnp.dot(att, out_full[layer], preferred_element_type=jnp.float32)
    branch = (
        lax.psum(a_part.astype(jnp.bfloat16), "tensor").astype(jnp.float32) + branch_bias[layer, 0]
    )
    upper_in = x + branch
    upper = layer_norm(upper_in, norm_gain[layer, 0], norm_bias[layer, 0])
    upper_b = upper.astype(jnp.bfloat16)
    pre = jnp.dot(upper_b, ffin_full[layer], preferred_element_type=jnp.float32) + ff_in_bias[layer]
    act = exact_gelu(pre).astype(jnp.bfloat16)
    f_part = jnp.dot(act, ffout_full[layer], preferred_element_type=jnp.float32)
    feed = (
        lax.psum(f_part.astype(jnp.bfloat16), "tensor").astype(jnp.float32) + branch_bias[layer, 1]
    )
    lower_in = upper + feed
    squares = [
        jnp.stack(
            [
                jnp.sum(row_ok * x * x),
                jnp.sum(row_ok * branch * branch),
                jnp.sum(row_ok * feed * feed),
            ]
        )
    ]
    saved = [(xb, query, pair, kept, lse, sub_lse, att, acc, upper_in, upper_b, pre, act, lower_in)]
    x = layer_norm(lower_in, norm_gain[layer, 1], norm_bias[layer, 1])
    output = x.astype(jnp.bfloat16).reshape(n_seq, rows_blk, width)
    grad = out_grad.astype(jnp.float32).reshape(total_rows, width)
    g_qkv, g_out, g_in, g_outf = ([], [], [], [])
    g_qvb, g_inb, g_branch, g_gain, g_shift = ([], [], [], [], [])
    for layer in reversed(range(layers)):
        xb, query, pair, kept, lse, sub_lse, att, acc, upper_in, upper_b, pre, act, lower_in = (
            saved[layer]
        )
        _, lower_back = jax.vjp(layer_norm, lower_in, norm_gain[layer, 1], norm_bias[layer, 1])
        d_lower, d_gain2, d_shift2 = lower_back(grad)
        d_feed = d_lower.astype(jnp.bfloat16)
        d_fbias = jnp.sum(d_feed.astype(jnp.float32), 0)
        g_outf.append(jnp.einsum("rf,rd->fd", act, d_feed, preferred_element_type=jnp.float32))
        d_act = jnp.einsum(
            "rd,fd->rf", d_feed, ffout_full[layer], preferred_element_type=jnp.float32
        )
        _, gelu_back = jax.vjp(exact_gelu, pre)
        d_pre = gelu_back(d_act)[0].astype(jnp.bfloat16)
        g_inb.append(jnp.sum(d_pre.astype(jnp.float32), 0))
        g_in.append(jnp.einsum("rd,rf->df", upper_b, d_pre, preferred_element_type=jnp.float32))
        ffn_part = jnp.einsum(
            "rf,df->rd", d_pre, ffin_full[layer], preferred_element_type=jnp.float32
        )
        d_upper = d_lower + lax.psum(ffn_part.astype(jnp.bfloat16), "tensor").astype(jnp.float32)
        _, upper_back = jax.vjp(layer_norm, upper_in, norm_gain[layer, 0], norm_bias[layer, 0])
        d_upper_in, d_gain1, d_shift1 = upper_back(d_upper)
        d_branch = d_upper_in.astype(jnp.bfloat16)
        d_abias = jnp.sum(d_branch.astype(jnp.float32), 0)
        g_out.append(jnp.einsum("rk,rd->kd", att, d_branch, preferred_element_type=jnp.float32))
        d_att = (
            jnp.einsum("rd,kd->rk", d_branch, out_full[layer], preferred_element_type=jnp.float32)
            .astype(jnp.bfloat16)
            .reshape(head_shape)
        )
        delta = jnp.einsum("nqhe,nqhe->nhq", d_att.astype(jnp.float32), acc)
        sub_query, sub_datt, sub_delta = (query, d_att, delta)
        block_keys = kept[0]
        block_found = scores(
            sub_query, block_keys, seq_mask(sub_bucket, sub_lengths, local_pos, whole_pos)
        )
        prob = jnp.exp(block_found - sub_lse[..., None])
        d_prob = jnp.einsum(
            "nqhe,nkhe->nhqk", sub_datt, kept[1], preferred_element_type=jnp.float32
        )
        d_scores = (prob * (d_prob - sub_delta[..., None])).astype(jnp.bfloat16)
        d_query = jnp.einsum(
            "nhqk,nkhe->nqhe", d_scores, block_keys, preferred_element_type=jnp.float32
        )
        d_keys = jnp.einsum(
            "nhqk,nqhe->nkhe", d_scores, sub_query, preferred_element_type=jnp.float32
        )
        d_values = jnp.einsum(
            "nhqk,nqhe->nkhe",
            prob.astype(jnp.bfloat16),
            sub_datt,
            preferred_element_type=jnp.float32,
        )
        sub_dq = d_query
        dpair_all = jnp.stack([d_keys * scale, d_values])
        sub_dpair = lax.psum_scatter(
            dpair_all.astype(jnp.bfloat16), "blk", scatter_dimension=2, tiled=True
        ).astype(jnp.float32)
        d_query, d_pair = (sub_dq, sub_dpair)
        dq_b = (d_query * scale).astype(jnp.bfloat16).reshape(total_rows, local_width)
        dk_b = d_pair[0].astype(jnp.bfloat16).reshape(total_rows, local_width)
        dv_b = d_pair[1].astype(jnp.bfloat16).reshape(total_rows, local_width)
        d_triple = jnp.stack([dq_b, dk_b, dv_b])
        g_qvb.append(
            jnp.stack([jnp.sum(dq_b.astype(jnp.float32), 0), jnp.sum(dv_b.astype(jnp.float32), 0)])
        )
        g_qkv.append(jnp.einsum("rd,crk->cdk", xb, d_triple, preferred_element_type=jnp.float32))
        attn_part = jnp.einsum(
            "crk,cdk->rd", d_triple, qkv_full[layer], preferred_element_type=jnp.float32
        )
        grad = d_upper_in + lax.psum(attn_part.astype(jnp.bfloat16), "tensor").astype(jnp.float32)
        g_branch.append(jnp.stack([d_abias, d_fbias]))
        g_gain.append(jnp.stack([d_gain1, d_gain2]))
        g_shift.append(jnp.stack([d_shift1, d_shift2]))

    def in_order(items):
        return jnp.stack(items[::-1])

    qkv_g, out_g, in_g, outf_g = (
        lax.psum_scatter(in_order(g_qkv), ("blk", "batch"), scatter_dimension=2, tiled=True),
        lax.psum_scatter(in_order(g_out), ("blk", "batch"), scatter_dimension=2, tiled=True),
        lax.psum_scatter(in_order(g_in), ("blk", "batch"), scatter_dimension=1, tiled=True),
        lax.psum_scatter(in_order(g_outf), ("blk", "batch"), scatter_dimension=2, tiled=True),
    )
    count = jnp.sum(row_ok)
    qvb_g, inb_g, branch_g, gain_g, shift_g, square_sums, count_all = lax.psum(
        (
            in_order(g_qvb),
            in_order(g_inb),
            in_order(g_branch),
            in_order(g_gain),
            in_order(g_shift),
            jnp.stack(squares),
            count,
        ),
        ("blk", "batch"),
    )
    rms = jnp.sqrt(square_sums / (count_all * width))
    tokens_grad = grad.reshape(n_seq, rows_blk, width)
    return (
        output,
        tokens_grad,
        qkv_g,
        qvb_g,
        out_g,
        in_g,
        inb_g,
        outf_g,
        branch_g,
        gain_g,
        shift_g,
        rms,
    )


MESH = pl.DeviceIdType.MESH
F32 = jnp.float32
BF16 = jnp.bfloat16
N_SEND = 48
N_RECV = 128


def dot_nn(a, b):
    return lax.dot_general(a, b, (((1,), (0,)), ((), ())), preferred_element_type=F32)


def dot_nt(a, b):
    return lax.dot_general(a, b, (((1,), (1,)), ((), ())), preferred_element_type=F32)


def dot_tn(a, b):
    return lax.dot_general(a, b, (((0,), (0,)), ((), ())), preferred_element_type=F32)


def slot_order(bucket_ref):
    first = jnp.where(bucket_ref[0] == 0, 0, jnp.where(bucket_ref[1] == 0, 1, 2))
    second = jnp.where(first == 0, 1, 0)
    third = jnp.where(first == 2, 1, 2)
    return first, second, third


class Net:
    def __init__(self, send_sems, recv_sems):
        self.send_sems, self.recv_sems = send_sems, recv_sems
        self.copies, self.n_recv = [], 0

    def slot(self):
        self.n_recv += 1
        assert self.n_recv <= N_RECV
        return self.n_recv - 1

    def send(self, src, dst, peer, slot=None):
        at = len(self.copies)
        if at >= N_SEND:
            self.copies[at - N_SEND].wait_send()
        copy = pltpu.make_async_remote_copy(
            src_ref=src,
            dst_ref=dst,
            send_sem=self.send_sems.at[at % N_SEND],
            recv_sem=self.recv_sems.at[self.slot() if slot is None else slot],
            device_id=peer,
            device_id_type=MESH,
        )
        copy.start()
        self.copies.append(copy)
        return copy

    def whole(self, ref, peer, slot):
        return pltpu.make_async_remote_copy(
            src_ref=ref,
            dst_ref=ref,
            send_sem=self.send_sems.at[0],
            recv_sem=self.recv_sems.at[slot],
            device_id=peer,
            device_id_type=MESH,
        )

    def finish(self):
        for copy in self.copies[-N_SEND:]:
            copy.wait_send()


class Gather:
    def __init__(self, net, view, at, near, split=False):
        self.net, self.view, self.near = net, view, near
        self.own, self.x, self.y, self.d, self.size = at
        self.half = self.size // 2
        self.slot = net.slot()
        self.late = net.slot() if split else self.slot

    def part(self, start, size):
        return self.view(pl.ds(pl.multiple_of(start, 16), size))

    def to_core(self, ref, late=False):
        self.net.send(ref, ref, self.near[2], self.late if late else self.slot)

    def issue(self, src=None):
        xnb, ynb, core = self.near
        to = self.part(self.own, self.size)
        src = to if src is None else src
        self.from_x = self.net.send(src, to, xnb)
        self.from_y = self.net.send(src, to, ynb)
        self.net.send(src, to, core, self.slot)

    def forward_x(self):
        xnb, ynb, core = self.near
        self.from_x.wait_recv()
        ref = self.part(self.x, self.half)
        self.first = self.net.send(ref, ref, ynb)
        self.to_core(self.part(self.x, self.size))

    def forward_y(self):
        xnb, ynb, core = self.near
        self.from_y.wait_recv()
        ref = self.part(self.y + self.half, self.half)
        self.second = self.net.send(ref, ref, xnb)
        self.to_core(self.part(self.y, self.size), True)

    def last(self):
        self.first.wait_recv()
        self.second.wait_recv()
        self.to_core(self.part(self.d, self.size), True)

    def ready(self):
        self.net.whole(self.part(0, 4 * self.size), self.near[2], self.slot).wait_recv()

    def ready_half(self, late):
        slot = self.late if late else self.slot
        self.net.whole(self.part(0, 2 * self.size), self.near[2], slot).wait_recv()


class Scatter:
    def __init__(self, net, refs, spot, near):
        self.net, self.spot, self.near = net, spot, near
        self.g, self.d, self.h, self.p1, self.s, self.p2 = refs
        self.rows = self.g.shape[3]
        self.half = self.rows // 2

    def core(self):
        c = self.spot[1]
        self.c1 = self.net.send(self.g.at[:, 1 - c], self.d, self.near[2])

    def first(self):
        yy, c, t = self.spot
        xnb, ynb, _ = self.near
        lo, hi = pl.ds(0, self.half), pl.ds(self.half, self.half)
        self.c1.wait_recv()
        for a in range(2):
            for b in range(2):
                self.h[a, b] = (self.g[a, c, b].astype(F32) + self.d[a, b].astype(F32)).astype(BF16)
        self.px = self.net.send(self.h.at[:, 1 - t, lo], self.p1.at[0], xnb)
        self.py = self.net.send(self.h.at[1 - yy, :, hi], self.p1.at[1], ynb)

    def second_x(self):
        yy, c, t = self.spot
        xnb, ynb, _ = self.near
        lo = pl.ds(0, self.half)
        self.px.wait_recv()
        self.s[0] = (self.h[1 - yy, t, lo].astype(F32) + self.p1[0, 1 - yy].astype(F32)).astype(BF16)
        self.qy = self.net.send(self.s.at[0], self.p2.at[0], ynb)

    def second_y(self):
        yy, c, t = self.spot
        xnb, ynb, _ = self.near
        hi = pl.ds(self.half, self.half)
        self.py.wait_recv()
        self.s[1] = (self.h[yy, 1 - t, hi].astype(F32) + self.p1[1, 1 - t].astype(F32)).astype(BF16)
        self.qx = self.net.send(self.s.at[1], self.p2.at[1], xnb)

    def result(self):
        yy, c, t = self.spot
        self.qy.wait_recv()
        self.qx.wait_recv()
        lo, hi = pl.ds(0, self.half), pl.ds(self.half, self.half)
        low = self.h[yy, t, lo].astype(F32) + self.p1[0, yy].astype(F32) + self.p2[0].astype(F32)
        high = self.h[yy, t, hi].astype(F32) + self.p1[1, t].astype(F32) + self.p2[1].astype(F32)
        return low, high


def fused_kernel(*refs):
    (
        bucket, lengths, tokens, out_grad, qkv_w, out_w, ffi_w, ffo_w, qv_bias, ffi_b, br_bias, gain, shift,
        out_hbm, tg_hbm, gq_hbm, go_hbm, gi_hbm, gf_hbm, vec_hbm, qvb_hbm,
        tok, cot, w_q, w_o, w_i, w_f, own_o, bias_r, own_q, xs, xs_t, q_r, kv_r, kv_a, p_a, p_b,
        att, att_r, ps, pr, xh1, rstd1, yb, act, gp, dh2, dfb, dab, df_t, yb_t, dpre, dh1, da_t,
        datt, datt_s, dkv_s, dkv_c, dkv_t, dkv_y, dtri, dx_p, dx_s, dx_1, dx_2, dx_t,
        sc_q, sc_o, sc_i, sc_f, z_o, z_i, z_f, t_o, t_i, t_f, vs, vr, vz, qs, qr,
        out_v, tg_v, gq_v, go_v, gi_v, gf_v, vec_v, qvb_v,
        local_sems, send_sems, recv_sems,
    ) = refs
    n_seq, n_rows, width = tok.shape
    blk_rows = ffi_w.shape[0]
    head_w = qkv_w.shape[2]
    pair_w = 2 * head_w
    heads = head_w // HEAD
    half, quart = n_rows // 2, n_rows // 4
    tile = 256
    n_tile = width // tile
    scale = HEAD ** (-0.5)

    r = lax.axis_index("blk")
    t = lax.axis_index("batch")
    z = lax.axis_index("tensor")
    yy, c = r // 2, r % 2
    pz, qz = z // 2, z % 2
    r1, r2 = r + 1 - 2 * c, (r + 2) % 4
    z1, z2 = z + 1 - 2 * qz, (z + 2) % 4
    core, xnb, ynb = (r1, t, z), (r, 1 - t, z), (r2, t, z)
    zn1, zn2 = (r, t, z1), (r, t, z2)
    peers = (zn2, zn1, xnb, ynb, core)
    near = (xnb, ynb, core)

    barrier = pltpu.get_barrier_semaphore()
    for peer in peers:
        pl.semaphore_signal(barrier, inc=1, device_id=peer, device_id_type=MESH)

    net = Net(send_sems, recv_sems)

    def block(rr, tt):
        return (rr * 2 + tt) * blk_rows

    at = (block(r, t), block(r, 1 - t), block(r2, t), block(r2, 1 - t), blk_rows)
    own = pl.ds(pl.multiple_of(block(r, t), 32), blk_rows)

    def gather(view, split=False):
        return Gather(net, view, at, near, split)

    ga_q = gather(lambda rows: w_q.at[rows])
    ga_o = [gather(lambda rows, k=k: w_o.at[k, rows]) for k in range(2)]
    ga_i = [gather(lambda rows, k=k: w_i.at[k, rows]) for k in range(2)]
    ga_f = [gather(lambda rows, k=k: w_f.at[k, rows], True) for k in range(2)]

    local = [
        pltpu.make_async_copy(src, dst, local_sems.at[k])
        for k, (src, dst) in enumerate(
            (
                (out_w, own_o),
                (tokens, tok),
                (qkv_w, own_q),
                (ffi_w, w_i.at[0, own]),
                (ffo_w, w_f.at[0, own]),
                (out_grad, cot),
            )
        )
    ]
    for copy in local:
        copy.start()
    stores = []

    def store(src, dst):
        copy = pltpu.make_async_copy(src, dst, local_sems.at[len(local) + len(stores)])
        copy.start()
        stores.append(copy)

    st = {}

    order = slot_order(bucket)

    def weights_first():
        local[0].wait()
        w_o[0, own] = jnp.transpose(own_o[...])
        local[2].wait()
        w_q[own] = jnp.concatenate([own_q[1], own_q[2], own_q[0]], 1)
        local[1].wait()
        for s in range(n_seq):
            xs[s * n_rows : (s + 1) * n_rows] = tok[order[s]]

    def enter():
        pl.semaphore_wait(barrier, len(peers))

    def far_weight(kind, src, buf):
        st["z" + kind] = net.send(src, buf.at[1, own], zn2)
        if kind == "i":
            st["zb"] = net.send(ffi_b, bias_r, zn2)

    def issue_second(kind, gather):
        st["z" + kind].wait_recv()
        gather.issue()

    def turn_x():
        xs_t[...] = jnp.transpose(xs[...])

    def keys_of(rr):
        return kv_a.at[pl.ds(pl.multiple_of(rr * n_rows, n_rows), n_rows)]

    def keys_values():
        ga_q.ready()
        bias = jnp.concatenate([jnp.zeros((1, head_w), F32), qv_bias[1:2, :]], 1)
        kv_r[...] = (dot_nn(xs[...], w_q[:, 0:pair_w]) + bias).astype(BF16)
        kv_a[pl.ds(pl.multiple_of(r * n_rows, n_rows), n_rows)] = kv_r[0:n_rows]
        st["kv_y"] = net.send(keys_of(r), keys_of(r), ynb)
        st["kv_c"] = [net.send(keys_of(r), keys_of(r), core)]

    def keys_pass():
        st["kv_y"].wait_recv()
        st["kv_c"].append(net.send(keys_of(r2), keys_of(r2), core))

    def queries():
        q_r[...] = (dot_nn(xs[...], w_q[:, pair_w:]) + qv_bias[0:1, :]).astype(BF16)

    lane_head = lax.broadcasted_iota(jnp.int32, (1, head_w), 1) // HEAD

    def of_head(value, h):
        return jnp.where(lane_head == h, value, jnp.zeros_like(value))

    def limit_of(s):
        index = order[s]
        return lengths[index, r], lengths[index, 0]

    own_half = pl.ds(pl.multiple_of(pz * half, half), half)
    other_half = pl.ds(pl.multiple_of((1 - pz) * half, half), half)
    key_at = lax.broadcasted_iota(jnp.int32, (1, n_rows), 1)

    def rows_at(s):
        return slice(s * n_rows, (s + 1) * n_rows)

    def few_at(s):
        return slice(s * half, (s + 1) * half)

    def attend(s):
        if s == 0:
            for copy in st["kv_c"]:
                copy.wait_recv()
            both, probs, key_ok = kv_a[...], p_a, None
        else:
            both, probs = kv_r[rows_at(s)], p_b.at[s - 1]
            key_ok = key_at < limit_of(s)[0]
        keys, values = both[:, 0:head_w], both[:, head_w:pair_w]
        query = q_r[rows_at(s)]
        total = jnp.zeros((n_rows, head_w), F32)
        for h in range(heads):
            score = dot_nt(of_head(query, h), keys) * scale
            if key_ok is not None:
                score = jnp.where(key_ok, score, NEG)
            e = jnp.exp(score - jnp.max(score, -1, keepdims=True))
            prob = e / jnp.sum(e, -1, keepdims=True)
            probs[h] = prob
            total = total + dot_nn(prob.astype(BF16), of_head(values, h))
        att[s] = total.astype(BF16)
        st["att", s] = net.send(att.at[s, other_half], att_r.at[s], zn2)

    def pair_send(k, s, value):
        ps[k, s] = value.astype(BF16)
        st["pair", k, s] = net.send(ps.at[k, s], pr.at[k, s], zn1)

    def pair_sum(k, s):
        st["pair", k, s].wait_recv()
        return ps[k, s].astype(F32) + pr[k, s].astype(F32)

    def ready(kind, gathers):
        if ("ready", kind) not in st:
            st["ready", kind] = True
            for gather in gathers:
                gather.ready()

    def project(s):
        ready("o", ga_o)
        st["att", s].wait_recv()
        pair_send(0, s, dot_nt(att[s, own_half], w_o[0]) + dot_nt(att_r[s], w_o[1]))

    vec = {k: jnp.zeros((1, width), F32) for k in range(12)}
    row_at = lax.broadcasted_iota(jnp.int32, (half, 1), 0)

    def row_ok(s):
        short, full = limit_of(s)
        place = row_at + pz * half
        ok = place + r * n_rows < full if s == 0 else place < short
        return ok.astype(F32)

    def tally(k, value):
        vec[k] = vec[k] + jnp.sum(value, 0, keepdims=True)

    def mean_of(value):
        return jnp.mean(value, -1, keepdims=True)

    def normed(h):
        cent = h - mean_of(h)
        rstd = lax.rsqrt(mean_of(cent * cent) + 1e-12)
        return cent * rstd, rstd

    def first_norm(s):
        here = few_at(s)
        x = xs[pl.ds(pl.multiple_of(s * n_rows + pz * half, half), half)].astype(F32)
        branch = pair_sum(0, s) + br_bias[0:1, :]
        ok = row_ok(s)
        tally(8, ok * (x * x))
        tally(9, ok * (branch * branch))
        tally(11, ok * jnp.ones((1, width), F32))
        hat, rstd = normed(x + branch)
        xh1[here] = hat
        rstd1[here] = rstd
        yb[here] = (hat * gain[0:1, :] + shift[0:1, :]).astype(BF16)

    def turn_y():
        yb_t[...] = jnp.transpose(yb[...])

    def hidden(s):
        if ("ready", "i") not in st:
            st["zb"].wait_recv()
            local[3].wait()
        ready("i", ga_i)
        here = few_at(s)
        for k in range(2):
            for n in range(n_tile):
                cols = slice(n * tile, (n + 1) * tile)
                bias = ffi_b[:, cols] if k == 0 else bias_r[:, cols]
                pre = dot_nn(yb[here], w_i[k, :, cols]) + bias
                phi = 0.5 * (1.0 + lax.erf(pre * (0.5**0.5)))
                act[k, here, cols] = (pre * phi).astype(BF16)
                gp[k, here, cols] = phi + pre * (jnp.exp(-0.5 * pre * pre) * 0.3989422804014327)

    def feed_out(late, s):
        if ("feed", late) not in st:
            st["feed", late] = True
            if not late:
                local[4].wait()
            for gather in ga_f:
                gather.ready_half(late)
        here = few_at(s)
        side = width // 2
        cols = pl.ds(pl.multiple_of(((1 - yy) if late else yy) * side, 128), side)
        value = dot_nt(act[0, here], w_f[0, cols]) + dot_nt(act[1, here], w_f[1, cols])
        ps[1, s, :, cols] = value.astype(BF16)
        st["feed", late, s] = net.send(ps.at[1, s, :, cols], pr.at[1, s, :, cols], zn1)

    def second_norm(s):
        here = few_at(s)
        if "cot" not in st:
            st["cot"] = True
            local[5].wait()
        for late in range(2):
            st["feed", late, s].wait_recv()
        feed = ps[1, s].astype(F32) + pr[1, s].astype(F32) + br_bias[1:2, :]
        tally(10, row_ok(s) * (feed * feed))
        hat, rstd = normed(xh1[here] * gain[0:1, :] + shift[0:1, :] + feed)
        out_v[s, own_half] = (hat * gain[1:2, :] + shift[1:2, :]).astype(BF16)
        g = cot[order[s], own_half].astype(F32)
        tally(1, g * hat)
        tally(2, g)
        g = g * gain[1:2, :]
        d = rstd * (g - mean_of(g) - hat * mean_of(g * hat))
        dh2[here] = d
        d = d.astype(BF16)
        dfb[here] = d
        tally(0, d.astype(F32))
        total = jnp.zeros((half, width), F32)
        for k in range(2):
            p = (dot_nn(d, w_f[k]) * gp[k, here]).astype(BF16)
            dpre[k, here] = p
            tally(3 + k, p.astype(F32))
            total = total + dot_nt(p, w_i[k])
        pair_send(2, s, total)

    quarter = pl.ds(pl.multiple_of(z * quart, quart), quart)
    quarter_2 = pl.ds(pl.multiple_of(z2 * quart, quart), quart)

    def out_far(s):
        here = out_v.at[s, quarter]
        st["out2", s] = net.send(here, here, zn2)

    def out_near(s):
        st["out2", s].wait_recv()
        there = out_v.at[s, quarter_2]
        st["out1", s] = net.send(there, there, zn1)

    def scatter(refs, k=None):
        views = refs if k is None else [ref.at[k] for ref in refs]
        return Scatter(net, views, (yy, c, t), near)

    rs_f = [scatter(sc_f, k) for k in range(2)]
    rs_i = [scatter(sc_i, k) for k in range(2)]
    rs_o = [scatter(sc_o, k) for k in range(2)]
    rs_q = scatter(sc_q)

    def grads(lhs, rhs, out):
        value = dot_nn(lhs, rhs).astype(BF16)
        for b in range(8):
            piece = value[b * blk_rows : (b + 1) * blk_rows]
            out[b // 4, (b // 2) % 2, b % 2] = piece

    def grads_wide(left, right, rs):
        for n in range(n_tile):
            cols = slice(n * tile, (n + 1) * tile)
            grads(left[...], right[:, cols], rs.g.at[:, :, :, :, cols])
        rs.core()

    def grad_f(k):
        if k == 1:
            df_t[...] = jnp.transpose(dfb[...])
        grads_wide(df_t, act.at[k], rs_f[k])

    def grad_i(k):
        grads_wide(yb_t, dpre.at[k], rs_i[k])

    def grad_o():
        da_t[...] = jnp.transpose(dab[...])
        rows_l = jnp.concatenate([att[s, own_half] for s in range(n_seq)], 0)
        rows_r = jnp.concatenate([att_r[s] for s in range(n_seq)], 0)
        grads(da_t[...], rows_r, rs_o[1].g)
        rs_o[1].core()
        grads(da_t[...], rows_l, rs_o[0].g)
        rs_o[0].core()

    def grad_q():
        grads(xs_t[...], dtri[...], rs_q.g)
        rs_q.core()

    def first_norm_back(s):
        here = few_at(s)
        hat = xh1[here]
        g = dh2[here] + pair_sum(2, s)
        tally(6, g * hat)
        tally(7, g)
        g = g * gain[0:1, :]
        d = rstd1[here] * (g - mean_of(g) - hat * mean_of(g * hat))
        dh1[here] = d
        d = d.astype(BF16)
        dab[here] = d
        tally(5, d.astype(F32))
        datt_s[s] = dot_nn(d, w_o[1]).astype(BF16)
        st["datt", s] = net.send(datt_s.at[s], datt.at[s, own_half], zn2)
        datt[s, own_half] = dot_nn(d, w_o[0]).astype(BF16)

    def vec_step(k):
        if k == 0:
            for n in range(12):
                vs[0, n : n + 1] = vec[n]
            vs[0, 12:16] = jnp.zeros((4, width), F32)
        else:
            st["vec"].wait_recv()
            vs[k] = vs[k - 1] + vr[k - 1]
        if k < 3:
            st["vec"] = net.send(vs.at[k], vr.at[k], (core, xnb, ynb)[k])
            return
        lane = lax.broadcasted_iota(jnp.int32, (1, width), 1)
        last = jnp.zeros((1, width), F32)
        for n in range(4):
            last = jnp.where(lane == n, jnp.sum(vs[3, 8 + n : 9 + n], 1, keepdims=True), last)
        vz[0, 0:3] = vs[3, 0:3]
        vz[0, 3:4] = vs[3, 4:5]
        vz[0, 4:7] = vs[3, 5:8]
        vz[0, 7:8] = last
        st["vec"] = net.send(vz.at[0], vz.at[1], zn2)

    def attend_back(s):
        st["datt", s].wait_recv()
        if s == 0:
            both, probs = kv_a[...], p_a
        else:
            both, probs = kv_r[rows_at(s)], p_b.at[s - 1]
        keys, values = both[:, 0:head_w], both[:, head_w:pair_w]
        query = q_r[rows_at(s)]
        d_att = datt[s]
        dq = jnp.zeros((n_rows, head_w), F32)
        dk = jnp.zeros(keys.shape, F32)
        dv = jnp.zeros(keys.shape, F32)
        for h in range(heads):
            prob = probs[h]
            d_h = of_head(d_att, h)
            dp = dot_nt(d_h, values)
            delta = jnp.sum(prob * dp, -1, keepdims=True)
            ds = (prob * (dp - delta)).astype(BF16)
            dq = dq + dot_nn(ds, of_head(keys, h))
            dk = dk + dot_tn(ds, of_head(query, h))
            dv = dv + dot_tn(prob.astype(BF16), d_h)
        dtri[rows_at(s), pair_w:] = (dq * scale).astype(BF16)
        both = jnp.concatenate([(dk * scale).astype(BF16), dv.astype(BF16)], 1)
        if s == 0:
            for a in range(4):
                dkv_s[a // 2, a % 2] = both[rows_at(a)]
            st["dkv1"] = net.send(dkv_s.at[:, 1 - c], dkv_c, core)
        else:
            dtri[rows_at(s), 0:pair_w] = both

    def keys_back():
        st["dkv1"].wait_recv()
        dkv_t[...] = (dkv_s[1 - yy, c].astype(F32) + dkv_c[1 - yy].astype(F32)).astype(BF16)
        st["dkv2"] = net.send(dkv_t, dkv_y, ynb)

    def dx_of(s):
        total = dot_nt(dtri[rows_at(s)], w_q[...])
        dx_p[s] = total
        for a in range(4):
            dx_s[a // 2, a % 2, s] = total[a * quart : (a + 1) * quart].astype(BF16)

    def half_rows(s):
        return pl.ds(pl.multiple_of(s * half + qz * quart, quart), quart)

    groups = {"b": (1, n_seq), "a": (0, 1)}

    def dx_first(group):
        lo, hi = groups[group]
        if group == "a":
            st["dkv2"].wait_recv()
            total = dkv_s[yy, c].astype(F32) + dkv_c[yy].astype(F32) + dkv_y[...].astype(F32)
            dtri[0:n_rows, 0:pair_w] = total.astype(BF16)
        for s in range(lo, hi):
            dx_of(s)
        st[group, 1] = net.send(dx_s.at[:, 1 - qz, lo:hi], dx_1.at[:, lo:hi], zn1)

    def dx_second(group):
        lo, hi = groups[group]
        st[group, 1].wait_recv()
        for s in range(lo, hi):
            dx_t[s] = (dx_p[s, quarter_2] + dx_1[1 - pz, s].astype(F32)).astype(BF16)
        st[group, 2] = net.send(dx_t.at[lo:hi], dx_2.at[lo:hi], zn2)

    def dx_third(group):
        lo, hi = groups[group]
        st[group, 2].wait_recv()
        for s in range(lo, hi):
            total = dx_p[s, quarter] + dx_1[pz, s].astype(F32) + dx_2[s].astype(F32)
            tg_v[s, quarter] = (total + dh1[half_rows(s)]).astype(BF16)
        here = tg_v.at[lo:hi, quarter]
        st[group, 3], st[group, 4] = net.send(here, here, zn2), net.send(here, here, zn1)

    def dx_last(group):
        lo, hi = groups[group]
        st[group, 3].wait_recv()
        there = tg_v.at[lo:hi, quarter_2]
        st[group, 5] = net.send(there, there, zn1)

    def bias_step(k):
        if k == 0:
            qs[0] = jnp.zeros(qs.shape[1:], F32)
            total = jnp.sum(dtri[...].astype(F32), 0, keepdims=True)
            qs[0, 0:1] = total[:, pair_w:]
            qs[0, 1:2] = total[:, head_w:pair_w]
        else:
            st["bias"].wait_recv()
            qs[k] = qs[k - 1] + qr[k - 1]
        st["bias"] = net.send(qs.at[k], qr.at[k], (core, xnb, ynb)[k])

    def to_z(kind, rs, buf, got):
        low, high = rs.result()
        n = low.shape[0]
        buf[0:n] = low.astype(BF16)
        buf[n : 2 * n] = high.astype(BF16)
        st["g" + kind] = net.send(buf, got, zn2)

    def put(kind, rs, out, to, got=None):
        low, high = rs.result()
        n = low.shape[0]
        if got is not None:
            st["g" + kind].wait_recv()
            low = low + got[0:n].astype(F32)
            high = high + got[n : 2 * n].astype(F32)
        out[0:n] = low
        out[n : 2 * n] = high
        store(out, to)

    def out_store():
        for s in range(n_seq):
            st["out1", s].wait_recv()
        store(out_v, out_hbm)

    def vec_store():
        st["vec"].wait_recv()
        vec_v[...] = vz[0] + vz[1]
        vec_v[3:4] = vs[3, 3:4] + vz[1, 3:4]
        store(vec_v, vec_hbm)

    def bias_store():
        st["bias"].wait_recv()
        qvb_v[...] = qs[2] + qr[2]
        store(qvb_v, qvb_hbm)

    def dx_store():
        for group in groups:
            for k in (4, 5):
                st[group, k].wait_recv()
        store(tg_v, tg_hbm)

    weights_first()
    enter()
    far_weight("o", w_o.at[0, own], w_o)
    ga_q.issue()
    ga_i[0].issue(ffi_w)
    far_weight("i", ffi_w, w_i)
    ga_q.forward_y()
    ga_q.forward_x()
    ga_o[0].issue()
    issue_second("o", ga_o[1])
    ga_f[0].issue(ffo_w)
    ga_i[0].forward_y()
    far_weight("f", ffo_w, w_f)
    ga_q.last()
    keys_values()
    queries()
    ga_o[0].forward_x()
    ga_o[1].forward_y()
    attend(1)
    ga_o[1].forward_x()
    issue_second("i", ga_i[1])
    ga_o[0].forward_y()
    attend(2)
    ga_i[0].forward_x()
    keys_pass()
    attend(0)
    issue_second("f", ga_f[1])
    ga_i[1].forward_x()
    ga_o[0].last()
    ga_f[0].forward_x()
    ga_o[1].last()
    project(2)
    ga_i[1].forward_y()
    project(1)
    ga_i[0].last()
    ga_f[0].forward_y()
    ga_f[1].forward_x()
    project(0)
    ga_f[1].forward_y()
    turn_x()
    ga_i[1].last()
    first_norm(2)
    hidden(2)
    ga_f[0].last()
    feed_out(0, 2)
    first_norm(1)
    hidden(1)
    ga_f[1].last()
    feed_out(0, 1)
    feed_out(1, 1)
    first_norm(0)
    feed_out(1, 2)
    hidden(0)
    feed_out(0, 0)
    feed_out(1, 0)
    second_norm(1)
    second_norm(2)
    second_norm(0)
    out_far(1)
    grad_f(1)
    turn_y()
    grad_i(0)
    rs_f[1].first()
    first_norm_back(1)
    first_norm_back(2)
    grad_i(1)
    first_norm_back(0)
    vec_step(0)
    vec_step(1)
    out_far(0)
    rs_f[1].second_y()
    rs_f[1].second_x()
    out_near(1)
    attend_back(1)
    rs_i[0].first()
    out_far(2)
    attend_back(2)
    dx_first("b")
    attend_back(0)
    grad_o()
    to_z("f", rs_f[1], t_f, z_f)
    keys_back()
    rs_o[1].first()
    rs_i[0].second_y()
    rs_i[1].first()
    dx_first("a")
    rs_o[0].first()
    grad_f(0)
    rs_o[1].second_y()
    dx_second("b")
    out_near(0)
    rs_o[1].second_x()
    bias_step(0)
    rs_f[0].first()
    dx_second("a")
    bias_step(1)
    vec_step(2)
    rs_i[0].second_x()
    rs_i[1].second_y()
    rs_i[1].second_x()
    dx_third("b")
    dx_third("a")
    grad_q()
    rs_q.first()
    to_z("o", rs_o[1], t_o, z_o)
    bias_step(2)
    out_near(2)
    rs_f[0].second_y()
    to_z("i", rs_i[1], t_i, z_i)
    dx_last("b")
    rs_o[0].second_x()
    rs_f[0].second_x()
    rs_o[0].second_y()
    dx_last("a")
    vec_step(3)
    rs_q.second_y()
    out_store()
    bias_store()
    rs_q.second_x()
    put("f", rs_f[0], gf_v, gf_hbm, z_f)
    put("q", rs_q, gq_v, gq_hbm)
    put("o", rs_o[0], go_v, go_hbm, z_o)
    dx_store()
    put("i", rs_i[0], gi_v, gi_hbm, z_i)
    vec_store()

    for copy in stores:
        copy.wait()
    net.finish()


def finish_kernel(
    bucket,
    out_i,
    tg_i,
    gq_i,
    go_i,
    gi_i,
    gf_i,
    vec_i,
    qvb_i,
    out_o,
    tg_o,
    gq_o,
    qvb_o,
    go_o,
    gi_o,
    inb_o,
    gf_o,
    br_o,
    gain_o,
    shift_o,
    rms_o,
):
    order = slot_order(bucket)
    for s in range(3):
        at = jnp.where(order[0] == s, 0, jnp.where(order[1] == s, 1, 2))
        out_o[s] = out_i[at]
        tg_o[s] = tg_i[at].astype(F32)
    n = gq_o.shape[2]
    value = gq_i[...]
    for k, part in enumerate((1, 2, 0)):
        gq_o[part] = value[:, k * n : (k + 1) * n]
    go_o[...] = jnp.transpose(go_i[...])
    gi_o[...] = gi_i[...]
    gf_o[...] = gf_i[...]
    qvb_o[...] = qvb_i[0:2]
    inb_o[...] = vec_i[3:4]
    br_o[0:1] = vec_i[4:5]
    br_o[1:2] = vec_i[0:1]
    gain_o[0:1] = vec_i[5:6]
    gain_o[1:2] = vec_i[1:2]
    shift_o[0:1] = vec_i[6:7]
    shift_o[1:2] = vec_i[2:3]
    rms_o[...] = jnp.sqrt(vec_i[7:8, 0:3] / vec_i[7:8, 3:4])


def fused_shards(
    tokens,
    out_grad,
    bucket,
    lengths,
    qkv_weight,
    qv_bias,
    out_weight,
    ff_in_weight,
    ff_in_bias,
    ff_out_weight,
    branch_bias,
    norm_gain,
    norm_bias,
):
    n_seq, n_rows, width = tokens.shape
    blk_rows, head_w = qkv_weight.shape[2:]
    ff = ff_in_weight.shape[2]
    heads = head_w // HEAD
    rows = n_seq * n_rows
    half, quart = n_rows // 2, n_rows // 4
    few = n_seq * half
    keys = 4 * n_rows
    vmem = pl.BlockSpec(memory_space=pltpu.VMEM)
    smem = pl.BlockSpec(memory_space=pltpu.SMEM)
    hbm = pl.BlockSpec(memory_space=pl.ANY)

    def v(*shape, dtype=BF16):
        return pltpu.VMEM(shape, dtype)

    def f(*shape):
        return pltpu.VMEM(shape, F32)

    wide = {"q": (blk_rows, 3 * head_w), "o": (blk_rows, head_w), "i": (blk_rows, ff), "f": (blk_rows, ff)}

    def scatter_bufs(kind):
        n, cols = wide[kind]
        lead = () if kind == "q" else (2,)
        dims = ((2, 2, 2, n), (2, 2, n), (2, 2, n), (2, 2, n // 2), (2, n // 2), (2, n // 2))
        return [v(*lead, *dim, cols) for dim in dims]

    scratch = [
        v(n_seq, n_rows, width),
        v(n_seq, n_rows, width),
        v(width, 3 * head_w),
        v(2, width, head_w),
        v(2, width, ff),
        v(2, width, ff),
        v(head_w, blk_rows),
        f(1, ff),
        v(3, blk_rows, head_w),
        v(rows, width),
        v(width, rows),
        v(rows, head_w),
        v(rows, 2 * head_w),
        v(keys, 2 * head_w),
        f(heads, n_rows, keys),
        f(n_seq - 1, heads, n_rows, n_rows),
        v(n_seq, n_rows, head_w),
        v(n_seq, half, head_w),
        v(3, n_seq, half, width),
        v(3, n_seq, half, width),
        f(few, width),
        f(few, 1),
        v(few, width),
        v(2, few, ff),
        f(2, few, ff),
        f(few, width),
        v(few, width),
        v(few, width),
        v(width, few),
        v(width, few),
        v(2, few, ff),
        f(few, width),
        v(width, few),
        v(n_seq, n_rows, head_w),
        v(n_seq, half, head_w),
        v(2, 2, n_rows, 2 * head_w),
        v(2, n_rows, 2 * head_w),
        v(n_rows, 2 * head_w),
        v(n_rows, 2 * head_w),
        v(rows, 3 * head_w),
        f(n_seq, n_rows, width),
        v(2, 2, n_seq, quart, width),
        v(2, n_seq, quart, width),
        v(n_seq, quart, width),
        v(n_seq, quart, width),
        scatter_bufs("q"),
        scatter_bufs("o"),
        scatter_bufs("i"),
        scatter_bufs("f"),
        v(*wide["o"]),
        v(*wide["i"]),
        v(*wide["f"]),
        v(*wide["o"]),
        v(*wide["i"]),
        v(*wide["f"]),
        f(4, 16, width),
        f(3, 16, width),
        f(2, 8, width),
        f(3, 8, head_w),
        f(3, 8, head_w),
        v(n_seq, n_rows, width),
        v(n_seq, n_rows, width),
        f(*wide["q"]),
        f(*wide["o"]),
        f(*wide["i"]),
        f(*wide["f"]),
        f(8, width),
        f(8, head_w),
        pltpu.SemaphoreType.DMA((14,)),
        pltpu.SemaphoreType.DMA((N_SEND,)),
        pltpu.SemaphoreType.DMA((N_RECV,)),
    ]

    def shape(*dims, dtype=F32):
        return jax.ShapeDtypeStruct(dims, dtype)

    main_out = [
        shape(n_seq, n_rows, width, dtype=BF16),
        shape(n_seq, n_rows, width, dtype=BF16),
        shape(*wide["q"]),
        shape(*wide["o"]),
        shape(*wide["i"]),
        shape(*wide["f"]),
        shape(8, width),
        shape(8, head_w),
    ]
    results = pl.pallas_call(
        fused_kernel,
        out_shape=main_out,
        in_specs=[smem, smem] + [hbm] * 6 + [vmem] * 5,
        out_specs=[hbm] * 8,
        scratch_shapes=scratch,
        compiler_params=pltpu.CompilerParams(
            collective_id=0, has_side_effects=True, vmem_limit_bytes=60 * 2**20
        ),
        name="encoder_layer",
    )(
        bucket,
        lengths,
        tokens,
        out_grad,
        qkv_weight[0],
        out_weight[0],
        ff_in_weight[0],
        jnp.transpose(ff_out_weight[0]),
        qv_bias[0],
        ff_in_bias,
        branch_bias[0],
        norm_gain[0],
        norm_bias[0],
    )
    final = pl.pallas_call(
        finish_kernel,
        out_shape=[
            shape(n_seq, n_rows, width, dtype=BF16),
            shape(n_seq, n_rows, width),
            shape(3, blk_rows, head_w),
            shape(2, head_w),
            shape(head_w, blk_rows),
            shape(blk_rows, ff),
            shape(1, ff),
            shape(blk_rows, ff),
            shape(2, width),
            shape(2, width),
            shape(2, width),
            shape(1, 3),
        ],
        in_specs=[smem] + [vmem] * 8,
        out_specs=[vmem] * 12,
        compiler_params=pltpu.CompilerParams(vmem_limit_bytes=60 * 2**20),
        name="finish",
    )(bucket, *results)
    out, tg, gq, qvb, go, gi, inb, gf, br, gain, shift, rms = final
    return (
        out,
        tg,
        gq[None],
        qvb[None],
        go[None],
        gi[None],
        inb,
        jnp.transpose(gf)[None],
        br[None],
        gain[None],
        shift[None],
        rms,
    )


def solution(mesh):
    placed = (
        P("batch", "blk", None),
        P("batch", "blk", None),
        P("batch"),
        P("batch", None),
        P(None, None, ("blk", "batch"), "tensor"),
        P(None, None, "tensor"),
        P(None, "tensor", ("blk", "batch")),
        P(None, ("blk", "batch"), "tensor"),
        P(None, "tensor"),
        P(None, "tensor", ("blk", "batch")),
        P(),
        P(),
        P(),
    )
    sizes = (mesh.shape["blk"], mesh.shape["batch"], mesh.shape["tensor"])
    body = fused_shards if sizes == (4, 2, 4) else general_shards
    return jax.shard_map(
        body,
        mesh=mesh,
        in_specs=placed,
        out_specs=(
            P("batch", "blk", None),
            P("batch", "blk", None),
            P(None, None, ("blk", "batch"), "tensor"),
            P(None, None, "tensor"),
            P(None, "tensor", ("blk", "batch")),
            P(None, ("blk", "batch"), "tensor"),
            P(None, "tensor"),
            P(None, "tensor", ("blk", "batch")),
            P(),
            P(),
            P(),
            P(),
        ),
        check_vma=False,
    )
```

```python
import jax
import jax.numpy as jnp
from jax import lax
from jax.experimental import pallas as pl
from jax.experimental.pallas import tpu as pltpu
from jax.sharding import PartitionSpec as P

HEAD = 64
SUB = 128


NEG = -1e30


def row_valid(bucket, lengths, pos):
    short = bucket[:, None] != 0
    pick = ((pos // SUB)[:, None] == jnp.arange(lengths.shape[1], dtype=jnp.int32)[None, :]).astype(
        jnp.int32
    )
    short_len = jnp.sum(lengths[:, None, :] * pick[None, :, :], axis=2)
    limit = jnp.where(short, short_len, lengths[:, :1])
    place = jnp.where(short, (pos % SUB)[None, :], pos[None, :])
    return place < limit


def seq_mask(bucket, lengths, qpos, kpos):
    short = bucket[:, None, None] != 0
    same = qpos[:, None] // SUB == kpos[None, :] // SUB
    allowed = jnp.logical_or(jnp.logical_not(short), same[None, :, :])
    return jnp.logical_and(row_valid(bucket, lengths, kpos)[:, None, :], allowed)


def layer_norm(h, gain, shift):
    mean = jnp.mean(h, -1, keepdims=True)
    cent = h - mean
    var = jnp.mean(cent * cent, -1, keepdims=True)
    return cent * lax.rsqrt(var + 1e-12) * gain + shift


def exact_gelu(value):
    return jax.nn.gelu(value, approximate=False)


def general_shards(
    tokens,
    out_grad,
    bucket,
    lengths,
    qkv_weight,
    qv_bias,
    out_weight,
    ff_in_weight,
    ff_in_bias,
    ff_out_weight,
    branch_bias,
    norm_gain,
    norm_bias,
):
    n_seq, rows_blk, width = tokens.shape
    blocks = lax.axis_size("blk")
    rank = lax.axis_index("blk")
    layers = qkv_weight.shape[0]
    local_width = qkv_weight.shape[3]
    heads_here = local_width // HEAD
    total_rows = n_seq * rows_blk
    scale = HEAD ** (-0.5)
    head_shape = (n_seq, rows_blk, heads_here, HEAD)
    qkv_full, out_full, ffin_full, ffout_full = (
        lax.all_gather(qkv_weight, ("blk", "batch"), axis=2, tiled=True),
        lax.all_gather(out_weight, ("blk", "batch"), axis=2, tiled=True),
        lax.all_gather(ff_in_weight, ("blk", "batch"), axis=1, tiled=True),
        lax.all_gather(ff_out_weight, ("blk", "batch"), axis=2, tiled=True),
    )
    local_pos = rank * rows_blk + jnp.arange(rows_blk, dtype=jnp.int32)
    row_ok = row_valid(bucket, lengths, local_pos).astype(jnp.float32).reshape(total_rows, 1)
    whole_pos = jnp.arange(blocks * rows_blk, dtype=jnp.int32)
    sub_bucket, sub_lengths = (bucket, lengths)

    def scores(query, keys, mask):
        found = (
            jnp.einsum("nqhe,nkhe->nhqk", query, keys, preferred_element_type=jnp.float32) * scale
        )
        return jnp.where(mask[:, None], found, NEG)

    x = tokens.astype(jnp.float32).reshape(total_rows, width)
    layer = 0
    xb = x.astype(jnp.bfloat16)
    triple = jnp.einsum("rd,cdk->crk", xb, qkv_full[layer], preferred_element_type=jnp.float32)
    query = (triple[0] + qv_bias[layer, 0]).astype(jnp.bfloat16).reshape(head_shape)
    keys = triple[1].astype(jnp.bfloat16).reshape(head_shape)
    values = (triple[2] + qv_bias[layer, 1]).astype(jnp.bfloat16).reshape(head_shape)
    pair = jnp.stack([keys, values])
    sub_query = query
    sub_pair = pair
    kept = lax.all_gather(sub_pair, "blk", axis=2, tiled=True)
    found = scores(sub_query, kept[0], seq_mask(sub_bucket, sub_lengths, local_pos, whole_pos))
    top = jnp.max(found, -1)
    sub_lse = top + jnp.log(jnp.sum(jnp.exp(found - top[..., None]), -1))
    weights = jnp.exp(found - sub_lse[..., None]).astype(jnp.bfloat16)
    sub_acc = jnp.einsum("nhqk,nkhe->nqhe", weights, kept[1], preferred_element_type=jnp.float32)
    lse = sub_lse
    acc = sub_acc
    att = acc.astype(jnp.bfloat16).reshape(total_rows, local_width)
    a_part = jnp.dot(att, out_full[layer], preferred_element_type=jnp.float32)
    branch = (
        lax.psum(a_part.astype(jnp.bfloat16), "tensor").astype(jnp.float32) + branch_bias[layer, 0]
    )
    upper_in = x + branch
    upper = layer_norm(upper_in, norm_gain[layer, 0], norm_bias[layer, 0])
    upper_b = upper.astype(jnp.bfloat16)
    pre = jnp.dot(upper_b, ffin_full[layer], preferred_element_type=jnp.float32) + ff_in_bias[layer]
    act = exact_gelu(pre).astype(jnp.bfloat16)
    f_part = jnp.dot(act, ffout_full[layer], preferred_element_type=jnp.float32)
    feed = (
        lax.psum(f_part.astype(jnp.bfloat16), "tensor").astype(jnp.float32) + branch_bias[layer, 1]
    )
    lower_in = upper + feed
    squares = [
        jnp.stack(
            [
                jnp.sum(row_ok * x * x),
                jnp.sum(row_ok * branch * branch),
                jnp.sum(row_ok * feed * feed),
            ]
        )
    ]
    saved = [(xb, query, pair, kept, lse, sub_lse, att, acc, upper_in, upper_b, pre, act, lower_in)]
    x = layer_norm(lower_in, norm_gain[layer, 1], norm_bias[layer, 1])
    output = x.astype(jnp.bfloat16).reshape(n_seq, rows_blk, width)
    grad = out_grad.astype(jnp.float32).reshape(total_rows, width)
    g_qkv, g_out, g_in, g_outf = ([], [], [], [])
    g_qvb, g_inb, g_branch, g_gain, g_shift = ([], [], [], [], [])
    for layer in reversed(range(layers)):
        xb, query, pair, kept, lse, sub_lse, att, acc, upper_in, upper_b, pre, act, lower_in = (
            saved[layer]
        )
        _, lower_back = jax.vjp(layer_norm, lower_in, norm_gain[layer, 1], norm_bias[layer, 1])
        d_lower, d_gain2, d_shift2 = lower_back(grad)
        d_feed = d_lower.astype(jnp.bfloat16)
        d_fbias = jnp.sum(d_feed.astype(jnp.float32), 0)
        g_outf.append(jnp.einsum("rf,rd->fd", act, d_feed, preferred_element_type=jnp.float32))
        d_act = jnp.einsum(
            "rd,fd->rf", d_feed, ffout_full[layer], preferred_element_type=jnp.float32
        )
        _, gelu_back = jax.vjp(exact_gelu, pre)
        d_pre = gelu_back(d_act)[0].astype(jnp.bfloat16)
        g_inb.append(jnp.sum(d_pre.astype(jnp.float32), 0))
        g_in.append(jnp.einsum("rd,rf->df", upper_b, d_pre, preferred_element_type=jnp.float32))
        ffn_part = jnp.einsum(
            "rf,df->rd", d_pre, ffin_full[layer], preferred_element_type=jnp.float32
        )
        d_upper = d_lower + lax.psum(ffn_part.astype(jnp.bfloat16), "tensor").astype(jnp.float32)
        _, upper_back = jax.vjp(layer_norm, upper_in, norm_gain[layer, 0], norm_bias[layer, 0])
        d_upper_in, d_gain1, d_shift1 = upper_back(d_upper)
        d_branch = d_upper_in.astype(jnp.bfloat16)
        d_abias = jnp.sum(d_branch.astype(jnp.float32), 0)
        g_out.append(jnp.einsum("rk,rd->kd", att, d_branch, preferred_element_type=jnp.float32))
        d_att = (
            jnp.einsum("rd,kd->rk", d_branch, out_full[layer], preferred_element_type=jnp.float32)
            .astype(jnp.bfloat16)
            .reshape(head_shape)
        )
        delta = jnp.einsum("nqhe,nqhe->nhq", d_att.astype(jnp.float32), acc)
        sub_query, sub_datt, sub_delta = (query, d_att, delta)
        block_keys = kept[0]
        block_found = scores(
            sub_query, block_keys, seq_mask(sub_bucket, sub_lengths, local_pos, whole_pos)
        )
        prob = jnp.exp(block_found - sub_lse[..., None])
        d_prob = jnp.einsum(
            "nqhe,nkhe->nhqk", sub_datt, kept[1], preferred_element_type=jnp.float32
        )
        d_scores = (prob * (d_prob - sub_delta[..., None])).astype(jnp.bfloat16)
        d_query = jnp.einsum(
            "nhqk,nkhe->nqhe", d_scores, block_keys, preferred_element_type=jnp.float32
        )
        d_keys = jnp.einsum(
            "nhqk,nqhe->nkhe", d_scores, sub_query, preferred_element_type=jnp.float32
        )
        d_values = jnp.einsum(
            "nhqk,nqhe->nkhe",
            prob.astype(jnp.bfloat16),
            sub_datt,
            preferred_element_type=jnp.float32,
        )
        sub_dq = d_query
        dpair_all = jnp.stack([d_keys * scale, d_values])
        sub_dpair = lax.psum_scatter(
            dpair_all.astype(jnp.bfloat16), "blk", scatter_dimension=2, tiled=True
        ).astype(jnp.float32)
        d_query, d_pair = (sub_dq, sub_dpair)
        dq_b = (d_query * scale).astype(jnp.bfloat16).reshape(total_rows, local_width)
        dk_b = d_pair[0].astype(jnp.bfloat16).reshape(total_rows, local_width)
        dv_b = d_pair[1].astype(jnp.bfloat16).reshape(total_rows, local_width)
        d_triple = jnp.stack([dq_b, dk_b, dv_b])
        g_qvb.append(
            jnp.stack([jnp.sum(dq_b.astype(jnp.float32), 0), jnp.sum(dv_b.astype(jnp.float32), 0)])
        )
        g_qkv.append(jnp.einsum("rd,crk->cdk", xb, d_triple, preferred_element_type=jnp.float32))
        attn_part = jnp.einsum(
            "crk,cdk->rd", d_triple, qkv_full[layer], preferred_element_type=jnp.float32
        )
        grad = d_upper_in + lax.psum(attn_part.astype(jnp.bfloat16), "tensor").astype(jnp.float32)
        g_branch.append(jnp.stack([d_abias, d_fbias]))
        g_gain.append(jnp.stack([d_gain1, d_gain2]))
        g_shift.append(jnp.stack([d_shift1, d_shift2]))

    def in_order(items):
        return jnp.stack(items[::-1])

    qkv_g, out_g, in_g, outf_g = (
        lax.psum_scatter(in_order(g_qkv), ("blk", "batch"), scatter_dimension=2, tiled=True),
        lax.psum_scatter(in_order(g_out), ("blk", "batch"), scatter_dimension=2, tiled=True),
        lax.psum_scatter(in_order(g_in), ("blk", "batch"), scatter_dimension=1, tiled=True),
        lax.psum_scatter(in_order(g_outf), ("blk", "batch"), scatter_dimension=2, tiled=True),
    )
    count = jnp.sum(row_ok)
    qvb_g, inb_g, branch_g, gain_g, shift_g, square_sums, count_all = lax.psum(
        (
            in_order(g_qvb),
            in_order(g_inb),
            in_order(g_branch),
            in_order(g_gain),
            in_order(g_shift),
            jnp.stack(squares),
            count,
        ),
        ("blk", "batch"),
    )
    rms = jnp.sqrt(square_sums / (count_all * width))
    tokens_grad = grad.reshape(n_seq, rows_blk, width)
    return (
        output,
        tokens_grad,
        qkv_g,
        qvb_g,
        out_g,
        in_g,
        inb_g,
        outf_g,
        branch_g,
        gain_g,
        shift_g,
        rms,
    )


MESH = pl.DeviceIdType.MESH
F32 = jnp.float32
BF16 = jnp.bfloat16
N_SEND = 48
N_RECV = 128


def dot_nn(a, b):
    return lax.dot_general(a, b, (((1,), (0,)), ((), ())), preferred_element_type=F32)


def dot_nt(a, b):
    return lax.dot_general(a, b, (((1,), (1,)), ((), ())), preferred_element_type=F32)


def dot_tn(a, b):
    return lax.dot_general(a, b, (((0,), (0,)), ((), ())), preferred_element_type=F32)


def slot_order(bucket_ref):
    first = jnp.where(bucket_ref[0] == 0, 0, jnp.where(bucket_ref[1] == 0, 1, 2))
    second = jnp.where(first == 0, 1, 0)
    third = jnp.where(first == 2, 1, 2)
    return first, second, third


class Net:
    def __init__(self, send_sems, recv_sems):
        self.send_sems, self.recv_sems = send_sems, recv_sems
        self.copies, self.n_recv = [], 0

    def slot(self):
        self.n_recv += 1
        assert self.n_recv <= N_RECV
        return self.n_recv - 1

    def send(self, src, dst, peer, slot=None):
        at = len(self.copies)
        if at >= N_SEND:
            self.copies[at - N_SEND].wait_send()
        copy = pltpu.make_async_remote_copy(
            src_ref=src,
            dst_ref=dst,
            send_sem=self.send_sems.at[at % N_SEND],
            recv_sem=self.recv_sems.at[self.slot() if slot is None else slot],
            device_id=peer,
            device_id_type=MESH,
        )
        copy.start()
        self.copies.append(copy)
        return copy

    def whole(self, ref, peer, slot):
        return pltpu.make_async_remote_copy(
            src_ref=ref,
            dst_ref=ref,
            send_sem=self.send_sems.at[0],
            recv_sem=self.recv_sems.at[slot],
            device_id=peer,
            device_id_type=MESH,
        )

    def finish(self):
        for copy in self.copies[-N_SEND:]:
            copy.wait_send()


class Gather:
    def __init__(self, net, view, at, near, split=False):
        self.net, self.view, self.near = net, view, near
        self.own, self.x, self.y, self.d, self.size = at
        self.half = self.size // 2
        self.slot = net.slot()
        self.late = net.slot() if split else self.slot

    def part(self, start, size):
        return self.view(pl.ds(pl.multiple_of(start, 16), size))

    def to_core(self, ref, late=False):
        self.net.send(ref, ref, self.near[2], self.late if late else self.slot)

    def issue(self, src=None):
        xnb, ynb, core = self.near
        to = self.part(self.own, self.size)
        src = to if src is None else src
        self.from_x = self.net.send(src, to, xnb)
        self.from_y = self.net.send(src, to, ynb)
        self.net.send(src, to, core, self.slot)

    def forward_x(self):
        xnb, ynb, core = self.near
        self.from_x.wait_recv()
        ref = self.part(self.x, self.half)
        self.first = self.net.send(ref, ref, ynb)
        self.to_core(self.part(self.x, self.size))

    def forward_y(self):
        xnb, ynb, core = self.near
        self.from_y.wait_recv()
        ref = self.part(self.y + self.half, self.half)
        self.second = self.net.send(ref, ref, xnb)
        self.to_core(self.part(self.y, self.size), True)

    def last(self):
        self.first.wait_recv()
        self.second.wait_recv()
        self.to_core(self.part(self.d, self.size), True)

    def ready(self):
        self.net.whole(self.part(0, 4 * self.size), self.near[2], self.slot).wait_recv()

    def ready_half(self, late):
        slot = self.late if late else self.slot
        self.net.whole(self.part(0, 2 * self.size), self.near[2], slot).wait_recv()


class Scatter:
    def __init__(self, net, refs, spot, near):
        self.net, self.spot, self.near = net, spot, near
        self.g, self.d, self.h, self.p1, self.s, self.p2 = refs
        self.rows = self.g.shape[3]
        self.half = self.rows // 2

    def core(self):
        c = self.spot[1]
        self.c1 = self.net.send(self.g.at[:, 1 - c], self.d, self.near[2])

    def first(self):
        yy, c, t = self.spot
        xnb, ynb, _ = self.near
        lo, hi = pl.ds(0, self.half), pl.ds(self.half, self.half)
        self.c1.wait_recv()
        for a in range(2):
            for b in range(2):
                self.h[a, b] = (self.g[a, c, b].astype(F32) + self.d[a, b].astype(F32)).astype(BF16)
        self.px = self.net.send(self.h.at[:, 1 - t, lo], self.p1.at[0], xnb)
        self.py = self.net.send(self.h.at[1 - yy, :, hi], self.p1.at[1], ynb)

    def second_x(self):
        yy, c, t = self.spot
        xnb, ynb, _ = self.near
        lo = pl.ds(0, self.half)
        self.px.wait_recv()
        self.s[0] = (self.h[1 - yy, t, lo].astype(F32) + self.p1[0, 1 - yy].astype(F32)).astype(BF16)
        self.qy = self.net.send(self.s.at[0], self.p2.at[0], ynb)

    def second_y(self):
        yy, c, t = self.spot
        xnb, ynb, _ = self.near
        hi = pl.ds(self.half, self.half)
        self.py.wait_recv()
        self.s[1] = (self.h[yy, 1 - t, hi].astype(F32) + self.p1[1, 1 - t].astype(F32)).astype(BF16)
        self.qx = self.net.send(self.s.at[1], self.p2.at[1], xnb)

    def result(self):
        yy, c, t = self.spot
        self.qy.wait_recv()
        self.qx.wait_recv()
        lo, hi = pl.ds(0, self.half), pl.ds(self.half, self.half)
        low = self.h[yy, t, lo].astype(F32) + self.p1[0, yy].astype(F32) + self.p2[0].astype(F32)
        high = self.h[yy, t, hi].astype(F32) + self.p1[1, t].astype(F32) + self.p2[1].astype(F32)
        return low, high


def fused_kernel(*refs):
    (
        bucket, lengths, tokens, out_grad, qkv_w, out_w, ffi_w, ffo_w, qv_bias, ffi_b, br_bias, gain, shift,
        out_hbm, tg_hbm, gq_hbm, go_hbm, gi_hbm, gf_hbm, vec_hbm, qvb_hbm,
        tok, cot, w_q, w_o, w_i, w_f, own_o, bias_r, own_q, xs, xs_t, q_r, kv_r, kv_a, p_a, p_b,
        att, att_r, ps, pr, xh1, rstd1, yb, act, gp, dh2, dfb, dab, df_t, yb_t, dpre, dh1, da_t,
        datt, datt_s, dkv_s, dkv_c, dkv_t, dkv_y, dtri, dx_p, dx_s, dx_1, dx_2, dx_t,
        sc_q, sc_o, sc_i, sc_f, z_o, z_i, z_f, t_o, t_i, t_f, vs, vr, vz, qs, qr,
        out_v, tg_v, gq_v, go_v, gi_v, gf_v, vec_v, qvb_v,
        local_sems, send_sems, recv_sems,
    ) = refs
    n_seq, n_rows, width = tok.shape
    blk_rows = ffi_w.shape[0]
    head_w = qkv_w.shape[2]
    pair_w = 2 * head_w
    heads = head_w // HEAD
    half, quart = n_rows // 2, n_rows // 4
    tile = 256
    n_tile = width // tile
    scale = HEAD ** (-0.5)

    r = lax.axis_index("blk")
    t = lax.axis_index("batch")
    z = lax.axis_index("tensor")
    yy, c = r // 2, r % 2
    pz, qz = z // 2, z % 2
    r1, r2 = r + 1 - 2 * c, (r + 2) % 4
    z1, z2 = z + 1 - 2 * qz, (z + 2) % 4
    core, xnb, ynb = (r1, t, z), (r, 1 - t, z), (r2, t, z)
    zn1, zn2 = (r, t, z1), (r, t, z2)
    peers = (zn2, zn1, xnb, ynb, core)
    near = (xnb, ynb, core)

    barrier = pltpu.get_barrier_semaphore()
    for peer in peers:
        pl.semaphore_signal(barrier, inc=1, device_id=peer, device_id_type=MESH)

    net = Net(send_sems, recv_sems)

    def block(rr, tt):
        return (rr * 2 + tt) * blk_rows

    at = (block(r, t), block(r, 1 - t), block(r2, t), block(r2, 1 - t), blk_rows)
    own = pl.ds(pl.multiple_of(block(r, t), 32), blk_rows)

    def gather(view, split=False):
        return Gather(net, view, at, near, split)

    ga_q = gather(lambda rows: w_q.at[rows])
    ga_o = [gather(lambda rows, k=k: w_o.at[k, rows]) for k in range(2)]
    ga_i = [gather(lambda rows, k=k: w_i.at[k, rows]) for k in range(2)]
    ga_f = [gather(lambda rows, k=k: w_f.at[k, rows], True) for k in range(2)]

    local = [
        pltpu.make_async_copy(src, dst, local_sems.at[k])
        for k, (src, dst) in enumerate(
            (
                (out_w, own_o),
                (tokens, tok),
                (qkv_w, own_q),
                (ffi_w, w_i.at[0, own]),
                (ffo_w, w_f.at[0, own]),
                (out_grad, cot),
            )
        )
    ]
    for copy in local:
        copy.start()
    stores = []

    def store(src, dst):
        copy = pltpu.make_async_copy(src, dst, local_sems.at[len(local) + len(stores)])
        copy.start()
        stores.append(copy)

    st = {}

    order = slot_order(bucket)

    def weights_first():
        local[0].wait()
        w_o[0, own] = jnp.transpose(own_o[...])
        local[2].wait()
        w_q[own] = jnp.concatenate([own_q[1], own_q[2], own_q[0]], 1)
        local[1].wait()
        for s in range(n_seq):
            xs[s * n_rows : (s + 1) * n_rows] = tok[order[s]]

    def enter():
        pl.semaphore_wait(barrier, len(peers))

    def far_weight(kind, src, buf):
        st["z" + kind] = net.send(src, buf.at[1, own], zn2)
        if kind == "i":
            st["zb"] = net.send(ffi_b, bias_r, zn2)

    def issue_second(kind, gather):
        st["z" + kind].wait_recv()
        gather.issue()

    def turn_x():
        xs_t[...] = jnp.transpose(xs[...])

    def keys_of(rr):
        return kv_a.at[pl.ds(pl.multiple_of(rr * n_rows, n_rows), n_rows)]

    def keys_values():
        ga_q.ready()
        bias = jnp.concatenate([jnp.zeros((1, head_w), F32), qv_bias[1:2, :]], 1)
        kv_r[...] = (dot_nn(xs[...], w_q[:, 0:pair_w]) + bias).astype(BF16)
        kv_a[pl.ds(pl.multiple_of(r * n_rows, n_rows), n_rows)] = kv_r[0:n_rows]
        st["kv_y"] = net.send(keys_of(r), keys_of(r), ynb)
        st["kv_c"] = [net.send(keys_of(r), keys_of(r), core)]

    def keys_pass():
        st["kv_y"].wait_recv()
        st["kv_c"].append(net.send(keys_of(r2), keys_of(r2), core))

    def queries():
        q_r[...] = (dot_nn(xs[...], w_q[:, pair_w:]) + qv_bias[0:1, :]).astype(BF16)

    lane_head = lax.broadcasted_iota(jnp.int32, (1, head_w), 1) // HEAD

    def of_head(value, h):
        return jnp.where(lane_head == h, value, jnp.zeros_like(value))

    def limit_of(s):
        index = order[s]
        return lengths[index, r], lengths[index, 0]

    own_half = pl.ds(pl.multiple_of(pz * half, half), half)
    other_half = pl.ds(pl.multiple_of((1 - pz) * half, half), half)
    key_at = lax.broadcasted_iota(jnp.int32, (1, n_rows), 1)

    def rows_at(s):
        return slice(s * n_rows, (s + 1) * n_rows)

    def few_at(s):
        return slice(s * half, (s + 1) * half)

    def attend(s):
        if s == 0:
            for copy in st["kv_c"]:
                copy.wait_recv()
            both, probs, key_ok = kv_a[...], p_a, None
        else:
            both, probs = kv_r[rows_at(s)], p_b.at[s - 1]
            key_ok = key_at < limit_of(s)[0]
        keys, values = both[:, 0:head_w], both[:, head_w:pair_w]
        query = q_r[rows_at(s)]
        total = jnp.zeros((n_rows, head_w), F32)
        for h in range(heads):
            score = dot_nt(of_head(query, h), keys) * scale
            if key_ok is not None:
                score = jnp.where(key_ok, score, NEG)
            e = jnp.exp(score - jnp.max(score, -1, keepdims=True))
            prob = e / jnp.sum(e, -1, keepdims=True)
            probs[h] = prob
            total = total + dot_nn(prob.astype(BF16), of_head(values, h))
        att[s] = total.astype(BF16)
        st["att", s] = net.send(att.at[s, other_half], att_r.at[s], zn2)

    def pair_send(k, s, value):
        ps[k, s] = value.astype(BF16)
        st["pair", k, s] = net.send(ps.at[k, s], pr.at[k, s], zn1)

    def pair_sum(k, s):
        st["pair", k, s].wait_recv()
        return ps[k, s].astype(F32) + pr[k, s].astype(F32)

    def ready(kind, gathers):
        if ("ready", kind) not in st:
            st["ready", kind] = True
            for gather in gathers:
                gather.ready()

    def project(s):
        ready("o", ga_o)
        st["att", s].wait_recv()
        pair_send(0, s, dot_nt(att[s, own_half], w_o[0]) + dot_nt(att_r[s], w_o[1]))

    vec = {k: jnp.zeros((1, width), F32) for k in range(12)}
    row_at = lax.broadcasted_iota(jnp.int32, (half, 1), 0)

    def row_ok(s):
        short, full = limit_of(s)
        place = row_at + pz * half
        ok = place + r * n_rows < full if s == 0 else place < short
        return ok.astype(F32)

    def tally(k, value):
        vec[k] = vec[k] + jnp.sum(value, 0, keepdims=True)

    def mean_of(value):
        return jnp.mean(value, -1, keepdims=True)

    def normed(h):
        cent = h - mean_of(h)
        rstd = lax.rsqrt(mean_of(cent * cent) + 1e-12)
        return cent * rstd, rstd

    def first_norm(s):
        here = few_at(s)
        x = xs[pl.ds(pl.multiple_of(s * n_rows + pz * half, half), half)].astype(F32)
        branch = pair_sum(0, s) + br_bias[0:1, :]
        ok = row_ok(s)
        tally(8, ok * (x * x))
        tally(9, ok * (branch * branch))
        tally(11, ok * jnp.ones((1, width), F32))
        hat, rstd = normed(x + branch)
        xh1[here] = hat
        rstd1[here] = rstd
        yb[here] = (hat * gain[0:1, :] + shift[0:1, :]).astype(BF16)

    def turn_y():
        yb_t[...] = jnp.transpose(yb[...])

    def hidden(s):
        if ("ready", "i") not in st:
            st["zb"].wait_recv()
            local[3].wait()
        ready("i", ga_i)
        here = few_at(s)
        for k in range(2):
            for n in range(n_tile):
                cols = slice(n * tile, (n + 1) * tile)
                bias = ffi_b[:, cols] if k == 0 else bias_r[:, cols]
                pre = dot_nn(yb[here], w_i[k, :, cols]) + bias
                phi = 0.5 * (1.0 + lax.erf(pre * (0.5**0.5)))
                act[k, here, cols] = (pre * phi).astype(BF16)
                gp[k, here, cols] = phi + pre * (jnp.exp(-0.5 * pre * pre) * 0.3989422804014327)

    def feed_out(late, s):
        if ("feed", late) not in st:
            st["feed", late] = True
            if not late:
                local[4].wait()
            for gather in ga_f:
                gather.ready_half(late)
        here = few_at(s)
        side = width // 2
        cols = pl.ds(pl.multiple_of(((1 - yy) if late else yy) * side, 128), side)
        value = dot_nt(act[0, here], w_f[0, cols]) + dot_nt(act[1, here], w_f[1, cols])
        ps[1, s, :, cols] = value.astype(BF16)
        st["feed", late, s] = net.send(ps.at[1, s, :, cols], pr.at[1, s, :, cols], zn1)

    def second_norm(s):
        here = few_at(s)
        if "cot" not in st:
            st["cot"] = True
            local[5].wait()
        for late in range(2):
            st["feed", late, s].wait_recv()
        feed = ps[1, s].astype(F32) + pr[1, s].astype(F32) + br_bias[1:2, :]
        tally(10, row_ok(s) * (feed * feed))
        hat, rstd = normed(xh1[here] * gain[0:1, :] + shift[0:1, :] + feed)
        out_v[s, own_half] = (hat * gain[1:2, :] + shift[1:2, :]).astype(BF16)
        g = cot[order[s], own_half].astype(F32)
        tally(1, g * hat)
        tally(2, g)
        g = g * gain[1:2, :]
        d = rstd * (g - mean_of(g) - hat * mean_of(g * hat))
        dh2[here] = d
        d = d.astype(BF16)
        dfb[here] = d
        tally(0, d.astype(F32))

    def feed_back(s):
        here = few_at(s)
        d = dfb[here]
        total = jnp.zeros((half, width), F32)
        for k in range(2):
            p = (dot_nn(d, w_f[k]) * gp[k, here]).astype(BF16)
            dpre[k, here] = p
            tally(3 + k, p.astype(F32))
            total = total + dot_nt(p, w_i[k])
        pair_send(2, s, total)

    quarter = pl.ds(pl.multiple_of(z * quart, quart), quart)
    quarter_2 = pl.ds(pl.multiple_of(z2 * quart, quart), quart)

    def out_far(s):
        here = out_v.at[s, quarter]
        st["out2", s] = net.send(here, here, zn2)

    def out_near(s):
        st["out2", s].wait_recv()
        there = out_v.at[s, quarter_2]
        st["out1", s] = net.send(there, there, zn1)

    def scatter(refs, k=None):
        views = refs if k is None else [ref.at[k] for ref in refs]
        return Scatter(net, views, (yy, c, t), near)

    rs_f = [scatter(sc_f, k) for k in range(2)]
    rs_i = [scatter(sc_i, k) for k in range(2)]
    rs_o = [scatter(sc_o, k) for k in range(2)]
    rs_q = scatter(sc_q)

    def grads(lhs, rhs, out):
        value = dot_nn(lhs, rhs).astype(BF16)
        for b in range(8):
            piece = value[b * blk_rows : (b + 1) * blk_rows]
            out[b // 4, (b // 2) % 2, b % 2] = piece

    def grads_wide(left, right, rs):
        for n in range(n_tile):
            cols = slice(n * tile, (n + 1) * tile)
            grads(left[...], right[:, cols], rs.g.at[:, :, :, :, cols])
        rs.core()

    def turn_d():
        df_t[...] = jnp.transpose(dfb[...])

    def grad_f(k):
        grads_wide(df_t, act.at[k], rs_f[k])

    def grad_i(k):
        grads_wide(yb_t, dpre.at[k], rs_i[k])

    def grad_o():
        da_t[...] = jnp.transpose(dab[...])
        rows_l = jnp.concatenate([att[s, own_half] for s in range(n_seq)], 0)
        rows_r = jnp.concatenate([att_r[s] for s in range(n_seq)], 0)
        grads(da_t[...], rows_r, rs_o[1].g)
        rs_o[1].core()
        grads(da_t[...], rows_l, rs_o[0].g)
        rs_o[0].core()

    def grad_q():
        grads(xs_t[...], dtri[...], rs_q.g)
        rs_q.core()

    def first_norm_back(s):
        here = few_at(s)
        hat = xh1[here]
        g = dh2[here] + pair_sum(2, s)
        tally(6, g * hat)
        tally(7, g)
        g = g * gain[0:1, :]
        d = rstd1[here] * (g - mean_of(g) - hat * mean_of(g * hat))
        dh1[here] = d
        d = d.astype(BF16)
        dab[here] = d
        tally(5, d.astype(F32))
        datt_s[s] = dot_nn(d, w_o[1]).astype(BF16)
        st["datt", s] = net.send(datt_s.at[s], datt.at[s, own_half], zn2)
        datt[s, own_half] = dot_nn(d, w_o[0]).astype(BF16)

    def vec_step(k):
        if k == 0:
            for n in range(12):
                vs[0, n : n + 1] = vec[n]
            vs[0, 12:16] = jnp.zeros((4, width), F32)
        else:
            st["vec"].wait_recv()
            vs[k] = vs[k - 1] + vr[k - 1]
        if k < 3:
            st["vec"] = net.send(vs.at[k], vr.at[k], (core, xnb, ynb)[k])
            return
        lane = lax.broadcasted_iota(jnp.int32, (1, width), 1)
        last = jnp.zeros((1, width), F32)
        for n in range(4):
            last = jnp.where(lane == n, jnp.sum(vs[3, 8 + n : 9 + n], 1, keepdims=True), last)
        vz[0, 0:3] = vs[3, 0:3]
        vz[0, 3:4] = vs[3, 4:5]
        vz[0, 4:7] = vs[3, 5:8]
        vz[0, 7:8] = last
        st["vec"] = net.send(vz.at[0], vz.at[1], zn2)

    def attend_back(s):
        st["datt", s].wait_recv()
        if s == 0:
            both, probs = kv_a[...], p_a
        else:
            both, probs = kv_r[rows_at(s)], p_b.at[s - 1]
        keys, values = both[:, 0:head_w], both[:, head_w:pair_w]
        query = q_r[rows_at(s)]
        d_att = datt[s]
        dq = jnp.zeros((n_rows, head_w), F32)
        dk = jnp.zeros(keys.shape, F32)
        dv = jnp.zeros(keys.shape, F32)
        for h in range(heads):
            prob = probs[h]
            d_h = of_head(d_att, h)
            dp = dot_nt(d_h, values)
            delta = jnp.sum(prob * dp, -1, keepdims=True)
            ds = (prob * (dp - delta)).astype(BF16)
            dq = dq + dot_nn(ds, of_head(keys, h))
            dk = dk + dot_tn(ds, of_head(query, h))
            dv = dv + dot_tn(prob.astype(BF16), d_h)
        dtri[rows_at(s), pair_w:] = (dq * scale).astype(BF16)
        both = jnp.concatenate([(dk * scale).astype(BF16), dv.astype(BF16)], 1)
        if s == 0:
            for a in range(4):
                dkv_s[a // 2, a % 2] = both[rows_at(a)]
            st["dkv1"] = net.send(dkv_s.at[:, 1 - c], dkv_c, core)
        else:
            dtri[rows_at(s), 0:pair_w] = both

    def keys_back():
        st["dkv1"].wait_recv()
        dkv_t[...] = (dkv_s[1 - yy, c].astype(F32) + dkv_c[1 - yy].astype(F32)).astype(BF16)
        st["dkv2"] = net.send(dkv_t, dkv_y, ynb)

    def dx_of(s):
        total = dot_nt(dtri[rows_at(s)], w_q[...])
        dx_p[s] = total
        for a in range(4):
            dx_s[a // 2, a % 2, s] = total[a * quart : (a + 1) * quart].astype(BF16)

    def half_rows(s):
        return pl.ds(pl.multiple_of(s * half + qz * quart, quart), quart)

    groups = {"b": (1, n_seq), "a": (0, 1)}

    def dx_first(group):
        lo, hi = groups[group]
        if group == "a":
            st["dkv2"].wait_recv()
            total = dkv_s[yy, c].astype(F32) + dkv_c[yy].astype(F32) + dkv_y[...].astype(F32)
            dtri[0:n_rows, 0:pair_w] = total.astype(BF16)
        for s in range(lo, hi):
            dx_of(s)
        st[group, 1] = net.send(dx_s.at[:, 1 - qz, lo:hi], dx_1.at[:, lo:hi], zn1)

    def dx_second(group):
        lo, hi = groups[group]
        st[group, 1].wait_recv()
        for s in range(lo, hi):
            dx_t[s] = (dx_p[s, quarter_2] + dx_1[1 - pz, s].astype(F32)).astype(BF16)
        st[group, 2] = net.send(dx_t.at[lo:hi], dx_2.at[lo:hi], zn2)

    def dx_third(group):
        lo, hi = groups[group]
        st[group, 2].wait_recv()
        for s in range(lo, hi):
            total = dx_p[s, quarter] + dx_1[pz, s].astype(F32) + dx_2[s].astype(F32)
            tg_v[s, quarter] = (total + dh1[half_rows(s)]).astype(BF16)
        here = tg_v.at[lo:hi, quarter]
        st[group, 3], st[group, 4] = net.send(here, here, zn2), net.send(here, here, zn1)

    def dx_last(group):
        lo, hi = groups[group]
        st[group, 3].wait_recv()
        there = tg_v.at[lo:hi, quarter_2]
        st[group, 5] = net.send(there, there, zn1)

    def bias_step(k):
        if k == 0:
            qs[0] = jnp.zeros(qs.shape[1:], F32)
            total = jnp.sum(dtri[...].astype(F32), 0, keepdims=True)
            qs[0, 0:1] = total[:, pair_w:]
            qs[0, 1:2] = total[:, head_w:pair_w]
        else:
            st["bias"].wait_recv()
            qs[k] = qs[k - 1] + qr[k - 1]
        st["bias"] = net.send(qs.at[k], qr.at[k], (core, xnb, ynb)[k])

    def to_z(kind, rs, buf, got):
        low, high = rs.result()
        n = low.shape[0]
        buf[0:n] = low.astype(BF16)
        buf[n : 2 * n] = high.astype(BF16)
        st["g" + kind] = net.send(buf, got, zn2)

    def put(kind, rs, out, to, got=None):
        low, high = rs.result()
        n = low.shape[0]
        if got is not None:
            st["g" + kind].wait_recv()
            low = low + got[0:n].astype(F32)
            high = high + got[n : 2 * n].astype(F32)
        out[0:n] = low
        out[n : 2 * n] = high
        store(out, to)

    def out_store():
        for s in range(n_seq):
            st["out1", s].wait_recv()
        store(out_v, out_hbm)

    def vec_store():
        st["vec"].wait_recv()
        vec_v[...] = vz[0] + vz[1]
        vec_v[3:4] = vs[3, 3:4] + vz[1, 3:4]
        store(vec_v, vec_hbm)

    def bias_store():
        st["bias"].wait_recv()
        qvb_v[...] = qs[2] + qr[2]
        store(qvb_v, qvb_hbm)

    def dx_store():
        for group in groups:
            for k in (4, 5):
                st[group, k].wait_recv()
        store(tg_v, tg_hbm)

    weights_first()
    enter()
    ga_o[0].issue()
    far_weight("o", w_o.at[0, own], w_o)
    far_weight("f", ffo_w, w_f)
    ga_q.issue()
    ga_i[0].issue(ffi_w)
    ga_o[0].forward_y()
    ga_o[0].forward_x()
    ga_q.forward_y()
    ga_q.forward_x()
    issue_second("o", ga_o[1])
    far_weight("i", ffi_w, w_i)
    ga_i[0].forward_x()
    ga_i[0].forward_y()
    ga_o[0].last()
    ga_f[0].issue(ffo_w)
    ga_o[1].forward_x()
    ga_q.last()
    ga_o[1].forward_y()
    keys_values()
    queries()
    issue_second("i", ga_i[1])
    attend(1)
    issue_second("f", ga_f[1])
    attend(2)
    ga_o[1].last()
    keys_pass()
    attend(0)
    project(1)
    project(2)
    ga_i[1].forward_x()
    ga_f[0].forward_x()
    ga_i[0].last()
    ga_i[1].forward_y()
    ga_f[0].forward_y()
    ga_f[1].forward_x()
    ga_f[1].forward_y()
    project(0)
    ga_i[1].last()
    first_norm(1)
    hidden(1)
    feed_out(0, 1)
    first_norm(2)
    hidden(2)
    ga_f[0].last()
    feed_out(0, 2)
    ga_f[1].last()
    feed_out(1, 1)
    feed_out(1, 2)
    first_norm(0)
    hidden(0)
    turn_y()
    feed_out(0, 0)
    feed_out(1, 0)
    second_norm(1)
    feed_back(1)
    second_norm(2)
    out_far(2)
    feed_back(2)
    turn_x()
    second_norm(0)
    turn_d()
    grad_f(1)
    feed_back(0)
    grad_i(1)
    rs_f[1].first()
    out_far(0)
    grad_i(0)
    first_norm_back(1)
    rs_i[1].first()
    grad_f(0)
    first_norm_back(2)
    first_norm_back(0)
    grad_o()
    rs_f[1].second_y()
    out_near(0)
    out_far(1)
    vec_step(0)
    rs_f[1].second_x()
    attend_back(1)
    attend_back(2)
    dx_first("b")
    vec_step(1)
    attend_back(0)
    to_z("f", rs_f[1], t_f, z_f)
    keys_back()
    vec_step(2)
    rs_o[1].first()
    rs_f[0].first()
    rs_i[1].second_x()
    dx_first("a")
    dx_second("b")
    grad_q()
    rs_o[0].first()
    rs_o[1].second_x()
    vec_step(3)
    rs_q.first()
    out_near(2)
    rs_i[1].second_y()
    dx_second("a")
    dx_third("b")
    out_near(1)
    rs_i[0].first()
    rs_q.second_x()
    dx_third("a")
    rs_o[0].second_y()
    rs_o[0].second_x()
    rs_q.second_y()
    bias_step(0)
    bias_step(1)
    vec_store()
    rs_o[1].second_y()
    rs_f[0].second_x()
    to_z("i", rs_i[1], t_i, z_i)
    dx_last("b")
    dx_last("a")
    bias_step(2)
    rs_f[0].second_y()
    to_z("o", rs_o[1], t_o, z_o)
    rs_i[0].second_y()
    rs_i[0].second_x()
    put("q", rs_q, gq_v, gq_hbm)
    bias_store()
    out_store()
    put("f", rs_f[0], gf_v, gf_hbm, z_f)
    dx_store()
    put("i", rs_i[0], gi_v, gi_hbm, z_i)
    put("o", rs_o[0], go_v, go_hbm, z_o)

    for copy in stores:
        copy.wait()
    net.finish()


def finish_kernel(
    bucket,
    out_i,
    tg_i,
    gq_i,
    go_i,
    gi_i,
    gf_i,
    vec_i,
    qvb_i,
    out_o,
    tg_o,
    gq_o,
    qvb_o,
    go_o,
    gi_o,
    inb_o,
    gf_o,
    br_o,
    gain_o,
    shift_o,
    rms_o,
):
    order = slot_order(bucket)
    for s in range(3):
        at = jnp.where(order[0] == s, 0, jnp.where(order[1] == s, 1, 2))
        out_o[s] = out_i[at]
        tg_o[s] = tg_i[at].astype(F32)
    n = gq_o.shape[2]
    value = gq_i[...]
    for k, part in enumerate((1, 2, 0)):
        gq_o[part] = value[:, k * n : (k + 1) * n]
    go_o[...] = jnp.transpose(go_i[...])
    gi_o[...] = gi_i[...]
    gf_o[...] = gf_i[...]
    qvb_o[...] = qvb_i[0:2]
    inb_o[...] = vec_i[3:4]
    br_o[0:1] = vec_i[4:5]
    br_o[1:2] = vec_i[0:1]
    gain_o[0:1] = vec_i[5:6]
    gain_o[1:2] = vec_i[1:2]
    shift_o[0:1] = vec_i[6:7]
    shift_o[1:2] = vec_i[2:3]
    rms_o[...] = jnp.sqrt(vec_i[7:8, 0:3] / vec_i[7:8, 3:4])


def fused_shards(
    tokens,
    out_grad,
    bucket,
    lengths,
    qkv_weight,
    qv_bias,
    out_weight,
    ff_in_weight,
    ff_in_bias,
    ff_out_weight,
    branch_bias,
    norm_gain,
    norm_bias,
):
    n_seq, n_rows, width = tokens.shape
    blk_rows, head_w = qkv_weight.shape[2:]
    ff = ff_in_weight.shape[2]
    heads = head_w // HEAD
    rows = n_seq * n_rows
    half, quart = n_rows // 2, n_rows // 4
    few = n_seq * half
    keys = 4 * n_rows
    vmem = pl.BlockSpec(memory_space=pltpu.VMEM)
    smem = pl.BlockSpec(memory_space=pltpu.SMEM)
    hbm = pl.BlockSpec(memory_space=pl.ANY)

    def v(*shape, dtype=BF16):
        return pltpu.VMEM(shape, dtype)

    def f(*shape):
        return pltpu.VMEM(shape, F32)

    wide = {"q": (blk_rows, 3 * head_w), "o": (blk_rows, head_w), "i": (blk_rows, ff), "f": (blk_rows, ff)}

    def scatter_bufs(kind):
        n, cols = wide[kind]
        lead = () if kind == "q" else (2,)
        dims = ((2, 2, 2, n), (2, 2, n), (2, 2, n), (2, 2, n // 2), (2, n // 2), (2, n // 2))
        return [v(*lead, *dim, cols) for dim in dims]

    scratch = [
        v(n_seq, n_rows, width),
        v(n_seq, n_rows, width),
        v(width, 3 * head_w),
        v(2, width, head_w),
        v(2, width, ff),
        v(2, width, ff),
        v(head_w, blk_rows),
        f(1, ff),
        v(3, blk_rows, head_w),
        v(rows, width),
        v(width, rows),
        v(rows, head_w),
        v(rows, 2 * head_w),
        v(keys, 2 * head_w),
        f(heads, n_rows, keys),
        f(n_seq - 1, heads, n_rows, n_rows),
        v(n_seq, n_rows, head_w),
        v(n_seq, half, head_w),
        v(3, n_seq, half, width),
        v(3, n_seq, half, width),
        f(few, width),
        f(few, 1),
        v(few, width),
        v(2, few, ff),
        f(2, few, ff),
        f(few, width),
        v(few, width),
        v(few, width),
        v(width, few),
        v(width, few),
        v(2, few, ff),
        f(few, width),
        v(width, few),
        v(n_seq, n_rows, head_w),
        v(n_seq, half, head_w),
        v(2, 2, n_rows, 2 * head_w),
        v(2, n_rows, 2 * head_w),
        v(n_rows, 2 * head_w),
        v(n_rows, 2 * head_w),
        v(rows, 3 * head_w),
        f(n_seq, n_rows, width),
        v(2, 2, n_seq, quart, width),
        v(2, n_seq, quart, width),
        v(n_seq, quart, width),
        v(n_seq, quart, width),
        scatter_bufs("q"),
        scatter_bufs("o"),
        scatter_bufs("i"),
        scatter_bufs("f"),
        v(*wide["o"]),
        v(*wide["i"]),
        v(*wide["f"]),
        v(*wide["o"]),
        v(*wide["i"]),
        v(*wide["f"]),
        f(4, 16, width),
        f(3, 16, width),
        f(2, 8, width),
        f(3, 8, head_w),
        f(3, 8, head_w),
        v(n_seq, n_rows, width),
        v(n_seq, n_rows, width),
        f(*wide["q"]),
        f(*wide["o"]),
        f(*wide["i"]),
        f(*wide["f"]),
        f(8, width),
        f(8, head_w),
        pltpu.SemaphoreType.DMA((14,)),
        pltpu.SemaphoreType.DMA((N_SEND,)),
        pltpu.SemaphoreType.DMA((N_RECV,)),
    ]

    def shape(*dims, dtype=F32):
        return jax.ShapeDtypeStruct(dims, dtype)

    main_out = [
        shape(n_seq, n_rows, width, dtype=BF16),
        shape(n_seq, n_rows, width, dtype=BF16),
        shape(*wide["q"]),
        shape(*wide["o"]),
        shape(*wide["i"]),
        shape(*wide["f"]),
        shape(8, width),
        shape(8, head_w),
    ]
    results = pl.pallas_call(
        fused_kernel,
        out_shape=main_out,
        in_specs=[smem, smem] + [hbm] * 6 + [vmem] * 5,
        out_specs=[hbm] * 8,
        scratch_shapes=scratch,
        compiler_params=pltpu.CompilerParams(
            collective_id=0, has_side_effects=True, vmem_limit_bytes=60 * 2**20
        ),
        name="encoder_layer",
    )(
        bucket,
        lengths,
        tokens,
        out_grad,
        qkv_weight[0],
        out_weight[0],
        ff_in_weight[0],
        jnp.transpose(ff_out_weight[0]),
        qv_bias[0],
        ff_in_bias,
        branch_bias[0],
        norm_gain[0],
        norm_bias[0],
    )
    final = pl.pallas_call(
        finish_kernel,
        out_shape=[
            shape(n_seq, n_rows, width, dtype=BF16),
            shape(n_seq, n_rows, width),
            shape(3, blk_rows, head_w),
            shape(2, head_w),
            shape(head_w, blk_rows),
            shape(blk_rows, ff),
            shape(1, ff),
            shape(blk_rows, ff),
            shape(2, width),
            shape(2, width),
            shape(2, width),
            shape(1, 3),
        ],
        in_specs=[smem] + [vmem] * 8,
        out_specs=[vmem] * 12,
        compiler_params=pltpu.CompilerParams(vmem_limit_bytes=60 * 2**20),
        name="finish",
    )(bucket, *results)
    out, tg, gq, qvb, go, gi, inb, gf, br, gain, shift, rms = final
    return (
        out,
        tg,
        gq[None],
        qvb[None],
        go[None],
        gi[None],
        inb,
        jnp.transpose(gf)[None],
        br[None],
        gain[None],
        shift[None],
        rms,
    )


def solution(mesh):
    placed = (
        P("batch", "blk", None),
        P("batch", "blk", None),
        P("batch"),
        P("batch", None),
        P(None, None, ("blk", "batch"), "tensor"),
        P(None, None, "tensor"),
        P(None, "tensor", ("blk", "batch")),
        P(None, ("blk", "batch"), "tensor"),
        P(None, "tensor"),
        P(None, "tensor", ("blk", "batch")),
        P(),
        P(),
        P(),
    )
    sizes = (mesh.shape["blk"], mesh.shape["batch"], mesh.shape["tensor"])
    body = fused_shards if sizes == (4, 2, 4) else general_shards
    return jax.shard_map(
        body,
        mesh=mesh,
        in_specs=placed,
        out_specs=(
            P("batch", "blk", None),
            P("batch", "blk", None),
            P(None, None, ("blk", "batch"), "tensor"),
            P(None, None, "tensor"),
            P(None, "tensor", ("blk", "batch")),
            P(None, ("blk", "batch"), "tensor"),
            P(None, "tensor"),
            P(None, "tensor", ("blk", "batch")),
            P(),
            P(),
            P(),
            P(),
        ),
        check_vma=False,
    )
```

```python
import jax
import jax.numpy as jnp
from jax import lax
from jax.experimental import pallas as pl
from jax.experimental.pallas import tpu as pltpu
from jax.sharding import PartitionSpec as P

HEAD = 64
SUB = 128


NEG = -1e30


def row_valid(bucket, lengths, pos):
    short = bucket[:, None] != 0
    pick = ((pos // SUB)[:, None] == jnp.arange(lengths.shape[1], dtype=jnp.int32)[None, :]).astype(
        jnp.int32
    )
    short_len = jnp.sum(lengths[:, None, :] * pick[None, :, :], axis=2)
    limit = jnp.where(short, short_len, lengths[:, :1])
    place = jnp.where(short, (pos % SUB)[None, :], pos[None, :])
    return place < limit


def seq_mask(bucket, lengths, qpos, kpos):
    short = bucket[:, None, None] != 0
    same = qpos[:, None] // SUB == kpos[None, :] // SUB
    allowed = jnp.logical_or(jnp.logical_not(short), same[None, :, :])
    return jnp.logical_and(row_valid(bucket, lengths, kpos)[:, None, :], allowed)


def layer_norm(h, gain, shift):
    mean = jnp.mean(h, -1, keepdims=True)
    cent = h - mean
    var = jnp.mean(cent * cent, -1, keepdims=True)
    return cent * lax.rsqrt(var + 1e-12) * gain + shift


def exact_gelu(value):
    return jax.nn.gelu(value, approximate=False)


def general_shards(
    tokens,
    out_grad,
    bucket,
    lengths,
    qkv_weight,
    qv_bias,
    out_weight,
    ff_in_weight,
    ff_in_bias,
    ff_out_weight,
    branch_bias,
    norm_gain,
    norm_bias,
):
    n_seq, rows_blk, width = tokens.shape
    blocks = lax.axis_size("blk")
    rank = lax.axis_index("blk")
    layers = qkv_weight.shape[0]
    local_width = qkv_weight.shape[3]
    heads_here = local_width // HEAD
    total_rows = n_seq * rows_blk
    scale = HEAD ** (-0.5)
    head_shape = (n_seq, rows_blk, heads_here, HEAD)
    qkv_full, out_full, ffin_full, ffout_full = (
        lax.all_gather(qkv_weight, ("blk", "batch"), axis=2, tiled=True),
        lax.all_gather(out_weight, ("blk", "batch"), axis=2, tiled=True),
        lax.all_gather(ff_in_weight, ("blk", "batch"), axis=1, tiled=True),
        lax.all_gather(ff_out_weight, ("blk", "batch"), axis=2, tiled=True),
    )
    local_pos = rank * rows_blk + jnp.arange(rows_blk, dtype=jnp.int32)
    row_ok = row_valid(bucket, lengths, local_pos).astype(jnp.float32).reshape(total_rows, 1)
    whole_pos = jnp.arange(blocks * rows_blk, dtype=jnp.int32)
    sub_bucket, sub_lengths = (bucket, lengths)

    def scores(query, keys, mask):
        found = (
            jnp.einsum("nqhe,nkhe->nhqk", query, keys, preferred_element_type=jnp.float32) * scale
        )
        return jnp.where(mask[:, None], found, NEG)

    x = tokens.astype(jnp.float32).reshape(total_rows, width)
    layer = 0
    xb = x.astype(jnp.bfloat16)
    triple = jnp.einsum("rd,cdk->crk", xb, qkv_full[layer], preferred_element_type=jnp.float32)
    query = (triple[0] + qv_bias[layer, 0]).astype(jnp.bfloat16).reshape(head_shape)
    keys = triple[1].astype(jnp.bfloat16).reshape(head_shape)
    values = (triple[2] + qv_bias[layer, 1]).astype(jnp.bfloat16).reshape(head_shape)
    pair = jnp.stack([keys, values])
    sub_query = query
    sub_pair = pair
    kept = lax.all_gather(sub_pair, "blk", axis=2, tiled=True)
    found = scores(sub_query, kept[0], seq_mask(sub_bucket, sub_lengths, local_pos, whole_pos))
    top = jnp.max(found, -1)
    sub_lse = top + jnp.log(jnp.sum(jnp.exp(found - top[..., None]), -1))
    weights = jnp.exp(found - sub_lse[..., None]).astype(jnp.bfloat16)
    sub_acc = jnp.einsum("nhqk,nkhe->nqhe", weights, kept[1], preferred_element_type=jnp.float32)
    lse = sub_lse
    acc = sub_acc
    att = acc.astype(jnp.bfloat16).reshape(total_rows, local_width)
    a_part = jnp.dot(att, out_full[layer], preferred_element_type=jnp.float32)
    branch = (
        lax.psum(a_part.astype(jnp.bfloat16), "tensor").astype(jnp.float32) + branch_bias[layer, 0]
    )
    upper_in = x + branch
    upper = layer_norm(upper_in, norm_gain[layer, 0], norm_bias[layer, 0])
    upper_b = upper.astype(jnp.bfloat16)
    pre = jnp.dot(upper_b, ffin_full[layer], preferred_element_type=jnp.float32) + ff_in_bias[layer]
    act = exact_gelu(pre).astype(jnp.bfloat16)
    f_part = jnp.dot(act, ffout_full[layer], preferred_element_type=jnp.float32)
    feed = (
        lax.psum(f_part.astype(jnp.bfloat16), "tensor").astype(jnp.float32) + branch_bias[layer, 1]
    )
    lower_in = upper + feed
    squares = [
        jnp.stack(
            [
                jnp.sum(row_ok * x * x),
                jnp.sum(row_ok * branch * branch),
                jnp.sum(row_ok * feed * feed),
            ]
        )
    ]
    saved = [(xb, query, pair, kept, lse, sub_lse, att, acc, upper_in, upper_b, pre, act, lower_in)]
    x = layer_norm(lower_in, norm_gain[layer, 1], norm_bias[layer, 1])
    output = x.astype(jnp.bfloat16).reshape(n_seq, rows_blk, width)
    grad = out_grad.astype(jnp.float32).reshape(total_rows, width)
    g_qkv, g_out, g_in, g_outf = ([], [], [], [])
    g_qvb, g_inb, g_branch, g_gain, g_shift = ([], [], [], [], [])
    for layer in reversed(range(layers)):
        xb, query, pair, kept, lse, sub_lse, att, acc, upper_in, upper_b, pre, act, lower_in = (
            saved[layer]
        )
        _, lower_back = jax.vjp(layer_norm, lower_in, norm_gain[layer, 1], norm_bias[layer, 1])
        d_lower, d_gain2, d_shift2 = lower_back(grad)
        d_feed = d_lower.astype(jnp.bfloat16)
        d_fbias = jnp.sum(d_feed.astype(jnp.float32), 0)
        g_outf.append(jnp.einsum("rf,rd->fd", act, d_feed, preferred_element_type=jnp.float32))
        d_act = jnp.einsum(
            "rd,fd->rf", d_feed, ffout_full[layer], preferred_element_type=jnp.float32
        )
        _, gelu_back = jax.vjp(exact_gelu, pre)
        d_pre = gelu_back(d_act)[0].astype(jnp.bfloat16)
        g_inb.append(jnp.sum(d_pre.astype(jnp.float32), 0))
        g_in.append(jnp.einsum("rd,rf->df", upper_b, d_pre, preferred_element_type=jnp.float32))
        ffn_part = jnp.einsum(
            "rf,df->rd", d_pre, ffin_full[layer], preferred_element_type=jnp.float32
        )
        d_upper = d_lower + lax.psum(ffn_part.astype(jnp.bfloat16), "tensor").astype(jnp.float32)
        _, upper_back = jax.vjp(layer_norm, upper_in, norm_gain[layer, 0], norm_bias[layer, 0])
        d_upper_in, d_gain1, d_shift1 = upper_back(d_upper)
        d_branch = d_upper_in.astype(jnp.bfloat16)
        d_abias = jnp.sum(d_branch.astype(jnp.float32), 0)
        g_out.append(jnp.einsum("rk,rd->kd", att, d_branch, preferred_element_type=jnp.float32))
        d_att = (
            jnp.einsum("rd,kd->rk", d_branch, out_full[layer], preferred_element_type=jnp.float32)
            .astype(jnp.bfloat16)
            .reshape(head_shape)
        )
        delta = jnp.einsum("nqhe,nqhe->nhq", d_att.astype(jnp.float32), acc)
        sub_query, sub_datt, sub_delta = (query, d_att, delta)
        block_keys = kept[0]
        block_found = scores(
            sub_query, block_keys, seq_mask(sub_bucket, sub_lengths, local_pos, whole_pos)
        )
        prob = jnp.exp(block_found - sub_lse[..., None])
        d_prob = jnp.einsum(
            "nqhe,nkhe->nhqk", sub_datt, kept[1], preferred_element_type=jnp.float32
        )
        d_scores = (prob * (d_prob - sub_delta[..., None])).astype(jnp.bfloat16)
        d_query = jnp.einsum(
            "nhqk,nkhe->nqhe", d_scores, block_keys, preferred_element_type=jnp.float32
        )
        d_keys = jnp.einsum(
            "nhqk,nqhe->nkhe", d_scores, sub_query, preferred_element_type=jnp.float32
        )
        d_values = jnp.einsum(
            "nhqk,nqhe->nkhe",
            prob.astype(jnp.bfloat16),
            sub_datt,
            preferred_element_type=jnp.float32,
        )
        sub_dq = d_query
        dpair_all = jnp.stack([d_keys * scale, d_values])
        sub_dpair = lax.psum_scatter(
            dpair_all.astype(jnp.bfloat16), "blk", scatter_dimension=2, tiled=True
        ).astype(jnp.float32)
        d_query, d_pair = (sub_dq, sub_dpair)
        dq_b = (d_query * scale).astype(jnp.bfloat16).reshape(total_rows, local_width)
        dk_b = d_pair[0].astype(jnp.bfloat16).reshape(total_rows, local_width)
        dv_b = d_pair[1].astype(jnp.bfloat16).reshape(total_rows, local_width)
        d_triple = jnp.stack([dq_b, dk_b, dv_b])
        g_qvb.append(
            jnp.stack([jnp.sum(dq_b.astype(jnp.float32), 0), jnp.sum(dv_b.astype(jnp.float32), 0)])
        )
        g_qkv.append(jnp.einsum("rd,crk->cdk", xb, d_triple, preferred_element_type=jnp.float32))
        attn_part = jnp.einsum(
            "crk,cdk->rd", d_triple, qkv_full[layer], preferred_element_type=jnp.float32
        )
        grad = d_upper_in + lax.psum(attn_part.astype(jnp.bfloat16), "tensor").astype(jnp.float32)
        g_branch.append(jnp.stack([d_abias, d_fbias]))
        g_gain.append(jnp.stack([d_gain1, d_gain2]))
        g_shift.append(jnp.stack([d_shift1, d_shift2]))

    def in_order(items):
        return jnp.stack(items[::-1])

    qkv_g, out_g, in_g, outf_g = (
        lax.psum_scatter(in_order(g_qkv), ("blk", "batch"), scatter_dimension=2, tiled=True),
        lax.psum_scatter(in_order(g_out), ("blk", "batch"), scatter_dimension=2, tiled=True),
        lax.psum_scatter(in_order(g_in), ("blk", "batch"), scatter_dimension=1, tiled=True),
        lax.psum_scatter(in_order(g_outf), ("blk", "batch"), scatter_dimension=2, tiled=True),
    )
    count = jnp.sum(row_ok)
    qvb_g, inb_g, branch_g, gain_g, shift_g, square_sums, count_all = lax.psum(
        (
            in_order(g_qvb),
            in_order(g_inb),
            in_order(g_branch),
            in_order(g_gain),
            in_order(g_shift),
            jnp.stack(squares),
            count,
        ),
        ("blk", "batch"),
    )
    rms = jnp.sqrt(square_sums / (count_all * width))
    tokens_grad = grad.reshape(n_seq, rows_blk, width)
    return (
        output,
        tokens_grad,
        qkv_g,
        qvb_g,
        out_g,
        in_g,
        inb_g,
        outf_g,
        branch_g,
        gain_g,
        shift_g,
        rms,
    )


MESH = pl.DeviceIdType.MESH
F32 = jnp.float32
BF16 = jnp.bfloat16
N_SEND = 48
N_RECV = 128


def dot_nn(a, b):
    return lax.dot_general(a, b, (((1,), (0,)), ((), ())), preferred_element_type=F32)


def dot_nt(a, b):
    return lax.dot_general(a, b, (((1,), (1,)), ((), ())), preferred_element_type=F32)


def dot_tn(a, b):
    return lax.dot_general(a, b, (((0,), (0,)), ((), ())), preferred_element_type=F32)


def slot_order(bucket_ref):
    first = jnp.where(bucket_ref[0] == 0, 0, jnp.where(bucket_ref[1] == 0, 1, 2))
    second = jnp.where(first == 0, 1, 0)
    third = jnp.where(first == 2, 1, 2)
    return first, second, third


class Net:
    def __init__(self, send_sems, recv_sems):
        self.send_sems, self.recv_sems = send_sems, recv_sems
        self.copies, self.n_recv = [], 0

    def slot(self):
        self.n_recv += 1
        assert self.n_recv <= N_RECV
        return self.n_recv - 1

    def send(self, src, dst, peer, slot=None):
        at = len(self.copies)
        if at >= N_SEND:
            self.copies[at - N_SEND].wait_send()
        copy = pltpu.make_async_remote_copy(
            src_ref=src,
            dst_ref=dst,
            send_sem=self.send_sems.at[at % N_SEND],
            recv_sem=self.recv_sems.at[self.slot() if slot is None else slot],
            device_id=peer,
            device_id_type=MESH,
        )
        copy.start()
        self.copies.append(copy)
        return copy

    def whole(self, ref, peer, slot):
        return pltpu.make_async_remote_copy(
            src_ref=ref,
            dst_ref=ref,
            send_sem=self.send_sems.at[0],
            recv_sem=self.recv_sems.at[slot],
            device_id=peer,
            device_id_type=MESH,
        )

    def finish(self):
        for copy in self.copies[-N_SEND:]:
            copy.wait_send()


class Gather:
    def __init__(self, net, view, at, near, split=False):
        self.net, self.view, self.near = net, view, near
        self.own, self.x, self.y, self.d, self.size = at
        self.half = self.size // 2
        self.slot = net.slot()
        self.late = net.slot() if split else self.slot

    def part(self, start, size):
        return self.view(pl.ds(pl.multiple_of(start, 16), size))

    def to_core(self, ref, late=False):
        self.net.send(ref, ref, self.near[2], self.late if late else self.slot)

    def issue(self, src=None):
        xnb, ynb, core = self.near
        to = self.part(self.own, self.size)
        src = to if src is None else src
        self.from_x = self.net.send(src, to, xnb)
        self.from_y = self.net.send(src, to, ynb)
        self.net.send(src, to, core, self.slot)

    def forward_x(self):
        xnb, ynb, core = self.near
        self.from_x.wait_recv()
        ref = self.part(self.x, self.half)
        self.first = self.net.send(ref, ref, ynb)
        self.to_core(self.part(self.x, self.size))

    def forward_y(self):
        xnb, ynb, core = self.near
        self.from_y.wait_recv()
        ref = self.part(self.y + self.half, self.half)
        self.second = self.net.send(ref, ref, xnb)
        self.to_core(self.part(self.y, self.size), True)

    def last(self):
        self.first.wait_recv()
        self.second.wait_recv()
        self.to_core(self.part(self.d, self.size), True)

    def ready(self):
        self.net.whole(self.part(0, 4 * self.size), self.near[2], self.slot).wait_recv()

    def ready_half(self, late):
        slot = self.late if late else self.slot
        self.net.whole(self.part(0, 2 * self.size), self.near[2], slot).wait_recv()


class Scatter:
    def __init__(self, net, refs, spot, near):
        self.net, self.spot, self.near = net, spot, near
        self.g, self.d, self.h, self.p1, self.s, self.p2 = refs
        self.rows = self.g.shape[3]
        self.half = self.rows // 2

    def core(self):
        c = self.spot[1]
        self.c1 = self.net.send(self.g.at[:, 1 - c], self.d, self.near[2])

    def first(self):
        yy, c, t = self.spot
        xnb, ynb, _ = self.near
        lo, hi = pl.ds(0, self.half), pl.ds(self.half, self.half)
        self.c1.wait_recv()
        for a in range(2):
            for b in range(2):
                self.h[a, b] = (self.g[a, c, b].astype(F32) + self.d[a, b].astype(F32)).astype(BF16)
        self.px = self.net.send(self.h.at[:, 1 - t, lo], self.p1.at[0], xnb)
        self.py = self.net.send(self.h.at[1 - yy, :, hi], self.p1.at[1], ynb)

    def second_x(self):
        yy, c, t = self.spot
        xnb, ynb, _ = self.near
        lo = pl.ds(0, self.half)
        self.px.wait_recv()
        self.s[0] = (self.h[1 - yy, t, lo].astype(F32) + self.p1[0, 1 - yy].astype(F32)).astype(BF16)
        self.qy = self.net.send(self.s.at[0], self.p2.at[0], ynb)

    def second_y(self):
        yy, c, t = self.spot
        xnb, ynb, _ = self.near
        hi = pl.ds(self.half, self.half)
        self.py.wait_recv()
        self.s[1] = (self.h[yy, 1 - t, hi].astype(F32) + self.p1[1, 1 - t].astype(F32)).astype(BF16)
        self.qx = self.net.send(self.s.at[1], self.p2.at[1], xnb)

    def result(self):
        yy, c, t = self.spot
        self.qy.wait_recv()
        self.qx.wait_recv()
        lo, hi = pl.ds(0, self.half), pl.ds(self.half, self.half)
        low = self.h[yy, t, lo].astype(F32) + self.p1[0, yy].astype(F32) + self.p2[0].astype(F32)
        high = self.h[yy, t, hi].astype(F32) + self.p1[1, t].astype(F32) + self.p2[1].astype(F32)
        return low, high


def fused_kernel(*refs):
    (
        bucket, lengths, tokens, out_grad, qkv_w, out_w, ffi_w, ffo_w, qv_bias, ffi_b, br_bias, gain, shift,
        out_hbm, tg_hbm, gq_hbm, go_hbm, gi_hbm, gf_hbm, vec_hbm, qvb_hbm,
        tok, cot, w_q, w_o, w_i, w_f, own_o, bias_r, own_q, xs, xs_t, q_r, kv_r, kv_a, p_a, p_b,
        att, att_r, ps, pr, xh1, rstd1, yb, act, gp, dh2, dfb, dab, df_t, yb_t, dpre, dh1, da_t,
        datt, datt_s, dkv_s, dkv_c, dkv_t, dkv_y, dtri, dx_p, dx_s, dx_1, dx_2, dx_t,
        sc_q, sc_o, sc_i, sc_f, z_o, z_i, z_f, t_o, t_i, t_f, vs, vr, vz, qs, qr,
        out_v, tg_v, gq_v, go_v, gi_v, gf_v, vec_v, qvb_v,
        local_sems, send_sems, recv_sems,
    ) = refs
    n_seq, n_rows, width = tok.shape
    blk_rows = ffi_w.shape[0]
    head_w = qkv_w.shape[2]
    pair_w = 2 * head_w
    heads = head_w // HEAD
    half, quart = n_rows // 2, n_rows // 4
    tile = 256
    n_tile = width // tile
    scale = HEAD ** (-0.5)

    r = lax.axis_index("blk")
    t = lax.axis_index("batch")
    z = lax.axis_index("tensor")
    yy, c = r // 2, r % 2
    pz, qz = z // 2, z % 2
    r1, r2 = r + 1 - 2 * c, (r + 2) % 4
    z1, z2 = z + 1 - 2 * qz, (z + 2) % 4
    core, xnb, ynb = (r1, t, z), (r, 1 - t, z), (r2, t, z)
    zn1, zn2 = (r, t, z1), (r, t, z2)
    peers = (zn2, zn1, xnb, ynb, core)
    near = (xnb, ynb, core)

    barrier = pltpu.get_barrier_semaphore()
    for peer in peers:
        pl.semaphore_signal(barrier, inc=1, device_id=peer, device_id_type=MESH)

    net = Net(send_sems, recv_sems)

    def block(rr, tt):
        return (rr * 2 + tt) * blk_rows

    at = (block(r, t), block(r, 1 - t), block(r2, t), block(r2, 1 - t), blk_rows)
    own = pl.ds(pl.multiple_of(block(r, t), 32), blk_rows)

    def gather(view, split=False):
        return Gather(net, view, at, near, split)

    ga_q = gather(lambda rows: w_q.at[rows])
    ga_o = [gather(lambda rows, k=k: w_o.at[k, rows]) for k in range(2)]
    ga_i = [gather(lambda rows, k=k: w_i.at[k, rows]) for k in range(2)]
    ga_f = [gather(lambda rows, k=k: w_f.at[k, rows], True) for k in range(2)]

    local = [
        pltpu.make_async_copy(src, dst, local_sems.at[k])
        for k, (src, dst) in enumerate(
            (
                (out_w, own_o),
                (tokens, tok),
                (qkv_w, own_q),
                (ffi_w, w_i.at[0, own]),
                (ffo_w, w_f.at[0, own]),
                (out_grad, cot),
            )
        )
    ]
    for copy in local:
        copy.start()
    stores = []

    def store(src, dst):
        copy = pltpu.make_async_copy(src, dst, local_sems.at[len(local) + len(stores)])
        copy.start()
        stores.append(copy)

    st = {}

    order = slot_order(bucket)

    def weights_first():
        local[2].wait()
        w_q[own] = jnp.concatenate([own_q[1], own_q[2], own_q[0]], 1)

    def out_weight_turn():
        local[0].wait()
        w_o[0, own] = jnp.transpose(own_o[...])

    def tokens_in_order():
        local[1].wait()
        for s in range(n_seq):
            xs[s * n_rows : (s + 1) * n_rows] = tok[order[s]]

    def enter():
        pl.semaphore_wait(barrier, len(peers))

    def far_weight(kind, src, buf):
        st["z" + kind] = net.send(src, buf.at[1, own], zn2)
        if kind == "i":
            st["zb"] = net.send(ffi_b, bias_r, zn2)

    def issue_second(kind, gather):
        st["z" + kind].wait_recv()
        gather.issue()

    def turn_x():
        xs_t[...] = jnp.transpose(xs[...])

    def keys_of(rr):
        return kv_a.at[pl.ds(pl.multiple_of(rr * n_rows, n_rows), n_rows)]

    def keys_values():
        ga_q.ready()
        bias = jnp.concatenate([jnp.zeros((1, head_w), F32), qv_bias[1:2, :]], 1)
        kv_r[...] = (dot_nn(xs[...], w_q[:, 0:pair_w]) + bias).astype(BF16)
        kv_a[pl.ds(pl.multiple_of(r * n_rows, n_rows), n_rows)] = kv_r[0:n_rows]
        st["kv_y"] = net.send(keys_of(r), keys_of(r), ynb)
        st["kv_c"] = [net.send(keys_of(r), keys_of(r), core)]

    def keys_pass():
        st["kv_y"].wait_recv()
        st["kv_c"].append(net.send(keys_of(r2), keys_of(r2), core))

    def queries():
        q_r[...] = (dot_nn(xs[...], w_q[:, pair_w:]) + qv_bias[0:1, :]).astype(BF16)

    lane_head = lax.broadcasted_iota(jnp.int32, (1, head_w), 1) // HEAD

    def of_head(value, h):
        return jnp.where(lane_head == h, value, jnp.zeros_like(value))

    def limit_of(s):
        index = order[s]
        return lengths[index, r], lengths[index, 0]

    own_half = pl.ds(pl.multiple_of(pz * half, half), half)
    other_half = pl.ds(pl.multiple_of((1 - pz) * half, half), half)
    key_at = lax.broadcasted_iota(jnp.int32, (1, n_rows), 1)

    def rows_at(s):
        return slice(s * n_rows, (s + 1) * n_rows)

    def few_at(s):
        return slice(s * half, (s + 1) * half)

    def attend(s):
        if s == 0:
            for copy in st["kv_c"]:
                copy.wait_recv()
            both, probs, key_ok = kv_a[...], p_a, None
        else:
            both, probs = kv_r[rows_at(s)], p_b.at[s - 1]
            key_ok = key_at < limit_of(s)[0]
        keys, values = both[:, 0:head_w], both[:, head_w:pair_w]
        query = q_r[rows_at(s)]
        total = jnp.zeros((n_rows, head_w), F32)
        for h in range(heads):
            score = dot_nt(of_head(query, h), keys) * scale
            if key_ok is not None:
                score = jnp.where(key_ok, score, NEG)
            e = jnp.exp(score - jnp.max(score, -1, keepdims=True))
            prob = e / jnp.sum(e, -1, keepdims=True)
            probs[h] = prob
            total = total + dot_nn(prob.astype(BF16), of_head(values, h))
        att[s] = total.astype(BF16)
        st["att", s] = net.send(att.at[s, other_half], att_r.at[s], zn2)

    def pair_send(k, s, value):
        ps[k, s] = value.astype(BF16)
        st["pair", k, s] = net.send(ps.at[k, s], pr.at[k, s], zn1)

    def pair_sum(k, s):
        st["pair", k, s].wait_recv()
        return ps[k, s].astype(F32) + pr[k, s].astype(F32)

    def ready(kind, gathers):
        if ("ready", kind) not in st:
            st["ready", kind] = True
            for gather in gathers:
                gather.ready()

    def project(s):
        ready("o", ga_o)
        st["att", s].wait_recv()
        pair_send(0, s, dot_nt(att[s, own_half], w_o[0]) + dot_nt(att_r[s], w_o[1]))

    vec = {k: jnp.zeros((1, width), F32) for k in range(12)}
    row_at = lax.broadcasted_iota(jnp.int32, (half, 1), 0)

    def row_ok(s):
        short, full = limit_of(s)
        place = row_at + pz * half
        ok = place + r * n_rows < full if s == 0 else place < short
        return ok.astype(F32)

    def tally(k, value):
        vec[k] = vec[k] + jnp.sum(value, 0, keepdims=True)

    def mean_of(value):
        return jnp.mean(value, -1, keepdims=True)

    def normed(h):
        cent = h - mean_of(h)
        rstd = lax.rsqrt(mean_of(cent * cent) + 1e-12)
        return cent * rstd, rstd

    def first_norm(s):
        here = few_at(s)
        x = xs[pl.ds(pl.multiple_of(s * n_rows + pz * half, half), half)].astype(F32)
        branch = pair_sum(0, s) + br_bias[0:1, :]
        ok = row_ok(s)
        tally(8, ok * (x * x))
        tally(9, ok * (branch * branch))
        tally(11, ok * jnp.ones((1, width), F32))
        hat, rstd = normed(x + branch)
        xh1[here] = hat
        rstd1[here] = rstd
        yb[here] = (hat * gain[0:1, :] + shift[0:1, :]).astype(BF16)

    def turn_y():
        yb_t[...] = jnp.transpose(yb[...])

    def hidden(s):
        if ("ready", "i") not in st:
            st["zb"].wait_recv()
            local[3].wait()
        ready("i", ga_i)
        here = few_at(s)
        for k in range(2):
            for n in range(n_tile):
                cols = slice(n * tile, (n + 1) * tile)
                bias = ffi_b[:, cols] if k == 0 else bias_r[:, cols]
                pre = dot_nn(yb[here], w_i[k, :, cols]) + bias
                phi = 0.5 * (1.0 + lax.erf(pre * (0.5**0.5)))
                act[k, here, cols] = (pre * phi).astype(BF16)
                gp[k, here, cols] = phi + pre * (jnp.exp(-0.5 * pre * pre) * 0.3989422804014327)

    def feed_out(late, s):
        if ("feed", late) not in st:
            st["feed", late] = True
            if not late:
                local[4].wait()
            for gather in ga_f:
                gather.ready_half(late)
        here = few_at(s)
        side = width // 2
        cols = pl.ds(pl.multiple_of(((1 - yy) if late else yy) * side, 128), side)
        value = dot_nt(act[0, here], w_f[0, cols]) + dot_nt(act[1, here], w_f[1, cols])
        ps[1, s, :, cols] = value.astype(BF16)
        st["feed", late, s] = net.send(ps.at[1, s, :, cols], pr.at[1, s, :, cols], zn1)

    def second_norm(s):
        here = few_at(s)
        if "cot" not in st:
            st["cot"] = True
            local[5].wait()
        for late in range(2):
            st["feed", late, s].wait_recv()
        feed = ps[1, s].astype(F32) + pr[1, s].astype(F32) + br_bias[1:2, :]
        tally(10, row_ok(s) * (feed * feed))
        hat, rstd = normed(xh1[here] * gain[0:1, :] + shift[0:1, :] + feed)
        out_v[s, own_half] = (hat * gain[1:2, :] + shift[1:2, :]).astype(BF16)
        g = cot[order[s], own_half].astype(F32)
        tally(1, g * hat)
        tally(2, g)
        g = g * gain[1:2, :]
        d = rstd * (g - mean_of(g) - hat * mean_of(g * hat))
        dh2[here] = d
        d = d.astype(BF16)
        dfb[here] = d
        tally(0, d.astype(F32))

    def feed_back(s):
        here = few_at(s)
        d = dfb[here]
        total = jnp.zeros((half, width), F32)
        for k in range(2):
            p = (dot_nn(d, w_f[k]) * gp[k, here]).astype(BF16)
            dpre[k, here] = p
            tally(3 + k, p.astype(F32))
            total = total + dot_nt(p, w_i[k])
        pair_send(2, s, total)

    quarter = pl.ds(pl.multiple_of(z * quart, quart), quart)
    quarter_2 = pl.ds(pl.multiple_of(z2 * quart, quart), quart)

    def out_far(s):
        here = out_v.at[s, quarter]
        st["out2", s] = net.send(here, here, zn2)

    def out_near(s):
        st["out2", s].wait_recv()
        there = out_v.at[s, quarter_2]
        st["out1", s] = net.send(there, there, zn1)

    def scatter(refs, k=None):
        views = refs if k is None else [ref.at[k] for ref in refs]
        return Scatter(net, views, (yy, c, t), near)

    rs_f = [scatter(sc_f, k) for k in range(2)]
    rs_i = [scatter(sc_i, k) for k in range(2)]
    rs_o = [scatter(sc_o, k) for k in range(2)]
    rs_q = scatter(sc_q)

    def grads(lhs, rhs, out):
        value = dot_nn(lhs, rhs).astype(BF16)
        for b in range(8):
            piece = value[b * blk_rows : (b + 1) * blk_rows]
            out[b // 4, (b // 2) % 2, b % 2] = piece

    def grads_wide(left, right, rs):
        for n in range(n_tile):
            cols = slice(n * tile, (n + 1) * tile)
            grads(left[...], right[:, cols], rs.g.at[:, :, :, :, cols])
        rs.core()

    def turn_d():
        df_t[...] = jnp.transpose(dfb[...])

    def grad_f(k):
        grads_wide(df_t, act.at[k], rs_f[k])

    def grad_i(k):
        grads_wide(yb_t, dpre.at[k], rs_i[k])

    def grad_o():
        da_t[...] = jnp.transpose(dab[...])
        rows_l = jnp.concatenate([att[s, own_half] for s in range(n_seq)], 0)
        rows_r = jnp.concatenate([att_r[s] for s in range(n_seq)], 0)
        grads(da_t[...], rows_r, rs_o[1].g)
        rs_o[1].core()
        grads(da_t[...], rows_l, rs_o[0].g)
        rs_o[0].core()

    def grad_q():
        grads(xs_t[...], dtri[...], rs_q.g)
        rs_q.core()

    def first_norm_back(s):
        here = few_at(s)
        hat = xh1[here]
        g = dh2[here] + pair_sum(2, s)
        tally(6, g * hat)
        tally(7, g)
        g = g * gain[0:1, :]
        d = rstd1[here] * (g - mean_of(g) - hat * mean_of(g * hat))
        dh1[here] = d
        d = d.astype(BF16)
        dab[here] = d
        tally(5, d.astype(F32))
        datt_s[s] = dot_nn(d, w_o[1]).astype(BF16)
        st["datt", s] = net.send(datt_s.at[s], datt.at[s, own_half], zn2)
        datt[s, own_half] = dot_nn(d, w_o[0]).astype(BF16)

    def vec_step(k):
        if k == 0:
            for n in range(12):
                vs[0, n : n + 1] = vec[n]
            vs[0, 12:16] = jnp.zeros((4, width), F32)
        else:
            st["vec"].wait_recv()
            vs[k] = vs[k - 1] + vr[k - 1]
        if k < 3:
            st["vec"] = net.send(vs.at[k], vr.at[k], (core, xnb, ynb)[k])
            return
        lane = lax.broadcasted_iota(jnp.int32, (1, width), 1)
        last = jnp.zeros((1, width), F32)
        for n in range(4):
            last = jnp.where(lane == n, jnp.sum(vs[3, 8 + n : 9 + n], 1, keepdims=True), last)
        vz[0, 0:3] = vs[3, 0:3]
        vz[0, 3:4] = vs[3, 4:5]
        vz[0, 4:7] = vs[3, 5:8]
        vz[0, 7:8] = last
        st["vec"] = net.send(vz.at[0], vz.at[1], zn2)

    def attend_back(s):
        st["datt", s].wait_recv()
        if s == 0:
            both, probs = kv_a[...], p_a
        else:
            both, probs = kv_r[rows_at(s)], p_b.at[s - 1]
        keys, values = both[:, 0:head_w], both[:, head_w:pair_w]
        query = q_r[rows_at(s)]
        d_att = datt[s]
        dq = jnp.zeros((n_rows, head_w), F32)
        dk = jnp.zeros(keys.shape, F32)
        dv = jnp.zeros(keys.shape, F32)
        for h in range(heads):
            prob = probs[h]
            d_h = of_head(d_att, h)
            dp = dot_nt(d_h, values)
            delta = jnp.sum(prob * dp, -1, keepdims=True)
            ds = (prob * (dp - delta)).astype(BF16)
            dq = dq + dot_nn(ds, of_head(keys, h))
            dk = dk + dot_tn(ds, of_head(query, h))
            dv = dv + dot_tn(prob.astype(BF16), d_h)
        dtri[rows_at(s), pair_w:] = (dq * scale).astype(BF16)
        both = jnp.concatenate([(dk * scale).astype(BF16), dv.astype(BF16)], 1)
        if s == 0:
            for a in range(4):
                dkv_s[a // 2, a % 2] = both[rows_at(a)]
            st["dkv1"] = net.send(dkv_s.at[:, 1 - c], dkv_c, core)
        else:
            dtri[rows_at(s), 0:pair_w] = both

    def keys_back():
        st["dkv1"].wait_recv()
        dkv_t[...] = (dkv_s[1 - yy, c].astype(F32) + dkv_c[1 - yy].astype(F32)).astype(BF16)
        st["dkv2"] = net.send(dkv_t, dkv_y, ynb)

    def dx_of(s):
        total = dot_nt(dtri[rows_at(s)], w_q[...])
        dx_p[s] = total
        for a in range(4):
            dx_s[a // 2, a % 2, s] = total[a * quart : (a + 1) * quart].astype(BF16)

    def half_rows(s):
        return pl.ds(pl.multiple_of(s * half + qz * quart, quart), quart)

    groups = {"b": (1, n_seq), "a": (0, 1)}

    def dx_first(group):
        lo, hi = groups[group]
        if group == "a":
            st["dkv2"].wait_recv()
            total = dkv_s[yy, c].astype(F32) + dkv_c[yy].astype(F32) + dkv_y[...].astype(F32)
            dtri[0:n_rows, 0:pair_w] = total.astype(BF16)
        for s in range(lo, hi):
            dx_of(s)
        st[group, 1] = net.send(dx_s.at[:, 1 - qz, lo:hi], dx_1.at[:, lo:hi], zn1)

    def dx_second(group):
        lo, hi = groups[group]
        st[group, 1].wait_recv()
        for s in range(lo, hi):
            dx_t[s] = (dx_p[s, quarter_2] + dx_1[1 - pz, s].astype(F32)).astype(BF16)
        st[group, 2] = net.send(dx_t.at[lo:hi], dx_2.at[lo:hi], zn2)

    def dx_third(group):
        lo, hi = groups[group]
        st[group, 2].wait_recv()
        for s in range(lo, hi):
            total = dx_p[s, quarter] + dx_1[pz, s].astype(F32) + dx_2[s].astype(F32)
            tg_v[s, quarter] = (total + dh1[half_rows(s)]).astype(BF16)
        here = tg_v.at[lo:hi, quarter]
        st[group, 3], st[group, 4] = net.send(here, here, zn2), net.send(here, here, zn1)

    def dx_last(group):
        lo, hi = groups[group]
        st[group, 3].wait_recv()
        there = tg_v.at[lo:hi, quarter_2]
        st[group, 5] = net.send(there, there, zn1)

    def bias_step(k):
        if k == 0:
            qs[0] = jnp.zeros(qs.shape[1:], F32)
            total = jnp.sum(dtri[...].astype(F32), 0, keepdims=True)
            qs[0, 0:1] = total[:, pair_w:]
            qs[0, 1:2] = total[:, head_w:pair_w]
        else:
            st["bias"].wait_recv()
            qs[k] = qs[k - 1] + qr[k - 1]
        st["bias"] = net.send(qs.at[k], qr.at[k], (core, xnb, ynb)[k])

    def to_z(kind, rs, buf, got):
        low, high = rs.result()
        n = low.shape[0]
        buf[0:n] = low.astype(BF16)
        buf[n : 2 * n] = high.astype(BF16)
        st["g" + kind] = net.send(buf, got, zn2)

    def put(kind, rs, out, to, got=None):
        low, high = rs.result()
        n = low.shape[0]
        if got is not None:
            st["g" + kind].wait_recv()
            low = low + got[0:n].astype(F32)
            high = high + got[n : 2 * n].astype(F32)
        out[0:n] = low
        out[n : 2 * n] = high
        store(out, to)

    def out_store():
        for s in range(n_seq):
            st["out1", s].wait_recv()
        store(out_v, out_hbm)

    def vec_store():
        st["vec"].wait_recv()
        vec_v[...] = vz[0] + vz[1]
        vec_v[3:4] = vs[3, 3:4] + vz[1, 3:4]
        store(vec_v, vec_hbm)

    def bias_store():
        st["bias"].wait_recv()
        qvb_v[...] = qs[2] + qr[2]
        store(qvb_v, qvb_hbm)

    def dx_store():
        for group in groups:
            lo, hi = groups[group]
            for k in (4, 5):
                st[group, k].wait_recv()
            store(tg_v.at[lo:hi], tg_hbm.at[lo:hi])

    weights_first()
    enter()
    ga_q.issue()
    out_weight_turn()
    ga_o[0].issue()
    far_weight("o", w_o.at[0, own], w_o)
    far_weight("f", ffo_w, w_f)
    ga_i[0].issue(ffi_w)
    ga_o[0].forward_y()
    ga_o[0].forward_x()
    ga_q.forward_y()
    ga_q.forward_x()
    issue_second("o", ga_o[1])
    far_weight("i", ffi_w, w_i)
    ga_i[0].forward_x()
    ga_i[0].forward_y()
    ga_o[0].last()
    ga_f[0].issue(ffo_w)
    ga_o[1].forward_x()
    ga_q.last()
    ga_o[1].forward_y()
    tokens_in_order()
    keys_values()
    queries()
    issue_second("i", ga_i[1])
    attend(1)
    issue_second("f", ga_f[1])
    attend(2)
    ga_o[1].last()
    keys_pass()
    attend(0)
    project(1)
    project(2)
    ga_i[1].forward_x()
    ga_f[0].forward_x()
    ga_i[0].last()
    ga_i[1].forward_y()
    ga_f[0].forward_y()
    ga_f[1].forward_x()
    ga_f[1].forward_y()
    project(0)
    ga_i[1].last()
    first_norm(1)
    hidden(1)
    feed_out(0, 1)
    first_norm(2)
    hidden(2)
    ga_f[0].last()
    feed_out(0, 2)
    ga_f[1].last()
    feed_out(1, 1)
    feed_out(1, 2)
    first_norm(0)
    hidden(0)
    turn_y()
    feed_out(0, 0)
    feed_out(1, 0)
    second_norm(1)
    feed_back(1)
    second_norm(2)
    out_far(2)
    feed_back(2)
    turn_x()
    second_norm(0)
    turn_d()
    grad_f(1)
    feed_back(0)
    grad_i(1)
    rs_f[1].first()
    out_far(0)
    grad_i(0)
    first_norm_back(1)
    rs_i[1].first()
    grad_f(0)
    first_norm_back(2)
    first_norm_back(0)
    grad_o()
    rs_f[1].second_y()
    out_near(0)
    out_far(1)
    vec_step(0)
    rs_f[1].second_x()
    attend_back(1)
    attend_back(2)
    dx_first("b")
    vec_step(1)
    attend_back(0)
    to_z("f", rs_f[1], t_f, z_f)
    keys_back()
    vec_step(2)
    rs_o[1].first()
    rs_f[0].first()
    rs_i[1].second_x()
    dx_first("a")
    dx_second("b")
    grad_q()
    rs_o[0].first()
    rs_o[1].second_x()
    vec_step(3)
    rs_q.first()
    out_near(2)
    rs_i[1].second_y()
    dx_second("a")
    dx_third("b")
    out_near(1)
    rs_i[0].first()
    rs_q.second_x()
    dx_third("a")
    rs_o[0].second_y()
    rs_o[0].second_x()
    rs_q.second_y()
    bias_step(0)
    bias_step(1)
    vec_store()
    rs_o[1].second_y()
    rs_f[0].second_x()
    to_z("i", rs_i[1], t_i, z_i)
    dx_last("b")
    dx_last("a")
    bias_step(2)
    rs_f[0].second_y()
    to_z("o", rs_o[1], t_o, z_o)
    rs_i[0].second_y()
    rs_i[0].second_x()
    put("q", rs_q, gq_v, gq_hbm)
    bias_store()
    out_store()
    put("f", rs_f[0], gf_v, gf_hbm, z_f)
    dx_store()
    put("i", rs_i[0], gi_v, gi_hbm, z_i)
    put("o", rs_o[0], go_v, go_hbm, z_o)

    for copy in stores:
        copy.wait()
    net.finish()


def finish_kernel(
    bucket,
    out_i,
    tg_i,
    gq_i,
    go_i,
    gi_i,
    gf_i,
    vec_i,
    qvb_i,
    out_o,
    tg_o,
    gq_o,
    qvb_o,
    go_o,
    gi_o,
    inb_o,
    gf_o,
    br_o,
    gain_o,
    shift_o,
    rms_o,
):
    order = slot_order(bucket)
    for s in range(3):
        at = jnp.where(order[0] == s, 0, jnp.where(order[1] == s, 1, 2))
        out_o[s] = out_i[at]
        tg_o[s] = tg_i[at].astype(F32)
    n = gq_o.shape[2]
    value = gq_i[...]
    for k, part in enumerate((1, 2, 0)):
        gq_o[part] = value[:, k * n : (k + 1) * n]
    go_o[...] = jnp.transpose(go_i[...])
    gi_o[...] = gi_i[...]
    gf_o[...] = gf_i[...]
    qvb_o[...] = qvb_i[0:2]
    inb_o[...] = vec_i[3:4]
    br_o[0:1] = vec_i[4:5]
    br_o[1:2] = vec_i[0:1]
    gain_o[0:1] = vec_i[5:6]
    gain_o[1:2] = vec_i[1:2]
    shift_o[0:1] = vec_i[6:7]
    shift_o[1:2] = vec_i[2:3]
    rms_o[...] = jnp.sqrt(vec_i[7:8, 0:3] / vec_i[7:8, 3:4])


def fused_shards(
    tokens,
    out_grad,
    bucket,
    lengths,
    qkv_weight,
    qv_bias,
    out_weight,
    ff_in_weight,
    ff_in_bias,
    ff_out_weight,
    branch_bias,
    norm_gain,
    norm_bias,
):
    n_seq, n_rows, width = tokens.shape
    blk_rows, head_w = qkv_weight.shape[2:]
    ff = ff_in_weight.shape[2]
    heads = head_w // HEAD
    rows = n_seq * n_rows
    half, quart = n_rows // 2, n_rows // 4
    few = n_seq * half
    keys = 4 * n_rows
    vmem = pl.BlockSpec(memory_space=pltpu.VMEM)
    smem = pl.BlockSpec(memory_space=pltpu.SMEM)
    hbm = pl.BlockSpec(memory_space=pl.ANY)

    def v(*shape, dtype=BF16):
        return pltpu.VMEM(shape, dtype)

    def f(*shape):
        return pltpu.VMEM(shape, F32)

    wide = {"q": (blk_rows, 3 * head_w), "o": (blk_rows, head_w), "i": (blk_rows, ff), "f": (blk_rows, ff)}

    def scatter_bufs(kind):
        n, cols = wide[kind]
        lead = () if kind == "q" else (2,)
        dims = ((2, 2, 2, n), (2, 2, n), (2, 2, n), (2, 2, n // 2), (2, n // 2), (2, n // 2))
        return [v(*lead, *dim, cols) for dim in dims]

    scratch = [
        v(n_seq, n_rows, width),
        v(n_seq, n_rows, width),
        v(width, 3 * head_w),
        v(2, width, head_w),
        v(2, width, ff),
        v(2, width, ff),
        v(head_w, blk_rows),
        f(1, ff),
        v(3, blk_rows, head_w),
        v(rows, width),
        v(width, rows),
        v(rows, head_w),
        v(rows, 2 * head_w),
        v(keys, 2 * head_w),
        f(heads, n_rows, keys),
        f(n_seq - 1, heads, n_rows, n_rows),
        v(n_seq, n_rows, head_w),
        v(n_seq, half, head_w),
        v(3, n_seq, half, width),
        v(3, n_seq, half, width),
        f(few, width),
        f(few, 1),
        v(few, width),
        v(2, few, ff),
        f(2, few, ff),
        f(few, width),
        v(few, width),
        v(few, width),
        v(width, few),
        v(width, few),
        v(2, few, ff),
        f(few, width),
        v(width, few),
        v(n_seq, n_rows, head_w),
        v(n_seq, half, head_w),
        v(2, 2, n_rows, 2 * head_w),
        v(2, n_rows, 2 * head_w),
        v(n_rows, 2 * head_w),
        v(n_rows, 2 * head_w),
        v(rows, 3 * head_w),
        f(n_seq, n_rows, width),
        v(2, 2, n_seq, quart, width),
        v(2, n_seq, quart, width),
        v(n_seq, quart, width),
        v(n_seq, quart, width),
        scatter_bufs("q"),
        scatter_bufs("o"),
        scatter_bufs("i"),
        scatter_bufs("f"),
        v(*wide["o"]),
        v(*wide["i"]),
        v(*wide["f"]),
        v(*wide["o"]),
        v(*wide["i"]),
        v(*wide["f"]),
        f(4, 16, width),
        f(3, 16, width),
        f(2, 8, width),
        f(3, 8, head_w),
        f(3, 8, head_w),
        v(n_seq, n_rows, width),
        v(n_seq, n_rows, width),
        f(*wide["q"]),
        f(*wide["o"]),
        f(*wide["i"]),
        f(*wide["f"]),
        f(8, width),
        f(8, head_w),
        pltpu.SemaphoreType.DMA((15,)),
        pltpu.SemaphoreType.DMA((N_SEND,)),
        pltpu.SemaphoreType.DMA((N_RECV,)),
    ]

    def shape(*dims, dtype=F32):
        return jax.ShapeDtypeStruct(dims, dtype)

    main_out = [
        shape(n_seq, n_rows, width, dtype=BF16),
        shape(n_seq, n_rows, width, dtype=BF16),
        shape(*wide["q"]),
        shape(*wide["o"]),
        shape(*wide["i"]),
        shape(*wide["f"]),
        shape(8, width),
        shape(8, head_w),
    ]
    results = pl.pallas_call(
        fused_kernel,
        out_shape=main_out,
        in_specs=[smem, smem] + [hbm] * 6 + [vmem] * 5,
        out_specs=[hbm] * 8,
        scratch_shapes=scratch,
        compiler_params=pltpu.CompilerParams(
            collective_id=0, has_side_effects=True, vmem_limit_bytes=60 * 2**20
        ),
        name="encoder_layer",
    )(
        bucket,
        lengths,
        tokens,
        out_grad,
        qkv_weight[0],
        out_weight[0],
        ff_in_weight[0],
        jnp.transpose(ff_out_weight[0]),
        qv_bias[0],
        ff_in_bias,
        branch_bias[0],
        norm_gain[0],
        norm_bias[0],
    )
    final = pl.pallas_call(
        finish_kernel,
        out_shape=[
            shape(n_seq, n_rows, width, dtype=BF16),
            shape(n_seq, n_rows, width),
            shape(3, blk_rows, head_w),
            shape(2, head_w),
            shape(head_w, blk_rows),
            shape(blk_rows, ff),
            shape(1, ff),
            shape(blk_rows, ff),
            shape(2, width),
            shape(2, width),
            shape(2, width),
            shape(1, 3),
        ],
        in_specs=[smem] + [vmem] * 8,
        out_specs=[vmem] * 12,
        compiler_params=pltpu.CompilerParams(vmem_limit_bytes=60 * 2**20),
        name="finish",
    )(bucket, *results)
    out, tg, gq, qvb, go, gi, inb, gf, br, gain, shift, rms = final
    return (
        out,
        tg,
        gq[None],
        qvb[None],
        go[None],
        gi[None],
        inb,
        jnp.transpose(gf)[None],
        br[None],
        gain[None],
        shift[None],
        rms,
    )


def solution(mesh):
    placed = (
        P("batch", "blk", None),
        P("batch", "blk", None),
        P("batch"),
        P("batch", None),
        P(None, None, ("blk", "batch"), "tensor"),
        P(None, None, "tensor"),
        P(None, "tensor", ("blk", "batch")),
        P(None, ("blk", "batch"), "tensor"),
        P(None, "tensor"),
        P(None, "tensor", ("blk", "batch")),
        P(),
        P(),
        P(),
    )
    sizes = (mesh.shape["blk"], mesh.shape["batch"], mesh.shape["tensor"])
    body = fused_shards if sizes == (4, 2, 4) else general_shards
    return jax.shard_map(
        body,
        mesh=mesh,
        in_specs=placed,
        out_specs=(
            P("batch", "blk", None),
            P("batch", "blk", None),
            P(None, None, ("blk", "batch"), "tensor"),
            P(None, None, "tensor"),
            P(None, "tensor", ("blk", "batch")),
            P(None, ("blk", "batch"), "tensor"),
            P(None, "tensor"),
            P(None, "tensor", ("blk", "batch")),
            P(),
            P(),
            P(),
            P(),
        ),
        check_vma=False,
    )
```
